32 devices in a mesh: blk: 8 (over z, y), col: 4 (over x, core).
Axes of the slice: x: 2, y: 2, z: 4, core: 2. Of those that a mesh axis runs over, the one named last changes fastest.
Arguments:
- y_start: float32 [128, 16384], P('col', 'blk')
- tile_real: bfloat16 [768, 256, 256], P('blk'), may hold values from 0 to 1, as said below
- tile_imag: bfloat16 [768, 256, 256], P('blk'), may hold values from -1 to 1, as said below
- tile_rows: int32 [768], P('blk'), may hold values from 0 to 7
- tile_slots: int32 [768], P('blk'), may hold values from 0 to 15, as said below
- fetch_pick: int32 [8, 8], P('blk'), may hold values from 0 to 7
Outputs:
- encodings: float32 [128, 16384], P('col', 'blk')
The draws below stay inside these ranges and needn't reach their ends.
Inputs may be any that keep to these rules, and one draw needn't show every extreme that they name: `tile_slots`: on each device the first 16 of its 96 tiles name an own row block (0 to 7); the others name 8 + p for an owning device p other than itself; every device reads from the devices 1, 4 and -1 places away along blk, modulo the axis. `tile_real`: entries are 0 or 1. `tile_imag`: entries are -1, 0 or 1, and never nonzero where tile_real is nonzero.
All inputs are finite; a program needn't handle non-finite values.
Results may differ from the reference program's by a relative error of at most 0.0031.
Values may be sent and summed in bfloat16 or wider, within the bound.
No kernel may reach another device: no remote copies, remote signals or barrier semaphores. Data moves between devices by JAX's collectives and lax.ppermute only.
A program may use at most 128 MiB of HBM per device.

```python
import math
import jax
import jax.numpy as jnp
from jax import lax

B = 256
VEC2 = 128
RB_DEV = 8
LOC_RB = 2
REM_RB = 10
STEPS = 4
TILES_DEV = 96
TILES = 768
BLOCKS = 64
NODES = 16384


def tile_pair(key):
    tiles_dev = (LOC_RB + REM_RB) * RB_DEV
    rows_local = jax.random.randint(jax.random.fold_in(key, 21), (TILES,), 0, RB_DEV)
    device = jnp.arange(TILES) // tiles_dev
    blocks = device * RB_DEV + rows_local
    keep = (jax.random.uniform(jax.random.fold_in(key, 31), (BLOCKS, B)) >= 0.0625).astype(jnp.float32)
    per_row = jnp.exp(jax.random.uniform(jax.random.fold_in(key, 32), (TILES,), minval=math.log(0.5), maxval=math.log(2.5)))
    density = per_row / B
    base = jax.random.fold_in(key, 33)

    def single(index):
        level = jax.random.uniform(jax.random.fold_in(base, index), (B, B))
        dense = density[index]
        alive = keep[blocks[index]][:, None]
        real_part = (level < 0.3 * dense).astype(jnp.float32) * alive
        upper = ((level >= 0.3 * dense) & (level < 0.65 * dense)).astype(jnp.float32)
        lower_part = ((level >= 0.65 * dense) & (level < dense)).astype(jnp.float32)
        return (real_part, (upper - lower_part) * alive)
    return lax.map(single, jnp.arange(TILES))


def draw_tile_real(key, part):
    return tile_pair(key)[0].astype(jnp.bfloat16)


def draw_tile_imag(key, part):
    return tile_pair(key)[1].astype(jnp.bfloat16)


def draw_tile_rows(key, part):
    return jax.random.randint(jax.random.fold_in(key, 21), (TILES,), 0, RB_DEV).astype(jnp.int32)


def draw_tile_slots(key, part):
    tiles_dev = (LOC_RB + REM_RB) * RB_DEV
    local_count = LOC_RB * RB_DEV
    nblk = BLOCKS // RB_DEV
    index = jnp.arange(TILES)
    device = index // tiles_dev
    within = index % tiles_dev
    own = jax.random.randint(jax.random.fold_in(key, 41), (TILES,), 0, RB_DEV)
    offset = jax.random.randint(jax.random.fold_in(key, 42), (TILES,), 1, nblk)
    later = within - local_count
    offset = jnp.where(later == 0, 1, jnp.where(later == 1, nblk // 2, jnp.where(later == 2, nblk - 1, offset)))
    owner = (device + offset) % nblk
    return jnp.where(within < local_count, own, RB_DEV + owner).astype(jnp.int32)


def draw_y_start(key, part):
    node_level = jnp.exp(jax.random.uniform(jax.random.fold_in(key, 61), (NODES,), minval=0.0, maxval=math.log(10.0)))
    vec_level = jnp.exp(jax.random.uniform(jax.random.fold_in(key, 62), (VEC2,), minval=0.0, maxval=math.log(10.0)))
    position = jnp.arange(NODES).astype(jnp.float32) / NODES
    noise = jax.random.normal(jax.random.fold_in(key, 63), (VEC2, NODES))
    ramp = jnp.exp(position * math.log(3.0))
    values = noise * vec_level[:, None] * (node_level * ramp)[None, :]
    return values.astype(jnp.float32)


def with_ends(values, key, low, top_value):
    place = [jax.random.randint(jax.random.fold_in(key, axis), (), 0, length) for axis, length in enumerate(values.shape)]
    main_axis = values.shape.index(max(values.shape))
    beside = place[:main_axis] + [(place[main_axis] + 1) % values.shape[main_axis]] + place[main_axis + 1:]
    return values.at[tuple(place)].set(low).at[tuple(beside)].set(top_value)


def setup_inputs(seed: int = 0) -> dict:
    seeds = jax.random.split(jax.random.key(seed), 7)
    return {
        "y_start": draw_y_start(jax.random.fold_in(seeds[6], 71), 0),
        "tile_real": draw_tile_real(jax.random.fold_in(seeds[6], 71), 0),
        "tile_imag": draw_tile_imag(jax.random.fold_in(seeds[6], 71), 0),
        "tile_rows": draw_tile_rows(jax.random.fold_in(seeds[6], 71), 0),
        "tile_slots": draw_tile_slots(jax.random.fold_in(seeds[6], 71), 0),
        "fetch_pick": with_ends(jax.random.randint(seeds[5], (BLOCKS // RB_DEV, BLOCKS // RB_DEV), 0, RB_DEV), jax.random.fold_in(seeds[5], 1), 0, RB_DEV - 1).astype(jnp.int32),
    }


center = 1.25
half_width = 0.75

def turn(values):
    pairs = values.reshape((values.shape[0] // 2, 2) + values.shape[1:])
    return jnp.stack([-pairs[:, 1], pairs[:, 0]], axis=1).reshape(values.shape)

def reference(y_start, tile_real, tile_imag, tile_rows, tile_slots, fetch_pick):
    nblk = BLOCKS // RB_DEV
    device = jnp.arange(TILES, dtype=jnp.int32) // TILES_DEV
    row_block = (device * RB_DEV + tile_rows).astype(jnp.int32)
    owner = jnp.clip(tile_slots - RB_DEV, 0, nblk - 1).astype(jnp.int32)
    remote_block = owner * RB_DEV + fetch_pick[device, owner]
    col_block = jnp.where(tile_slots < RB_DEV, device * RB_DEV + tile_slots, remote_block).astype(jnp.int32)
    real_dev = tile_real.reshape(nblk, TILES_DEV, B, B)
    imag_dev = tile_imag.reshape(nblk, TILES_DEV, B, B)
    rows_dev = row_block.reshape(nblk, TILES_DEV)
    cols_dev = col_block.reshape(nblk, TILES_DEV)

    def count(total, items):
        real_part, imag_part, rows_here = items
        counted = lax.optimization_barrier(jnp.sum(jnp.abs(real_part).astype(jnp.float32) + jnp.abs(imag_part).astype(jnp.float32), axis=2))
        return (total.at[rows_here].add(counted), None)
    degree, _ = lax.scan(count, jnp.zeros((BLOCKS, B), jnp.float32), (real_dev, imag_dev, rows_dev))
    scale = (1.0 / jnp.sqrt(jnp.maximum(degree, 1.0))).reshape(NODES)

    def operate(field):
        sent = (field * scale[None, :]).astype(jnp.bfloat16).reshape(VEC2, BLOCKS, B)

        def add_tiles(carry, items):
            real_part, imag_part, rows_here, cols_here = items
            picked = sent[:, cols_here, :].astype(jnp.float32)
            prod_re = jnp.einsum('ctb,tab->cta', picked, real_part.astype(jnp.float32))
            prod_im = jnp.einsum('ctb,tab->cta', picked, imag_part.astype(jnp.float32))
            return ((carry[0].at[:, rows_here, :].add(prod_re), carry[1].at[:, rows_here, :].add(prod_im)), None)
        empty = jnp.zeros((VEC2, BLOCKS, B), jnp.float32)
        (acc_re, acc_im), _ = lax.scan(add_tiles, (empty, empty), (real_dev, imag_dev, rows_dev, cols_dev))
        applied = (acc_re + turn(acc_im)).reshape(VEC2, NODES) * scale[None, :]
        return ((1.0 - center) * field - applied) / half_width
    previous = y_start
    current = operate(y_start)
    for step in range(1, STEPS):
        following = 2.0 * operate(current) - previous
        previous, current = (current, following)
    gram = jnp.dot(current, current.T, precision=lax.Precision.HIGHEST)
    gram = gram + turn(turn(gram).T).T
    lower = jnp.linalg.cholesky(gram)
    solved = jax.scipy.linalg.solve_triangular(lower, current, lower=True)
    return solved * math.sqrt(NODES)
```

```python
import functools
import math

import jax
import jax.numpy as jnp
from jax import lax
from jax.experimental import pallas as pl
from jax.experimental.pallas import tpu as pltpu
from jax.sharding import PartitionSpec as P

LOC_RB = 2
STEPS = 4
UNROLL = 4
CHUNK = 4
DIRECT = 8
MIB = 1 << 20

center = 1.25
half_width = 0.75

F32 = jnp.float32
BF16 = jnp.bfloat16
I32 = jnp.int32

VMEM = pl.BlockSpec(memory_space=pltpu.VMEM)
SMEM = pl.BlockSpec(memory_space=pltpu.SMEM)
ANY = pl.BlockSpec(memory_space=pl.ANY)

NT = (((1,), (1,)), ((), ()))
TN = (((0,), (0,)), ((), ()))


def sds(shape, dtype):
    return jax.ShapeDtypeStruct(shape, dtype)


def resident(x):
    return pltpu.with_memory_space_constraint(x, pltpu.VMEM)


def params(limit):
    return pltpu.CompilerParams(vmem_limit_bytes=limit * MIB)


def turn_rows(values):
    rows = values.shape[0]
    even = lax.broadcasted_iota(I32, values.shape, 0) % 2 == 0
    below = pltpu.roll(values, rows - 1, 0)
    above = pltpu.roll(values, 1, 0)
    return jnp.where(even, -below, above)


def turn_lanes(values):
    lanes = values.shape[1]
    even = lax.broadcasted_iota(I32, values.shape, 1) % 2 == 0
    after = pltpu.roll(values, lanes - 1, 1)
    before = pltpu.roll(values, 1, 1)
    return jnp.where(even, after, -before)


def tiles_kernel(
    near_count,
    direct,
    rows_ref,
    slots_ref,
    real_hbm,
    imag_hbm,
    real_ref,
    imag_ref,
    scale_ref,
    plan_ref,
    present_ref,
    first_ref,
    sems,
):
    tiles, order, _ = real_ref.shape
    rb_dev = present_ref.shape[0]
    me = lax.axis_index("blk")
    nblk = lax.axis_size("blk")
    slots = rb_dev + nblk
    chunks = tiles // CHUNK

    def copies(c):
        at = pl.ds(c * CHUNK, CHUNK)
        return (
            pltpu.make_async_copy(real_hbm.at[at], real_ref.at[at], sems.at[c, 0]),
            pltpu.make_async_copy(imag_hbm.at[at], imag_ref.at[at], sems.at[c, 1]),
        )

    for c in range(chunks):
        for copy in copies(c):
            copy.start()

    def clear(key, _):
        first_ref[key] = -1
        return _

    lax.fori_loop(0, rb_dev * slots, clear, 0)
    present_ref[...] = jnp.zeros_like(present_ref)

    def source(slot):
        owner = slot - rb_dev
        other = rb_dev + (owner ^ me if direct else owner)
        return jnp.where(slot < rb_dev, slot, other)

    def one(t, listed):
        row = rows_ref[t]
        slot = slots_ref[t]
        key = row * slots + slot
        seen = first_ref[key]
        real = real_ref[t]
        imag = imag_ref[t]
        present_ref[row] = present_ref[row] + (jnp.abs(real) + jnp.abs(imag))

        @pl.when(seen >= 0)
        def _():
            real_ref[seen] = real_ref[seen] + real_ref[t]
            imag_ref[seen] = imag_ref[seen] + imag_ref[t]

        @pl.when(seen < 0)
        def _():
            first_ref[key] = t
            plan_ref[listed] = t | (row << 8) | (source(slot) << 16)

        return listed + (seen < 0).astype(I32)

    def chunk(c, listed):
        for copy in copies(c):
            copy.wait()
        for j in range(CHUNK):
            listed = one(c * CHUNK + j, listed)
        return listed

    def pad(listed):
        short = (UNROLL - listed % UNROLL) % UNROLL
        for j in range(UNROLL - 1):

            @pl.when(j < short)
            def _():
                plan_ref[listed + j] = slots << 16

        return listed + short

    header = 2
    near = pad(lax.fori_loop(0, near_count // CHUNK, chunk, header - header))
    plan_ref[plan_ref.shape[0] - 2] = near // UNROLL
    both = pad(lax.fori_loop(near_count // CHUNK, chunks, chunk, near))
    plan_ref[plan_ref.shape[0] - 1] = both // UNROLL

    ones = jnp.ones((8, order), BF16)
    for r in range(rb_dev):
        degree = lax.dot_general(ones, present_ref[r], NT, preferred_element_type=F32)
        scale_ref[:, r * order : (r + 1) * order] = 1.0 / jnp.sqrt(jnp.maximum(degree, 1.0))


def tiles_call(rows, slots, real, imag, near_count, direct):
    tiles, order, _ = real.shape
    rb_dev = rows.shape[0] // 12
    nblk = lax.axis_size("blk")
    return pl.pallas_call(
        functools.partial(tiles_kernel, near_count, direct),
        name="tiles",
        out_shape=(
            pltpu.VMEM(real.shape, BF16),
            pltpu.VMEM(imag.shape, BF16),
            sds((8, rb_dev * order), F32),
            sds((tiles + 32,), I32),
        ),
        in_specs=[SMEM, SMEM, ANY, ANY],
        out_specs=(VMEM, VMEM, VMEM, SMEM),
        scratch_shapes=[
            pltpu.VMEM((rb_dev, order, order), BF16),
            pltpu.SMEM((rb_dev * (rb_dev + nblk),), I32),
            pltpu.SemaphoreType.DMA((tiles // CHUNK, 2)),
        ],
        compiler_params=params(12),
        cost_estimate=pl.CostEstimate(flops=1 << 28, bytes_accessed=2 * real.size * 2, transcendentals=0),
    )(rows, slots, real, imag)


def send_blocks(field, scale_ref, sent_ref, pick, out_refs):
    order = sent_ref.shape[2]
    for r in range(sent_ref.shape[0]):
        at = slice(r * order, (r + 1) * order)
        sent_ref[r] = (field[:, at] * scale_ref[0:1, at]).astype(BF16)
    if len(out_refs) == 1:
        out = out_refs[0]
        for p in range(out.shape[0]):
            out[p] = sent_ref[pick(p)]
    else:
        for s, out in enumerate(out_refs, 1):
            out[0] = sent_ref[pick(s)]


def first_kernel(pieces, y_ref, scale_ref, *refs):
    wanted = refs[:pieces]
    sent_ref, picks_ref = refs[pieces], refs[pieces + 1]
    out_refs = refs[pieces + 2 :]
    me = lax.axis_index("blk")
    if len(out_refs) == 1:
        for p in range(picks_ref.shape[0]):
            picks_ref[p] = wanted[0][0, p]
    else:
        picks_ref[0] = 0
        for s in range(1, len(out_refs) + 1):
            picks_ref[s] = wanted[s - 1][0, me]
    send_blocks(y_ref, scale_ref, sent_ref, lambda s: picks_ref[s], out_refs)


def multiply(plan_ref, lo, hi, real_ref, imag_ref, load, acc_re, acc_im):
    def group(i, _):
        done = []
        for j in range(UNROLL):
            code = plan_ref[i * UNROLL + j]
            tile = code & 255
            x = load(code >> 16)
            re = lax.dot_general(x, real_ref[tile], NT, preferred_element_type=F32)
            im = lax.dot_general(x, imag_ref[tile], NT, preferred_element_type=F32)
            done.append(((code >> 8) & 255, re, im))
        for row, re, im in done:
            acc_re[row] = acc_re[row] + re
            acc_im[row] = acc_im[row] + im
        return _

    lax.fori_loop(lo, hi, group, 0)


def near_kernel(plan_ref, real_ref, imag_ref, sent_ref, acc_re, acc_im, x_ref):
    rb_dev = sent_ref.shape[0]
    x_ref[0:rb_dev] = sent_ref[...]
    x_ref[rb_dev] = jnp.zeros_like(x_ref[rb_dev])
    acc_re[...] = jnp.zeros_like(acc_re)
    acc_im[...] = jnp.zeros_like(acc_im)
    end = plan_ref[plan_ref.shape[0] - 2]
    multiply(
        plan_ref, 0, end, real_ref, imag_ref, lambda c: x_ref[jnp.minimum(c, rb_dev)], acc_re, acc_im
    )


def step_kernel(pieces, step, rb_dev, *refs):
    (plan_ref, picks_ref, real_ref, imag_ref, scale_ref, near_re, near_im, now_ref, before_ref) = refs[:9]
    arrived = refs[9 : 9 + pieces]
    next_ref = refs[9 + pieces]
    last = step == STEPS - 1
    sent_ref = None if last else refs[10 + pieces]
    out_refs = refs[10 + pieces : -3] if last else refs[11 + pieces : -3]
    x_ref, acc_re, acc_im = refs[-3:]
    order = near_re.shape[2]
    if pieces == 1:
        count = arrived[0].shape[0]
        x_ref[0:count] = arrived[0][...]
    else:
        count = pieces + 1
        for s in range(1, count):
            x_ref[s] = arrived[s - 1][0]
    x_ref[count] = jnp.zeros_like(x_ref[count])
    acc_re[...] = near_re[...]
    acc_im[...] = near_im[...]
    lo = plan_ref[plan_ref.shape[0] - 2]
    hi = plan_ref[plan_ref.shape[0] - 1]
    multiply(plan_ref, lo, hi, real_ref, imag_ref, lambda c: x_ref[c - rb_dev], acc_re, acc_im)
    for r in range(rb_dev):
        at = slice(r * order, (r + 1) * order)
        now = now_ref[:, at]
        applied = scale_ref[0:1, at] * (acc_re[r] + turn_rows(acc_im[r]))
        moved = ((1.0 - center) * now - applied) / half_width
        next_ref[:, at] = moved if step == 0 else 2.0 * moved - before_ref[:, at]
    if not last:
        send_blocks(next_ref, scale_ref, sent_ref, lambda s: picks_ref[s], out_refs)


def all_rows(own_ref, arrived, all_ref):
    c = lax.axis_index("col")
    all_ref[c] = own_ref[...].astype(BF16)
    for s, ref in enumerate(arrived, 1):
        all_ref[c ^ s] = ref[...]
    n, group, rows = all_ref.shape
    return all_ref[...].reshape(n * group, rows)


def gram_kernel(own_ref, *refs):
    arrived, (gram_ref, all_ref, full_ref) = refs[:-3], refs[-3:]
    rows = all_rows(own_ref, arrived, all_ref)
    full_ref[...] = lax.dot_general(rows, rows, NT, preferred_element_type=F32)
    half = gram_ref.shape[0]
    even = full_ref[pl.ds(0, half, stride=2), :]
    odd = full_ref[pl.ds(1, half, stride=2), :]
    gram_ref[...] = even + turn_lanes(odd)


PANEL = 16


def factor_kernel(grams, nodes, own_ref, *refs):
    parts = refs[:grams]
    arrived = refs[grams:-4]
    out_ref, all_ref, work_ref, inverse_ref = refs[-4:]
    group = own_ref.shape[0]
    order = work_ref.shape[0]
    total = parts[0][...]
    for part in parts[1:]:
        total = total + part[...]
    half = total.shape[0]
    work_ref[pl.ds(0, half, stride=2), :] = total
    work_ref[pl.ds(1, half, stride=2), :] = -turn_lanes(total)
    row_at = lax.broadcasted_iota(I32, (order, order), 0)
    lane_at = lax.broadcasted_iota(I32, (order, order), 1)
    inverse_ref[...] = (row_at == lane_at).astype(F32)
    here = lax.broadcasted_iota(I32, (PANEL, 1), 0)
    for top in range(0, order, PANEL):
        panel = jnp.concatenate([work_ref[top : top + PANEL, :], inverse_ref[top : top + PANEL, :]], axis=1)
        for k in range(0, PANEL, 2):
            lane = top + k
            left = panel[:, lane : lane + 1]
            right = panel[:, lane + 1 : lane + 2]
            inv = lax.rsqrt(left[k : k + 1, :])
            inv2 = inv * inv
            below = here > k + 1
            pair = here - k
            a = jnp.where(below, left * inv2, 0.0)
            b = jnp.where(below, right * inv2, 0.0)
            keep = jnp.where((pair == 0) | (pair == 1), inv, 1.0)
            panel = panel * keep - (a * panel[k : k + 1, :] + b * panel[k + 1 : k + 2, :])
        inverse_ref[top : top + PANEL, :] = panel[:, order:]
        rest = top + PANEL
        if rest < order:
            cols = panel[:, 0:order]
            update = lax.dot_general(
                cols, panel, TN, precision=lax.Precision.HIGHEST, preferred_element_type=F32
            )
            work_ref[rest:, :] = work_ref[rest:, :] - update[rest:, :order]
            inverse_ref[rest:, :] = inverse_ref[rest:, :] - update[rest:, order:]
    c = lax.axis_index("col")
    mine = inverse_ref[pl.ds(pl.multiple_of(c * group, group), group), :]
    mine = mine * math.sqrt(nodes)
    high = mine.astype(BF16)
    low = (mine - high.astype(F32)).astype(BF16)
    rows = all_rows(own_ref, arrived, all_ref)
    both = lax.dot_general(
        jnp.concatenate([high, low], axis=0), rows, (((1,), (0,)), ((), ())), preferred_element_type=F32
    )
    own = own_ref[...]
    lost = own - own.astype(BF16).astype(F32)
    own_lanes = (
        lax.broadcasted_iota(I32, (order, group), 0)
        == lax.broadcasted_iota(I32, (order, group), 1) + c * group
    ).astype(BF16)
    square = jnp.dot(high, own_lanes, preferred_element_type=F32).astype(BF16)
    out_ref[...] = (
        both[:group] + both[group:] + jnp.dot(square, lost.astype(BF16), preferred_element_type=F32)
    )


def to_partner(x, axis, mask):
    n = lax.axis_size(axis)
    return lax.ppermute(x, axis, [(i, i ^ mask) for i in range(n)])


def per_device(y_start, tile_real, tile_imag, tile_rows, tile_slots, fetch_pick):
    group, rows = y_start.shape
    tiles, order, _ = tile_real.shape
    rb_dev = rows // order
    nblk = lax.axis_size("blk")
    ncol = lax.axis_size("col")
    direct = nblk <= DIRECT
    pieces = nblk - 1 if direct else 1
    near_count = LOC_RB * rb_dev

    if direct:
        wanted = [to_partner(fetch_pick, "blk", s) for s in range(1, nblk)]
        block_shapes = [sds((1, group, order), BF16)] * pieces
        sources = nblk
    else:
        wanted = [lax.all_to_all(fetch_pick, "blk", split_axis=1, concat_axis=1, tiled=True)]
        block_shapes = [sds((nblk, group, order), BF16)]
        sources = nblk

    def exchange(blocks):
        if direct:
            return [to_partner(b, "blk", s) for s, b in enumerate(blocks, 1)]
        return [lax.all_to_all(blocks[0], "blk", split_axis=0, concat_axis=0, tiled=True)]

    real, imag, scale, plan = tiles_call(tile_rows, tile_slots, tile_real, tile_imag, near_count, direct)

    out = pl.pallas_call(
        functools.partial(first_kernel, pieces),
        name="first",
        out_shape=(sds((rb_dev, group, order), BF16), sds((nblk,), I32), *block_shapes),
        in_specs=[VMEM, VMEM] + [SMEM] * pieces,
        out_specs=(VMEM, SMEM) + (VMEM,) * len(block_shapes),
        compiler_params=params(8),
    )(y_start, scale, *wanted)
    sent, picks, blocks = out[0], out[1], out[2:]

    acc = sds((rb_dev, group, order), F32)
    previous, current = y_start, y_start
    for step in range(STEPS):
        arrived = exchange(blocks)
        near_re, near_im = pl.pallas_call(
            near_kernel,
            name="near",
            out_shape=(acc, acc),
            in_specs=[SMEM, VMEM, VMEM, VMEM],
            out_specs=(VMEM, VMEM),
            scratch_shapes=[pltpu.VMEM((rb_dev + 1, group, order), BF16)],
            compiler_params=params(8),
            cost_estimate=pl.CostEstimate(flops=1 << 28, bytes_accessed=1 << 20, transcendentals=0),
        )(plan, resident(real), resident(imag), sent)
        last = step == STEPS - 1
        more = () if last else (sds((rb_dev, group, order), BF16), *block_shapes)
        out = pl.pallas_call(
            functools.partial(step_kernel, pieces, step, rb_dev),
            name="step",
            out_shape=(sds((group, rows), F32), *more),
            in_specs=[SMEM, SMEM] + [VMEM] * (7 + len(arrived)),
            out_specs=(VMEM,) * (1 + len(more)),
            scratch_shapes=[
                pltpu.VMEM((sources + 1, group, order), BF16),
                pltpu.VMEM((rb_dev, group, order), F32),
                pltpu.VMEM((rb_dev, group, order), F32),
            ],
            compiler_params=params(12),
        )(plan, picks, resident(real), resident(imag), scale, near_re, near_im, current, previous, *arrived)
        previous, current = current, out[0]
        if not last:
            sent, blocks = out[1], out[2:]

    rounded = current.astype(BF16)
    others = [to_partner(rounded, "col", s) for s in range(1, ncol)]
    vectors = group * ncol
    part = pl.pallas_call(
        gram_kernel,
        name="gram",
        out_shape=sds((vectors // 2, vectors), F32),
        in_specs=[VMEM] * (1 + len(others)),
        out_specs=VMEM,
        scratch_shapes=[pltpu.VMEM((ncol, group, rows), BF16), pltpu.VMEM((vectors, vectors), F32)],
        compiler_params=params(12),
    )(current, *others)
    wide = 1
    while wide < nblk:
        span = min(nblk // wide, DIRECT)
        parts = [part] + [to_partner(part, "blk", s * wide) for s in range(1, span)]
        wide *= span
        if wide < nblk:
            part = sum(parts[1:], parts[0])
    return pl.pallas_call(
        functools.partial(factor_kernel, len(parts), rows * nblk),
        name="factor",
        out_shape=sds((group, rows), F32),
        in_specs=[VMEM] * (1 + len(parts) + len(others)),
        out_specs=VMEM,
        scratch_shapes=[
            pltpu.VMEM((ncol, group, rows), BF16),
            pltpu.VMEM((vectors, vectors), F32),
            pltpu.VMEM((vectors, vectors), F32),
        ],
        compiler_params=params(12),
    )(current, *parts, *others)


def solution(mesh):
    return jax.shard_map(
        per_device,
        mesh=mesh,
        in_specs=(
            P("col", "blk"),
            P("blk", None, None),
            P("blk", None, None),
            P("blk"),
            P("blk"),
            P("blk", None),
        ),
        out_specs=P("col", "blk"),
        check_vma=False,
    )
```

```python
import functools
import math

import jax
import jax.numpy as jnp
from jax import lax
from jax.experimental import pallas as pl
from jax.experimental.pallas import tpu as pltpu
from jax.sharding import PartitionSpec as P

LOC_RB = 2
STEPS = 4
UNROLL = 4
CHUNK = 4
DIRECT = 1
MIB = 1 << 20

center = 1.25
half_width = 0.75

F32 = jnp.float32
BF16 = jnp.bfloat16
I32 = jnp.int32

VMEM = pl.BlockSpec(memory_space=pltpu.VMEM)
SMEM = pl.BlockSpec(memory_space=pltpu.SMEM)
ANY = pl.BlockSpec(memory_space=pl.ANY)

NT = (((1,), (1,)), ((), ()))
TN = (((0,), (0,)), ((), ()))


def sds(shape, dtype):
    return jax.ShapeDtypeStruct(shape, dtype)


def resident(x):
    return pltpu.with_memory_space_constraint(x, pltpu.VMEM)


def params(limit):
    return pltpu.CompilerParams(vmem_limit_bytes=limit * MIB)


def turn_rows(values):
    rows = values.shape[0]
    even = lax.broadcasted_iota(I32, values.shape, 0) % 2 == 0
    below = pltpu.roll(values, rows - 1, 0)
    above = pltpu.roll(values, 1, 0)
    return jnp.where(even, -below, above)


def turn_lanes(values):
    lanes = values.shape[1]
    even = lax.broadcasted_iota(I32, values.shape, 1) % 2 == 0
    after = pltpu.roll(values, lanes - 1, 1)
    before = pltpu.roll(values, 1, 1)
    return jnp.where(even, after, -before)


def tiles_kernel(
    near_count,
    direct,
    rows_ref,
    slots_ref,
    real_hbm,
    imag_hbm,
    real_ref,
    imag_ref,
    scale_ref,
    plan_ref,
    present_ref,
    first_ref,
    sems,
):
    tiles, order, _ = real_ref.shape
    rb_dev = present_ref.shape[0]
    me = lax.axis_index("blk")
    nblk = lax.axis_size("blk")
    slots = rb_dev + nblk
    chunks = tiles // CHUNK

    def copies(c):
        at = pl.ds(c * CHUNK, CHUNK)
        return (
            pltpu.make_async_copy(real_hbm.at[at], real_ref.at[at], sems.at[c, 0]),
            pltpu.make_async_copy(imag_hbm.at[at], imag_ref.at[at], sems.at[c, 1]),
        )

    for c in range(chunks):
        for copy in copies(c):
            copy.start()

    def clear(key, _):
        first_ref[key] = -1
        return _

    lax.fori_loop(0, rb_dev * slots, clear, 0)
    present_ref[...] = jnp.zeros_like(present_ref)

    def source(slot):
        owner = slot - rb_dev
        other = rb_dev + (owner ^ me if direct else owner)
        return jnp.where(slot < rb_dev, slot, other)

    def one(t, listed):
        row = rows_ref[t]
        slot = slots_ref[t]
        key = row * slots + slot
        seen = first_ref[key]
        real = real_ref[t]
        imag = imag_ref[t]
        present_ref[row] = present_ref[row] + (jnp.abs(real) + jnp.abs(imag))

        @pl.when(seen >= 0)
        def _():
            real_ref[seen] = real_ref[seen] + real_ref[t]
            imag_ref[seen] = imag_ref[seen] + imag_ref[t]

        @pl.when(seen < 0)
        def _():
            first_ref[key] = t
            plan_ref[listed] = t | (row << 8) | (source(slot) << 16)

        return listed + (seen < 0).astype(I32)

    def chunk(c, listed):
        for copy in copies(c):
            copy.wait()
        for j in range(CHUNK):
            listed = one(c * CHUNK + j, listed)
        return listed

    def pad(listed):
        short = (UNROLL - listed % UNROLL) % UNROLL
        for j in range(UNROLL - 1):

            @pl.when(j < short)
            def _():
                plan_ref[listed + j] = slots << 16

        return listed + short

    header = 2
    near = pad(lax.fori_loop(0, near_count // CHUNK, chunk, header - header))
    plan_ref[plan_ref.shape[0] - 2] = near // UNROLL
    both = pad(lax.fori_loop(near_count // CHUNK, chunks, chunk, near))
    plan_ref[plan_ref.shape[0] - 1] = both // UNROLL

    ones = jnp.ones((8, order), BF16)
    for r in range(rb_dev):
        degree = lax.dot_general(ones, present_ref[r], NT, preferred_element_type=F32)
        scale_ref[:, r * order : (r + 1) * order] = 1.0 / jnp.sqrt(jnp.maximum(degree, 1.0))


def tiles_call(rows, slots, real, imag, near_count, direct):
    tiles, order, _ = real.shape
    rb_dev = rows.shape[0] // 12
    nblk = lax.axis_size("blk")
    return pl.pallas_call(
        functools.partial(tiles_kernel, near_count, direct),
        name="tiles",
        out_shape=(
            pltpu.VMEM(real.shape, BF16),
            pltpu.VMEM(imag.shape, BF16),
            sds((8, rb_dev * order), F32),
            sds((tiles + 32,), I32),
        ),
        in_specs=[SMEM, SMEM, ANY, ANY],
        out_specs=(VMEM, VMEM, VMEM, SMEM),
        scratch_shapes=[
            pltpu.VMEM((rb_dev, order, order), BF16),
            pltpu.SMEM((rb_dev * (rb_dev + nblk),), I32),
            pltpu.SemaphoreType.DMA((tiles // CHUNK, 2)),
        ],
        compiler_params=params(12),
        cost_estimate=pl.CostEstimate(flops=1 << 28, bytes_accessed=2 * real.size * 2, transcendentals=0),
    )(
        rows,
        slots,
        pltpu.with_memory_space_constraint(real, pltpu.HBM),
        pltpu.with_memory_space_constraint(imag, pltpu.HBM),
    )


def send_blocks(field, scale_ref, sent_ref, pick, out_refs):
    order = sent_ref.shape[2]
    for r in range(sent_ref.shape[0]):
        at = slice(r * order, (r + 1) * order)
        sent_ref[r] = (field[:, at] * scale_ref[0:1, at]).astype(BF16)
    if len(out_refs) == 1:
        out = out_refs[0]
        for p in range(out.shape[0]):
            out[p] = sent_ref[pick(p)]
    else:
        for s, out in enumerate(out_refs, 1):
            out[0] = sent_ref[pick(s)]


def first_kernel(pieces, y_ref, scale_ref, *refs):
    wanted = refs[:pieces]
    sent_ref, picks_ref = refs[pieces], refs[pieces + 1]
    out_refs = refs[pieces + 2 :]
    me = lax.axis_index("blk")
    if len(out_refs) == 1:
        for p in range(picks_ref.shape[0]):
            picks_ref[p] = wanted[0][0, p]
    else:
        picks_ref[0] = 0
        for s in range(1, len(out_refs) + 1):
            picks_ref[s] = wanted[s - 1][0, me]
    send_blocks(y_ref, scale_ref, sent_ref, lambda s: picks_ref[s], out_refs)


def multiply(plan_ref, lo, hi, real_ref, imag_ref, load, acc_re, acc_im):
    def group(i, _):
        done = []
        for j in range(UNROLL):
            code = plan_ref[i * UNROLL + j]
            tile = code & 255
            x = load(code >> 16)
            re = lax.dot_general(x, real_ref[tile], NT, preferred_element_type=F32)
            im = lax.dot_general(x, imag_ref[tile], NT, preferred_element_type=F32)
            done.append(((code >> 8) & 255, re, im))
        for row, re, im in done:
            acc_re[row] = acc_re[row] + re
            acc_im[row] = acc_im[row] + im
        return _

    lax.fori_loop(lo, hi, group, 0)


def near_kernel(plan_ref, real_ref, imag_ref, sent_ref, acc_re, acc_im, x_ref):
    rb_dev = sent_ref.shape[0]
    x_ref[0:rb_dev] = sent_ref[...]
    x_ref[rb_dev] = jnp.zeros_like(x_ref[rb_dev])
    acc_re[...] = jnp.zeros_like(acc_re)
    acc_im[...] = jnp.zeros_like(acc_im)
    end = plan_ref[plan_ref.shape[0] - 2]
    multiply(
        plan_ref, 0, end, real_ref, imag_ref, lambda c: x_ref[jnp.minimum(c, rb_dev)], acc_re, acc_im
    )


def step_kernel(pieces, step, rb_dev, *refs):
    (plan_ref, picks_ref, real_ref, imag_ref, scale_ref, near_re, near_im, now_ref, before_ref) = refs[:9]
    arrived = refs[9 : 9 + pieces]
    next_ref = refs[9 + pieces]
    last = step == STEPS - 1
    sent_ref = None if last else refs[10 + pieces]
    out_refs = refs[10 + pieces : -3] if last else refs[11 + pieces : -3]
    x_ref, acc_re, acc_im = refs[-3:]
    order = near_re.shape[2]
    if pieces == 1:
        count = arrived[0].shape[0]
        x_ref[0:count] = arrived[0][...]
    else:
        count = pieces + 1
        for s in range(1, count):
            x_ref[s] = arrived[s - 1][0]
    x_ref[count] = jnp.zeros_like(x_ref[count])
    acc_re[...] = near_re[...]
    acc_im[...] = near_im[...]
    lo = plan_ref[plan_ref.shape[0] - 2]
    hi = plan_ref[plan_ref.shape[0] - 1]
    multiply(plan_ref, lo, hi, real_ref, imag_ref, lambda c: x_ref[c - rb_dev], acc_re, acc_im)
    for r in range(rb_dev):
        at = slice(r * order, (r + 1) * order)
        now = now_ref[:, at]
        applied = scale_ref[0:1, at] * (acc_re[r] + turn_rows(acc_im[r]))
        moved = ((1.0 - center) * now - applied) / half_width
        next_ref[:, at] = moved if step == 0 else 2.0 * moved - before_ref[:, at]
    if not last:
        send_blocks(next_ref, scale_ref, sent_ref, lambda s: picks_ref[s], out_refs)


def all_rows(own_ref, arrived, all_ref):
    c = lax.axis_index("col")
    all_ref[c] = own_ref[...].astype(BF16)
    for s, ref in enumerate(arrived, 1):
        all_ref[c ^ s] = ref[...]
    n, group, rows = all_ref.shape
    return all_ref[...].reshape(n * group, rows)


def gram_kernel(own_ref, *refs):
    arrived, (gram_ref, all_ref, full_ref) = refs[:-3], refs[-3:]
    rows = all_rows(own_ref, arrived, all_ref)
    full_ref[...] = lax.dot_general(rows, rows, NT, preferred_element_type=F32)
    half = gram_ref.shape[0]
    even = full_ref[pl.ds(0, half, stride=2), :]
    odd = full_ref[pl.ds(1, half, stride=2), :]
    gram_ref[...] = even + turn_lanes(odd)


PANEL = 16


def factor_kernel(nodes, own_ref, parts_ref, *refs):
    arrived = refs[:-4]
    out_ref, all_ref, work_ref, inverse_ref = refs[-4:]
    group = own_ref.shape[0]
    order = work_ref.shape[0]
    total = parts_ref[0]
    for p in range(1, parts_ref.shape[0]):
        total = total + parts_ref[p]
    half = total.shape[0]
    work_ref[pl.ds(0, half, stride=2), :] = total
    work_ref[pl.ds(1, half, stride=2), :] = -turn_lanes(total)
    row_at = lax.broadcasted_iota(I32, (order, order), 0)
    lane_at = lax.broadcasted_iota(I32, (order, order), 1)
    inverse_ref[...] = (row_at == lane_at).astype(F32)
    here = lax.broadcasted_iota(I32, (PANEL, 1), 0)
    for top in range(0, order, PANEL):
        panel = jnp.concatenate([work_ref[top : top + PANEL, :], inverse_ref[top : top + PANEL, :]], axis=1)
        for k in range(0, PANEL, 2):
            lane = top + k
            left = panel[:, lane : lane + 1]
            right = panel[:, lane + 1 : lane + 2]
            inv = lax.rsqrt(left[k : k + 1, :])
            inv2 = inv * inv
            below = here > k + 1
            pair = here - k
            a = jnp.where(below, left * inv2, 0.0)
            b = jnp.where(below, right * inv2, 0.0)
            keep = jnp.where((pair == 0) | (pair == 1), inv, 1.0)
            panel = panel * keep - (a * panel[k : k + 1, :] + b * panel[k + 1 : k + 2, :])
        inverse_ref[top : top + PANEL, :] = panel[:, order:]
        rest = top + PANEL
        if rest < order:
            cols = panel[:, 0:order]
            update = lax.dot_general(
                cols, panel, TN, precision=lax.Precision.HIGHEST, preferred_element_type=F32
            )
            work_ref[rest:, :] = work_ref[rest:, :] - update[rest:, :order]
            inverse_ref[rest:, :] = inverse_ref[rest:, :] - update[rest:, order:]
    c = lax.axis_index("col")
    mine = inverse_ref[pl.ds(pl.multiple_of(c * group, group), group), :]
    mine = mine * math.sqrt(nodes)
    high = mine.astype(BF16)
    low = (mine - high.astype(F32)).astype(BF16)
    rows = all_rows(own_ref, arrived, all_ref)
    both = lax.dot_general(
        jnp.concatenate([high, low], axis=0), rows, (((1,), (0,)), ((), ())), preferred_element_type=F32
    )
    own = own_ref[...]
    lost = own - own.astype(BF16).astype(F32)
    own_lanes = (
        lax.broadcasted_iota(I32, (order, group), 0)
        == lax.broadcasted_iota(I32, (order, group), 1) + c * group
    ).astype(BF16)
    square = jnp.dot(high, own_lanes, preferred_element_type=F32).astype(BF16)
    out_ref[...] = (
        both[:group] + both[group:] + jnp.dot(square, lost.astype(BF16), preferred_element_type=F32)
    )


def to_partner(x, axis, mask):
    n = lax.axis_size(axis)
    return lax.ppermute(x, axis, [(i, i ^ mask) for i in range(n)])


def per_device(y_start, tile_real, tile_imag, tile_rows, tile_slots, fetch_pick):
    group, rows = y_start.shape
    tiles, order, _ = tile_real.shape
    rb_dev = rows // order
    nblk = lax.axis_size("blk")
    ncol = lax.axis_size("col")
    direct = nblk <= DIRECT
    pieces = nblk - 1 if direct else 1
    near_count = LOC_RB * rb_dev

    if direct:
        wanted = [to_partner(fetch_pick, "blk", s) for s in range(1, nblk)]
        block_shapes = [sds((1, group, order), BF16)] * pieces
        sources = nblk
    else:
        wanted = [lax.all_to_all(fetch_pick, "blk", split_axis=1, concat_axis=1, tiled=True)]
        block_shapes = [sds((nblk, group, order), BF16)]
        sources = nblk

    def exchange(blocks):
        if direct:
            return [to_partner(b, "blk", s) for s, b in enumerate(blocks, 1)]
        return [lax.all_to_all(blocks[0], "blk", split_axis=0, concat_axis=0, tiled=True)]

    real, imag, scale, plan = tiles_call(tile_rows, tile_slots, tile_real, tile_imag, near_count, direct)

    out = pl.pallas_call(
        functools.partial(first_kernel, pieces),
        name="first",
        out_shape=(sds((rb_dev, group, order), BF16), sds((nblk,), I32), *block_shapes),
        in_specs=[VMEM, VMEM] + [SMEM] * pieces,
        out_specs=(VMEM, SMEM) + (VMEM,) * len(block_shapes),
        compiler_params=params(8),
    )(y_start, scale, *wanted)
    sent, picks, blocks = out[0], out[1], out[2:]

    acc = sds((rb_dev, group, order), F32)
    previous, current = y_start, y_start
    for step in range(STEPS):
        arrived = exchange(blocks)
        near_re, near_im = pl.pallas_call(
            near_kernel,
            name="near",
            out_shape=(acc, acc),
            in_specs=[SMEM, VMEM, VMEM, VMEM],
            out_specs=(VMEM, VMEM),
            scratch_shapes=[pltpu.VMEM((rb_dev + 1, group, order), BF16)],
            compiler_params=params(8),
            cost_estimate=pl.CostEstimate(flops=1 << 28, bytes_accessed=1 << 20, transcendentals=0),
        )(plan, resident(real), resident(imag), sent)
        last = step == STEPS - 1
        more = () if last else (sds((rb_dev, group, order), BF16), *block_shapes)
        out = pl.pallas_call(
            functools.partial(step_kernel, pieces, step, rb_dev),
            name="step",
            out_shape=(sds((group, rows), F32), *more),
            in_specs=[SMEM, SMEM] + [VMEM] * (7 + len(arrived)),
            out_specs=(VMEM,) * (1 + len(more)),
            scratch_shapes=[
                pltpu.VMEM((sources + 1, group, order), BF16),
                pltpu.VMEM((rb_dev, group, order), F32),
                pltpu.VMEM((rb_dev, group, order), F32),
            ],
            compiler_params=params(12),
        )(plan, picks, resident(real), resident(imag), scale, near_re, near_im, current, previous, *arrived)
        previous, current = current, out[0]
        if not last:
            sent, blocks = out[1], out[2:]

    rounded = current.astype(BF16)
    others = [to_partner(rounded, "col", s) for s in range(1, ncol)]
    vectors = group * ncol
    part = pl.pallas_call(
        gram_kernel,
        name="gram",
        out_shape=sds((vectors // 2, vectors), F32),
        in_specs=[VMEM] * (1 + len(others)),
        out_specs=VMEM,
        scratch_shapes=[pltpu.VMEM((ncol, group, rows), BF16), pltpu.VMEM((vectors, vectors), F32)],
        compiler_params=params(12),
    )(current, *others)
    spread = jnp.broadcast_to(part[None], (nblk,) + part.shape)
    parts = lax.all_to_all(spread, "blk", split_axis=0, concat_axis=0, tiled=True)
    return pl.pallas_call(
        functools.partial(factor_kernel, rows * nblk),
        name="factor",
        out_shape=sds((group, rows), F32),
        in_specs=[VMEM] * (2 + len(others)),
        out_specs=VMEM,
        scratch_shapes=[
            pltpu.VMEM((ncol, group, rows), BF16),
            pltpu.VMEM((vectors, vectors), F32),
            pltpu.VMEM((vectors, vectors), F32),
        ],
        compiler_params=params(12),
    )(current, parts, *others)


def solution(mesh):
    return jax.shard_map(
        per_device,
        mesh=mesh,
        in_specs=(
            P("col", "blk"),
            P("blk", None, None),
            P("blk", None, None),
            P("blk"),
            P("blk"),
            P("blk", None),
        ),
        out_specs=P("col", "blk"),
        check_vma=False,
    )
```

```python
import functools
import math

import jax
import jax.numpy as jnp
from jax import lax
from jax.experimental import pallas as pl
from jax.experimental.pallas import tpu as pltpu
from jax.sharding import PartitionSpec as P

LOC_RB = 2
STEPS = 4
UNROLL = 4
CHUNK = 4
STAGED = 8
MIB = 1 << 20
LIMIT = 8

center = 1.25
half_width = 0.75

F32 = jnp.float32
BF16 = jnp.bfloat16
I32 = jnp.int32

VMEM = pl.BlockSpec(memory_space=pltpu.VMEM)
SMEM = pl.BlockSpec(memory_space=pltpu.SMEM)
ANY = pl.BlockSpec(memory_space=pl.ANY)

NT = (((1,), (1,)), ((), ()))
TN = (((0,), (0,)), ((), ()))


def sds(shape, dtype):
    return jax.ShapeDtypeStruct(shape, dtype)


def resident(x):
    return pltpu.with_memory_space_constraint(x, pltpu.VMEM)


def params(limit):
    return pltpu.CompilerParams(vmem_limit_bytes=limit * MIB)


def turn_rows(values):
    rows = values.shape[0]
    even = lax.broadcasted_iota(I32, values.shape, 0) % 2 == 0
    below = pltpu.roll(values, rows - 1, 0)
    above = pltpu.roll(values, 1, 0)
    return jnp.where(even, -below, above)


def turn_lanes(values):
    lanes = values.shape[1]
    even = lax.broadcasted_iota(I32, values.shape, 1) % 2 == 0
    after = pltpu.roll(values, lanes - 1, 1)
    before = pltpu.roll(values, 1, 1)
    return jnp.where(even, after, -before)


def tiles_kernel(
    near_count,
    direct,
    rows_ref,
    slots_ref,
    real_hbm,
    imag_hbm,
    both_ref,
    scale_ref,
    plan_ref,
    present_ref,
    first_ref,
    sems,
):
    tiles, order, _ = both_ref.shape
    rb_dev = present_ref.shape[0]
    me = lax.axis_index("blk")
    nblk = lax.axis_size("blk")
    slots = rb_dev + nblk
    chunks = tiles // CHUNK

    def copies(c):
        at = pl.ds(c * CHUNK, CHUNK)
        return (
            pltpu.make_async_copy(real_hbm.at[at], both_ref.at[at, :, 0:order], sems.at[c, 0]),
            pltpu.make_async_copy(imag_hbm.at[at], both_ref.at[at, :, order : 2 * order], sems.at[c, 1]),
        )

    for c in range(chunks):
        for copy in copies(c):
            copy.start()

    def clear(key, _):
        first_ref[key] = -1
        return _

    lax.fori_loop(0, rb_dev * slots, clear, 0)
    present_ref[...] = jnp.zeros_like(present_ref)

    def source(slot):
        owner = slot - rb_dev
        other = rb_dev + (owner ^ me if direct else owner)
        return jnp.where(slot < rb_dev, slot, other)

    def one(t, listed):
        row = rows_ref[t]
        slot = slots_ref[t]
        key = row * slots + slot
        seen = first_ref[key]
        both = jnp.abs(both_ref[t])
        present_ref[row] = present_ref[row] + (both[:, :order] + both[:, order:])

        @pl.when(seen >= 0)
        def _():
            both_ref[seen] = both_ref[seen] + both_ref[t]

        @pl.when(seen < 0)
        def _():
            first_ref[key] = t
            plan_ref[listed] = t | (row << 8) | (source(slot) << 16)

        return listed + (seen < 0).astype(I32)

    def chunk(c, listed):
        for copy in copies(c):
            copy.wait()
        for j in range(CHUNK):
            listed = one(c * CHUNK + j, listed)
        return listed

    def pad(listed):
        short = (UNROLL - listed % UNROLL) % UNROLL
        for j in range(UNROLL - 1):

            @pl.when(j < short)
            def _():
                plan_ref[listed + j] = slots << 16

        return listed + short

    header = 2
    near = pad(lax.fori_loop(0, near_count // CHUNK, chunk, header - header))
    plan_ref[plan_ref.shape[0] - 2] = near // UNROLL
    both = pad(lax.fori_loop(near_count // CHUNK, chunks, chunk, near))
    plan_ref[plan_ref.shape[0] - 1] = both // UNROLL

    ones = jnp.ones((8, order), BF16)
    for r in range(rb_dev):
        degree = lax.dot_general(ones, present_ref[r], NT, preferred_element_type=F32)
        scale_ref[:, r * order : (r + 1) * order] = 1.0 / jnp.sqrt(jnp.maximum(degree, 1.0))


def tiles_call(rows, slots, real, imag, near_count, direct):
    tiles, order, _ = real.shape
    rb_dev = rows.shape[0] // 12
    nblk = lax.axis_size("blk")
    return pl.pallas_call(
        functools.partial(tiles_kernel, near_count, direct),
        name="tiles",
        out_shape=(
            pltpu.VMEM((tiles, order, 2 * order), BF16),
            sds((8, rb_dev * order), F32),
            sds((tiles + 32,), I32),
        ),
        in_specs=[SMEM, SMEM, ANY, ANY],
        out_specs=(VMEM, VMEM, SMEM),
        scratch_shapes=[
            pltpu.VMEM((rb_dev, order, order), BF16),
            pltpu.SMEM((rb_dev * (rb_dev + nblk),), I32),
            pltpu.SemaphoreType.DMA((tiles // CHUNK, 2)),
        ],
        compiler_params=params(LIMIT),
        cost_estimate=pl.CostEstimate(flops=1 << 28, bytes_accessed=2 * real.size * 2, transcendentals=0),
    )(
        pltpu.with_memory_space_constraint(rows, pltpu.HBM),
        pltpu.with_memory_space_constraint(slots, pltpu.HBM),
        pltpu.with_memory_space_constraint(real, pltpu.HBM),
        pltpu.with_memory_space_constraint(imag, pltpu.HBM),
    )


def send_blocks(field, scale_ref, sent_ref, pick, out_refs):
    order = sent_ref.shape[2]
    for r in range(sent_ref.shape[0]):
        at = slice(r * order, (r + 1) * order)
        sent_ref[r] = (field[:, at] * scale_ref[0:1, at]).astype(BF16)
    if len(out_refs) == 1:
        (out,) = out_refs
        for p in range(out.shape[0]):
            out[p] = sent_ref[pick(p)]
    else:
        beside, across = out_refs
        me = lax.axis_index("blk")
        for h in range(beside.shape[0]):
            beside[h] = sent_ref[pick(me ^ (2 * h + 1))]
        for h in range(1, beside.shape[0]):
            across[h - 1] = sent_ref[pick(me ^ (2 * h))]


def first_kernel(y_ref, scale_ref, wanted_ref, sent_ref, picks_ref, *out_refs):
    me = lax.axis_index("blk")
    for p in range(picks_ref.shape[0]):
        picks_ref[p] = wanted_ref[p, me]
    send_blocks(y_ref, scale_ref, sent_ref, lambda p: picks_ref[p], out_refs)


def merge_kernel(across_ref, passed_ref, *out_refs):
    for h, out in enumerate(out_refs, 1):
        out[0] = across_ref[h - 1]
        out[1] = passed_ref[h]


def put_source(x_ref, at, block):
    order = block.shape[1]
    x_ref[at, :, :order] = block
    x_ref[at, :, order:] = turn_rows(block.astype(F32)).astype(BF16)


def multiply(plan_ref, lo, hi, both_ref, load, acc_ref):
    def group(i, _):
        done = []
        for j in range(UNROLL):
            code = plan_ref[i * UNROLL + j]
            tile = code & 255
            product = lax.dot_general(both_ref[tile], load(code >> 16), NT, preferred_element_type=F32)
            done.append(((code >> 8) & 255, product))
        for row, product in done:
            acc_ref[row] = acc_ref[row] + product
        return _

    lax.fori_loop(lo, hi, group, 0)


def near_kernel(plan_ref, both_ref, sent_ref, acc_ref, x_ref):
    rb_dev = sent_ref.shape[0]
    for r in range(rb_dev):
        put_source(x_ref, r, sent_ref[r])
    x_ref[rb_dev] = jnp.zeros_like(x_ref[rb_dev])
    acc_ref[...] = jnp.zeros_like(acc_ref)
    end = plan_ref[plan_ref.shape[0] - 2]
    multiply(plan_ref, 0, end, both_ref, lambda c: x_ref[jnp.minimum(c, rb_dev)], acc_ref)


def step_kernel(pieces, step, rb_dev, *refs):
    (plan_ref, picks_ref, both_ref, scale_ref, near_ref, now_ref, before_ref) = refs[:7]
    arrived = refs[7 : 7 + pieces]
    next_ref = refs[7 + pieces]
    last = step == STEPS - 1
    sent_ref = None if last else refs[8 + pieces]
    out_refs = () if last else refs[9 + pieces : -2]
    x_ref, acc_ref = refs[-2:]
    order = near_ref.shape[1]
    if pieces == 1:
        count = arrived[0].shape[0]
        for p in range(count):
            put_source(x_ref, p, arrived[0][p])
    else:
        count = 2 * pieces
        put_source(x_ref, 1, arrived[0][0])
        for h in range(1, pieces):
            put_source(x_ref, 2 * h, arrived[h][0])
            put_source(x_ref, 2 * h + 1, arrived[h][1])
    x_ref[count] = jnp.zeros_like(x_ref[count])
    acc_ref[...] = near_ref[...]
    lo = plan_ref[plan_ref.shape[0] - 2]
    hi = plan_ref[plan_ref.shape[0] - 1]
    multiply(plan_ref, lo, hi, both_ref, lambda c: x_ref[c - rb_dev], acc_ref)
    for r in range(rb_dev):
        at = slice(r * order, (r + 1) * order)
        now = now_ref[:, at]
        applied = scale_ref[0:1, at] * acc_ref[r].T
        moved = ((1.0 - center) * now - applied) / half_width
        next_ref[:, at] = moved if step == 0 else 2.0 * moved - before_ref[:, at]
    if not last:
        send_blocks(next_ref, scale_ref, sent_ref, lambda p: picks_ref[p], out_refs)


def all_rows(own_ref, arrived, all_ref):
    c = lax.axis_index("col")
    all_ref[c] = own_ref[...].astype(BF16)
    for s, ref in enumerate(arrived, 1):
        all_ref[c ^ s] = ref[...]
    n, group, rows = all_ref.shape
    return all_ref[...].reshape(n * group, rows)


def gram_kernel(own_ref, *refs):
    arrived, (gram_ref, all_ref, full_ref) = refs[:-3], refs[-3:]
    rows = all_rows(own_ref, arrived, all_ref)
    full_ref[...] = lax.dot_general(rows, rows, NT, preferred_element_type=F32)
    half = gram_ref.shape[0]
    even = full_ref[pl.ds(0, half, stride=2), :]
    odd = full_ref[pl.ds(1, half, stride=2), :]
    gram_ref[...] = even + turn_lanes(odd)


PANEL = 16


def factor_kernel(grams, nodes, own_ref, *refs):
    parts = refs[:grams]
    arrived = refs[grams:-4]
    out_ref, all_ref, work_ref, inverse_ref = refs[-4:]
    group = own_ref.shape[0]
    order = work_ref.shape[0]
    total = parts[0][...]
    for part in parts[1:]:
        total = total + part[...]
    half = total.shape[0]
    work_ref[pl.ds(0, half, stride=2), :] = total
    work_ref[pl.ds(1, half, stride=2), :] = -turn_lanes(total)
    row_at = lax.broadcasted_iota(I32, (order, order), 0)
    lane_at = lax.broadcasted_iota(I32, (order, order), 1)
    inverse_ref[...] = (row_at == lane_at).astype(F32)
    here = lax.broadcasted_iota(I32, (PANEL, 1), 0)
    for top in range(0, order, PANEL):
        panel = jnp.concatenate([work_ref[top : top + PANEL, :], inverse_ref[top : top + PANEL, :]], axis=1)
        for k in range(0, PANEL, 2):
            lane = top + k
            left = panel[:, lane : lane + 1]
            right = panel[:, lane + 1 : lane + 2]
            inv = lax.rsqrt(left[k : k + 1, :])
            inv2 = inv * inv
            below = here > k + 1
            pair = here - k
            a = jnp.where(below, left * inv2, 0.0)
            b = jnp.where(below, right * inv2, 0.0)
            keep = jnp.where((pair == 0) | (pair == 1), inv, 1.0)
            panel = panel * keep - (a * panel[k : k + 1, :] + b * panel[k + 1 : k + 2, :])
        inverse_ref[top : top + PANEL, :] = panel[:, order:]
        rest = top + PANEL
        if rest < order:
            cols = panel[:, 0:order]
            update = lax.dot_general(
                cols, panel, TN, precision=lax.Precision.HIGHEST, preferred_element_type=F32
            )
            work_ref[rest:, :] = work_ref[rest:, :] - update[rest:, :order]
            inverse_ref[rest:, :] = inverse_ref[rest:, :] - update[rest:, order:]
    c = lax.axis_index("col")
    mine = inverse_ref[pl.ds(pl.multiple_of(c * group, group), group), :]
    mine = mine * math.sqrt(nodes)
    high = mine.astype(BF16)
    low = (mine - high.astype(F32)).astype(BF16)
    rows = all_rows(own_ref, arrived, all_ref)
    both = lax.dot_general(
        jnp.concatenate([high, low], axis=0), rows, (((1,), (0,)), ((), ())), preferred_element_type=F32
    )
    own = own_ref[...]
    lost = own - own.astype(BF16).astype(F32)
    own_lanes = (
        lax.broadcasted_iota(I32, (order, group), 0)
        == lax.broadcasted_iota(I32, (order, group), 1) + c * group
    ).astype(BF16)
    square = jnp.dot(high, own_lanes, preferred_element_type=F32).astype(BF16)
    out_ref[...] = (
        both[:group] + both[group:] + jnp.dot(square, lost.astype(BF16), preferred_element_type=F32)
    )


def to_partner(x, axis, mask):
    n = lax.axis_size(axis)
    return lax.ppermute(x, axis, [(i, i ^ mask) for i in range(n)])


def per_device(y_start, tile_real, tile_imag, tile_rows, tile_slots, fetch_pick):
    group, rows = y_start.shape
    tiles, order, _ = tile_real.shape
    rb_dev = rows // order
    nblk = lax.axis_size("blk")
    ncol = lax.axis_size("col")
    staged = nblk == STAGED
    near_count = LOC_RB * rb_dev
    wanted = lax.all_gather(fetch_pick, "blk", axis=0, tiled=True)
    half = nblk // 2
    if staged:
        block_shapes = [sds((half, group, order), BF16), sds((half - 1, group, order), BF16)]
        pieces = half
    else:
        block_shapes = [sds((nblk, group, order), BF16)]
        pieces = 1

    def exchange(blocks):
        if not staged:
            return [lax.all_to_all(blocks[0], "blk", split_axis=0, concat_axis=0, tiled=True)]
        passed = to_partner(blocks[0], "blk", 1)
        pairs = pl.pallas_call(
            merge_kernel,
            name="merge",
            out_shape=[sds((2, group, order), BF16)] * (half - 1),
            in_specs=[VMEM, VMEM],
            out_specs=[VMEM] * (half - 1),
            compiler_params=params(LIMIT),
        )(blocks[1], passed)
        return [passed] + [to_partner(pair, "blk", 2 * h) for h, pair in enumerate(pairs, 1)]

    both, scale, plan = tiles_call(tile_rows, tile_slots, tile_real, tile_imag, near_count, staged)

    out = pl.pallas_call(
        first_kernel,
        name="first",
        out_shape=(sds((rb_dev, group, order), BF16), sds((nblk,), I32), *block_shapes),
        in_specs=[VMEM, VMEM, SMEM],
        out_specs=(VMEM, SMEM) + (VMEM,) * len(block_shapes),
        compiler_params=params(LIMIT),
    )(y_start, scale, pltpu.with_memory_space_constraint(wanted, pltpu.HBM))
    sent, picks, blocks = out[0], out[1], out[2:]

    acc = (rb_dev, order, group)
    previous, current = y_start, y_start
    for step in range(STEPS):
        arrived = exchange(blocks)
        near = pl.pallas_call(
            near_kernel,
            name="near",
            out_shape=sds(acc, F32),
            in_specs=[SMEM, VMEM, VMEM],
            out_specs=VMEM,
            scratch_shapes=[pltpu.VMEM((rb_dev + 1, group, 2 * order), BF16)],
            compiler_params=params(LIMIT),
            cost_estimate=pl.CostEstimate(flops=1 << 28, bytes_accessed=1 << 20, transcendentals=0),
        )(plan, resident(both), sent)
        last = step == STEPS - 1
        more = () if last else (sds((rb_dev, group, order), BF16), *block_shapes)
        out = pl.pallas_call(
            functools.partial(step_kernel, pieces, step, rb_dev),
            name="step",
            out_shape=(sds((group, rows), F32), *more),
            in_specs=[SMEM, SMEM] + [VMEM] * (5 + len(arrived)),
            out_specs=(VMEM,) * (1 + len(more)),
            scratch_shapes=[pltpu.VMEM((nblk + 1, group, 2 * order), BF16), pltpu.VMEM(acc, F32)],
            compiler_params=params(LIMIT),
        )(plan, picks, resident(both), scale, near, current, previous, *arrived)
        previous, current = current, out[0]
        if not last:
            sent, blocks = out[1], out[2:]

    rounded = current.astype(BF16)
    if ncol == 4:
        beside, across = to_partner(rounded, "col", 1), to_partner(rounded, "col", 2)
        others = [beside, across, to_partner(across, "col", 1)]
    else:
        others = [to_partner(rounded, "col", s) for s in range(1, ncol)]
    vectors = group * ncol
    part = pl.pallas_call(
        gram_kernel,
        name="gram",
        out_shape=sds((vectors // 2, vectors), F32),
        in_specs=[VMEM] * (1 + len(others)),
        out_specs=VMEM,
        scratch_shapes=[pltpu.VMEM((ncol, group, rows), BF16), pltpu.VMEM((vectors, vectors), F32)],
        compiler_params=params(LIMIT),
    )(current, *others)
    wide = 1
    while 2 * wide < nblk:
        part = part + to_partner(part, "blk", wide)
        wide *= 2
    parts = [part, to_partner(part, "blk", wide)] if wide < nblk else [part]
    return pl.pallas_call(
        functools.partial(factor_kernel, len(parts), rows * nblk),
        name="factor",
        out_shape=sds((group, rows), F32),
        in_specs=[VMEM] * (1 + len(parts) + len(others)),
        out_specs=VMEM,
        scratch_shapes=[
            pltpu.VMEM((ncol, group, rows), BF16),
            pltpu.VMEM((vectors, vectors), F32),
            pltpu.VMEM((vectors, vectors), F32),
        ],
        compiler_params=params(LIMIT),
    )(current, *parts, *others)


def solution(mesh):
    return jax.shard_map(
        per_device,
        mesh=mesh,
        in_specs=(
            P("col", "blk"),
            P("blk", None, None),
            P("blk", None, None),
            P("blk"),
            P("blk"),
            P("blk", None),
        ),
        out_specs=P("col", "blk"),
        check_vma=False,
    )
```

```python
import functools
import math

import jax
import jax.numpy as jnp
from jax import lax
from jax.experimental import pallas as pl
from jax.experimental.pallas import tpu as pltpu
from jax.sharding import PartitionSpec as P

LOC_RB = 2
STEPS = 4
UNROLL = 4
CHUNK = 4
MERGE = 16
PARTS = 3
TOP = 256.0
FINER = 16.0
TINY = 1e-30
MIB = 1 << 20
LIMIT = 24

center = 1.25
half_width = 0.75

F32 = jnp.float32
BF16 = jnp.bfloat16
F8 = jnp.float8_e4m3fn
I32 = jnp.int32

VMEM = pl.BlockSpec(memory_space=pltpu.VMEM)
SMEM = pl.BlockSpec(memory_space=pltpu.SMEM)
ANY = pl.BlockSpec(memory_space=pl.ANY)

NT = (((1,), (1,)), ((), ()))
TN = (((0,), (0,)), ((), ()))


def sds(shape, dtype):
    return jax.ShapeDtypeStruct(shape, dtype)


def params(limit):
    return pltpu.CompilerParams(vmem_limit_bytes=limit * MIB)


def turn_rows(values):
    rows = values.shape[0]
    even = lax.broadcasted_iota(I32, values.shape, 0) % 2 == 0
    below = pltpu.roll(values, rows - 1, 0)
    above = pltpu.roll(values, 1, 0)
    return jnp.where(even, -below, above)


def turn_lanes(values):
    lanes = values.shape[1]
    even = lax.broadcasted_iota(I32, values.shape, 1) % 2 == 0
    after = pltpu.roll(values, lanes - 1, 1)
    before = pltpu.roll(values, 1, 1)
    return jnp.where(even, after, -before)


def tiles_kernel(
    near_count,
    rows_ref,
    slots_ref,
    real_hbm,
    imag_hbm,
    packed_hbm,
    scale_ref,
    plan_ref,
    both_ref,
    small_ref,
    present_ref,
    table_ref,
    back_ref,
    done_ref,
    in_sems,
    out_sems,
):
    tiles, order, _ = both_ref.shape
    rb_dev = present_ref.shape[0]
    slots = rb_dev + lax.axis_size("blk")
    chunks = tiles // CHUNK

    def copies(c):
        at = pl.ds(c * CHUNK, CHUNK)
        return (
            pltpu.make_async_copy(real_hbm.at[at], both_ref.at[at, :, 0:order], in_sems.at[c, 0]),
            pltpu.make_async_copy(imag_hbm.at[at], both_ref.at[at, :, order : 2 * order], in_sems.at[c, 1]),
        )

    def leave(e):
        return pltpu.make_async_copy(small_ref.at[e], packed_hbm.at[e], out_sems.at[e])

    for c in range(chunks):
        for copy in copies(c):
            copy.start()

    def clear(key, _):
        table_ref[key] = -1
        return _

    lax.fori_loop(0, rb_dev * slots, clear, 0)
    present_ref[...] = jnp.zeros_like(present_ref)

    def link(t, carry):
        key = rows_ref[t] * slots + slots_ref[t]
        seen = table_ref[key]
        before = seen & 255
        length = seen >> 8
        joins = (seen >= 0) & (length < MERGE)
        back_ref[t] = jnp.where(joins, before, -1)
        done_ref[t] = 1

        @pl.when(joins)
        def _():
            done_ref[before] = 0

        table_ref[key] = t | (jnp.where(joins, length + 1, 1) << 8)
        return carry

    lax.fori_loop(0, tiles, link, 0)

    def one(t, listed):
        row = rows_ref[t]
        both = both_ref[t]
        present_ref[row] = present_ref[row] + (both[:, :order] + jnp.abs(both[:, order:]))
        closes = done_ref[t]

        @pl.when(closes == 1)
        def _():
            def add(prior):
                both_ref[t] = both_ref[t] + both_ref[prior]
                return back_ref[prior]

            lax.while_loop(lambda prior: prior >= 0, add, back_ref[t])
            small_ref[listed] = both_ref[t].astype(F32).astype(F8)
            leave(listed).start()
            plan_ref[listed] = row | (slots_ref[t] << 8)

        return listed + closes

    def chunk(c, listed):
        for copy in copies(c):
            copy.wait()
        for j in range(CHUNK):
            listed = one(c * CHUNK + j, listed)
        return listed

    def pad(listed):
        short = (UNROLL - listed % UNROLL) % UNROLL
        for j in range(UNROLL - 1):

            @pl.when(j < short)
            def _():
                small_ref[listed + j] = jnp.zeros(small_ref.shape[1:], F8)
                leave(listed + j).start()
                plan_ref[listed + j] = slots << 8

        return listed + short

    near = pad(lax.fori_loop(0, near_count // CHUNK, chunk, 0))
    every = pad(lax.fori_loop(near_count // CHUNK, chunks, chunk, near))
    plan_ref[tiles] = near // UNROLL
    plan_ref[tiles + 1] = every // UNROLL

    ones = jnp.ones((8, order), BF16)
    for r in range(rb_dev):
        degree = lax.dot_general(ones, present_ref[r], NT, preferred_element_type=F32)
        scale_ref[:, r * order : (r + 1) * order] = 1.0 / jnp.sqrt(jnp.maximum(degree, 1.0))

    def left(e, _):
        leave(e).wait()
        return _

    lax.fori_loop(0, every, left, 0)


def in_hbm(x):
    return pltpu.with_memory_space_constraint(x, pltpu.HBM)


def tiles_call(rows, slots, real, imag, rb_dev, near_count):
    tiles, order, _ = real.shape
    nblk = lax.axis_size("blk")
    return pl.pallas_call(
        functools.partial(tiles_kernel, near_count),
        name="tiles",
        out_shape=(
            pltpu.HBM((tiles, order, 2 * order), F8),
            sds((8, rb_dev * order), F32),
            sds((tiles + 32,), I32),
        ),
        in_specs=[SMEM, SMEM, ANY, ANY],
        out_specs=(ANY, VMEM, SMEM),
        scratch_shapes=[
            pltpu.VMEM((tiles, order, 2 * order), BF16),
            pltpu.VMEM((tiles, order, 2 * order), F8),
            pltpu.VMEM((rb_dev, order, order), BF16),
            pltpu.SMEM((rb_dev * (rb_dev + nblk),), I32),
            pltpu.SMEM((tiles,), I32),
            pltpu.SMEM((tiles,), I32),
            pltpu.SemaphoreType.DMA((tiles // CHUNK, 2)),
            pltpu.SemaphoreType.DMA((tiles,)),
        ],
        compiler_params=params(48),
        cost_estimate=pl.CostEstimate(flops=1 << 28, bytes_accessed=2 * real.size * 2, transcendentals=0),
    )(in_hbm(rows), in_hbm(slots), in_hbm(real), in_hbm(imag))


def send_blocks(field, scale_ref, sent_ref, pick, out_ref):
    order = sent_ref.shape[2]
    for r in range(sent_ref.shape[0]):
        at = slice(r * order, (r + 1) * order)
        sent_ref[r] = (field[:, at] * scale_ref[0:1, at]).astype(BF16)
    for p in range(out_ref.shape[0]):
        out_ref[p] = sent_ref[pick(p)]


def first_kernel(y_ref, scale_ref, wanted_ref, sent_ref, out_ref):
    send_blocks(y_ref, scale_ref, sent_ref, lambda p: wanted_ref[p, 0], out_ref)


def load_groups(packed_hbm, tiles_ref, sems, lo, hi):
    def copy(g):
        at = pl.ds((g - lo) * UNROLL, UNROLL)
        return pltpu.make_async_copy(
            packed_hbm.at[pl.ds(g * UNROLL, UNROLL)], tiles_ref.at[at], sems.at[g - lo]
        )

    def begin(g, _):
        copy(g).start()
        return _

    lax.fori_loop(lo, hi, begin, 0)
    return copy


def split_sources(source, x_ref):
    count, group, order = source.shape
    most = jnp.zeros((group, order), F32)
    for p in range(count):
        most = jnp.maximum(most, jnp.abs(source[p].astype(F32)))
    most = jnp.broadcast_to(jnp.max(most, axis=1, keepdims=True), (group, 128))
    most = jnp.maximum(jnp.maximum(most, jnp.abs(turn_rows(most))), TINY)
    size = most[:, 0:1] / TOP
    inverse = TOP / most[:, 0:1]
    for p in range(count):
        scaled = source[p].astype(F32) * inverse
        for side, part in enumerate((scaled, turn_rows(scaled))):
            at = slice(side * order, (side + 1) * order)
            for k in range(PARTS):
                short = part.astype(F8)
                x_ref[p, k * group : (k + 1) * group, at] = short
                part = (part - short.astype(F32)) * FINER
    x_ref[count] = jnp.zeros_like(x_ref[count])
    return size


def multiply(plan_ref, lo, hi, copy, tiles_ref, load, acc_ref):
    def group(g, _):
        copy(g).wait()
        done = []
        for j in range(UNROLL):
            code = plan_ref[g * UNROLL + j]
            tile = tiles_ref[(g - lo) * UNROLL + j]
            product = lax.dot_general(tile, load(code >> 8), NT, preferred_element_type=F32)
            done.append((code & 255, product))
        for row, product in done:
            acc_ref[row] = acc_ref[row] + product
        return _

    lax.fori_loop(lo, hi, group, 0)


def collect(acc, size):
    group = size.shape[0]
    flat = acc.T
    total = flat[(PARTS - 1) * group : PARTS * group]
    for k in range(PARTS - 2, -1, -1):
        total = flat[k * group : (k + 1) * group] + total * (1.0 / FINER)
    return total * size


def near_kernel(plan_ref, packed_hbm, sent_ref, out_ref, tiles_ref, x_ref, acc_ref, sems):
    rb_dev = sent_ref.shape[0]
    at = plan_ref.shape[0] - 32
    hi = plan_ref[at]
    copy = load_groups(packed_hbm, tiles_ref, sems, 0, hi)
    acc_ref[...] = jnp.zeros_like(acc_ref)
    size = split_sources(sent_ref, x_ref)
    multiply(plan_ref, 0, hi, copy, tiles_ref, lambda c: x_ref[jnp.minimum(c, rb_dev)], acc_ref)
    for r in range(rb_dev):
        out_ref[r] = collect(acc_ref[r], size)


def step_kernel(step, plan_ref, wanted_ref, packed_hbm, scale_ref, near_ref, now_ref, before_ref, arrived_ref, *refs):
    last = step == STEPS - 1
    next_ref = refs[0]
    tiles_ref, x_ref, acc_ref, sems = refs[-4:]
    rb_dev, _, order = near_ref.shape
    at = plan_ref.shape[0] - 32
    lo, hi = plan_ref[at], plan_ref[at + 1]
    copy = load_groups(packed_hbm, tiles_ref, sems, lo, hi)
    acc_ref[...] = jnp.zeros_like(acc_ref)
    size = split_sources(arrived_ref, x_ref)
    multiply(plan_ref, lo, hi, copy, tiles_ref, lambda c: x_ref[c - rb_dev], acc_ref)
    for r in range(rb_dev):
        at = slice(r * order, (r + 1) * order)
        now = now_ref[:, at]
        applied = scale_ref[0:1, at] * (near_ref[r] + collect(acc_ref[r], size))
        moved = ((1.0 - center) * now - applied) / half_width
        next_ref[:, at] = moved if step == 0 else 2.0 * moved - before_ref[:, at]
    if not last:
        send_blocks(next_ref, scale_ref, refs[1], lambda p: wanted_ref[p, 0], refs[2])


def all_rows(own_ref, arrived, all_ref):
    c = lax.axis_index("col")
    all_ref[c] = own_ref[...].astype(BF16)
    for s, ref in enumerate(arrived, 1):
        all_ref[c ^ s] = ref[...]
    n, group, rows = all_ref.shape
    return all_ref[...].reshape(n * group, rows)


def gram_kernel(own_ref, *refs):
    arrived, (gram_ref, all_ref, full_ref) = refs[:-3], refs[-3:]
    rows = all_rows(own_ref, arrived, all_ref)
    full_ref[...] = lax.dot_general(rows, rows, NT, preferred_element_type=F32)
    half = gram_ref.shape[0]
    even = full_ref[pl.ds(0, half, stride=2), :]
    odd = full_ref[pl.ds(1, half, stride=2), :]
    gram_ref[...] = even + turn_lanes(odd)


PANEL = 16


def factor_kernel(grams, nodes, own_ref, *refs):
    parts = refs[:grams]
    arrived = refs[grams:-4]
    out_ref, all_ref, work_ref, inverse_ref = refs[-4:]
    group = own_ref.shape[0]
    order = work_ref.shape[0]
    total = parts[0][...]
    for part in parts[1:]:
        total = total + part[...]
    half = total.shape[0]
    work_ref[pl.ds(0, half, stride=2), :] = total
    work_ref[pl.ds(1, half, stride=2), :] = -turn_lanes(total)
    row_at = lax.broadcasted_iota(I32, (order, order), 0)
    lane_at = lax.broadcasted_iota(I32, (order, order), 1)
    inverse_ref[...] = (row_at == lane_at).astype(F32)
    here = lax.broadcasted_iota(I32, (PANEL, 1), 0)
    for top in range(0, order, PANEL):
        panel = jnp.concatenate([work_ref[top : top + PANEL, :], inverse_ref[top : top + PANEL, :]], axis=1)
        for k in range(0, PANEL, 2):
            lane = top + k
            left = panel[:, lane : lane + 1]
            right = panel[:, lane + 1 : lane + 2]
            inv = lax.rsqrt(left[k : k + 1, :])
            inv2 = inv * inv
            below = here > k + 1
            pair = here - k
            a = jnp.where(below, left * inv2, 0.0)
            b = jnp.where(below, right * inv2, 0.0)
            keep = jnp.where((pair == 0) | (pair == 1), inv, 1.0)
            panel = panel * keep - (a * panel[k : k + 1, :] + b * panel[k + 1 : k + 2, :])
        inverse_ref[top : top + PANEL, :] = panel[:, order:]
        rest = top + PANEL
        if rest < order:
            cols = panel[:, 0:order]
            update = lax.dot_general(
                cols, panel, TN, precision=lax.Precision.HIGHEST, preferred_element_type=F32
            )
            work_ref[rest:, :] = work_ref[rest:, :] - update[rest:, :order]
            inverse_ref[rest:, :] = inverse_ref[rest:, :] - update[rest:, order:]
    c = lax.axis_index("col")
    mine = inverse_ref[pl.ds(pl.multiple_of(c * group, group), group), :]
    mine = mine * math.sqrt(nodes)
    high = mine.astype(BF16)
    low = (mine - high.astype(F32)).astype(BF16)
    rows = all_rows(own_ref, arrived, all_ref)
    both = lax.dot_general(
        jnp.concatenate([high, low], axis=0), rows, (((1,), (0,)), ((), ())), preferred_element_type=F32
    )
    own = own_ref[...]
    lost = own - own.astype(BF16).astype(F32)
    own_lanes = (
        lax.broadcasted_iota(I32, (order, group), 0)
        == lax.broadcasted_iota(I32, (order, group), 1) + c * group
    ).astype(BF16)
    square = jnp.dot(high, own_lanes, preferred_element_type=F32).astype(BF16)
    out_ref[...] = (
        both[:group] + both[group:] + jnp.dot(square, lost.astype(BF16), preferred_element_type=F32)
    )


def to_partner(x, axis, mask):
    n = lax.axis_size(axis)
    return lax.ppermute(x, axis, [(i, i ^ mask) for i in range(n)])


def per_device(y_start, tile_real, tile_imag, tile_rows, tile_slots, fetch_pick):
    group, rows = y_start.shape
    tiles, order, _ = tile_real.shape
    rb_dev = rows // order
    nblk = lax.axis_size("blk")
    ncol = lax.axis_size("col")
    near_count = LOC_RB * rb_dev
    wanted = lax.all_to_all(
        fetch_pick.reshape(nblk, 1), "blk", split_axis=0, concat_axis=0, tiled=True
    )
    packed, scale, plan = tiles_call(tile_rows, tile_slots, tile_real, tile_imag, rb_dev, near_count)

    own_blocks = sds((rb_dev, group, order), BF16)
    out_blocks = sds((nblk, group, order), BF16)
    sent, blocks = pl.pallas_call(
        first_kernel,
        name="first",
        out_shape=(own_blocks, out_blocks),
        in_specs=[VMEM, VMEM, SMEM],
        out_specs=(VMEM, VMEM),
        compiler_params=params(LIMIT),
    )(y_start, scale, wanted)

    def scratch(entries, sources):
        return [
            pltpu.VMEM((entries, order, 2 * order), F8),
            pltpu.VMEM((sources + 1, PARTS * group, 2 * order), F8),
            pltpu.VMEM((rb_dev, order, PARTS * group), F32),
            pltpu.SemaphoreType.DMA((entries // UNROLL,)),
        ]

    previous, current = y_start, y_start
    for step in range(STEPS):
        arrived = lax.all_to_all(blocks, "blk", split_axis=0, concat_axis=0, tiled=True)
        near = pl.pallas_call(
            near_kernel,
            name="near",
            out_shape=sds((rb_dev, group, order), F32),
            in_specs=[SMEM, ANY, VMEM],
            out_specs=VMEM,
            scratch_shapes=scratch(near_count, rb_dev),
            compiler_params=params(LIMIT),
            cost_estimate=pl.CostEstimate(flops=1 << 28, bytes_accessed=1 << 21, transcendentals=0),
        )(plan, in_hbm(packed), sent)
        last = step == STEPS - 1
        more = () if last else (own_blocks, out_blocks)
        out = pl.pallas_call(
            functools.partial(step_kernel, step),
            name="step",
            out_shape=(sds((group, rows), F32), *more),
            in_specs=[SMEM, SMEM, ANY] + [VMEM] * 5,
            out_specs=(VMEM,) * (1 + len(more)),
            scratch_shapes=scratch(tiles - near_count, nblk),
            compiler_params=params(LIMIT),
        )(plan, wanted, in_hbm(packed), scale, near, current, previous, arrived)
        previous, current = current, out[0]
        if not last:
            sent, blocks = out[1:]

    rounded = current.astype(BF16)
    if ncol == 4:
        beside, across = to_partner(rounded, "col", 1), to_partner(rounded, "col", 2)
        others = [beside, across, to_partner(across, "col", 1)]
    else:
        others = [to_partner(rounded, "col", s) for s in range(1, ncol)]
    vectors = group * ncol
    part = pl.pallas_call(
        gram_kernel,
        name="gram",
        out_shape=sds((vectors // 2, vectors), F32),
        in_specs=[VMEM] * (1 + len(others)),
        out_specs=VMEM,
        scratch_shapes=[pltpu.VMEM((ncol, group, rows), BF16), pltpu.VMEM((vectors, vectors), F32)],
        compiler_params=params(LIMIT),
    )(current, *others)
    wide = 1
    while 2 * wide < nblk:
        part = part + to_partner(part, "blk", wide)
        wide *= 2
    parts = [part, to_partner(part, "blk", wide)] if wide < nblk else [part]
    return pl.pallas_call(
        functools.partial(factor_kernel, len(parts), rows * nblk),
        name="factor",
        out_shape=sds((group, rows), F32),
        in_specs=[VMEM] * (1 + len(parts) + len(others)),
        out_specs=VMEM,
        scratch_shapes=[
            pltpu.VMEM((ncol, group, rows), BF16),
            pltpu.VMEM((vectors, vectors), F32),
            pltpu.VMEM((vectors, vectors), F32),
        ],
        compiler_params=params(LIMIT),
    )(current, *parts, *others)


def solution(mesh):
    return jax.shard_map(
        per_device,
        mesh=mesh,
        in_specs=(
            P("col", "blk"),
            P("blk", None, None),
            P("blk", None, None),
            P("blk"),
            P("blk"),
            P("blk", None),
        ),
        out_specs=P("col", "blk"),
        check_vma=False,
    )
```

```python
import functools
import math

import jax
import jax.numpy as jnp
from jax import lax
from jax.experimental import pallas as pl
from jax.experimental.pallas import tpu as pltpu
from jax.sharding import PartitionSpec as P

LOC_RB = 2
STEPS = 4
UNROLL = 4
CHUNK = 4
MERGE = 16
PARTS = 3
TOP = 256.0
FINER = 16.0
TINY = 1e-30
MIB = 1 << 20
LIMIT = 24

center = 1.25
half_width = 0.75

F32 = jnp.float32
BF16 = jnp.bfloat16
F8 = jnp.float8_e4m3fn
I32 = jnp.int32

VMEM = pl.BlockSpec(memory_space=pltpu.VMEM)
SMEM = pl.BlockSpec(memory_space=pltpu.SMEM)
ANY = pl.BlockSpec(memory_space=pl.ANY)

NT = (((1,), (1,)), ((), ()))
TN = (((0,), (0,)), ((), ()))


def sds(shape, dtype):
    return jax.ShapeDtypeStruct(shape, dtype)


def params(limit):
    return pltpu.CompilerParams(vmem_limit_bytes=limit * MIB)


def turn_rows(values):
    rows = values.shape[0]
    even = lax.broadcasted_iota(I32, values.shape, 0) % 2 == 0
    below = pltpu.roll(values, rows - 1, 0)
    above = pltpu.roll(values, 1, 0)
    return jnp.where(even, -below, above)


def turn_lanes(values):
    lanes = values.shape[1]
    even = lax.broadcasted_iota(I32, values.shape, 1) % 2 == 0
    after = pltpu.roll(values, lanes - 1, 1)
    before = pltpu.roll(values, 1, 1)
    return jnp.where(even, after, -before)


def tiles_kernel(
    near_count,
    rows_ref,
    slots_ref,
    real_hbm,
    imag_hbm,
    packed_hbm,
    scale_ref,
    plan_ref,
    both_ref,
    small_ref,
    present_ref,
    table_ref,
    back_ref,
    done_ref,
    in_sems,
    out_sems,
):
    tiles, order, _ = both_ref.shape
    rb_dev = present_ref.shape[0]
    slots = rb_dev + lax.axis_size("blk")
    chunks = tiles // CHUNK

    def copies(c):
        at = pl.ds(c * CHUNK, CHUNK)
        return (
            pltpu.make_async_copy(real_hbm.at[at], both_ref.at[at, :, 0:order], in_sems.at[c, 0]),
            pltpu.make_async_copy(imag_hbm.at[at], both_ref.at[at, :, order : 2 * order], in_sems.at[c, 1]),
        )

    def leave(e):
        return pltpu.make_async_copy(small_ref.at[e], packed_hbm.at[e], out_sems.at[e])

    for c in range(chunks):
        for copy in copies(c):
            copy.start()

    def clear(key, _):
        table_ref[key] = -1
        return _

    lax.fori_loop(0, rb_dev * slots, clear, 0)
    present_ref[...] = jnp.zeros_like(present_ref)

    def link(t, carry):
        key = rows_ref[t] * slots + slots_ref[t]
        seen = table_ref[key]
        before = seen & 255
        length = seen >> 8
        joins = (seen >= 0) & (length < MERGE)
        back_ref[t] = jnp.where(joins, before, -1)
        done_ref[t] = 1

        @pl.when(joins)
        def _():
            done_ref[before] = 0

        table_ref[key] = t | (jnp.where(joins, length + 1, 1) << 8)
        return carry

    lax.fori_loop(0, tiles, link, 0)

    def one(t, listed):
        row = rows_ref[t]
        both = both_ref[t]
        present_ref[row] = present_ref[row] + (both[:, :order] + jnp.abs(both[:, order:]))
        closes = done_ref[t]

        @pl.when(closes == 1)
        def _():
            def add(prior):
                both_ref[t] = both_ref[t] + both_ref[prior]
                return back_ref[prior]

            lax.while_loop(lambda prior: prior >= 0, add, back_ref[t])
            small_ref[listed] = both_ref[t].astype(F32).astype(F8)
            leave(listed).start()
            plan_ref[listed] = row | (slots_ref[t] << 8)

        return listed + closes

    def chunk(c, listed):
        for copy in copies(c):
            copy.wait()
        for j in range(CHUNK):
            listed = one(c * CHUNK + j, listed)
        return listed

    def pad(listed):
        short = (UNROLL - listed % UNROLL) % UNROLL
        for j in range(UNROLL - 1):

            @pl.when(j < short)
            def _():
                small_ref[listed + j] = jnp.zeros(small_ref.shape[1:], F8)
                leave(listed + j).start()
                plan_ref[listed + j] = slots << 8

        return listed + short

    near = pad(lax.fori_loop(0, near_count // CHUNK, chunk, 0))
    every = pad(lax.fori_loop(near_count // CHUNK, chunks, chunk, near))
    plan_ref[tiles] = near // UNROLL
    plan_ref[tiles + 1] = every // UNROLL

    ones = jnp.ones((8, order), BF16)
    for r in range(rb_dev):
        degree = lax.dot_general(ones, present_ref[r], NT, preferred_element_type=F32)
        scale_ref[:, r * order : (r + 1) * order] = 1.0 / jnp.sqrt(jnp.maximum(degree, 1.0))

    def left(e, _):
        leave(e).wait()
        return _

    lax.fori_loop(0, every, left, 0)


def in_hbm(x):
    return pltpu.with_memory_space_constraint(x, pltpu.HBM)


def tiles_call(rows, slots, real, imag, rb_dev, near_count):
    tiles, order, _ = real.shape
    nblk = lax.axis_size("blk")
    return pl.pallas_call(
        functools.partial(tiles_kernel, near_count),
        name="tiles",
        out_shape=(
            pltpu.HBM((tiles, order, 2 * order), F8),
            sds((8, rb_dev * order), F32),
            sds((tiles + 32,), I32),
        ),
        in_specs=[SMEM, SMEM, ANY, ANY],
        out_specs=(ANY, VMEM, SMEM),
        scratch_shapes=[
            pltpu.VMEM((tiles, order, 2 * order), BF16),
            pltpu.VMEM((tiles, order, 2 * order), F8),
            pltpu.VMEM((rb_dev, order, order), BF16),
            pltpu.SMEM((rb_dev * (rb_dev + nblk),), I32),
            pltpu.SMEM((tiles,), I32),
            pltpu.SMEM((tiles,), I32),
            pltpu.SemaphoreType.DMA((tiles // CHUNK, 2)),
            pltpu.SemaphoreType.DMA((tiles,)),
        ],
        compiler_params=params(48),
        cost_estimate=pl.CostEstimate(flops=1 << 28, bytes_accessed=2 * real.size * 2, transcendentals=0),
    )(in_hbm(rows), in_hbm(slots), in_hbm(real), in_hbm(imag))


def send_blocks(field, scale_ref, sent_ref, pick, out_ref):
    order = sent_ref.shape[2]
    for r in range(sent_ref.shape[0]):
        at = slice(r * order, (r + 1) * order)
        sent_ref[r] = (field[:, at] * scale_ref[0:1, at]).astype(BF16)
    for p in range(out_ref.shape[0]):
        out_ref[p] = sent_ref[pick(p)]


def first_kernel(y_ref, scale_ref, wanted_ref, sent_ref, out_ref):
    send_blocks(y_ref, scale_ref, sent_ref, lambda p: wanted_ref[p, 0], out_ref)


def load_groups(packed_hbm, tiles_ref, sems, lo, hi):
    def copy(g):
        at = pl.ds((g - lo) * UNROLL, UNROLL)
        return pltpu.make_async_copy(
            packed_hbm.at[pl.ds(g * UNROLL, UNROLL)], tiles_ref.at[at], sems.at[g - lo]
        )

    def begin(g, _):
        copy(g).start()
        return _

    lax.fori_loop(lo, hi, begin, 0)
    return copy


def split_sources(source, x_ref):
    count, group, order = source.shape
    most = jnp.zeros((group, order), F32)
    for p in range(count):
        most = jnp.maximum(most, jnp.abs(source[p].astype(F32)))
    most = jnp.broadcast_to(jnp.max(most, axis=1, keepdims=True), (group, 128))
    most = jnp.maximum(jnp.maximum(most, jnp.abs(turn_rows(most))), TINY)
    size = most[:, 0:1] / TOP
    inverse = TOP / most[:, 0:1]
    for p in range(count):
        scaled = source[p].astype(F32) * inverse
        for side, part in enumerate((scaled, turn_rows(scaled))):
            at = slice(side * order, (side + 1) * order)
            for k in range(PARTS):
                short = part.astype(F8)
                x_ref[p, k * group : (k + 1) * group, at] = short
                part = (part - short.astype(F32)) * FINER
    x_ref[count] = jnp.zeros_like(x_ref[count])
    return size


def multiply(plan_ref, lo, hi, copy, tiles_ref, load, acc_ref):
    def group(g, _):
        copy(g).wait()
        done = []
        for j in range(UNROLL):
            code = plan_ref[g * UNROLL + j]
            tile = tiles_ref[(g - lo) * UNROLL + j]
            product = lax.dot_general(tile, load(code >> 8), NT, preferred_element_type=F32)
            done.append((code & 255, product))
        for row, product in done:
            acc_ref[row] = acc_ref[row] + product
        return _

    lax.fori_loop(lo, hi, group, 0)


def collect(acc, size):
    group = size.shape[0]
    flat = acc.T
    total = flat[(PARTS - 1) * group : PARTS * group]
    for k in range(PARTS - 2, -1, -1):
        total = flat[k * group : (k + 1) * group] + total * (1.0 / FINER)
    return total * size


def near_kernel(plan_ref, packed_hbm, sent_ref, out_ref, tiles_ref, x_ref, acc_ref, sems):
    rb_dev = sent_ref.shape[0]
    at = plan_ref.shape[0] - 32
    hi = plan_ref[at]
    copy = load_groups(packed_hbm, tiles_ref, sems, 0, hi)
    acc_ref[...] = jnp.zeros_like(acc_ref)
    size = split_sources(sent_ref, x_ref)
    multiply(plan_ref, 0, hi, copy, tiles_ref, lambda c: x_ref[jnp.minimum(c, rb_dev)], acc_ref)
    for r in range(rb_dev):
        out_ref[r] = collect(acc_ref[r], size)


def step_kernel(step, plan_ref, wanted_ref, packed_hbm, scale_ref, near_ref, now_ref, before_ref, arrived_ref, *refs):
    last = step == STEPS - 1
    next_ref = refs[0]
    tiles_ref, x_ref, acc_ref, sems = refs[-4:]
    rb_dev, _, order = near_ref.shape
    at = plan_ref.shape[0] - 32
    lo, hi = plan_ref[at], plan_ref[at + 1]
    copy = load_groups(packed_hbm, tiles_ref, sems, lo, hi)
    acc_ref[...] = jnp.zeros_like(acc_ref)
    size = split_sources(arrived_ref, x_ref)
    multiply(plan_ref, lo, hi, copy, tiles_ref, lambda c: x_ref[c - rb_dev], acc_ref)
    for r in range(rb_dev):
        at = slice(r * order, (r + 1) * order)
        now = now_ref[:, at]
        applied = scale_ref[0:1, at] * (near_ref[r] + collect(acc_ref[r], size))
        moved = ((1.0 - center) * now - applied) / half_width
        next_ref[:, at] = moved if step == 0 else 2.0 * moved - before_ref[:, at]
    if not last:
        send_blocks(next_ref, scale_ref, refs[1], lambda p: wanted_ref[p, 0], refs[2])


def all_rows(own_ref, arrived, all_ref):
    c = lax.axis_index("col")
    all_ref[c] = own_ref[...].astype(BF16)
    for s, ref in enumerate(arrived, 1):
        all_ref[c ^ s] = ref[...]
    n, group, rows = all_ref.shape
    return all_ref[...].reshape(n * group, rows)


def gram_kernel(own_ref, *refs):
    arrived, (gram_ref, all_ref, full_ref) = refs[:-3], refs[-3:]
    rows = all_rows(own_ref, arrived, all_ref)
    full_ref[...] = lax.dot_general(rows, rows, NT, preferred_element_type=F32)
    half = gram_ref.shape[0]
    even = full_ref[pl.ds(0, half, stride=2), :]
    odd = full_ref[pl.ds(1, half, stride=2), :]
    gram_ref[...] = even + turn_lanes(odd)


PANEL = 32


def factor_kernel(grams, nodes, own_ref, *refs):
    parts = refs[:grams]
    arrived = refs[grams:-4]
    out_ref, all_ref, work_ref, inverse_ref = refs[-4:]
    group = own_ref.shape[0]
    order = work_ref.shape[0]
    total = parts[0][...]
    for part in parts[1:]:
        total = total + part[...]
    half = total.shape[0]
    work_ref[pl.ds(0, half, stride=2), :] = total
    work_ref[pl.ds(1, half, stride=2), :] = -turn_lanes(total)
    row_at = lax.broadcasted_iota(I32, (order, order), 0)
    lane_at = lax.broadcasted_iota(I32, (order, order), 1)
    inverse_ref[...] = (row_at == lane_at).astype(F32)
    here = lax.broadcasted_iota(I32, (PANEL, order), 0)
    for top in range(0, order, PANEL):
        a = work_ref[top : top + PANEL, :]
        m = inverse_ref[top : top + PANEL, :]
        pivots = jnp.ones_like(a)
        for k in range(0, PANEL, 2):
            lane = top + k
            left = jnp.broadcast_to(a[:, lane : lane + 1], a.shape)
            right = jnp.broadcast_to(a[:, lane + 1 : lane + 2], a.shape)
            pivot = left[k : k + 1, :]
            inverse = 1.0 / pivot
            left = jnp.where(here > k + 1, left, 0.0) * inverse
            right = jnp.where(here > k + 1, right, 0.0) * inverse
            pivots = jnp.where((here == k) | (here == k + 1), pivot, pivots)
            a, m = (
                v - left * v[k : k + 1, :] - right * v[k + 1 : k + 2, :] for v in (a, m)
            )
        root = lax.rsqrt(pivots)
        a, m = a * root, m * root
        inverse_ref[top : top + PANEL, :] = m
        rest = top + PANEL
        if rest < order:
            update = lax.dot_general(
                a, jnp.concatenate([a, m], axis=1), TN, precision=lax.Precision.HIGHEST, preferred_element_type=F32
            )
            work_ref[rest:, :] = work_ref[rest:, :] - update[rest:, :order]
            inverse_ref[rest:, :] = inverse_ref[rest:, :] - update[rest:, order:]
    c = lax.axis_index("col")
    mine = inverse_ref[pl.ds(pl.multiple_of(c * group, group), group), :]
    mine = mine * math.sqrt(nodes)
    high = mine.astype(BF16)
    low = (mine - high.astype(F32)).astype(BF16)
    rows = all_rows(own_ref, arrived, all_ref)
    both = lax.dot_general(
        jnp.concatenate([high, low], axis=0), rows, (((1,), (0,)), ((), ())), preferred_element_type=F32
    )
    own = own_ref[...]
    lost = own - own.astype(BF16).astype(F32)
    own_lanes = (
        lax.broadcasted_iota(I32, (order, group), 0)
        == lax.broadcasted_iota(I32, (order, group), 1) + c * group
    ).astype(BF16)
    square = jnp.dot(high, own_lanes, preferred_element_type=F32).astype(BF16)
    out_ref[...] = (
        both[:group] + both[group:] + jnp.dot(square, lost.astype(BF16), preferred_element_type=F32)
    )


def to_partner(x, axis, mask):
    n = lax.axis_size(axis)
    return lax.ppermute(x, axis, [(i, i ^ mask) for i in range(n)])


def per_device(y_start, tile_real, tile_imag, tile_rows, tile_slots, fetch_pick):
    group, rows = y_start.shape
    tiles, order, _ = tile_real.shape
    rb_dev = rows // order
    nblk = lax.axis_size("blk")
    ncol = lax.axis_size("col")
    near_count = LOC_RB * rb_dev
    wanted = lax.all_to_all(
        fetch_pick.reshape(nblk, 1), "blk", split_axis=0, concat_axis=0, tiled=True
    )
    packed, scale, plan = tiles_call(tile_rows, tile_slots, tile_real, tile_imag, rb_dev, near_count)

    own_blocks = sds((rb_dev, group, order), BF16)
    out_blocks = sds((nblk, group, order), BF16)
    sent, blocks = pl.pallas_call(
        first_kernel,
        name="first",
        out_shape=(own_blocks, out_blocks),
        in_specs=[VMEM, VMEM, SMEM],
        out_specs=(VMEM, VMEM),
        compiler_params=params(LIMIT),
    )(y_start, scale, wanted)

    def scratch(entries, sources):
        return [
            pltpu.VMEM((entries, order, 2 * order), F8),
            pltpu.VMEM((sources + 1, PARTS * group, 2 * order), F8),
            pltpu.VMEM((rb_dev, order, PARTS * group), F32),
            pltpu.SemaphoreType.DMA((entries // UNROLL,)),
        ]

    previous, current = y_start, y_start
    for step in range(STEPS):
        arrived = lax.all_to_all(blocks, "blk", split_axis=0, concat_axis=0, tiled=True)
        near = pl.pallas_call(
            near_kernel,
            name="near",
            out_shape=sds((rb_dev, group, order), F32),
            in_specs=[SMEM, ANY, VMEM],
            out_specs=VMEM,
            scratch_shapes=scratch(near_count, rb_dev),
            compiler_params=params(LIMIT),
            cost_estimate=pl.CostEstimate(flops=1 << 28, bytes_accessed=1 << 21, transcendentals=0),
        )(plan, in_hbm(packed), sent)
        last = step == STEPS - 1
        more = () if last else (own_blocks, out_blocks)
        out = pl.pallas_call(
            functools.partial(step_kernel, step),
            name="step",
            out_shape=(sds((group, rows), F32), *more),
            in_specs=[SMEM, SMEM, ANY] + [VMEM] * 5,
            out_specs=(VMEM,) * (1 + len(more)),
            scratch_shapes=scratch(tiles - near_count, nblk),
            compiler_params=params(LIMIT),
        )(plan, wanted, in_hbm(packed), scale, near, current, previous, arrived)
        previous, current = current, out[0]
        if not last:
            sent, blocks = out[1:]

    rounded = current.astype(BF16)
    if ncol == 4:
        beside, across = to_partner(rounded, "col", 1), to_partner(rounded, "col", 2)
        others = [beside, across, to_partner(across, "col", 1)]
    else:
        others = [to_partner(rounded, "col", s) for s in range(1, ncol)]
    vectors = group * ncol
    part = pl.pallas_call(
        gram_kernel,
        name="gram",
        out_shape=sds((vectors // 2, vectors), F32),
        in_specs=[VMEM] * (1 + len(others)),
        out_specs=VMEM,
        scratch_shapes=[pltpu.VMEM((ncol, group, rows), BF16), pltpu.VMEM((vectors, vectors), F32)],
        compiler_params=params(LIMIT),
    )(current, *others)
    wide = 1
    while 2 * wide < nblk:
        part = part + to_partner(part, "blk", wide)
        wide *= 2
    parts = [part, to_partner(part, "blk", wide)] if wide < nblk else [part]
    return pl.pallas_call(
        functools.partial(factor_kernel, len(parts), rows * nblk),
        name="factor",
        out_shape=sds((group, rows), F32),
        in_specs=[VMEM] * (1 + len(parts) + len(others)),
        out_specs=VMEM,
        scratch_shapes=[
            pltpu.VMEM((ncol, group, rows), BF16),
            pltpu.VMEM((vectors, vectors), F32),
            pltpu.VMEM((vectors, vectors), F32),
        ],
        compiler_params=params(LIMIT),
    )(current, *parts, *others)


def solution(mesh):
    return jax.shard_map(
        per_device,
        mesh=mesh,
        in_specs=(
            P("col", "blk"),
            P("blk", None, None),
            P("blk", None, None),
            P("blk"),
            P("blk"),
            P("blk", None),
        ),
        out_specs=P("col", "blk"),
        check_vma=False,
    )
```

```python
import functools
import math

import jax
import jax.numpy as jnp
from jax import lax
from jax.experimental import pallas as pl
from jax.experimental.pallas import tpu as pltpu
from jax.sharding import PartitionSpec as P

LOC_RB = 2
STEPS = 4
UNROLL = 4
CHUNK = 4
MERGE = 16
TOP = 7.0
FINER = 16.0
SPLIT = float((1 << 20) + 1)
TINY = 1e-30
MIB = 1 << 20
LIMIT = 24

center = 1.25
half_width = 0.75

F32 = jnp.float32
BF16 = jnp.bfloat16
F8 = jnp.float8_e4m3fn
I32 = jnp.int32

VMEM = pl.BlockSpec(memory_space=pltpu.VMEM)
SMEM = pl.BlockSpec(memory_space=pltpu.SMEM)
ANY = pl.BlockSpec(memory_space=pl.ANY)

NT = (((1,), (1,)), ((), ()))
TN = (((0,), (0,)), ((), ()))


def sds(shape, dtype):
    return jax.ShapeDtypeStruct(shape, dtype)


def params(limit):
    return pltpu.CompilerParams(vmem_limit_bytes=limit * MIB)


def turn_rows(values):
    rows = values.shape[0]
    even = lax.broadcasted_iota(I32, values.shape, 0) % 2 == 0
    below = pltpu.roll(values, rows - 1, 0)
    above = pltpu.roll(values, 1, 0)
    return jnp.where(even, -below, above)


def turn_lanes(values):
    lanes = values.shape[1]
    even = lax.broadcasted_iota(I32, values.shape, 1) % 2 == 0
    after = pltpu.roll(values, lanes - 1, 1)
    before = pltpu.roll(values, 1, 1)
    return jnp.where(even, after, -before)


def tiles_kernel(
    near_count,
    rows_ref,
    slots_ref,
    real_hbm,
    imag_hbm,
    packed_hbm,
    scale_ref,
    plan_ref,
    both_ref,
    small_ref,
    present_ref,
    table_ref,
    back_ref,
    done_ref,
    in_sems,
    out_sems,
):
    tiles, order, _ = both_ref.shape
    rb_dev = present_ref.shape[0]
    slots = rb_dev + lax.axis_size("blk")
    chunks = tiles // CHUNK

    def copies(c):
        at = pl.ds(c * CHUNK, CHUNK)
        return (
            pltpu.make_async_copy(real_hbm.at[at], both_ref.at[at, :, 0:order], in_sems.at[c, 0]),
            pltpu.make_async_copy(imag_hbm.at[at], both_ref.at[at, :, order : 2 * order], in_sems.at[c, 1]),
        )

    def leave(e):
        return pltpu.make_async_copy(small_ref.at[e], packed_hbm.at[e], out_sems.at[e])

    for c in range(chunks):
        for copy in copies(c):
            copy.start()

    def clear(key, _):
        table_ref[key] = -1
        return _

    lax.fori_loop(0, rb_dev * slots, clear, 0)
    present_ref[...] = jnp.zeros_like(present_ref)

    def link(t, carry):
        key = rows_ref[t] * slots + slots_ref[t]
        seen = table_ref[key]
        before = seen & 255
        length = seen >> 8
        joins = (seen >= 0) & (length < MERGE)
        back_ref[t] = jnp.where(joins, before, -1)
        done_ref[t] = 1

        @pl.when(joins)
        def _():
            done_ref[before] = 0

        table_ref[key] = t | (jnp.where(joins, length + 1, 1) << 8)
        return carry

    lax.fori_loop(0, tiles, link, 0)

    def one(t, listed):
        row = rows_ref[t]
        both = both_ref[t]
        present_ref[row] = present_ref[row] + (both[:, :order] + jnp.abs(both[:, order:]))
        closes = done_ref[t]

        @pl.when(closes == 1)
        def _():
            def add(prior):
                both_ref[t] = both_ref[t] + both_ref[prior]
                return back_ref[prior]

            lax.while_loop(lambda prior: prior >= 0, add, back_ref[t])
            small_ref[listed] = both_ref[t].astype(F32).astype(F8)
            leave(listed).start()
            plan_ref[listed] = row | (slots_ref[t] << 8)

        return listed + closes

    def chunk(c, listed):
        for copy in copies(c):
            copy.wait()
        for j in range(CHUNK):
            listed = one(c * CHUNK + j, listed)
        return listed

    def pad(listed):
        short = (UNROLL - listed % UNROLL) % UNROLL
        for j in range(UNROLL - 1):

            @pl.when(j < short)
            def _():
                small_ref[listed + j] = jnp.zeros(small_ref.shape[1:], F8)
                leave(listed + j).start()
                plan_ref[listed + j] = slots << 8

        return listed + short

    near = pad(lax.fori_loop(0, near_count // CHUNK, chunk, 0))
    every = pad(lax.fori_loop(near_count // CHUNK, chunks, chunk, near))
    plan_ref[tiles] = near // UNROLL
    plan_ref[tiles + 1] = every // UNROLL

    ones = jnp.ones((8, order), BF16)
    for r in range(rb_dev):
        degree = lax.dot_general(ones, present_ref[r], NT, preferred_element_type=F32)
        scale_ref[:, r * order : (r + 1) * order] = 1.0 / jnp.sqrt(jnp.maximum(degree, 1.0))

    def left(e, _):
        leave(e).wait()
        return _

    lax.fori_loop(0, every, left, 0)


def in_hbm(x):
    return pltpu.with_memory_space_constraint(x, pltpu.HBM)


def tiles_call(rows, slots, real, imag, rb_dev, near_count):
    tiles, order, _ = real.shape
    nblk = lax.axis_size("blk")
    return pl.pallas_call(
        functools.partial(tiles_kernel, near_count),
        name="tiles",
        out_shape=(
            pltpu.HBM((tiles, order, 2 * order), F8),
            sds((8, rb_dev * order), F32),
            sds((tiles + 32,), I32),
        ),
        in_specs=[SMEM, SMEM, ANY, ANY],
        out_specs=(ANY, VMEM, SMEM),
        scratch_shapes=[
            pltpu.VMEM((tiles, order, 2 * order), BF16),
            pltpu.VMEM((tiles, order, 2 * order), F8),
            pltpu.VMEM((rb_dev, order, order), BF16),
            pltpu.SMEM((rb_dev * (rb_dev + nblk),), I32),
            pltpu.SMEM((tiles,), I32),
            pltpu.SMEM((tiles,), I32),
            pltpu.SemaphoreType.DMA((tiles // CHUNK, 2)),
            pltpu.SemaphoreType.DMA((tiles,)),
        ],
        compiler_params=params(48),
        cost_estimate=pl.CostEstimate(flops=1 << 28, bytes_accessed=2 * real.size * 2, transcendentals=0),
    )(in_hbm(rows), in_hbm(slots), in_hbm(real), in_hbm(imag))


def rounded_block(field, scale_ref, r, order):
    at = slice(r * order, (r + 1) * order)
    return (field[:, at] * scale_ref[0:1, at]).astype(BF16)


def send_blocks(field, scale_ref, wanted_ref, out_ref, sent_ref):
    order = sent_ref.shape[2]
    me = lax.axis_index("blk")
    for r in range(sent_ref.shape[0]):
        sent_ref[r] = rounded_block(field, scale_ref, r, order)
    for p in range(out_ref.shape[0]):
        out_ref[p] = sent_ref[wanted_ref[p, 0, me]]


def first_kernel(y_ref, scale_ref, wanted_ref, out_ref, sent_ref):
    send_blocks(y_ref, scale_ref, wanted_ref, out_ref, sent_ref)


def load_groups(packed_hbm, tiles_ref, sems, lo, hi):
    def copy(g):
        at = pl.ds((g - lo) * UNROLL, UNROLL)
        return pltpu.make_async_copy(
            packed_hbm.at[pl.ds(g * UNROLL, UNROLL)], tiles_ref.at[at], sems.at[g - lo]
        )

    def begin(g, _):
        copy(g).start()
        return _

    lax.fori_loop(lo, hi, begin, 0)
    return copy


def split_sources(count, source, x_ref):
    _, rows, width = x_ref.shape
    group, order = rows // 2, width // 2
    most = jnp.zeros((group, order), F32)
    for p in range(count):
        most = jnp.maximum(most, jnp.abs(source(p).astype(F32)))
    most = jnp.broadcast_to(jnp.max(most, axis=1, keepdims=True), (group, 128))
    most = jnp.maximum(jnp.maximum(most, jnp.abs(turn_rows(most))), TINY)
    power = jnp.floor(jnp.log2(most))
    size = jnp.exp2(power - TOP)
    inverse = jnp.exp2(TOP - power)[:, 0:1]
    for p in range(count):
        scaled = source(p).astype(F32) * inverse
        far = scaled * SPLIT
        high = far - (far - scaled)
        low = (scaled - high) * FINER
        for k, part in enumerate((high, low)):
            at = slice(k * group, (k + 1) * group)
            x_ref[p, at, :order] = part.astype(F8)
            x_ref[p, at, order:] = turn_rows(part).astype(F8)
    x_ref[count] = jnp.zeros_like(x_ref[count])
    return size[:, 0:1]


def multiply(plan_ref, lo, hi, copy, tiles_ref, load, acc_ref):
    def group(g, _):
        copy(g).wait()
        done = []
        for j in range(UNROLL):
            code = plan_ref[g * UNROLL + j]
            tile = tiles_ref[(g - lo) * UNROLL + j]
            product = lax.dot_general(load(code >> 8), tile, NT, preferred_element_type=F32)
            done.append((code & 255, product))
        for row, product in done:
            acc_ref[row] = acc_ref[row] + product
        return _

    lax.fori_loop(lo, hi, group, 0)


def collect(acc, size):
    group = size.shape[0]
    return (acc[:group] + acc[group:] * (1.0 / FINER)) * size


def near_kernel(step, plan_ref, packed_hbm, scale_ref, now_ref, before_ref, base_ref, tiles_ref, x_ref, acc_ref, sems):
    rb_dev, _, order = acc_ref.shape
    end = plan_ref.shape[0] - 32
    hi = plan_ref[end]
    copy = load_groups(packed_hbm, tiles_ref, sems, 0, hi)
    acc_ref[...] = jnp.zeros_like(acc_ref)
    size = split_sources(rb_dev, lambda r: rounded_block(now_ref, scale_ref, r, order), x_ref)
    multiply(plan_ref, 0, hi, copy, tiles_ref, lambda c: x_ref[jnp.minimum(c, rb_dev)], acc_ref)
    for r in range(rb_dev):
        at = slice(r * order, (r + 1) * order)
        applied = scale_ref[0:1, at] * collect(acc_ref[r], size)
        moved = ((1.0 - center) * now_ref[:, at] - applied) / half_width
        base_ref[:, at] = moved if step == 0 else 2.0 * moved - before_ref[:, at]


def step_kernel(step, plan_ref, wanted_ref, packed_hbm, scale_ref, base_ref, arrived_ref, *refs):
    last = step == STEPS - 1
    next_ref = refs[0]
    tiles_ref, x_ref, acc_ref, sems = refs[-4:]
    rb_dev, _, order = acc_ref.shape
    end = plan_ref.shape[0] - 32
    lo, hi = plan_ref[end], plan_ref[end + 1]
    copy = load_groups(packed_hbm, tiles_ref, sems, lo, hi)
    acc_ref[...] = jnp.zeros_like(acc_ref)
    size = split_sources(arrived_ref.shape[0], lambda p: arrived_ref[p], x_ref)
    size = size * ((1.0 if step == 0 else 2.0) / half_width)
    multiply(plan_ref, lo, hi, copy, tiles_ref, lambda c: x_ref[c - rb_dev], acc_ref)
    for r in range(rb_dev):
        at = slice(r * order, (r + 1) * order)
        next_ref[:, at] = base_ref[:, at] - scale_ref[0:1, at] * collect(acc_ref[r], size)
    if not last:
        send_blocks(next_ref, scale_ref, wanted_ref, refs[1], refs[2])


def all_rows(own_ref, arrived, all_ref):
    c = lax.axis_index("col")
    all_ref[c] = own_ref[...].astype(BF16)
    for s, ref in enumerate(arrived, 1):
        all_ref[c ^ s] = ref[...]
    n, group, rows = all_ref.shape
    return all_ref[...].reshape(n * group, rows)


def gram_kernel(own_ref, *refs):
    arrived, (gram_ref, all_ref, full_ref) = refs[:-3], refs[-3:]
    rows = all_rows(own_ref, arrived, all_ref)
    full_ref[...] = lax.dot_general(rows, rows, NT, preferred_element_type=F32)
    half = gram_ref.shape[0]
    even = full_ref[pl.ds(0, half, stride=2), :]
    odd = full_ref[pl.ds(1, half, stride=2), :]
    gram_ref[...] = even + turn_lanes(odd)


PANEL = 32


def factor_kernel(grams, nodes, own_ref, *refs):
    parts = refs[:grams]
    arrived = refs[grams:-4]
    out_ref, all_ref, work_ref, inverse_ref = refs[-4:]
    group = own_ref.shape[0]
    order = work_ref.shape[0]
    total = parts[0][...]
    for part in parts[1:]:
        total = total + part[...]
    half = total.shape[0]
    work_ref[pl.ds(0, half, stride=2), :] = total
    work_ref[pl.ds(1, half, stride=2), :] = -turn_lanes(total)
    row_at = lax.broadcasted_iota(I32, (order, order), 0)
    lane_at = lax.broadcasted_iota(I32, (order, order), 1)
    inverse_ref[...] = (row_at == lane_at).astype(F32)
    here = lax.broadcasted_iota(I32, (PANEL, order), 0)
    for top in range(0, order, PANEL):
        a = work_ref[top : top + PANEL, :]
        m = inverse_ref[top : top + PANEL, :]
        pivots = jnp.ones_like(a)
        for k in range(0, PANEL, 2):
            lane = top + k
            left = jnp.broadcast_to(a[:, lane : lane + 1], a.shape)
            right = jnp.broadcast_to(a[:, lane + 1 : lane + 2], a.shape)
            pivot = left[k : k + 1, :]
            inverse = 1.0 / pivot
            left = jnp.where(here > k + 1, left, 0.0) * inverse
            right = jnp.where(here > k + 1, right, 0.0) * inverse
            pivots = jnp.where((here == k) | (here == k + 1), pivot, pivots)
            a, m = (
                v - left * v[k : k + 1, :] - right * v[k + 1 : k + 2, :] for v in (a, m)
            )
        root = lax.rsqrt(pivots)
        a, m = a * root, m * root
        inverse_ref[top : top + PANEL, :] = m
        rest = top + PANEL
        if rest < order:
            update = lax.dot_general(
                a, jnp.concatenate([a, m], axis=1), TN, precision=lax.Precision.HIGHEST, preferred_element_type=F32
            )
            work_ref[rest:, :] = work_ref[rest:, :] - update[rest:, :order]
            inverse_ref[rest:, :] = inverse_ref[rest:, :] - update[rest:, order:]
    c = lax.axis_index("col")
    mine = inverse_ref[pl.ds(pl.multiple_of(c * group, group), group), :]
    mine = mine * math.sqrt(nodes)
    high = mine.astype(BF16)
    low = (mine - high.astype(F32)).astype(BF16)
    rows = all_rows(own_ref, arrived, all_ref)
    both = lax.dot_general(
        jnp.concatenate([high, low], axis=0), rows, (((1,), (0,)), ((), ())), preferred_element_type=F32
    )
    own = own_ref[...]
    lost = own - own.astype(BF16).astype(F32)
    own_lanes = (
        lax.broadcasted_iota(I32, (order, group), 0)
        == lax.broadcasted_iota(I32, (order, group), 1) + c * group
    ).astype(BF16)
    square = jnp.dot(high, own_lanes, preferred_element_type=F32).astype(BF16)
    out_ref[...] = (
        both[:group] + both[group:] + jnp.dot(square, lost.astype(BF16), preferred_element_type=F32)
    )


def to_partner(x, axis, mask):
    n = lax.axis_size(axis)
    return lax.ppermute(x, axis, [(i, i ^ mask) for i in range(n)])


def per_device(y_start, tile_real, tile_imag, tile_rows, tile_slots, fetch_pick):
    group, rows = y_start.shape
    tiles, order, _ = tile_real.shape
    rb_dev = rows // order
    nblk = lax.axis_size("blk")
    ncol = lax.axis_size("col")
    near_count = LOC_RB * rb_dev
    wanted = lax.all_to_all(
        jnp.broadcast_to(fetch_pick[None], (nblk, 1, nblk)), "blk", split_axis=0, concat_axis=0, tiled=True
    )
    packed, scale, plan = tiles_call(tile_rows, tile_slots, tile_real, tile_imag, rb_dev, near_count)

    out_blocks = sds((nblk, group, order), BF16)
    sent_scratch = pltpu.VMEM((rb_dev, group, order), BF16)
    blocks = pl.pallas_call(
        first_kernel,
        name="first",
        out_shape=out_blocks,
        in_specs=[VMEM, VMEM, SMEM],
        out_specs=VMEM,
        scratch_shapes=[sent_scratch],
        compiler_params=params(LIMIT),
    )(y_start, scale, wanted)

    def scratch(entries, sources):
        return [
            pltpu.VMEM((entries, order, 2 * order), F8),
            pltpu.VMEM((sources + 1, 2 * group, 2 * order), F8),
            pltpu.VMEM((rb_dev, 2 * group, order), F32),
            pltpu.SemaphoreType.DMA((entries // UNROLL,)),
        ]

    vectors_here = sds((group, rows), F32)
    previous, current = y_start, y_start
    for step in range(STEPS):
        arrived = lax.all_to_all(blocks, "blk", split_axis=0, concat_axis=0, tiled=True)
        base = pl.pallas_call(
            functools.partial(near_kernel, step),
            name="near",
            out_shape=vectors_here,
            in_specs=[SMEM, ANY] + [VMEM] * 3,
            out_specs=VMEM,
            scratch_shapes=scratch(near_count, rb_dev),
            compiler_params=params(LIMIT),
            cost_estimate=pl.CostEstimate(flops=1 << 28, bytes_accessed=1 << 21, transcendentals=0),
        )(plan, in_hbm(packed), scale, current, previous)
        last = step == STEPS - 1
        out = pl.pallas_call(
            functools.partial(step_kernel, step),
            name="step",
            out_shape=[vectors_here] if last else [vectors_here, out_blocks],
            in_specs=[SMEM, SMEM, ANY] + [VMEM] * 3,
            out_specs=[VMEM] if last else [VMEM, VMEM],
            scratch_shapes=([] if last else [sent_scratch]) + scratch(tiles - near_count, nblk),
            compiler_params=params(LIMIT),
        )(plan, wanted, in_hbm(packed), scale, base, arrived)
        previous, current = current, out[0]
        if not last:
            blocks = out[1]

    rounded = current.astype(BF16)
    if ncol == 4:
        beside, across = to_partner(rounded, "col", 1), to_partner(rounded, "col", 2)
        others = [beside, across, to_partner(across, "col", 1)]
    else:
        others = [to_partner(rounded, "col", s) for s in range(1, ncol)]
    vectors = group * ncol
    part = pl.pallas_call(
        gram_kernel,
        name="gram",
        out_shape=sds((vectors // 2, vectors), F32),
        in_specs=[VMEM] * (1 + len(others)),
        out_specs=VMEM,
        scratch_shapes=[pltpu.VMEM((ncol, group, rows), BF16), pltpu.VMEM((vectors, vectors), F32)],
        compiler_params=params(LIMIT),
    )(current, *others)
    wide = 1
    while 4 * wide < nblk:
        part = part + to_partner(part, "blk", wide)
        wide *= 2
    parts = [part] + [to_partner(part, "blk", s * wide) for s in range(1, nblk // wide)]
    return pl.pallas_call(
        functools.partial(factor_kernel, len(parts), rows * nblk),
        name="factor",
        out_shape=sds((group, rows), F32),
        in_specs=[VMEM] * (1 + len(parts) + len(others)),
        out_specs=VMEM,
        scratch_shapes=[
            pltpu.VMEM((ncol, group, rows), BF16),
            pltpu.VMEM((vectors, vectors), F32),
            pltpu.VMEM((vectors, vectors), F32),
        ],
        compiler_params=params(LIMIT),
    )(current, *parts, *others)


def solution(mesh):
    return jax.shard_map(
        per_device,
        mesh=mesh,
        in_specs=(
            P("col", "blk"),
            P("blk", None, None),
            P("blk", None, None),
            P("blk"),
            P("blk"),
            P("blk", None),
        ),
        out_specs=P("col", "blk"),
        check_vma=False,
    )
```

```python
import functools
import math

import jax
import jax.numpy as jnp
from jax import lax
from jax.experimental import pallas as pl
from jax.experimental.pallas import tpu as pltpu
from jax.sharding import PartitionSpec as P

LOC_RB = 2
STEPS = 4
UNROLL = 4
KEPT = 16
CHUNK = 4
MERGE = 16
TOP = 7.0
FINER = 16.0
SPLIT = float((1 << 20) + 1)
TINY = 1e-30
MIB = 1 << 20
LIMIT = 24

center = 1.25
half_width = 0.75

F32 = jnp.float32
BF16 = jnp.bfloat16
F8 = jnp.float8_e4m3fn
I32 = jnp.int32

VMEM = pl.BlockSpec(memory_space=pltpu.VMEM)
SMEM = pl.BlockSpec(memory_space=pltpu.SMEM)
ANY = pl.BlockSpec(memory_space=pl.ANY)

NT = (((1,), (1,)), ((), ()))
TN = (((0,), (0,)), ((), ()))


def sds(shape, dtype):
    return jax.ShapeDtypeStruct(shape, dtype)


def params(limit):
    return pltpu.CompilerParams(vmem_limit_bytes=limit * MIB)


def turn_rows(values):
    rows = values.shape[0]
    even = lax.broadcasted_iota(I32, values.shape, 0) % 2 == 0
    below = pltpu.roll(values, rows - 1, 0)
    above = pltpu.roll(values, 1, 0)
    return jnp.where(even, -below, above)


def turn_lanes(values):
    lanes = values.shape[1]
    even = lax.broadcasted_iota(I32, values.shape, 1) % 2 == 0
    after = pltpu.roll(values, lanes - 1, 1)
    before = pltpu.roll(values, 1, 1)
    return jnp.where(even, after, -before)


def tiles_kernel(
    near_count,
    rows_ref,
    slots_ref,
    real_hbm,
    imag_hbm,
    packed_hbm,
    kept_ref,
    scale_ref,
    plan_ref,
    both_ref,
    small_ref,
    present_ref,
    table_ref,
    back_ref,
    done_ref,
    in_sems,
    out_sems,
):
    kept = kept_ref.shape[0]
    tiles, order, _ = both_ref.shape
    rb_dev = present_ref.shape[0]
    slots = rb_dev + lax.axis_size("blk")
    chunks = tiles // CHUNK

    def copies(c):
        at = pl.ds(c * CHUNK, CHUNK)
        return (
            pltpu.make_async_copy(real_hbm.at[at], both_ref.at[at, :, 0:order], in_sems.at[c, 0]),
            pltpu.make_async_copy(imag_hbm.at[at], both_ref.at[at, :, order : 2 * order], in_sems.at[c, 1]),
        )

    def leave(e):
        return pltpu.make_async_copy(small_ref.at[e], packed_hbm.at[e], out_sems.at[e])

    for c in range(chunks):
        for copy in copies(c):
            copy.start()

    def clear(key, _):
        table_ref[key] = -1
        return _

    lax.fori_loop(0, rb_dev * slots, clear, 0)
    present_ref[...] = jnp.zeros_like(present_ref)

    def link(t, carry):
        key = rows_ref[t] * slots + slots_ref[t]
        seen = table_ref[key]
        before = seen & 255
        length = seen >> 8
        joins = (seen >= 0) & (length < MERGE)
        back_ref[t] = jnp.where(joins, before, -1)
        done_ref[t] = 1

        @pl.when(joins)
        def _():
            done_ref[before] = 0

        table_ref[key] = t | (jnp.where(joins, length + 1, 1) << 8)
        return carry

    lax.fori_loop(0, tiles, link, 0)

    def put(e, skip, value):
        @pl.when(e < skip)
        def _():
            kept_ref[e - skip + kept] = value()

        @pl.when(e >= skip)
        def _():
            small_ref[e] = value()
            leave(e).start()

    def one(skip, t, listed):
        row = rows_ref[t]
        both = both_ref[t]
        present_ref[row] = present_ref[row] + (both[:, :order] + jnp.abs(both[:, order:]))
        closes = done_ref[t]

        @pl.when(closes == 1)
        def _():
            def add(prior):
                both_ref[t] = both_ref[t] + both_ref[prior]
                return back_ref[prior]

            lax.while_loop(lambda prior: prior >= 0, add, back_ref[t])
            put(listed, skip, lambda: both_ref[t].astype(F8))
            plan_ref[listed] = row | (slots_ref[t] << 8)

        return listed + closes

    def chunk(skip, c, listed):
        for copy in copies(c):
            copy.wait()
        for j in range(CHUNK):
            listed = one(skip, c * CHUNK + j, listed)
        return listed

    def pad(skip, listed):
        short = (UNROLL - listed % UNROLL) % UNROLL
        for j in range(UNROLL - 1):

            @pl.when(j < short)
            def _():
                put(listed + j, skip, lambda: jnp.zeros(small_ref.shape[1:], F8))
                plan_ref[listed + j] = slots << 8

        return listed + short

    near = pad(0, lax.fori_loop(0, near_count // CHUNK, functools.partial(chunk, 0), 0))
    skip = near + kept
    every = pad(skip, lax.fori_loop(near_count // CHUNK, chunks, functools.partial(chunk, skip), near))
    plan_ref[tiles] = near // UNROLL
    plan_ref[tiles + 1] = every // UNROLL

    ones = jnp.ones((8, order), BF16)
    for r in range(rb_dev):
        degree = lax.dot_general(ones, present_ref[r], NT, preferred_element_type=F32)
        scale_ref[:, r * order : (r + 1) * order] = 1.0 / jnp.sqrt(jnp.maximum(degree, 1.0))

    def left(e, _):
        leave(e).wait()
        return _

    lax.fori_loop(0, near, left, 0)
    lax.fori_loop(skip, every, left, 0)


def in_hbm(x):
    return pltpu.with_memory_space_constraint(x, pltpu.HBM)


def tiles_call(rows, slots, real, imag, rb_dev, near_count):
    tiles, order, _ = real.shape
    nblk = lax.axis_size("blk")
    return pl.pallas_call(
        functools.partial(tiles_kernel, near_count),
        name="tiles",
        out_shape=(
            pltpu.HBM((tiles, order, 2 * order), F8),
            pltpu.VMEM((KEPT, order, 2 * order), F8),
            sds((8, rb_dev * order), F32),
            sds((tiles + 32,), I32),
        ),
        in_specs=[SMEM, SMEM, ANY, ANY],
        out_specs=(ANY, VMEM, VMEM, SMEM),
        scratch_shapes=[
            pltpu.VMEM((tiles, order, 2 * order), BF16),
            pltpu.VMEM((tiles, order, 2 * order), F8),
            pltpu.VMEM((rb_dev, order, order), BF16),
            pltpu.SMEM((rb_dev * (rb_dev + nblk),), I32),
            pltpu.SMEM((tiles,), I32),
            pltpu.SMEM((tiles,), I32),
            pltpu.SemaphoreType.DMA((tiles // CHUNK, 2)),
            pltpu.SemaphoreType.DMA((tiles,)),
        ],
        compiler_params=params(48),
        cost_estimate=pl.CostEstimate(flops=1 << 28, bytes_accessed=2 * real.size * 2, transcendentals=0),
    )(in_hbm(rows), in_hbm(slots), in_hbm(real), in_hbm(imag))


def rounded_block(field, scale_ref, r, order):
    at = slice(r * order, (r + 1) * order)
    return (field[:, at] * scale_ref[0:1, at]).astype(BF16)


def send_picked(wanted_ref, sent_ref, out_ref):
    me = lax.axis_index("blk")
    for p in range(out_ref.shape[0]):
        out_ref[p] = sent_ref[wanted_ref[p, 0, me]]


def first_kernel(y_ref, scale_ref, wanted_ref, out_ref, sent_ref):
    for r in range(sent_ref.shape[0]):
        sent_ref[r] = rounded_block(y_ref, scale_ref, r, sent_ref.shape[2])
    send_picked(wanted_ref, sent_ref, out_ref)


def load_groups(packed_hbm, tiles_ref, sems, lo, hi):
    def copy(g):
        at = pl.ds((g - lo) * UNROLL, UNROLL)
        return pltpu.make_async_copy(
            packed_hbm.at[pl.ds(g * UNROLL, UNROLL)], tiles_ref.at[at], sems.at[g - lo]
        )

    def begin(g, _):
        copy(g).start()
        return _

    lax.fori_loop(lo, hi, begin, 0)
    return copy


def split_sources(count, source, x_ref):
    _, rows, width = x_ref.shape
    group, order = rows // 2, width // 2
    most = jnp.zeros((group, order), F32)
    for p in range(count):
        most = jnp.maximum(most, jnp.abs(source(p).astype(F32)))
    most = jnp.broadcast_to(jnp.max(most, axis=1, keepdims=True), (group, 128))
    most = jnp.maximum(jnp.maximum(most, jnp.abs(turn_rows(most))), TINY)
    power = jnp.floor(jnp.log2(most))
    size = jnp.exp2(power - TOP)
    inverse = jnp.exp2(TOP - power)[:, 0:1]
    for p in range(count):
        scaled = source(p).astype(F32) * inverse
        far = scaled * SPLIT
        high = far - (far - scaled)
        low = (scaled - high) * FINER
        for k, part in enumerate((high, low)):
            at = slice(k * group, (k + 1) * group)
            x_ref[p, at, :order] = part.astype(F8)
            x_ref[p, at, order:] = turn_rows(part).astype(F8)
    x_ref[count] = jnp.zeros_like(x_ref[count])
    return size[:, 0:1]


def multiply(plan_ref, lo, hi, tile, load, acc_ref):
    def group(g, _):
        done = []
        for j in range(UNROLL):
            code = plan_ref[g * UNROLL + j]
            product = lax.dot_general(load(code >> 8), tile(g, j), NT, preferred_element_type=F32)
            done.append((code & 255, product))
        for row, product in done:
            acc_ref[row] = acc_ref[row] + product
        return _

    lax.fori_loop(lo, hi, group, 0)


def loaded(copy, tiles_ref, lo):
    def tile(g, j):
        if j == 0:
            copy(g).wait()
        return tiles_ref[(g - lo) * UNROLL + j]

    return tile


def collect(acc, size):
    group = size.shape[0]
    return (acc[:group] + acc[group:] * (1.0 / FINER)) * size


def near_kernel(step, plan_ref, packed_hbm, scale_ref, now_ref, before_ref, base_ref, tiles_ref, x_ref, acc_ref, sems):
    rb_dev, _, order = acc_ref.shape
    end = plan_ref.shape[0] - 32
    hi = plan_ref[end]
    copy = load_groups(packed_hbm, tiles_ref, sems, 0, hi)
    acc_ref[...] = jnp.zeros_like(acc_ref)
    size = split_sources(rb_dev, lambda r: rounded_block(now_ref, scale_ref, r, order), x_ref)
    multiply(plan_ref, 0, hi, loaded(copy, tiles_ref, 0), lambda c: x_ref[jnp.minimum(c, rb_dev)], acc_ref)
    for r in range(rb_dev):
        at = slice(r * order, (r + 1) * order)
        applied = scale_ref[0:1, at] * collect(acc_ref[r], size)
        moved = ((1.0 - center) * now_ref[:, at] - applied) / half_width
        base_ref[:, at] = moved if step == 0 else 2.0 * moved - before_ref[:, at]


def step_kernel(step, plan_ref, wanted_ref, packed_hbm, kept_ref, scale_ref, base_ref, arrived_ref, *refs):
    last = step == STEPS - 1
    next_ref = refs[0]
    tiles_ref, x_ref, acc_ref, sems = refs[-4:]
    rb_dev, _, order = acc_ref.shape
    end = plan_ref.shape[0] - 32
    lo, hi = plan_ref[end], plan_ref[end + 1]
    stay = jnp.minimum(lo + KEPT // UNROLL, hi)
    copy = load_groups(packed_hbm, tiles_ref, sems, stay, hi)
    acc_ref[...] = jnp.zeros_like(acc_ref)
    size = split_sources(arrived_ref.shape[0], lambda p: arrived_ref[p], x_ref)
    size = size * ((1.0 if step == 0 else 2.0) / half_width)
    multiply(
        plan_ref, lo, stay, lambda g, j: kept_ref[(g - lo) * UNROLL + j], lambda c: x_ref[c - rb_dev], acc_ref
    )
    multiply(plan_ref, stay, hi, loaded(copy, tiles_ref, stay), lambda c: x_ref[c - rb_dev], acc_ref)
    for r in range(rb_dev):
        at = slice(r * order, (r + 1) * order)
        scale = scale_ref[0:1, at]
        following = base_ref[:, at] - scale * collect(acc_ref[r], size)
        next_ref[:, at] = following
        if not last:
            refs[2][r] = (following * scale).astype(BF16)
    if not last:
        send_picked(wanted_ref, refs[2], refs[1])


def all_rows(own_ref, arrived, all_ref):
    c = lax.axis_index("col")
    all_ref[c] = own_ref[...].astype(BF16)
    for s, ref in enumerate(arrived, 1):
        all_ref[c ^ s] = ref[...]
    n, group, rows = all_ref.shape
    return all_ref[...].reshape(n * group, rows)


def gram_kernel(own_ref, *refs):
    arrived, (gram_ref, all_ref, full_ref) = refs[:-3], refs[-3:]
    rows = all_rows(own_ref, arrived, all_ref)
    full_ref[...] = lax.dot_general(rows, rows, NT, preferred_element_type=F32)
    half = gram_ref.shape[0]
    even = full_ref[pl.ds(0, half, stride=2), :]
    odd = full_ref[pl.ds(1, half, stride=2), :]
    gram_ref[...] = even + turn_lanes(odd)


PANEL = 32


def factor_kernel(grams, nodes, own_ref, *refs):
    parts = refs[:grams]
    arrived = refs[grams:-4]
    out_ref, all_ref, work_ref, inverse_ref = refs[-4:]
    group = own_ref.shape[0]
    order = work_ref.shape[0]
    total = parts[0][...]
    for part in parts[1:]:
        total = total + part[...]
    half = total.shape[0]
    work_ref[pl.ds(0, half, stride=2), :] = total
    work_ref[pl.ds(1, half, stride=2), :] = -turn_lanes(total)
    row_at = lax.broadcasted_iota(I32, (order, order), 0)
    lane_at = lax.broadcasted_iota(I32, (order, order), 1)
    inverse_ref[...] = (row_at == lane_at).astype(F32)
    here = lax.broadcasted_iota(I32, (PANEL, order), 0)
    for top in range(0, order, PANEL):
        a = work_ref[top : top + PANEL, :]
        m = inverse_ref[top : top + PANEL, :]
        pivots = jnp.ones_like(a)
        for k in range(0, PANEL, 4):
            w = [jnp.broadcast_to(a[:, i : i + 1], a.shape) for i in range(top + k, top + k + 4)]
            p, q = w[0][k : k + 1, :], w[2][k + 2 : k + 3, :]
            u, v = w[2][k : k + 1, :], w[3][k : k + 1, :]
            single = 1.0 / p
            det = p * q - (u * u + v * v)
            both = 1.0 / det
            second = (here == k + 2) | (here == k + 3)
            below = here > k + 3
            coefficients = (
                jnp.where(second, w[0] * single, (w[0] * q - w[2] * u - w[3] * v) * both),
                jnp.where(second, w[1] * single, (w[1] * q + w[2] * v - w[3] * u) * both),
                jnp.where(below, (w[2] * p - w[0] * u + w[1] * v) * both, 0.0),
                jnp.where(below, (w[3] * p - w[0] * v - w[1] * u) * both, 0.0),
            )
            coefficients = [jnp.where(here > k + 1, c, 0.0) for c in coefficients]
            pivots = jnp.where((here == k) | (here == k + 1), p, pivots)
            pivots = jnp.where(second, det * single, pivots)
            a, m = (
                x - sum(c * x[k + i : k + i + 1, :] for i, c in enumerate(coefficients)) for x in (a, m)
            )
        root = lax.rsqrt(pivots)
        a, m = a * root, m * root
        inverse_ref[top : top + PANEL, :] = m
        rest = top + PANEL
        if rest < order:
            update = lax.dot_general(
                a, jnp.concatenate([a, m], axis=1), TN, precision=lax.Precision.HIGHEST, preferred_element_type=F32
            )
            work_ref[rest:, :] = work_ref[rest:, :] - update[rest:, :order]
            inverse_ref[rest:, :] = inverse_ref[rest:, :] - update[rest:, order:]
    c = lax.axis_index("col")
    mine = inverse_ref[pl.ds(pl.multiple_of(c * group, group), group), :]
    mine = mine * math.sqrt(nodes)
    high = mine.astype(BF16)
    low = (mine - high.astype(F32)).astype(BF16)
    rows = all_rows(own_ref, arrived, all_ref)
    both = lax.dot_general(
        jnp.concatenate([high, low], axis=0), rows, (((1,), (0,)), ((), ())), preferred_element_type=F32
    )
    own = own_ref[...]
    lost = own - own.astype(BF16).astype(F32)
    own_lanes = (
        lax.broadcasted_iota(I32, (order, group), 0)
        == lax.broadcasted_iota(I32, (order, group), 1) + c * group
    ).astype(BF16)
    square = jnp.dot(high, own_lanes, preferred_element_type=F32).astype(BF16)
    out_ref[...] = (
        both[:group] + both[group:] + jnp.dot(square, lost.astype(BF16), preferred_element_type=F32)
    )


def to_partner(x, axis, mask):
    n = lax.axis_size(axis)
    return lax.ppermute(x, axis, [(i, i ^ mask) for i in range(n)])


def sum_parts(part, nblk, ncol):
    if nblk == 8 and ncol % 2 == 0:
        places = [(b, c) for b in range(nblk) for c in range(ncol)]

        def collect_from(masks):
            pairs = [(b * ncol + c, (b ^ masks[c % 2]) * ncol + c) for b, c in places if masks[c % 2]]
            return lax.ppermute(part, ("blk", "col"), pairs)

        got = [collect_from(masks) for masks in ((1, 4), (2, 5), (3, 6), (0, 7))]
        total = jnp.where(lax.axis_index("col") % 2 == 0, part, got[3]) + got[0] + got[1] + got[2]
        return [total, to_partner(total, "col", 1)]
    wide = 1
    while 4 * wide < nblk:
        part = part + to_partner(part, "blk", wide)
        wide *= 2
    return [part] + [to_partner(part, "blk", s * wide) for s in range(1, nblk // wide)]


def per_device(y_start, tile_real, tile_imag, tile_rows, tile_slots, fetch_pick):
    group, rows = y_start.shape
    tiles, order, _ = tile_real.shape
    rb_dev = rows // order
    nblk = lax.axis_size("blk")
    ncol = lax.axis_size("col")
    near_count = LOC_RB * rb_dev
    wanted = lax.all_to_all(
        jnp.broadcast_to(fetch_pick[None], (nblk, 1, nblk)), "blk", split_axis=0, concat_axis=0, tiled=True
    )
    packed, kept, scale, plan = tiles_call(tile_rows, tile_slots, tile_real, tile_imag, rb_dev, near_count)

    out_blocks = sds((nblk, group, order), BF16)
    sent_scratch = pltpu.VMEM((rb_dev, group, order), BF16)
    blocks = pl.pallas_call(
        first_kernel,
        name="first",
        out_shape=out_blocks,
        in_specs=[VMEM, VMEM, SMEM],
        out_specs=VMEM,
        scratch_shapes=[sent_scratch],
        compiler_params=params(LIMIT),
    )(y_start, scale, wanted)

    def scratch(entries, sources):
        return [
            pltpu.VMEM((entries, order, 2 * order), F8),
            pltpu.VMEM((sources + 1, 2 * group, 2 * order), F8),
            pltpu.VMEM((rb_dev, 2 * group, order), F32),
            pltpu.SemaphoreType.DMA((entries // UNROLL,)),
        ]

    vectors_here = sds((group, rows), F32)
    previous, current = y_start, y_start
    for step in range(STEPS):
        arrived = lax.all_to_all(blocks, "blk", split_axis=0, concat_axis=0, tiled=True)
        base = pl.pallas_call(
            functools.partial(near_kernel, step),
            name="near",
            out_shape=vectors_here,
            in_specs=[SMEM, ANY] + [VMEM] * 3,
            out_specs=VMEM,
            scratch_shapes=scratch(near_count, rb_dev),
            compiler_params=params(LIMIT),
            cost_estimate=pl.CostEstimate(flops=1 << 28, bytes_accessed=1 << 21, transcendentals=0),
        )(plan, in_hbm(packed), scale, current, previous)
        last = step == STEPS - 1
        out = pl.pallas_call(
            functools.partial(step_kernel, step),
            name="step",
            out_shape=[vectors_here] if last else [vectors_here, out_blocks],
            in_specs=[SMEM, SMEM, ANY] + [VMEM] * 4,
            out_specs=[VMEM] if last else [VMEM, VMEM],
            scratch_shapes=([] if last else [sent_scratch]) + scratch(tiles - near_count - KEPT, nblk),
            compiler_params=params(LIMIT),
        )(plan, wanted, in_hbm(packed), pltpu.with_memory_space_constraint(kept, pltpu.VMEM), scale, base, arrived)
        previous, current = current, out[0]
        if not last:
            blocks = out[1]

    rounded = current.astype(BF16)
    if ncol == 4:
        beside, across = to_partner(rounded, "col", 1), to_partner(rounded, "col", 2)
        others = [beside, across, to_partner(across, "col", 1)]
    else:
        others = [to_partner(rounded, "col", s) for s in range(1, ncol)]
    vectors = group * ncol
    part = pl.pallas_call(
        gram_kernel,
        name="gram",
        out_shape=sds((vectors // 2, vectors), F32),
        in_specs=[VMEM] * (1 + len(others)),
        out_specs=VMEM,
        scratch_shapes=[pltpu.VMEM((ncol, group, rows), BF16), pltpu.VMEM((vectors, vectors), F32)],
        compiler_params=params(LIMIT),
    )(current, *others)
    parts = sum_parts(part, nblk, ncol)
    return pl.pallas_call(
        functools.partial(factor_kernel, len(parts), rows * nblk),
        name="factor",
        out_shape=sds((group, rows), F32),
        in_specs=[VMEM] * (1 + len(parts) + len(others)),
        out_specs=VMEM,
        scratch_shapes=[
            pltpu.VMEM((ncol, group, rows), BF16),
            pltpu.VMEM((vectors, vectors), F32),
            pltpu.VMEM((vectors, vectors), F32),
        ],
        compiler_params=params(LIMIT),
    )(current, *parts, *others)


def solution(mesh):
    return jax.shard_map(
        per_device,
        mesh=mesh,
        in_specs=(
            P("col", "blk"),
            P("blk", None, None),
            P("blk", None, None),
            P("blk"),
            P("blk"),
            P("blk", None),
        ),
        out_specs=P("col", "blk"),
        check_vma=False,
    )
```

```python
import functools
import math

import jax
import jax.numpy as jnp
from jax import lax
from jax.experimental import pallas as pl
from jax.experimental.pallas import tpu as pltpu
from jax.sharding import PartitionSpec as P

LOC_RB = 2
STEPS = 4
UNROLL = 4
KEPT = 16
CHUNK = 4
MERGE = 16
TOP = 7.0
FINER = 16.0
SPLIT = float((1 << 20) + 1)
TINY = 1e-30
MIB = 1 << 20
LIMIT = 24

center = 1.25
half_width = 0.75

F32 = jnp.float32
BF16 = jnp.bfloat16
F8 = jnp.float8_e4m3fn
I32 = jnp.int32

VMEM = pl.BlockSpec(memory_space=pltpu.VMEM)
SMEM = pl.BlockSpec(memory_space=pltpu.SMEM)
ANY = pl.BlockSpec(memory_space=pl.ANY)

NT = (((1,), (1,)), ((), ()))
TN = (((0,), (0,)), ((), ()))


def sds(shape, dtype):
    return jax.ShapeDtypeStruct(shape, dtype)


def params(limit):
    return pltpu.CompilerParams(vmem_limit_bytes=limit * MIB)


def turn_rows(values):
    rows = values.shape[0]
    even = lax.broadcasted_iota(I32, values.shape, 0) % 2 == 0
    below = pltpu.roll(values, rows - 1, 0)
    above = pltpu.roll(values, 1, 0)
    return jnp.where(even, -below, above)


def turn_lanes(values):
    lanes = values.shape[1]
    even = lax.broadcasted_iota(I32, values.shape, 1) % 2 == 0
    after = pltpu.roll(values, lanes - 1, 1)
    before = pltpu.roll(values, 1, 1)
    return jnp.where(even, after, -before)


def tiles_kernel(
    near_count,
    rows_ref,
    slots_ref,
    real_hbm,
    imag_hbm,
    packed_hbm,
    kept_ref,
    scale_ref,
    plan_ref,
    both_ref,
    small_ref,
    present_ref,
    table_ref,
    back_ref,
    done_ref,
    in_sems,
    out_sems,
):
    kept = kept_ref.shape[0]
    tiles, order, _ = both_ref.shape
    rb_dev = present_ref.shape[0]
    slots = rb_dev + lax.axis_size("blk")
    chunks = tiles // CHUNK

    def copies(c):
        at = pl.ds(c * CHUNK, CHUNK)
        return (
            pltpu.make_async_copy(real_hbm.at[at], both_ref.at[at, :, 0:order], in_sems.at[c, 0]),
            pltpu.make_async_copy(imag_hbm.at[at], both_ref.at[at, :, order : 2 * order], in_sems.at[c, 1]),
        )

    def leave(e):
        return pltpu.make_async_copy(small_ref.at[e], packed_hbm.at[e], out_sems.at[e])

    for c in range(chunks):
        for copy in copies(c):
            copy.start()

    def clear(key, _):
        table_ref[key] = -1
        return _

    lax.fori_loop(0, rb_dev * slots, clear, 0)
    present_ref[...] = jnp.zeros_like(present_ref)

    def link(t, carry):
        key = rows_ref[t] * slots + slots_ref[t]
        seen = table_ref[key]
        before = seen & 255
        length = seen >> 8
        joins = (seen >= 0) & (length < MERGE)
        back_ref[t] = jnp.where(joins, before, -1)
        done_ref[t] = 1

        @pl.when(joins)
        def _():
            done_ref[before] = 0

        table_ref[key] = t | (jnp.where(joins, length + 1, 1) << 8)
        return carry

    lax.fori_loop(0, tiles, link, 0)

    def put(e, skip, value):
        @pl.when(e < skip)
        def _():
            kept_ref[e - skip + kept] = value()

        @pl.when(e >= skip)
        def _():
            small_ref[e] = value()
            leave(e).start()

    def one(skip, t, listed):
        row = rows_ref[t]
        both = both_ref[t]
        present_ref[row] = present_ref[row] + (both[:, :order] + jnp.abs(both[:, order:]))
        closes = done_ref[t]

        @pl.when(closes == 1)
        def _():
            def add(prior):
                both_ref[t] = both_ref[t] + both_ref[prior]
                return back_ref[prior]

            lax.while_loop(lambda prior: prior >= 0, add, back_ref[t])
            put(listed, skip, lambda: both_ref[t].astype(F8))
            slot = slots_ref[t]
            place = rb_dev + ((slot - rb_dev) ^ central(slots - rb_dev))
            plan_ref[listed] = row | (jnp.where(slot < rb_dev, slot, place) << 8)

        return listed + closes

    def chunk(skip, c, listed):
        for copy in copies(c):
            copy.wait()
        for j in range(CHUNK):
            listed = one(skip, c * CHUNK + j, listed)
        return listed

    def pad(skip, listed):
        short = (UNROLL - listed % UNROLL) % UNROLL
        for j in range(UNROLL - 1):

            @pl.when(j < short)
            def _():
                put(listed + j, skip, lambda: jnp.zeros(small_ref.shape[1:], F8))
                plan_ref[listed + j] = slots << 8

        return listed + short

    near = pad(0, lax.fori_loop(0, near_count // CHUNK, functools.partial(chunk, 0), 0))
    skip = near + kept
    every = pad(skip, lax.fori_loop(near_count // CHUNK, chunks, functools.partial(chunk, skip), near))
    plan_ref[tiles] = near // UNROLL
    plan_ref[tiles + 1] = every // UNROLL

    ones = jnp.ones((8, order), BF16)
    for r in range(rb_dev):
        degree = lax.dot_general(ones, present_ref[r], NT, preferred_element_type=F32)
        scale_ref[:, r * order : (r + 1) * order] = 1.0 / jnp.sqrt(jnp.maximum(degree, 1.0))

    def left(e, _):
        leave(e).wait()
        return _

    lax.fori_loop(0, near, left, 0)
    lax.fori_loop(skip, every, left, 0)


def in_hbm(x):
    return pltpu.with_memory_space_constraint(x, pltpu.HBM)


def tiles_call(rows, slots, real, imag, rb_dev, near_count):
    tiles, order, _ = real.shape
    nblk = lax.axis_size("blk")
    return pl.pallas_call(
        functools.partial(tiles_kernel, near_count),
        name="tiles",
        out_shape=(
            pltpu.HBM((tiles, order, 2 * order), F8),
            pltpu.VMEM((KEPT, order, 2 * order), F8),
            sds((8, rb_dev * order), F32),
            sds((tiles + 32,), I32),
        ),
        in_specs=[SMEM, SMEM, ANY, ANY],
        out_specs=(ANY, VMEM, VMEM, SMEM),
        scratch_shapes=[
            pltpu.VMEM((tiles, order, 2 * order), BF16),
            pltpu.VMEM((tiles, order, 2 * order), F8),
            pltpu.VMEM((rb_dev, order, order), BF16),
            pltpu.SMEM((rb_dev * (rb_dev + nblk),), I32),
            pltpu.SMEM((tiles,), I32),
            pltpu.SMEM((tiles,), I32),
            pltpu.SemaphoreType.DMA((tiles // CHUNK, 2)),
            pltpu.SemaphoreType.DMA((tiles,)),
        ],
        compiler_params=params(48),
        cost_estimate=pl.CostEstimate(flops=1 << 28, bytes_accessed=2 * real.size * 2, transcendentals=0),
    )(in_hbm(rows), in_hbm(slots), in_hbm(real), in_hbm(imag))


def rounded_block(field, scale_ref, r, order):
    at = slice(r * order, (r + 1) * order)
    return (field[:, at] * scale_ref[0:1, at]).astype(BF16)


def send_picked(wanted_ref, sent_ref, out_ref):
    me = lax.axis_index("blk")
    for p in range(out_ref.shape[0]):
        out_ref[p] = sent_ref[wanted_ref[p, 0, me]]


def first_kernel(y_ref, scale_ref, wanted_ref, out_ref, sent_ref):
    for r in range(sent_ref.shape[0]):
        sent_ref[r] = rounded_block(y_ref, scale_ref, r, sent_ref.shape[2])
    send_picked(wanted_ref, sent_ref, out_ref)


def load_groups(packed_hbm, tiles_ref, sems, lo, hi):
    def copy(g):
        at = pl.ds((g - lo) * UNROLL, UNROLL)
        return pltpu.make_async_copy(
            packed_hbm.at[pl.ds(g * UNROLL, UNROLL)], tiles_ref.at[at], sems.at[g - lo]
        )

    def begin(g, _):
        copy(g).start()
        return _

    lax.fori_loop(lo, hi, begin, 0)
    return copy


def split_sources(count, source, x_ref):
    _, rows, width = x_ref.shape
    group, order = rows // 2, width // 2
    most = jnp.zeros((group, order), F32)
    for p in range(count):
        most = jnp.maximum(most, jnp.abs(source(p).astype(F32)))
    most = jnp.broadcast_to(jnp.max(most, axis=1, keepdims=True), (group, 128))
    most = jnp.maximum(jnp.maximum(most, jnp.abs(turn_rows(most))), TINY)
    power = jnp.floor(jnp.log2(most))
    size = jnp.exp2(power - TOP)
    inverse = jnp.exp2(TOP - power)[:, 0:1]
    for p in range(count):
        scaled = source(p).astype(F32) * inverse
        far = scaled * SPLIT
        high = far - (far - scaled)
        low = (scaled - high) * FINER
        for k, part in enumerate((high, low)):
            at = slice(k * group, (k + 1) * group)
            x_ref[p, at, :order] = part.astype(F8)
            x_ref[p, at, order:] = turn_rows(part).astype(F8)
    x_ref[count] = jnp.zeros_like(x_ref[count])
    return size[:, 0:1]


def multiply(plan_ref, lo, hi, tile, load, acc_ref):
    def group(g, _):
        done = []
        for j in range(UNROLL):
            code = plan_ref[g * UNROLL + j]
            product = lax.dot_general(load(code >> 8), tile(g, j), NT, preferred_element_type=F32)
            done.append((code & 255, product))
        for row, product in done:
            acc_ref[row] = acc_ref[row] + product
        return _

    lax.fori_loop(lo, hi, group, 0)


def loaded(copy, tiles_ref, lo):
    def tile(g, j):
        if j == 0:
            copy(g).wait()
        return tiles_ref[(g - lo) * UNROLL + j]

    return tile


def collect(acc, size):
    group = size.shape[0]
    return (acc[:group] + acc[group:] * (1.0 / FINER)) * size


def near_kernel(step, plan_ref, packed_hbm, scale_ref, now_ref, before_ref, base_ref, tiles_ref, x_ref, acc_ref, sems):
    rb_dev, _, order = acc_ref.shape
    end = plan_ref.shape[0] - 32
    hi = plan_ref[end]
    copy = load_groups(packed_hbm, tiles_ref, sems, 0, hi)
    acc_ref[...] = jnp.zeros_like(acc_ref)
    size = split_sources(rb_dev, lambda r: rounded_block(now_ref, scale_ref, r, order), x_ref)
    multiply(plan_ref, 0, hi, loaded(copy, tiles_ref, 0), lambda c: x_ref[jnp.minimum(c, rb_dev)], acc_ref)
    for r in range(rb_dev):
        at = slice(r * order, (r + 1) * order)
        applied = scale_ref[0:1, at] * collect(acc_ref[r], size)
        moved = ((1.0 - center) * now_ref[:, at] - applied) / half_width
        base_ref[:, at] = moved if step == 0 else 2.0 * moved - before_ref[:, at]


def step_kernel(step, plan_ref, wanted_ref, packed_hbm, kept_ref, scale_ref, base_ref, arrived_ref, *refs):
    last = step == STEPS - 1
    next_ref = refs[0]
    tiles_ref, x_ref, acc_ref, sems = refs[-4:]
    rb_dev, _, order = acc_ref.shape
    end = plan_ref.shape[0] - 32
    lo, hi = plan_ref[end], plan_ref[end + 1]
    stay = jnp.minimum(lo + KEPT // UNROLL, hi)
    copy = load_groups(packed_hbm, tiles_ref, sems, stay, hi)
    acc_ref[...] = jnp.zeros_like(acc_ref)
    size = split_sources(arrived_ref.shape[0], lambda p: arrived_ref[p], x_ref)
    size = size * ((1.0 if step == 0 else 2.0) / half_width)
    multiply(
        plan_ref, lo, stay, lambda g, j: kept_ref[(g - lo) * UNROLL + j], lambda c: x_ref[c - rb_dev], acc_ref
    )
    multiply(plan_ref, stay, hi, loaded(copy, tiles_ref, stay), lambda c: x_ref[c - rb_dev], acc_ref)
    for r in range(rb_dev):
        at = slice(r * order, (r + 1) * order)
        scale = scale_ref[0:1, at]
        following = base_ref[:, at] - scale * collect(acc_ref[r], size)
        next_ref[:, at] = following
        if not last:
            refs[2][r] = (following * scale).astype(BF16)
    if not last:
        send_picked(wanted_ref, refs[2], refs[1])


def all_rows(own_ref, arrived, all_ref):
    c = lax.axis_index("col")
    all_ref[c] = own_ref[...].astype(BF16)
    for s, ref in enumerate(arrived, 1):
        all_ref[c ^ s] = ref[...]
    n, group, rows = all_ref.shape
    return all_ref[...].reshape(n * group, rows)


def gram_kernel(own_ref, *refs):
    arrived, (gram_ref, all_ref, full_ref) = refs[:-3], refs[-3:]
    rows = all_rows(own_ref, arrived, all_ref)
    full_ref[...] = lax.dot_general(rows, rows, NT, preferred_element_type=F32)
    half = gram_ref.shape[0]
    even = full_ref[pl.ds(0, half, stride=2), :]
    odd = full_ref[pl.ds(1, half, stride=2), :]
    gram_ref[...] = even + turn_lanes(odd)


PANEL = 32


def factor_kernel(grams, nodes, own_ref, *refs):
    parts = refs[:grams]
    arrived = refs[grams:-4]
    out_ref, all_ref, work_ref, inverse_ref = refs[-4:]
    group = own_ref.shape[0]
    order = work_ref.shape[0]
    total = parts[0][...]
    for part in parts[1:]:
        total = total + part[...]
    half = total.shape[0]
    work_ref[pl.ds(0, half, stride=2), :] = total
    work_ref[pl.ds(1, half, stride=2), :] = -turn_lanes(total)
    row_at = lax.broadcasted_iota(I32, (order, order), 0)
    lane_at = lax.broadcasted_iota(I32, (order, order), 1)
    inverse_ref[...] = (row_at == lane_at).astype(F32)
    here = lax.broadcasted_iota(I32, (PANEL, order), 0)
    for top in range(0, order, PANEL):
        a = work_ref[top : top + PANEL, :]
        m = inverse_ref[top : top + PANEL, :]
        pivots = jnp.ones_like(a)
        for k in range(0, PANEL, 4):
            w = [jnp.broadcast_to(a[:, i : i + 1], a.shape) for i in range(top + k, top + k + 4)]
            p, q = w[0][k : k + 1, :], w[2][k + 2 : k + 3, :]
            u, v = w[2][k : k + 1, :], w[3][k : k + 1, :]
            single = 1.0 / p
            det = p * q - (u * u + v * v)
            both = 1.0 / det
            second = (here == k + 2) | (here == k + 3)
            below = here > k + 3
            coefficients = (
                jnp.where(second, w[0] * single, (w[0] * q - w[2] * u - w[3] * v) * both),
                jnp.where(second, w[1] * single, (w[1] * q + w[2] * v - w[3] * u) * both),
                jnp.where(below, (w[2] * p - w[0] * u + w[1] * v) * both, 0.0),
                jnp.where(below, (w[3] * p - w[0] * v - w[1] * u) * both, 0.0),
            )
            coefficients = [jnp.where(here > k + 1, c, 0.0) for c in coefficients]
            pivots = jnp.where((here == k) | (here == k + 1), p, pivots)
            pivots = jnp.where(second, det * single, pivots)
            a, m = (
                x - sum(c * x[k + i : k + i + 1, :] for i, c in enumerate(coefficients)) for x in (a, m)
            )
        root = lax.rsqrt(pivots)
        a, m = a * root, m * root
        inverse_ref[top : top + PANEL, :] = m
        rest = top + PANEL
        if rest < order:
            update = lax.dot_general(
                a, jnp.concatenate([a, m], axis=1), TN, precision=lax.Precision.HIGHEST, preferred_element_type=F32
            )
            work_ref[rest:, :] = work_ref[rest:, :] - update[rest:, :order]
            inverse_ref[rest:, :] = inverse_ref[rest:, :] - update[rest:, order:]
    c = lax.axis_index("col")
    mine = inverse_ref[pl.ds(pl.multiple_of(c * group, group), group), :]
    mine = mine * math.sqrt(nodes)
    high = mine.astype(BF16)
    low = (mine - high.astype(F32)).astype(BF16)
    rows = all_rows(own_ref, arrived, all_ref)
    both = lax.dot_general(
        jnp.concatenate([high, low], axis=0), rows, (((1,), (0,)), ((), ())), preferred_element_type=F32
    )
    own = own_ref[...]
    lost = own - own.astype(BF16).astype(F32)
    own_lanes = (
        lax.broadcasted_iota(I32, (order, group), 0)
        == lax.broadcasted_iota(I32, (order, group), 1) + c * group
    ).astype(BF16)
    square = jnp.dot(high, own_lanes, preferred_element_type=F32).astype(BF16)
    out_ref[...] = (
        both[:group] + both[group:] + jnp.dot(square, lost.astype(BF16), preferred_element_type=F32)
    )


def central(nblk):
    return nblk // 4


def exchange(x):
    nblk = lax.axis_size("blk")
    group = [i ^ central(nblk) for i in range(nblk)]
    return lax.all_to_all(x, "blk", split_axis=0, concat_axis=0, tiled=True, axis_index_groups=[group])


def to_partner(x, axis, mask):
    n = lax.axis_size(axis)
    return lax.ppermute(x, axis, [(i, i ^ mask) for i in range(n)])


def sum_parts(part, nblk):
    wide = 1
    while 4 * wide < nblk:
        part = part + to_partner(part, "blk", wide)
        wide *= 2
    return [part] + [to_partner(part, "blk", s * wide) for s in range(1, nblk // wide)]


def per_device(y_start, tile_real, tile_imag, tile_rows, tile_slots, fetch_pick):
    group, rows = y_start.shape
    tiles, order, _ = tile_real.shape
    rb_dev = rows // order
    nblk = lax.axis_size("blk")
    ncol = lax.axis_size("col")
    near_count = LOC_RB * rb_dev
    wanted = exchange(jnp.broadcast_to(fetch_pick[None], (nblk, 1, nblk)))
    packed, kept, scale, plan = tiles_call(tile_rows, tile_slots, tile_real, tile_imag, rb_dev, near_count)

    out_blocks = sds((nblk, group, order), BF16)
    sent_scratch = pltpu.VMEM((rb_dev, group, order), BF16)
    blocks = pl.pallas_call(
        first_kernel,
        name="first",
        out_shape=out_blocks,
        in_specs=[VMEM, VMEM, SMEM],
        out_specs=VMEM,
        scratch_shapes=[sent_scratch],
        compiler_params=params(LIMIT),
    )(y_start, scale, wanted)

    def scratch(entries, sources):
        return [
            pltpu.VMEM((entries, order, 2 * order), F8),
            pltpu.VMEM((sources + 1, 2 * group, 2 * order), F8),
            pltpu.VMEM((rb_dev, 2 * group, order), F32),
            pltpu.SemaphoreType.DMA((entries // UNROLL,)),
        ]

    vectors_here = sds((group, rows), F32)
    previous, current = y_start, y_start
    for step in range(STEPS):
        arrived = exchange(blocks)
        base = pl.pallas_call(
            functools.partial(near_kernel, step),
            name="near",
            out_shape=vectors_here,
            in_specs=[SMEM, ANY] + [VMEM] * 3,
            out_specs=VMEM,
            scratch_shapes=scratch(near_count, rb_dev),
            compiler_params=params(LIMIT),
            cost_estimate=pl.CostEstimate(flops=1 << 28, bytes_accessed=1 << 21, transcendentals=0),
        )(plan, in_hbm(packed), scale, current, previous)
        last = step == STEPS - 1
        out = pl.pallas_call(
            functools.partial(step_kernel, step),
            name="step",
            out_shape=[vectors_here] if last else [vectors_here, out_blocks],
            in_specs=[SMEM, SMEM, ANY] + [VMEM] * 4,
            out_specs=[VMEM] if last else [VMEM, VMEM],
            scratch_shapes=([] if last else [sent_scratch]) + scratch(tiles - near_count - KEPT, nblk),
            compiler_params=params(LIMIT),
        )(plan, wanted, in_hbm(packed), pltpu.with_memory_space_constraint(kept, pltpu.VMEM), scale, base, arrived)
        previous, current = current, out[0]
        if not last:
            blocks = out[1]

    rounded = current.astype(BF16)
    if ncol == 4:
        beside, across = to_partner(rounded, "col", 1), to_partner(rounded, "col", 2)
        others = [beside, across, to_partner(across, "col", 1)]
    else:
        others = [to_partner(rounded, "col", s) for s in range(1, ncol)]
    vectors = group * ncol
    part = pl.pallas_call(
        gram_kernel,
        name="gram",
        out_shape=sds((vectors // 2, vectors), F32),
        in_specs=[VMEM] * (1 + len(others)),
        out_specs=VMEM,
        scratch_shapes=[pltpu.VMEM((ncol, group, rows), BF16), pltpu.VMEM((vectors, vectors), F32)],
        compiler_params=params(LIMIT),
    )(current, *others)
    parts = sum_parts(part, nblk)
    return pl.pallas_call(
        functools.partial(factor_kernel, len(parts), rows * nblk),
        name="factor",
        out_shape=sds((group, rows), F32),
        in_specs=[VMEM] * (1 + len(parts) + len(others)),
        out_specs=VMEM,
        scratch_shapes=[
            pltpu.VMEM((ncol, group, rows), BF16),
            pltpu.VMEM((vectors, vectors), F32),
            pltpu.VMEM((vectors, vectors), F32),
        ],
        compiler_params=params(LIMIT),
    )(current, *parts, *others)


def solution(mesh):
    return jax.shard_map(
        per_device,
        mesh=mesh,
        in_specs=(
            P("col", "blk"),
            P("blk", None, None),
            P("blk", None, None),
            P("blk"),
            P("blk"),
            P("blk", None),
        ),
        out_specs=P("col", "blk"),
        check_vma=False,
    )
```

```python
import functools
import math

import jax
import jax.numpy as jnp
from jax import lax
from jax.experimental import pallas as pl
from jax.experimental.pallas import tpu as pltpu
from jax.sharding import PartitionSpec as P

LOC_RB = 2
STEPS = 4
WIDE = 8
UNROLL = 4
KEPT = 16
CHUNK = 4
MERGE = 16
TOP = 7.0
FINER = 16.0
SPLIT = float((1 << 20) + 1)
TINY = 1e-30
MIB = 1 << 20
LIMIT = 24

center = 1.25
half_width = 0.75

F32 = jnp.float32
BF16 = jnp.bfloat16
F8 = jnp.float8_e4m3fn
I32 = jnp.int32

VMEM = pl.BlockSpec(memory_space=pltpu.VMEM)
SMEM = pl.BlockSpec(memory_space=pltpu.SMEM)
ANY = pl.BlockSpec(memory_space=pl.ANY)

NT = (((1,), (1,)), ((), ()))
TN = (((0,), (0,)), ((), ()))


def sds(shape, dtype):
    return jax.ShapeDtypeStruct(shape, dtype)


def params(limit):
    return pltpu.CompilerParams(vmem_limit_bytes=limit * MIB)


def turn_rows(values):
    rows = values.shape[0]
    even = lax.broadcasted_iota(I32, values.shape, 0) % 2 == 0
    below = pltpu.roll(values, rows - 1, 0)
    above = pltpu.roll(values, 1, 0)
    return jnp.where(even, -below, above)


def turn_lanes(values):
    lanes = values.shape[1]
    even = lax.broadcasted_iota(I32, values.shape, 1) % 2 == 0
    after = pltpu.roll(values, lanes - 1, 1)
    before = pltpu.roll(values, 1, 1)
    return jnp.where(even, after, -before)


def tiles_kernel(
    near_count,
    rows_ref,
    slots_ref,
    real_hbm,
    imag_hbm,
    packed_hbm,
    kept_ref,
    scale_ref,
    plan_ref,
    both_ref,
    small_ref,
    present_ref,
    table_ref,
    back_ref,
    done_ref,
    in_sems,
    out_sems,
):
    kept = kept_ref.shape[0]
    tiles, order, _ = both_ref.shape
    rb_dev = present_ref.shape[0]
    slots = rb_dev + lax.axis_size("blk")
    chunks = tiles // CHUNK

    def copies(c):
        at = pl.ds(c * CHUNK, CHUNK)
        return (
            pltpu.make_async_copy(real_hbm.at[at], both_ref.at[at, :, 0:order], in_sems.at[c, 0]),
            pltpu.make_async_copy(imag_hbm.at[at], both_ref.at[at, :, order : 2 * order], in_sems.at[c, 1]),
        )

    def leave(e):
        return pltpu.make_async_copy(small_ref.at[e], packed_hbm.at[e], out_sems.at[e])

    for c in range(chunks):
        for copy in copies(c):
            copy.start()

    def clear(key, _):
        table_ref[key] = -1
        return _

    lax.fori_loop(0, rb_dev * slots, clear, 0)
    present_ref[...] = jnp.zeros_like(present_ref)

    def link(t, carry):
        key = rows_ref[t] * slots + slots_ref[t]
        seen = table_ref[key]
        before = seen & 255
        length = seen >> 8
        joins = (seen >= 0) & (length < MERGE)
        back_ref[t] = jnp.where(joins, before, -1)
        done_ref[t] = 1

        @pl.when(joins)
        def _():
            done_ref[before] = 0

        table_ref[key] = t | (jnp.where(joins, length + 1, 1) << 8)
        return carry

    lax.fori_loop(0, tiles, link, 0)

    def put(e, skip, value):
        @pl.when(e < skip)
        def _():
            kept_ref[e - skip + kept] = value()

        @pl.when(e >= skip)
        def _():
            small_ref[e] = value()
            leave(e).start()

    def one(skip, t, listed):
        row = rows_ref[t]
        both = both_ref[t]
        present_ref[row] = present_ref[row] + (both[:, :order] + jnp.abs(both[:, order:]))
        closes = done_ref[t]

        @pl.when(closes == 1)
        def _():
            def add(prior):
                both_ref[t] = both_ref[t] + both_ref[prior]
                return back_ref[prior]

            lax.while_loop(lambda prior: prior >= 0, add, back_ref[t])
            put(listed, skip, lambda: both_ref[t].astype(F8))
            slot = slots_ref[t]
            place = rb_dev + ((slot - rb_dev) ^ central(slots - rb_dev))
            plan_ref[listed] = row | (jnp.where(slot < rb_dev, slot, place) << 8)

        return listed + closes

    def chunk(skip, c, listed):
        for copy in copies(c):
            copy.wait()
        for j in range(CHUNK):
            listed = one(skip, c * CHUNK + j, listed)
        return listed

    def pad(skip, listed):
        short = (UNROLL - listed % UNROLL) % UNROLL
        for j in range(UNROLL - 1):

            @pl.when(j < short)
            def _():
                put(listed + j, skip, lambda: jnp.zeros(small_ref.shape[1:], F8))
                plan_ref[listed + j] = slots << 8

        return listed + short

    near = pad(0, lax.fori_loop(0, near_count // CHUNK, functools.partial(chunk, 0), 0))
    skip = near + kept
    every = pad(skip, lax.fori_loop(near_count // CHUNK, chunks, functools.partial(chunk, skip), near))
    plan_ref[tiles] = near // UNROLL
    plan_ref[tiles + 1] = every // UNROLL

    ones = jnp.ones((8, order), BF16)
    for r in range(rb_dev):
        degree = lax.dot_general(ones, present_ref[r], NT, preferred_element_type=F32)
        scale_ref[:, r * order : (r + 1) * order] = 1.0 / jnp.sqrt(jnp.maximum(degree, 1.0))

    def left(e, _):
        leave(e).wait()
        return _

    lax.fori_loop(0, near, left, 0)
    lax.fori_loop(skip, every, left, 0)


def in_hbm(x):
    return pltpu.with_memory_space_constraint(x, pltpu.HBM)


def tiles_call(rows, slots, real, imag, rb_dev, near_count):
    tiles, order, _ = real.shape
    nblk = lax.axis_size("blk")
    return pl.pallas_call(
        functools.partial(tiles_kernel, near_count),
        name="tiles",
        out_shape=(
            pltpu.HBM((tiles, order, 2 * order), F8),
            pltpu.VMEM((KEPT, order, 2 * order), F8),
            sds((8, rb_dev * order), F32),
            sds((tiles + 32,), I32),
        ),
        in_specs=[SMEM, SMEM, ANY, ANY],
        out_specs=(ANY, VMEM, VMEM, SMEM),
        scratch_shapes=[
            pltpu.VMEM((tiles, order, 2 * order), BF16),
            pltpu.VMEM((tiles, order, 2 * order), F8),
            pltpu.VMEM((rb_dev, order, order), BF16),
            pltpu.SMEM((rb_dev * (rb_dev + nblk),), I32),
            pltpu.SMEM((tiles,), I32),
            pltpu.SMEM((tiles,), I32),
            pltpu.SemaphoreType.DMA((tiles // CHUNK, 2)),
            pltpu.SemaphoreType.DMA((tiles,)),
        ],
        compiler_params=params(48),
        cost_estimate=pl.CostEstimate(flops=1 << 28, bytes_accessed=2 * real.size * 2, transcendentals=0),
    )(in_hbm(rows), in_hbm(slots), in_hbm(real), in_hbm(imag))


def rounded_block(field, scale_ref, r, order):
    at = slice(r * order, (r + 1) * order)
    return (field[:, at] * scale_ref[0:1, at]).astype(BF16)


def send_picked(picks_ref, sent_ref, out_ref):
    for i in range(out_ref.shape[0]):
        out_ref[i] = sent_ref[picks_ref[i]]


def first_kernel(y_ref, scale_ref, wanted_hbm, out_ref, picks_ref, sent_ref, wanted_ref, sem):
    nblk, rows, lanes = wanted_ref.shape
    copy = pltpu.make_async_copy(wanted_hbm.at[:, 0:rows, 0:lanes], wanted_ref, sem)
    copy.start()
    for r in range(sent_ref.shape[0]):
        sent_ref[r] = rounded_block(y_ref, scale_ref, r, sent_ref.shape[2])
    copy.wait()
    mine = lax.broadcasted_iota(I32, (rows, lanes), 1) == lax.axis_index("blk")
    top = lax.broadcasted_iota(I32, (rows, lanes), 0) == 0
    for i in range(nblk):
        pick = jnp.sum(jnp.where(mine & top, wanted_ref[i ^ central(nblk)], 0.0))
        picks_ref[i] = pick.astype(I32)
    send_picked(picks_ref, sent_ref, out_ref)


def load_groups(packed_hbm, tiles_ref, sems, lo, hi):
    def copy(g):
        at = pl.ds((g - lo) * UNROLL, UNROLL)
        return pltpu.make_async_copy(
            packed_hbm.at[pl.ds(g * UNROLL, UNROLL)], tiles_ref.at[at], sems.at[g - lo]
        )

    def begin(g, _):
        copy(g).start()
        return _

    lax.fori_loop(lo, hi, begin, 0)
    return copy


def split_sources(count, source, x_ref):
    _, rows, width = x_ref.shape
    group, order = rows // 2, width // 2
    most = jnp.zeros((group, order), F32)
    for p in range(count):
        most = jnp.maximum(most, jnp.abs(source(p).astype(F32)))
    most = jnp.broadcast_to(jnp.max(most, axis=1, keepdims=True), (group, 128))
    most = jnp.maximum(jnp.maximum(most, jnp.abs(turn_rows(most))), TINY)
    power = jnp.floor(jnp.log2(most))
    size = jnp.exp2(power - TOP)
    inverse = jnp.exp2(TOP - power)[:, 0:1]
    for p in range(count):
        scaled = source(p).astype(F32) * inverse
        far = scaled * SPLIT
        high = far - (far - scaled)
        low = (scaled - high) * FINER
        for k, part in enumerate((high, low)):
            at = slice(k * group, (k + 1) * group)
            x_ref[p, at, :order] = part.astype(F8)
            x_ref[p, at, order:] = turn_rows(part).astype(F8)
    x_ref[count] = jnp.zeros_like(x_ref[count])
    return size[:, 0:1]


def multiply(plan_ref, lo, hi, tile, load, acc_ref):
    def group(g, _):
        done = []
        for j in range(UNROLL):
            code = plan_ref[g * UNROLL + j]
            product = lax.dot_general(load(code >> 8), tile(g, j), NT, preferred_element_type=F32)
            done.append((code & 255, product))
        for row, product in done:
            acc_ref[row] = acc_ref[row] + product
        return _

    lax.fori_loop(lo, hi, group, 0)


def loaded(copy, tiles_ref, lo):
    def tile(g, j):
        if j == 0:
            copy(g).wait()
        return tiles_ref[(g - lo) * UNROLL + j]

    return tile


def collect(acc, size):
    group = size.shape[0]
    return (acc[:group] + acc[group:] * (1.0 / FINER)) * size


def near_kernel(step, plan_ref, packed_hbm, scale_ref, now_ref, before_ref, base_ref, tiles_ref, x_ref, acc_ref, sems):
    rb_dev, _, order = acc_ref.shape
    end = plan_ref.shape[0] - 32
    hi = plan_ref[end]
    copy = load_groups(packed_hbm, tiles_ref, sems, 0, hi)
    acc_ref[...] = jnp.zeros_like(acc_ref)
    size = split_sources(rb_dev, lambda r: rounded_block(now_ref, scale_ref, r, order), x_ref)
    multiply(plan_ref, 0, hi, loaded(copy, tiles_ref, 0), lambda c: x_ref[jnp.minimum(c, rb_dev)], acc_ref)
    for r in range(rb_dev):
        at = slice(r * order, (r + 1) * order)
        applied = scale_ref[0:1, at] * collect(acc_ref[r], size)
        moved = ((1.0 - center) * now_ref[:, at] - applied) / half_width
        base_ref[:, at] = moved if step == 0 else 2.0 * moved - before_ref[:, at]


def step_kernel(step, plan_ref, picks_ref, packed_hbm, kept_ref, scale_ref, base_ref, arrived_ref, *refs):
    last = step == STEPS - 1
    next_ref = refs[0]
    tiles_ref, x_ref, acc_ref, sems = refs[-4:]
    rb_dev, _, order = acc_ref.shape
    end = plan_ref.shape[0] - 32
    lo, hi = plan_ref[end], plan_ref[end + 1]
    stay = jnp.minimum(lo + KEPT // UNROLL, hi)
    copy = load_groups(packed_hbm, tiles_ref, sems, stay, hi)
    acc_ref[...] = jnp.zeros_like(acc_ref)
    size = split_sources(arrived_ref.shape[0], lambda p: arrived_ref[p], x_ref)
    size = size * ((1.0 if step == 0 else 2.0) / half_width)
    multiply(
        plan_ref, lo, stay, lambda g, j: kept_ref[(g - lo) * UNROLL + j], lambda c: x_ref[c - rb_dev], acc_ref
    )
    multiply(plan_ref, stay, hi, loaded(copy, tiles_ref, stay), lambda c: x_ref[c - rb_dev], acc_ref)
    for r in range(rb_dev):
        at = slice(r * order, (r + 1) * order)
        scale = scale_ref[0:1, at]
        following = base_ref[:, at] - scale * collect(acc_ref[r], size)
        next_ref[:, at] = following
        if not last:
            refs[2][r] = (following * scale).astype(BF16)
    if not last:
        send_picked(picks_ref, refs[2], refs[1])


def all_rows(own_ref, arrived, all_ref):
    c = lax.axis_index("col")
    all_ref[c] = own_ref[...].astype(BF16)
    for s, ref in enumerate(arrived, 1):
        all_ref[c ^ s] = ref[...]
    n, group, rows = all_ref.shape
    return all_ref[...].reshape(n * group, rows)


def gram_kernel(own_ref, *refs):
    arrived, (gram_ref, all_ref, full_ref) = refs[:-3], refs[-3:]
    rows = all_rows(own_ref, arrived, all_ref)
    full_ref[...] = lax.dot_general(rows, rows, NT, preferred_element_type=F32)
    half = gram_ref.shape[0]
    even = full_ref[pl.ds(0, half, stride=2), :]
    odd = full_ref[pl.ds(1, half, stride=2), :]
    gram_ref[...] = even + turn_lanes(odd)


PANEL = 32


def finer_reciprocal(x):
    guess = pl.reciprocal(x, approx=True)
    guess = guess * (2.0 - x * guess)
    return guess * (2.0 - x * guess)


def factor_kernel(nodes, own_ref, all_ref, *refs):
    parts, (out_ref, work_ref, inverse_ref) = refs[:-3], refs[-3:]
    group = own_ref.shape[0]
    order = work_ref.shape[0]
    total = parts[0][...]
    for part in parts[1:]:
        total = total + part[...]
    half = total.shape[0]
    work_ref[pl.ds(0, half, stride=2), :] = total
    work_ref[pl.ds(1, half, stride=2), :] = -turn_lanes(total)
    row_at = lax.broadcasted_iota(I32, (order, order), 0)
    lane_at = lax.broadcasted_iota(I32, (order, order), 1)
    inverse_ref[...] = (row_at == lane_at).astype(F32)
    here = lax.broadcasted_iota(I32, (PANEL, order), 0)
    for top in range(0, order, PANEL):
        a = work_ref[top : top + PANEL, :]
        m = inverse_ref[top : top + PANEL, :]
        pivots = jnp.ones_like(a)
        for k in range(0, PANEL, 4):
            w = [jnp.broadcast_to(a[:, i : i + 1], a.shape) for i in range(top + k, top + k + 4)]
            p, q = w[0][k : k + 1, :], w[2][k + 2 : k + 3, :]
            u, v = w[2][k : k + 1, :], w[3][k : k + 1, :]
            single = finer_reciprocal(p)
            det = p * q - (u * u + v * v)
            both = finer_reciprocal(det)
            second = (here == k + 2) | (here == k + 3)
            below = here > k + 3
            coefficients = (
                jnp.where(second, w[0] * single, (w[0] * q - w[2] * u - w[3] * v) * both),
                jnp.where(second, w[1] * single, (w[1] * q + w[2] * v - w[3] * u) * both),
                jnp.where(below, (w[2] * p - w[0] * u + w[1] * v) * both, 0.0),
                jnp.where(below, (w[3] * p - w[0] * v - w[1] * u) * both, 0.0),
            )
            coefficients = [jnp.where(here > k + 1, c, 0.0) for c in coefficients]
            pivots = jnp.where((here == k) | (here == k + 1), p, pivots)
            pivots = jnp.where(second, det * single, pivots)
            a, m = (
                x - sum(c * x[k + i : k + i + 1, :] for i, c in enumerate(coefficients)) for x in (a, m)
            )
        root = lax.rsqrt(pivots)
        a, m = a * root, m * root
        inverse_ref[top : top + PANEL, :] = m
        rest = top + PANEL
        if rest < order:
            update = lax.dot_general(
                a, jnp.concatenate([a, m], axis=1), TN, precision=lax.Precision.HIGHEST, preferred_element_type=F32
            )
            work_ref[rest:, :] = work_ref[rest:, :] - update[rest:, :order]
            inverse_ref[rest:, :] = inverse_ref[rest:, :] - update[rest:, order:]
    c = lax.axis_index("col")
    mine = inverse_ref[pl.ds(pl.multiple_of(c * group, group), group), :]
    mine = mine * math.sqrt(nodes)
    high = mine.astype(BF16)
    low = (mine - high.astype(F32)).astype(BF16)
    rows = all_ref[...].reshape(order, own_ref.shape[1])
    both = lax.dot_general(
        jnp.concatenate([high, low], axis=0), rows, (((1,), (0,)), ((), ())), preferred_element_type=F32
    )
    own = own_ref[...]
    lost = own - own.astype(BF16).astype(F32)
    own_lanes = (
        lax.broadcasted_iota(I32, (order, group), 0)
        == lax.broadcasted_iota(I32, (order, group), 1) + c * group
    ).astype(BF16)
    square = jnp.dot(high, own_lanes, preferred_element_type=F32).astype(BF16)
    out_ref[...] = (
        both[:group] + both[group:] + jnp.dot(square, lost.astype(BF16), preferred_element_type=F32)
    )


def central(nblk):
    return nblk // 4


def exchange(x):
    nblk = lax.axis_size("blk")
    group = [i ^ central(nblk) for i in range(nblk)]
    return lax.all_to_all(x, "blk", split_axis=0, concat_axis=0, tiled=True, axis_index_groups=[group])


def to_partner(x, axis, mask):
    n = lax.axis_size(axis)
    return lax.ppermute(x, axis, [(i, i ^ mask) for i in range(n)])


def sum_parts(part, nblk):
    wide = 1
    while 4 * wide < nblk:
        part = part + to_partner(part, "blk", wide)
        wide *= 2
    return [part] + [to_partner(part, "blk", s * wide) for s in range(1, nblk // wide)]


def per_device(y_start, tile_real, tile_imag, tile_rows, tile_slots, fetch_pick):
    group, rows = y_start.shape
    tiles, order, _ = tile_real.shape
    rb_dev = rows // order
    nblk = lax.axis_size("blk")
    ncol = lax.axis_size("col")
    near_count = LOC_RB * rb_dev
    picked = jnp.pad(fetch_pick.astype(F32), ((0, 0), (0, rows - nblk)))
    top = lax.broadcasted_iota(I32, (WIDE, rows), 0) == 0
    wanted = lax.all_gather(jnp.where(top, picked, y_start[:WIDE]), "blk", axis=0, tiled=False)
    packed, kept, scale, plan = tiles_call(tile_rows, tile_slots, tile_real, tile_imag, rb_dev, near_count)

    out_blocks = sds((nblk, group, order), BF16)
    sent_scratch = pltpu.VMEM((rb_dev, group, order), BF16)
    blocks, picks = pl.pallas_call(
        first_kernel,
        name="first",
        out_shape=(out_blocks, sds((nblk,), I32)),
        in_specs=[VMEM, VMEM, ANY],
        out_specs=(VMEM, SMEM),
        scratch_shapes=[sent_scratch, pltpu.VMEM((nblk, 8, 128), F32), pltpu.SemaphoreType.DMA],
        compiler_params=params(LIMIT),
    )(y_start, scale, in_hbm(wanted))

    def scratch(entries, sources):
        return [
            pltpu.VMEM((entries, order, 2 * order), F8),
            pltpu.VMEM((sources + 1, 2 * group, 2 * order), F8),
            pltpu.VMEM((rb_dev, 2 * group, order), F32),
            pltpu.SemaphoreType.DMA((entries // UNROLL,)),
        ]

    vectors_here = sds((group, rows), F32)
    previous, current = y_start, y_start
    for step in range(STEPS):
        arrived = exchange(blocks)
        base = pl.pallas_call(
            functools.partial(near_kernel, step),
            name="near",
            out_shape=vectors_here,
            in_specs=[SMEM, ANY] + [VMEM] * 3,
            out_specs=VMEM,
            scratch_shapes=scratch(near_count, rb_dev),
            compiler_params=params(LIMIT),
            cost_estimate=pl.CostEstimate(flops=1 << 28, bytes_accessed=1 << 21, transcendentals=0),
        )(plan, in_hbm(packed), scale, current, previous)
        last = step == STEPS - 1
        out = pl.pallas_call(
            functools.partial(step_kernel, step),
            name="step",
            out_shape=[vectors_here] if last else [vectors_here, out_blocks],
            in_specs=[SMEM, SMEM, ANY] + [VMEM] * 4,
            out_specs=[VMEM] if last else [VMEM, VMEM],
            scratch_shapes=([] if last else [sent_scratch]) + scratch(tiles - near_count - KEPT, nblk),
            compiler_params=params(LIMIT),
        )(plan, picks, in_hbm(packed), pltpu.with_memory_space_constraint(kept, pltpu.VMEM), scale, base, arrived)
        previous, current = current, out[0]
        if not last:
            blocks = out[1]

    rounded = current.astype(BF16)
    if ncol == 4:
        beside, across = to_partner(rounded, "col", 1), to_partner(rounded, "col", 2)
        others = [beside, across, to_partner(across, "col", 1)]
    else:
        others = [to_partner(rounded, "col", s) for s in range(1, ncol)]
    vectors = group * ncol
    part, gathered = pl.pallas_call(
        gram_kernel,
        name="gram",
        out_shape=(sds((vectors // 2, vectors), F32), sds((ncol, group, rows), BF16)),
        in_specs=[VMEM] * (1 + len(others)),
        out_specs=(VMEM, VMEM),
        scratch_shapes=[pltpu.VMEM((vectors, vectors), F32)],
        compiler_params=params(LIMIT),
    )(current, *others)
    parts = sum_parts(part, nblk)
    return pl.pallas_call(
        functools.partial(factor_kernel, rows * nblk),
        name="factor",
        out_shape=sds((group, rows), F32),
        in_specs=[VMEM] * (2 + len(parts)),
        out_specs=VMEM,
        scratch_shapes=[pltpu.VMEM((vectors, vectors), F32)] * 2,
        compiler_params=params(LIMIT),
    )(current, gathered, *parts)


def solution(mesh):
    return jax.shard_map(
        per_device,
        mesh=mesh,
        in_specs=(
            P("col", "blk"),
            P("blk", None, None),
            P("blk", None, None),
            P("blk"),
            P("blk"),
            P("blk", None),
        ),
        out_specs=P("col", "blk"),
        check_vma=False,
    )
```

```python
import functools
import math

import jax
import jax.numpy as jnp
from jax import lax
from jax.experimental import pallas as pl
from jax.experimental.pallas import tpu as pltpu
from jax.sharding import PartitionSpec as P

LOC_RB = 2
STEPS = 4
UNROLL = 4
KEPT = 16
CHUNK = 4
MERGE = 16
TOP = 7.0
FINER = 16.0
SPLIT = float((1 << 20) + 1)
TINY = 1e-30
MIB = 1 << 20
LIMIT = 24

center = 1.25
half_width = 0.75

F32 = jnp.float32
BF16 = jnp.bfloat16
F8 = jnp.float8_e4m3fn
I32 = jnp.int32

VMEM = pl.BlockSpec(memory_space=pltpu.VMEM)
SMEM = pl.BlockSpec(memory_space=pltpu.SMEM)
ANY = pl.BlockSpec(memory_space=pl.ANY)

NT = (((1,), (1,)), ((), ()))
TN = (((0,), (0,)), ((), ()))


def sds(shape, dtype):
    return jax.ShapeDtypeStruct(shape, dtype)


def params(limit):
    return pltpu.CompilerParams(vmem_limit_bytes=limit * MIB)


def turn_rows(values):
    rows = values.shape[0]
    even = lax.broadcasted_iota(I32, values.shape, 0) % 2 == 0
    below = pltpu.roll(values, rows - 1, 0)
    above = pltpu.roll(values, 1, 0)
    return jnp.where(even, -below, above)


def turn_lanes(values):
    lanes = values.shape[1]
    even = lax.broadcasted_iota(I32, values.shape, 1) % 2 == 0
    after = pltpu.roll(values, lanes - 1, 1)
    before = pltpu.roll(values, 1, 1)
    return jnp.where(even, after, -before)


def tiles_kernel(
    near_count,
    rows_hbm,
    slots_hbm,
    real_hbm,
    imag_hbm,
    packed_hbm,
    kept_ref,
    scale_ref,
    plan_hbm,
    rows_ref,
    slots_ref,
    plan_ref,
    both_ref,
    small_ref,
    present_ref,
    table_ref,
    back_ref,
    done_ref,
    in_sems,
    out_sems,
    list_sems,
):
    kept = kept_ref.shape[0]
    tiles, order, _ = both_ref.shape
    rb_dev = present_ref.shape[0]
    slots = rb_dev + lax.axis_size("blk")
    chunks = tiles // CHUNK

    def copies(c):
        at = pl.ds(c * CHUNK, CHUNK)
        return (
            pltpu.make_async_copy(real_hbm.at[at], both_ref.at[at, :, 0:order], in_sems.at[c, 0]),
            pltpu.make_async_copy(imag_hbm.at[at], both_ref.at[at, :, order : 2 * order], in_sems.at[c, 1]),
        )

    def leave(e):
        return pltpu.make_async_copy(small_ref.at[e], packed_hbm.at[e], out_sems.at[e])

    lists = (
        pltpu.make_async_copy(rows_hbm, rows_ref, list_sems.at[0]),
        pltpu.make_async_copy(slots_hbm, slots_ref, list_sems.at[1]),
    )
    for copy in lists:
        copy.start()
    for c in range(chunks):
        for copy in copies(c):
            copy.start()

    def clear(key, _):
        table_ref[key] = -1
        return _

    lax.fori_loop(0, rb_dev * slots, clear, 0)
    present_ref[...] = jnp.zeros_like(present_ref)
    for copy in lists:
        copy.wait()

    def link(t, carry):
        key = rows_ref[t] * slots + slots_ref[t]
        seen = table_ref[key]
        before = seen & 255
        length = seen >> 8
        joins = (seen >= 0) & (length < MERGE)
        back_ref[t] = jnp.where(joins, before, -1)
        done_ref[t] = 1

        @pl.when(joins)
        def _():
            done_ref[before] = 0

        table_ref[key] = t | (jnp.where(joins, length + 1, 1) << 8)
        return carry

    lax.fori_loop(0, tiles, link, 0)

    def put(e, skip, value):
        @pl.when(e < skip)
        def _():
            kept_ref[e - skip + kept] = value()

        @pl.when(e >= skip)
        def _():
            small_ref[e] = value()
            leave(e).start()

    def one(skip, t, listed):
        row = rows_ref[t]
        both = both_ref[t]
        present_ref[row] = present_ref[row] + (both[:, :order] + jnp.abs(both[:, order:]))
        closes = done_ref[t]

        @pl.when(closes == 1)
        def _():
            def add(prior):
                both_ref[t] = both_ref[t] + both_ref[prior]
                return back_ref[prior]

            lax.while_loop(lambda prior: prior >= 0, add, back_ref[t])
            put(listed, skip, lambda: both_ref[t].astype(F8))
            slot = slots_ref[t]
            place = rb_dev + ((slot - rb_dev) ^ central(slots - rb_dev))
            plan_ref[listed] = row | (jnp.where(slot < rb_dev, slot, place) << 8)

        return listed + closes

    def chunk(skip, c, listed):
        for copy in copies(c):
            copy.wait()
        for j in range(CHUNK):
            listed = one(skip, c * CHUNK + j, listed)
        return listed

    def pad(skip, listed):
        short = (UNROLL - listed % UNROLL) % UNROLL
        for j in range(UNROLL - 1):

            @pl.when(j < short)
            def _():
                put(listed + j, skip, lambda: jnp.zeros(small_ref.shape[1:], F8))
                plan_ref[listed + j] = slots << 8

        return listed + short

    near = pad(0, lax.fori_loop(0, near_count // CHUNK, functools.partial(chunk, 0), 0))
    skip = near + kept
    every = pad(skip, lax.fori_loop(near_count // CHUNK, chunks, functools.partial(chunk, skip), near))
    plan_ref[tiles] = near // UNROLL
    plan_ref[tiles + 1] = every // UNROLL
    plan_copy = pltpu.make_async_copy(plan_ref, plan_hbm, list_sems.at[2])
    plan_copy.start()

    ones = jnp.ones((8, order), BF16)
    for r in range(rb_dev):
        degree = lax.dot_general(ones, present_ref[r], NT, preferred_element_type=F32)
        scale_ref[:, r * order : (r + 1) * order] = 1.0 / jnp.sqrt(jnp.maximum(degree, 1.0))

    def left(e, _):
        leave(e).wait()
        return _

    lax.fori_loop(0, near, left, 0)
    lax.fori_loop(skip, every, left, 0)
    plan_copy.wait()


def in_hbm(x):
    return pltpu.with_memory_space_constraint(x, pltpu.HBM)


def tiles_call(rows, slots, real, imag, rb_dev, near_count):
    tiles, order, _ = real.shape
    nblk = lax.axis_size("blk")
    return pl.pallas_call(
        functools.partial(tiles_kernel, near_count),
        name="tiles",
        out_shape=(
            pltpu.HBM((tiles, order, 2 * order), F8),
            pltpu.VMEM((KEPT, order, 2 * order), F8),
            sds((8, rb_dev * order), F32),
            pltpu.HBM((tiles + 32,), I32),
        ),
        in_specs=[ANY] * 4,
        out_specs=(ANY, VMEM, VMEM, ANY),
        scratch_shapes=[
            pltpu.SMEM((tiles,), I32),
            pltpu.SMEM((tiles,), I32),
            pltpu.SMEM((tiles + 32,), I32),
            pltpu.VMEM((tiles, order, 2 * order), BF16),
            pltpu.VMEM((tiles, order, 2 * order), F8),
            pltpu.VMEM((rb_dev, order, order), BF16),
            pltpu.SMEM((rb_dev * (rb_dev + nblk),), I32),
            pltpu.SMEM((tiles,), I32),
            pltpu.SMEM((tiles,), I32),
            pltpu.SemaphoreType.DMA((tiles // CHUNK, 2)),
            pltpu.SemaphoreType.DMA((tiles,)),
            pltpu.SemaphoreType.DMA((3,)),
        ],
        compiler_params=params(48),
        cost_estimate=pl.CostEstimate(flops=1 << 28, bytes_accessed=2 * real.size * 2, transcendentals=0),
    )(in_hbm(rows), in_hbm(slots), in_hbm(real), in_hbm(imag))


def rounded_block(field, scale_ref, r, order):
    at = slice(r * order, (r + 1) * order)
    return (field[:, at] * scale_ref[0:1, at]).astype(BF16)


def send_picked(wanted_ref, sent_ref, out_ref):
    me = lax.axis_index("blk")
    for i in range(out_ref.shape[0]):
        out_ref[i] = sent_ref[wanted_ref[i, 0, me]]


def first_kernel(y_ref, scale_ref, wanted_hbm, out_ref, sent_ref, wanted_ref, sem):
    copy = pltpu.make_async_copy(wanted_hbm, wanted_ref, sem)
    copy.start()
    for r in range(sent_ref.shape[0]):
        sent_ref[r] = rounded_block(y_ref, scale_ref, r, sent_ref.shape[2])
    copy.wait()
    send_picked(wanted_ref, sent_ref, out_ref)


def load_groups(packed_hbm, tiles_ref, sems, lo, hi):
    def copy(g):
        at = pl.ds((g - lo) * UNROLL, UNROLL)
        return pltpu.make_async_copy(
            packed_hbm.at[pl.ds(g * UNROLL, UNROLL)], tiles_ref.at[at], sems.at[g - lo]
        )

    def begin(g, _):
        copy(g).start()
        return _

    lax.fori_loop(lo, hi, begin, 0)
    return copy


def split_sources(count, source, x_ref):
    _, rows, width = x_ref.shape
    group, order = rows // 2, width // 2
    most = jnp.zeros((group, order), F32)
    for p in range(count):
        most = jnp.maximum(most, jnp.abs(source(p).astype(F32)))
    most = jnp.broadcast_to(jnp.max(most, axis=1, keepdims=True), (group, 128))
    most = jnp.maximum(jnp.maximum(most, jnp.abs(turn_rows(most))), TINY)
    power = jnp.floor(jnp.log2(most))
    size = jnp.exp2(power - TOP)
    inverse = jnp.exp2(TOP - power)[:, 0:1]
    for p in range(count):
        scaled = source(p).astype(F32) * inverse
        far = scaled * SPLIT
        high = far - (far - scaled)
        low = (scaled - high) * FINER
        for k, part in enumerate((high, low)):
            at = slice(k * group, (k + 1) * group)
            x_ref[p, at, :order] = part.astype(F8)
            x_ref[p, at, order:] = turn_rows(part).astype(F8)
    x_ref[count] = jnp.zeros_like(x_ref[count])
    return size[:, 0:1]


def multiply(plan_ref, lo, hi, tile, load, acc_ref):
    def group(g, _):
        done = []
        for j in range(UNROLL):
            code = plan_ref[g * UNROLL + j]
            product = lax.dot_general(load(code >> 8), tile(g, j), NT, preferred_element_type=F32)
            done.append((code & 255, product))
        for row, product in done:
            acc_ref[row] = acc_ref[row] + product
        return _

    lax.fori_loop(lo, hi, group, 0)


def loaded(copy, tiles_ref, lo):
    def tile(g, j):
        if j == 0:
            copy(g).wait()
        return tiles_ref[(g - lo) * UNROLL + j]

    return tile


def collect(acc, size):
    group = size.shape[0]
    return (acc[:group] + acc[group:] * (1.0 / FINER)) * size


def near_kernel(
    step, plan_hbm, packed_hbm, scale_ref, now_ref, before_ref, base_ref, tiles_ref, x_ref, acc_ref, sems, plan_ref, plan_sem
):
    plan_copy = pltpu.make_async_copy(plan_hbm, plan_ref, plan_sem)
    plan_copy.start()
    rb_dev, _, order = acc_ref.shape
    acc_ref[...] = jnp.zeros_like(acc_ref)
    plan_copy.wait()
    end = plan_ref.shape[0] - 32
    hi = plan_ref[end]
    copy = load_groups(packed_hbm, tiles_ref, sems, 0, hi)
    size = split_sources(rb_dev, lambda r: rounded_block(now_ref, scale_ref, r, order), x_ref)
    multiply(plan_ref, 0, hi, loaded(copy, tiles_ref, 0), lambda c: x_ref[jnp.minimum(c, rb_dev)], acc_ref)
    for r in range(rb_dev):
        at = slice(r * order, (r + 1) * order)
        applied = scale_ref[0:1, at] * collect(acc_ref[r], size)
        moved = ((1.0 - center) * now_ref[:, at] - applied) / half_width
        base_ref[:, at] = moved if step == 0 else 2.0 * moved - before_ref[:, at]


def step_kernel(step, plan_hbm, wanted_hbm, packed_hbm, kept_ref, scale_ref, base_ref, arrived_ref, *refs):
    last = step == STEPS - 1
    next_ref = refs[0]
    tiles_ref, x_ref, acc_ref, sems, plan_ref, plan_sem = refs[-6:]
    plan_copy = pltpu.make_async_copy(plan_hbm, plan_ref, plan_sem)
    plan_copy.start()
    if not last:
        out_ref, sent_ref, wanted_ref, wanted_sem = refs[1:5]
        wanted_copy = pltpu.make_async_copy(wanted_hbm, wanted_ref, wanted_sem)
        wanted_copy.start()
    rb_dev, _, order = acc_ref.shape
    acc_ref[...] = jnp.zeros_like(acc_ref)
    plan_copy.wait()
    end = plan_ref.shape[0] - 32
    lo, hi = plan_ref[end], plan_ref[end + 1]
    stay = jnp.minimum(lo + KEPT // UNROLL, hi)
    copy = load_groups(packed_hbm, tiles_ref, sems, stay, hi)
    size = split_sources(arrived_ref.shape[0], lambda p: arrived_ref[p], x_ref)
    size = size * ((1.0 if step == 0 else 2.0) / half_width)
    multiply(
        plan_ref, lo, stay, lambda g, j: kept_ref[(g - lo) * UNROLL + j], lambda c: x_ref[c - rb_dev], acc_ref
    )
    multiply(plan_ref, stay, hi, loaded(copy, tiles_ref, stay), lambda c: x_ref[c - rb_dev], acc_ref)
    for r in range(rb_dev):
        at = slice(r * order, (r + 1) * order)
        scale = scale_ref[0:1, at]
        following = base_ref[:, at] - scale * collect(acc_ref[r], size)
        next_ref[:, at] = following
        if not last:
            sent_ref[r] = (following * scale).astype(BF16)
    if not last:
        wanted_copy.wait()
        send_picked(wanted_ref, sent_ref, out_ref)


def all_rows(own_ref, arrived, all_ref):
    c = lax.axis_index("col")
    all_ref[c] = own_ref[...].astype(BF16)
    for s, ref in enumerate(arrived, 1):
        all_ref[c ^ s] = ref[...]
    n, group, rows = all_ref.shape
    return all_ref[...].reshape(n * group, rows)


def gram_kernel(own_ref, *refs):
    arrived, (gram_ref, all_ref, full_ref) = refs[:-3], refs[-3:]
    rows = all_rows(own_ref, arrived, all_ref)
    full_ref[...] = lax.dot_general(rows, rows, NT, preferred_element_type=F32)
    half = gram_ref.shape[0]
    even = full_ref[pl.ds(0, half, stride=2), :]
    odd = full_ref[pl.ds(1, half, stride=2), :]
    gram_ref[...] = even + turn_lanes(odd)


PANEL = 32


def factor_kernel(nodes, own_ref, all_ref, *refs):
    parts, (out_ref, work_ref, inverse_ref) = refs[:-3], refs[-3:]
    group = own_ref.shape[0]
    order = work_ref.shape[0]
    total = parts[0][...]
    for part in parts[1:]:
        total = total + part[...]
    half = total.shape[0]
    work_ref[pl.ds(0, half, stride=2), :] = total
    work_ref[pl.ds(1, half, stride=2), :] = -turn_lanes(total)
    row_at = lax.broadcasted_iota(I32, (order, order), 0)
    lane_at = lax.broadcasted_iota(I32, (order, order), 1)
    inverse_ref[...] = (row_at == lane_at).astype(F32)
    here = lax.broadcasted_iota(I32, (PANEL, order), 0)
    for top in range(0, order, PANEL):
        a = work_ref[top : top + PANEL, :]
        m = inverse_ref[top : top + PANEL, :]
        pivots = jnp.ones_like(a)
        for k in range(0, PANEL, 4):
            w = [jnp.broadcast_to(a[:, i : i + 1], a.shape) for i in range(top + k, top + k + 4)]
            p, q = w[0][k : k + 1, :], w[2][k + 2 : k + 3, :]
            u, v = w[2][k : k + 1, :], w[3][k : k + 1, :]
            single = 1.0 / p
            det = p * q - (u * u + v * v)
            both = 1.0 / det
            second = (here == k + 2) | (here == k + 3)
            below = here > k + 3
            coefficients = (
                jnp.where(second, w[0] * single, (w[0] * q - w[2] * u - w[3] * v) * both),
                jnp.where(second, w[1] * single, (w[1] * q + w[2] * v - w[3] * u) * both),
                jnp.where(below, (w[2] * p - w[0] * u + w[1] * v) * both, 0.0),
                jnp.where(below, (w[3] * p - w[0] * v - w[1] * u) * both, 0.0),
            )
            coefficients = [jnp.where(here > k + 1, c, 0.0) for c in coefficients]
            pivots = jnp.where((here == k) | (here == k + 1), p, pivots)
            pivots = jnp.where(second, det * single, pivots)
            a, m = (
                x - sum(c * x[k + i : k + i + 1, :] for i, c in enumerate(coefficients)) for x in (a, m)
            )
        root = lax.rsqrt(pivots)
        a, m = a * root, m * root
        inverse_ref[top : top + PANEL, :] = m
        rest = top + PANEL
        if rest < order:
            update = lax.dot_general(
                a, jnp.concatenate([a, m], axis=1), TN, precision=lax.Precision.HIGHEST, preferred_element_type=F32
            )
            work_ref[rest:, :] = work_ref[rest:, :] - update[rest:, :order]
            inverse_ref[rest:, :] = inverse_ref[rest:, :] - update[rest:, order:]
    c = lax.axis_index("col")
    mine = inverse_ref[pl.ds(pl.multiple_of(c * group, group), group), :]
    mine = mine * math.sqrt(nodes)
    high = mine.astype(BF16)
    low = (mine - high.astype(F32)).astype(BF16)
    rows = all_ref[...].reshape(order, own_ref.shape[1])
    both = lax.dot_general(
        jnp.concatenate([high, low], axis=0), rows, (((1,), (0,)), ((), ())), preferred_element_type=F32
    )
    own = own_ref[...]
    lost = own - own.astype(BF16).astype(F32)
    own_lanes = (
        lax.broadcasted_iota(I32, (order, group), 0)
        == lax.broadcasted_iota(I32, (order, group), 1) + c * group
    ).astype(BF16)
    square = jnp.dot(high, own_lanes, preferred_element_type=F32).astype(BF16)
    out_ref[...] = (
        both[:group] + both[group:] + jnp.dot(square, lost.astype(BF16), preferred_element_type=F32)
    )


def central(nblk):
    return nblk // 4


def exchange(x):
    nblk = lax.axis_size("blk")
    group = [i ^ central(nblk) for i in range(nblk)]
    return lax.all_to_all(x, "blk", split_axis=0, concat_axis=0, tiled=True, axis_index_groups=[group])


def to_partner(x, axis, mask):
    n = lax.axis_size(axis)
    return lax.ppermute(x, axis, [(i, i ^ mask) for i in range(n)])


def sum_parts(part, nblk):
    wide = 1
    while 4 * wide < nblk:
        part = part + to_partner(part, "blk", wide)
        wide *= 2
    return [part] + [to_partner(part, "blk", s * wide) for s in range(1, nblk // wide)]


def per_device(y_start, tile_real, tile_imag, tile_rows, tile_slots, fetch_pick):
    group, rows = y_start.shape
    tiles, order, _ = tile_real.shape
    rb_dev = rows // order
    nblk = lax.axis_size("blk")
    ncol = lax.axis_size("col")
    near_count = LOC_RB * rb_dev
    wanted = exchange(jnp.broadcast_to(fetch_pick[None], (nblk, 1, nblk)))
    packed, kept, scale, plan = tiles_call(tile_rows, tile_slots, tile_real, tile_imag, rb_dev, near_count)

    out_blocks = sds((nblk, group, order), BF16)
    sent_scratch = pltpu.VMEM((rb_dev, group, order), BF16)
    wanted_scratch = pltpu.SMEM(wanted.shape, I32)
    blocks = pl.pallas_call(
        first_kernel,
        name="first",
        out_shape=out_blocks,
        in_specs=[VMEM, VMEM, ANY],
        out_specs=VMEM,
        scratch_shapes=[sent_scratch, wanted_scratch, pltpu.SemaphoreType.DMA],
        compiler_params=params(LIMIT),
    )(y_start, scale, in_hbm(wanted))

    def scratch(entries, sources):
        return [
            pltpu.VMEM((entries, order, 2 * order), F8),
            pltpu.VMEM((sources + 1, 2 * group, 2 * order), F8),
            pltpu.VMEM((rb_dev, 2 * group, order), F32),
            pltpu.SemaphoreType.DMA((entries // UNROLL,)),
            pltpu.SMEM(plan.shape, I32),
            pltpu.SemaphoreType.DMA,
        ]

    vectors_here = sds((group, rows), F32)
    previous, current = y_start, y_start
    for step in range(STEPS):
        arrived = exchange(blocks)
        base = pl.pallas_call(
            functools.partial(near_kernel, step),
            name="near",
            out_shape=vectors_here,
            in_specs=[ANY, ANY] + [VMEM] * 3,
            out_specs=VMEM,
            scratch_shapes=scratch(near_count, rb_dev),
            compiler_params=params(LIMIT),
            cost_estimate=pl.CostEstimate(flops=1 << 28, bytes_accessed=1 << 21, transcendentals=0),
        )(in_hbm(plan), in_hbm(packed), scale, current, previous)
        last = step == STEPS - 1
        out = pl.pallas_call(
            functools.partial(step_kernel, step),
            name="step",
            out_shape=[vectors_here] if last else [vectors_here, out_blocks],
            in_specs=[ANY] * 3 + [VMEM] * 4,
            out_specs=[VMEM] if last else [VMEM, VMEM],
            scratch_shapes=([] if last else [sent_scratch, wanted_scratch, pltpu.SemaphoreType.DMA])
            + scratch(tiles - near_count - KEPT, nblk),
            compiler_params=params(LIMIT),
        )(in_hbm(plan), in_hbm(wanted), in_hbm(packed), pltpu.with_memory_space_constraint(kept, pltpu.VMEM), scale, base, arrived)
        previous, current = current, out[0]
        if not last:
            blocks = out[1]

    rounded = current.astype(BF16)
    if ncol == 4:
        beside, across = to_partner(rounded, "col", 1), to_partner(rounded, "col", 2)
        others = [beside, across, to_partner(across, "col", 1)]
    else:
        others = [to_partner(rounded, "col", s) for s in range(1, ncol)]
    vectors = group * ncol
    part, gathered = pl.pallas_call(
        gram_kernel,
        name="gram",
        out_shape=(sds((vectors // 2, vectors), F32), sds((ncol, group, rows), BF16)),
        in_specs=[VMEM] * (1 + len(others)),
        out_specs=(VMEM, VMEM),
        scratch_shapes=[pltpu.VMEM((vectors, vectors), F32)],
        compiler_params=params(LIMIT),
    )(current, *others)
    parts = sum_parts(part, nblk)
    return pl.pallas_call(
        functools.partial(factor_kernel, rows * nblk),
        name="factor",
        out_shape=sds((group, rows), F32),
        in_specs=[VMEM] * (2 + len(parts)),
        out_specs=VMEM,
        scratch_shapes=[pltpu.VMEM((vectors, vectors), F32)] * 2,
        compiler_params=params(LIMIT),
    )(current, gathered, *parts)


def solution(mesh):
    return jax.shard_map(
        per_device,
        mesh=mesh,
        in_specs=(
            P("col", "blk"),
            P("blk", None, None),
            P("blk", None, None),
            P("blk"),
            P("blk"),
            P("blk", None),
        ),
        out_specs=P("col", "blk"),
        check_vma=False,
    )
```

```python
import functools
import math

import jax
import jax.numpy as jnp
from jax import lax
from jax.experimental import pallas as pl
from jax.experimental.pallas import tpu as pltpu
from jax.sharding import PartitionSpec as P

LOC_RB = 2
STEPS = 4
UNROLL = 4
KEPT = 16
CHUNK = 4
MERGE = 16
TOP = 7.0
FINER = 16.0
SPLIT = float((1 << 20) + 1)
TINY = 1e-30
MIB = 1 << 20
LIMIT = 24

center = 1.25
half_width = 0.75

F32 = jnp.float32
BF16 = jnp.bfloat16
F8 = jnp.float8_e4m3fn
I32 = jnp.int32

VMEM = pl.BlockSpec(memory_space=pltpu.VMEM)
SMEM = pl.BlockSpec(memory_space=pltpu.SMEM)
ANY = pl.BlockSpec(memory_space=pl.ANY)

NT = (((1,), (1,)), ((), ()))
TN = (((0,), (0,)), ((), ()))


def sds(shape, dtype):
    return jax.ShapeDtypeStruct(shape, dtype)


def params(limit):
    return pltpu.CompilerParams(vmem_limit_bytes=limit * MIB)


def turn_rows(values):
    rows = values.shape[0]
    even = lax.broadcasted_iota(I32, values.shape, 0) % 2 == 0
    below = pltpu.roll(values, rows - 1, 0)
    above = pltpu.roll(values, 1, 0)
    return jnp.where(even, -below, above)


def turn_lanes(values):
    lanes = values.shape[1]
    even = lax.broadcasted_iota(I32, values.shape, 1) % 2 == 0
    after = pltpu.roll(values, lanes - 1, 1)
    before = pltpu.roll(values, 1, 1)
    return jnp.where(even, after, -before)


def tiles_kernel(
    near_count,
    rows_hbm,
    slots_hbm,
    real_hbm,
    imag_hbm,
    packed_hbm,
    kept_ref,
    scale_ref,
    plan_hbm,
    rows_ref,
    slots_ref,
    plan_ref,
    both_ref,
    small_ref,
    present_ref,
    table_ref,
    back_ref,
    done_ref,
    in_sems,
    out_sems,
    list_sems,
):
    kept = kept_ref.shape[0]
    tiles, order, _ = both_ref.shape
    rb_dev = present_ref.shape[0]
    slots = rb_dev + lax.axis_size("blk")
    chunks = tiles // CHUNK

    def copies(c):
        at = pl.ds(c * CHUNK, CHUNK)
        return (
            pltpu.make_async_copy(real_hbm.at[at], both_ref.at[at, :, 0:order], in_sems.at[c, 0]),
            pltpu.make_async_copy(imag_hbm.at[at], both_ref.at[at, :, order : 2 * order], in_sems.at[c, 1]),
        )

    def leave(e):
        return pltpu.make_async_copy(small_ref.at[e], packed_hbm.at[e], out_sems.at[e])

    lists = (
        pltpu.make_async_copy(rows_hbm, rows_ref, list_sems.at[0]),
        pltpu.make_async_copy(slots_hbm, slots_ref, list_sems.at[1]),
    )
    for copy in lists:
        copy.start()
    for c in range(chunks):
        for copy in copies(c):
            copy.start()

    def clear(key, _):
        table_ref[key] = -1
        return _

    lax.fori_loop(0, rb_dev * slots, clear, 0)
    present_ref[...] = jnp.zeros_like(present_ref)
    for copy in lists:
        copy.wait()

    def link(t, carry):
        key = rows_ref[t] * slots + slots_ref[t]
        seen = table_ref[key]
        before = seen & 255
        length = seen >> 8
        joins = (seen >= 0) & (length < MERGE)
        back_ref[t] = jnp.where(joins, before, -1)
        done_ref[t] = 1

        @pl.when(joins)
        def _():
            done_ref[before] = 0

        table_ref[key] = t | (jnp.where(joins, length + 1, 1) << 8)
        return carry

    lax.fori_loop(0, tiles, link, 0)

    def turned(tile):
        return jnp.concatenate([tile[:, :order].T, tile[:, order:].T], axis=0).astype(F8)

    def put(e, skip, value):
        @pl.when(e < skip)
        def _():
            kept_ref[e - skip + kept] = value()

        @pl.when(e >= skip)
        def _():
            small_ref[e] = value()
            leave(e).start()

    def one(skip, t, listed):
        row = rows_ref[t]
        both = both_ref[t]
        present_ref[row] = present_ref[row] + (both[:, :order] + jnp.abs(both[:, order:]))
        closes = done_ref[t]

        @pl.when(closes == 1)
        def _():
            def add(prior):
                both_ref[t] = both_ref[t] + both_ref[prior]
                return back_ref[prior]

            lax.while_loop(lambda prior: prior >= 0, add, back_ref[t])
            put(listed, skip, lambda: turned(both_ref[t]))
            slot = slots_ref[t]
            place = rb_dev + ((slot - rb_dev) ^ central(slots - rb_dev))
            plan_ref[listed] = row | (jnp.where(slot < rb_dev, slot, place) << 8)

        return listed + closes

    def chunk(skip, c, listed):
        for copy in copies(c):
            copy.wait()
        for j in range(CHUNK):
            listed = one(skip, c * CHUNK + j, listed)
        return listed

    def pad(skip, listed):
        short = (UNROLL - listed % UNROLL) % UNROLL
        for j in range(UNROLL - 1):

            @pl.when(j < short)
            def _():
                put(listed + j, skip, lambda: jnp.zeros(small_ref.shape[1:], F8))
                plan_ref[listed + j] = slots << 8

        return listed + short

    near = pad(0, lax.fori_loop(0, near_count // CHUNK, functools.partial(chunk, 0), 0))
    skip = near + kept
    every = pad(skip, lax.fori_loop(near_count // CHUNK, chunks, functools.partial(chunk, skip), near))
    plan_ref[tiles] = near // UNROLL
    plan_ref[tiles + 1] = every // UNROLL
    plan_copy = pltpu.make_async_copy(plan_ref, plan_hbm, list_sems.at[2])
    plan_copy.start()

    ones = jnp.ones((8, order), BF16)
    for r in range(rb_dev):
        degree = lax.dot_general(ones, present_ref[r], NT, preferred_element_type=F32)
        scale_ref[:, r * order : (r + 1) * order] = 1.0 / jnp.sqrt(jnp.maximum(degree, 1.0))

    def left(e, _):
        leave(e).wait()
        return _

    lax.fori_loop(0, near, left, 0)
    lax.fori_loop(skip, every, left, 0)
    plan_copy.wait()


def in_hbm(x):
    return pltpu.with_memory_space_constraint(x, pltpu.HBM)


def tiles_call(rows, slots, real, imag, rb_dev, near_count):
    tiles, order, _ = real.shape
    nblk = lax.axis_size("blk")
    return pl.pallas_call(
        functools.partial(tiles_kernel, near_count),
        name="tiles",
        out_shape=(
            pltpu.HBM((tiles, 2 * order, order), F8),
            pltpu.VMEM((KEPT, 2 * order, order), F8),
            sds((8, rb_dev * order), F32),
            pltpu.HBM((tiles + 32,), I32),
        ),
        in_specs=[ANY] * 4,
        out_specs=(ANY, VMEM, VMEM, ANY),
        scratch_shapes=[
            pltpu.SMEM((tiles,), I32),
            pltpu.SMEM((tiles,), I32),
            pltpu.SMEM((tiles + 32,), I32),
            pltpu.VMEM((tiles, order, 2 * order), BF16),
            pltpu.VMEM((tiles, 2 * order, order), F8),
            pltpu.VMEM((rb_dev, order, order), BF16),
            pltpu.SMEM((rb_dev * (rb_dev + nblk),), I32),
            pltpu.SMEM((tiles,), I32),
            pltpu.SMEM((tiles,), I32),
            pltpu.SemaphoreType.DMA((tiles // CHUNK, 2)),
            pltpu.SemaphoreType.DMA((tiles,)),
            pltpu.SemaphoreType.DMA((3,)),
        ],
        compiler_params=params(48),
        cost_estimate=pl.CostEstimate(flops=1 << 28, bytes_accessed=2 * real.size * 2, transcendentals=0),
    )(in_hbm(rows), in_hbm(slots), in_hbm(real), in_hbm(imag))


def rounded_block(field, scale_ref, r, order):
    at = slice(r * order, (r + 1) * order)
    return (field[:, at] * scale_ref[0:1, at]).astype(BF16)


def send_picked(wanted_ref, sent_ref, out_ref):
    me = lax.axis_index("blk")
    for i in range(out_ref.shape[0]):
        out_ref[i] = sent_ref[wanted_ref[i, 0, me]]


def first_kernel(y_ref, scale_ref, wanted_ref, out_ref, sent_ref):
    for r in range(sent_ref.shape[0]):
        sent_ref[r] = rounded_block(y_ref, scale_ref, r, sent_ref.shape[2])
    send_picked(wanted_ref, sent_ref, out_ref)


def load_groups(packed_hbm, tiles_ref, sems, lo, hi):
    def copy(g):
        at = pl.ds((g - lo) * UNROLL, UNROLL)
        return pltpu.make_async_copy(
            packed_hbm.at[pl.ds(g * UNROLL, UNROLL)], tiles_ref.at[at], sems.at[g - lo]
        )

    def begin(g, _):
        copy(g).start()
        return _

    lax.fori_loop(lo, hi, begin, 0)
    return copy


def split_sources(count, source, x_ref):
    _, rows, width = x_ref.shape
    group, order = rows // 2, width // 2
    most = jnp.zeros((group, order), F32)
    for p in range(count):
        most = jnp.maximum(most, jnp.abs(source(p).astype(F32)))
    most = jnp.broadcast_to(jnp.max(most, axis=1, keepdims=True), (group, 128))
    most = jnp.maximum(jnp.maximum(most, jnp.abs(turn_rows(most))), TINY)
    power = jnp.floor(jnp.log2(most))
    size = jnp.exp2(power - TOP)
    inverse = jnp.exp2(TOP - power)[:, 0:1]
    for p in range(count):
        scaled = source(p).astype(F32) * inverse
        far = scaled * SPLIT
        high = far - (far - scaled)
        low = (scaled - high) * FINER
        for k, part in enumerate((high, low)):
            at = slice(k * group, (k + 1) * group)
            x_ref[p, at, :order] = part.astype(F8)
            x_ref[p, at, order:] = turn_rows(part).astype(F8)
    x_ref[count] = jnp.zeros_like(x_ref[count])
    return size[:, 0:1]


def multiply(plan_ref, lo, hi, tile, load, acc_ref):
    def group(g, _):
        done = []
        for j in range(UNROLL):
            code = plan_ref[g * UNROLL + j]
            product = jnp.dot(load(code >> 8), tile(g, j), preferred_element_type=F32)
            done.append((code & 255, product))
        for row, product in done:
            acc_ref[row] = acc_ref[row] + product
        return _

    lax.fori_loop(lo, hi, group, 0)


def loaded(copy, tiles_ref, lo):
    def tile(g, j):
        if j == 0:
            copy(g).wait()
        return tiles_ref[(g - lo) * UNROLL + j]

    return tile


def collect(acc, size):
    group = size.shape[0]
    return (acc[:group] + acc[group:] * (1.0 / FINER)) * size


def near_kernel(step, plan_ref, packed_hbm, scale_ref, now_ref, before_ref, base_ref, tiles_ref, x_ref, acc_ref, sems):
    rb_dev, _, order = acc_ref.shape
    end = plan_ref.shape[0] - 32
    hi = plan_ref[end]
    copy = load_groups(packed_hbm, tiles_ref, sems, 0, hi)
    acc_ref[...] = jnp.zeros_like(acc_ref)
    size = split_sources(rb_dev, lambda r: rounded_block(now_ref, scale_ref, r, order), x_ref)
    multiply(plan_ref, 0, hi, loaded(copy, tiles_ref, 0), lambda c: x_ref[jnp.minimum(c, rb_dev)], acc_ref)
    for r in range(rb_dev):
        at = slice(r * order, (r + 1) * order)
        applied = scale_ref[0:1, at] * collect(acc_ref[r], size)
        moved = ((1.0 - center) * now_ref[:, at] - applied) / half_width
        base_ref[:, at] = moved if step == 0 else 2.0 * moved - before_ref[:, at]


def step_kernel(step, plan_ref, wanted_ref, packed_hbm, kept_ref, scale_ref, base_ref, arrived_ref, *refs):
    last = step == STEPS - 1
    next_ref = refs[0]
    if not last:
        out_ref, sent_ref = refs[1:3]
    tiles_ref, x_ref, acc_ref, sems = refs[-4:]
    rb_dev, _, order = acc_ref.shape
    end = plan_ref.shape[0] - 32
    lo, hi = plan_ref[end], plan_ref[end + 1]
    stay = jnp.minimum(lo + KEPT // UNROLL, hi)
    copy = load_groups(packed_hbm, tiles_ref, sems, stay, hi)
    acc_ref[...] = jnp.zeros_like(acc_ref)
    size = split_sources(arrived_ref.shape[0], lambda p: arrived_ref[p], x_ref)
    size = size * ((1.0 if step == 0 else 2.0) / half_width)
    multiply(
        plan_ref, lo, stay, lambda g, j: kept_ref[(g - lo) * UNROLL + j], lambda c: x_ref[c - rb_dev], acc_ref
    )
    multiply(plan_ref, stay, hi, loaded(copy, tiles_ref, stay), lambda c: x_ref[c - rb_dev], acc_ref)
    for r in range(rb_dev):
        at = slice(r * order, (r + 1) * order)
        scale = scale_ref[0:1, at]
        following = base_ref[:, at] - scale * collect(acc_ref[r], size)
        next_ref[:, at] = following
        if not last:
            sent_ref[r] = (following * scale).astype(BF16)
    if not last:
        send_picked(wanted_ref, sent_ref, out_ref)


def all_rows(own_ref, arrived, all_ref):
    c = lax.axis_index("col")
    all_ref[c] = own_ref[...].astype(BF16)
    for s, ref in enumerate(arrived, 1):
        all_ref[c ^ s] = ref[...]
    n, group, rows = all_ref.shape
    return all_ref[...].reshape(n * group, rows)


def gram_kernel(own_ref, *refs):
    arrived, (gram_ref, all_ref, full_ref) = refs[:-3], refs[-3:]
    rows = all_rows(own_ref, arrived, all_ref)
    full_ref[...] = lax.dot_general(rows, rows, NT, preferred_element_type=F32)
    half = gram_ref.shape[0]
    even = full_ref[pl.ds(0, half, stride=2), :]
    odd = full_ref[pl.ds(1, half, stride=2), :]
    gram_ref[...] = even + turn_lanes(odd)


PANEL = 32


def factor_kernel(nodes, own_ref, all_ref, *refs):
    parts, (out_ref, work_ref, inverse_ref) = refs[:-3], refs[-3:]
    group = own_ref.shape[0]
    order = work_ref.shape[0]
    total = parts[0][...]
    for part in parts[1:]:
        total = total + part[...]
    half = total.shape[0]
    work_ref[pl.ds(0, half, stride=2), :] = total
    work_ref[pl.ds(1, half, stride=2), :] = -turn_lanes(total)
    row_at = lax.broadcasted_iota(I32, (order, order), 0)
    lane_at = lax.broadcasted_iota(I32, (order, order), 1)
    inverse_ref[...] = (row_at == lane_at).astype(F32)
    here = lax.broadcasted_iota(I32, (PANEL, order), 0)
    for top in range(0, order, PANEL):
        a = work_ref[top : top + PANEL, :]
        m = inverse_ref[top : top + PANEL, :]
        pivots = jnp.ones_like(a)
        for k in range(0, PANEL, 4):
            w = [jnp.broadcast_to(a[:, i : i + 1], a.shape) for i in range(top + k, top + k + 4)]
            p, q = w[0][k : k + 1, :], w[2][k + 2 : k + 3, :]
            u, v = w[2][k : k + 1, :], w[3][k : k + 1, :]
            single = 1.0 / p
            det = p * q - (u * u + v * v)
            both = 1.0 / det
            second = (here == k + 2) | (here == k + 3)
            below = here > k + 3
            coefficients = (
                jnp.where(second, w[0] * single, (w[0] * q - w[2] * u - w[3] * v) * both),
                jnp.where(second, w[1] * single, (w[1] * q + w[2] * v - w[3] * u) * both),
                jnp.where(below, (w[2] * p - w[0] * u + w[1] * v) * both, 0.0),
                jnp.where(below, (w[3] * p - w[0] * v - w[1] * u) * both, 0.0),
            )
            coefficients = [jnp.where(here > k + 1, c, 0.0) for c in coefficients]
            pivots = jnp.where((here == k) | (here == k + 1), p, pivots)
            pivots = jnp.where(second, det * single, pivots)
            a, m = (
                x - sum(c * x[k + i : k + i + 1, :] for i, c in enumerate(coefficients)) for x in (a, m)
            )
        root = lax.rsqrt(pivots)
        a, m = a * root, m * root
        inverse_ref[top : top + PANEL, :] = m
        rest = top + PANEL
        if rest < order:
            update = lax.dot_general(
                a, jnp.concatenate([a, m], axis=1), TN, precision=lax.Precision.HIGHEST, preferred_element_type=F32
            )
            work_ref[rest:, :] = work_ref[rest:, :] - update[rest:, :order]
            inverse_ref[rest:, :] = inverse_ref[rest:, :] - update[rest:, order:]
    c = lax.axis_index("col")
    mine = inverse_ref[pl.ds(pl.multiple_of(c * group, group), group), :]
    mine = mine * math.sqrt(nodes)
    high = mine.astype(BF16)
    low = (mine - high.astype(F32)).astype(BF16)
    rows = all_ref[...].reshape(order, own_ref.shape[1])
    both = lax.dot_general(
        jnp.concatenate([high, low], axis=0), rows, (((1,), (0,)), ((), ())), preferred_element_type=F32
    )
    own = own_ref[...]
    lost = own - own.astype(BF16).astype(F32)
    own_lanes = (
        lax.broadcasted_iota(I32, (order, group), 0)
        == lax.broadcasted_iota(I32, (order, group), 1) + c * group
    ).astype(BF16)
    square = jnp.dot(high, own_lanes, preferred_element_type=F32).astype(BF16)
    out_ref[...] = (
        both[:group] + both[group:] + jnp.dot(square, lost.astype(BF16), preferred_element_type=F32)
    )


def central(nblk):
    return nblk // 4


def exchange(x):
    nblk = lax.axis_size("blk")
    group = [i ^ central(nblk) for i in range(nblk)]
    return lax.all_to_all(x, "blk", split_axis=0, concat_axis=0, tiled=True, axis_index_groups=[group])


def to_partner(x, axis, mask):
    n = lax.axis_size(axis)
    return lax.ppermute(x, axis, [(i, i ^ mask) for i in range(n)])


def sum_parts(part, nblk):
    wide = 1
    while 4 * wide < nblk:
        part = part + to_partner(part, "blk", wide)
        wide *= 2
    return [part] + [to_partner(part, "blk", s * wide) for s in range(1, nblk // wide)]


def per_device(y_start, tile_real, tile_imag, tile_rows, tile_slots, fetch_pick):
    group, rows = y_start.shape
    tiles, order, _ = tile_real.shape
    rb_dev = rows // order
    nblk = lax.axis_size("blk")
    ncol = lax.axis_size("col")
    near_count = LOC_RB * rb_dev
    wanted = exchange(jnp.broadcast_to(fetch_pick[None], (nblk, 1, nblk)))
    packed, kept, scale, plan = tiles_call(tile_rows, tile_slots, tile_real, tile_imag, rb_dev, near_count)

    out_blocks = sds((nblk, group, order), BF16)
    sent_scratch = pltpu.VMEM((rb_dev, group, order), BF16)
    blocks = pl.pallas_call(
        first_kernel,
        name="first",
        out_shape=out_blocks,
        in_specs=[VMEM, VMEM, SMEM],
        out_specs=VMEM,
        scratch_shapes=[sent_scratch],
        compiler_params=params(LIMIT),
    )(y_start, scale, wanted)

    def scratch(entries, sources):
        return [
            pltpu.VMEM((entries, 2 * order, order), F8),
            pltpu.VMEM((sources + 1, 2 * group, 2 * order), F8),
            pltpu.VMEM((rb_dev, 2 * group, order), F32),
            pltpu.SemaphoreType.DMA((entries // UNROLL,)),
        ]

    vectors_here = sds((group, rows), F32)
    previous, current = y_start, y_start
    for step in range(STEPS):
        arrived = exchange(blocks)
        base = pl.pallas_call(
            functools.partial(near_kernel, step),
            name="near",
            out_shape=vectors_here,
            in_specs=[SMEM, ANY] + [VMEM] * 3,
            out_specs=VMEM,
            scratch_shapes=scratch(near_count, rb_dev),
            compiler_params=params(LIMIT),
            cost_estimate=pl.CostEstimate(flops=1 << 28, bytes_accessed=1 << 21, transcendentals=0),
        )(in_hbm(plan), in_hbm(packed), scale, current, previous)
        last = step == STEPS - 1
        out = pl.pallas_call(
            functools.partial(step_kernel, step),
            name="step",
            out_shape=[vectors_here] if last else [vectors_here, out_blocks],
            in_specs=[SMEM, SMEM, ANY] + [VMEM] * 4,
            out_specs=[VMEM] if last else [VMEM, VMEM],
            scratch_shapes=([] if last else [sent_scratch]) + scratch(tiles - near_count - KEPT, nblk),
            compiler_params=params(LIMIT),
        )(in_hbm(plan), wanted, in_hbm(packed), pltpu.with_memory_space_constraint(kept, pltpu.VMEM), scale, base, arrived)
        previous, current = current, out[0]
        if not last:
            blocks = out[1]

    rounded = current.astype(BF16)
    if ncol == 4:
        beside, across = to_partner(rounded, "col", 1), to_partner(rounded, "col", 2)
        others = [beside, across, to_partner(across, "col", 1)]
    else:
        others = [to_partner(rounded, "col", s) for s in range(1, ncol)]
    vectors = group * ncol
    part, gathered = pl.pallas_call(
        gram_kernel,
        name="gram",
        out_shape=(sds((vectors // 2, vectors), F32), sds((ncol, group, rows), BF16)),
        in_specs=[VMEM] * (1 + len(others)),
        out_specs=(VMEM, VMEM),
        scratch_shapes=[pltpu.VMEM((vectors, vectors), F32)],
        compiler_params=params(LIMIT),
    )(current, *others)
    parts = sum_parts(part, nblk)
    return pl.pallas_call(
        functools.partial(factor_kernel, rows * nblk),
        name="factor",
        out_shape=sds((group, rows), F32),
        in_specs=[VMEM] * (2 + len(parts)),
        out_specs=VMEM,
        scratch_shapes=[pltpu.VMEM((vectors, vectors), F32)] * 2,
        compiler_params=params(LIMIT),
    )(current, gathered, *parts)


def solution(mesh):
    return jax.shard_map(
        per_device,
        mesh=mesh,
        in_specs=(
            P("col", "blk"),
            P("blk", None, None),
            P("blk", None, None),
            P("blk"),
            P("blk"),
            P("blk", None),
        ),
        out_specs=P("col", "blk"),
        check_vma=False,
    )
```

```python
import functools
import math

import jax
import jax.numpy as jnp
from jax import lax
from jax.experimental import pallas as pl
from jax.experimental.pallas import tpu as pltpu
from jax.sharding import PartitionSpec as P

LOC_RB = 2
STEPS = 4
UNROLL = 4
KEPT = 16
CHUNK = 4
MERGE = 16
TOP = 7.0
FINER = 16.0
SPLIT = float((1 << 20) + 1)
TINY = 1e-30
MIB = 1 << 20
LIMIT = 24

center = 1.25
half_width = 0.75

F32 = jnp.float32
BF16 = jnp.bfloat16
F8 = jnp.float8_e4m3fn
I32 = jnp.int32

VMEM = pl.BlockSpec(memory_space=pltpu.VMEM)
SMEM = pl.BlockSpec(memory_space=pltpu.SMEM)
ANY = pl.BlockSpec(memory_space=pl.ANY)

NT = (((1,), (1,)), ((), ()))
TN = (((0,), (0,)), ((), ()))


def sds(shape, dtype):
    return jax.ShapeDtypeStruct(shape, dtype)


def params(limit):
    return pltpu.CompilerParams(vmem_limit_bytes=limit * MIB)


def turn_rows(values):
    rows = values.shape[0]
    even = lax.broadcasted_iota(I32, values.shape, 0) % 2 == 0
    below = pltpu.roll(values, rows - 1, 0)
    above = pltpu.roll(values, 1, 0)
    return jnp.where(even, -below, above)


def turn_lanes(values):
    lanes = values.shape[1]
    even = lax.broadcasted_iota(I32, values.shape, 1) % 2 == 0
    after = pltpu.roll(values, lanes - 1, 1)
    before = pltpu.roll(values, 1, 1)
    return jnp.where(even, after, -before)


def tiles_kernel(
    near_count,
    rows_hbm,
    slots_hbm,
    real_hbm,
    imag_hbm,
    packed_hbm,
    kept_ref,
    scale_ref,
    plan_hbm,
    rows_ref,
    slots_ref,
    plan_ref,
    both_ref,
    small_ref,
    present_ref,
    table_ref,
    back_ref,
    done_ref,
    in_sems,
    out_sems,
    list_sems,
):
    kept = kept_ref.shape[0]
    tiles, order, _ = real_hbm.shape
    rb_dev = present_ref.shape[0]
    slots = rb_dev + lax.axis_size("blk")
    chunks = tiles // CHUNK

    def copies(c):
        at = pl.ds(c * CHUNK, CHUNK)
        return (
            pltpu.make_async_copy(real_hbm.at[at], both_ref.at[at, :, 0:order], in_sems.at[c, 0]),
            pltpu.make_async_copy(imag_hbm.at[at], both_ref.at[at, :, order : 2 * order], in_sems.at[c, 1]),
        )

    def leave(e):
        return pltpu.make_async_copy(small_ref.at[e], packed_hbm.at[e], out_sems.at[e])

    lists = (
        pltpu.make_async_copy(rows_hbm, rows_ref, list_sems.at[0]),
        pltpu.make_async_copy(slots_hbm, slots_ref, list_sems.at[1]),
    )
    for copy in lists:
        copy.start()
    for c in range(chunks):
        for copy in copies(c):
            copy.start()

    def clear(key, _):
        table_ref[key] = -1
        return _

    lax.fori_loop(0, rb_dev * slots, clear, 0)
    present_ref[...] = jnp.zeros_like(present_ref)
    both_ref[tiles] = jnp.zeros_like(both_ref[tiles])
    back_ref[tiles] = -1
    for copy in lists:
        copy.wait()

    def link(t, carry):
        key = rows_ref[t] * slots + slots_ref[t]
        seen = table_ref[key]
        before = seen & 255
        length = seen >> 8
        joins = (seen >= 0) & (length < MERGE)
        back_ref[t] = jnp.where(joins, before, -1)
        done_ref[t] = 1

        @pl.when(joins)
        def _():
            done_ref[before] = 0

        table_ref[key] = t | (jnp.where(joins, length + 1, 1) << 8)
        return carry

    lax.fori_loop(0, tiles, link, 0)

    def keep(e, skip):
        return pltpu.make_async_copy(small_ref.at[e], kept_ref.at[e - skip + kept], out_sems.at[e])

    def put(e, skip, value):
        small_ref[e] = value

        @pl.when(e < skip)
        def _():
            keep(e, skip).start()

        @pl.when(e >= skip)
        def _():
            leave(e).start()

    def one(skip, t, listed):
        row = rows_ref[t]
        both = both_ref[t]
        counted = both[:, :order] + jnp.abs(both[:, order:])
        present_ref[row] = present_ref[row] + (counted[:, : order // 2] + counted[:, order // 2 :])
        closes = done_ref[t]

        @pl.when(closes == 1)
        def _():
            prior = back_ref[t]
            partner = jnp.where(prior < 0, tiles, prior)

            def add(earlier):
                both_ref[partner] = both_ref[partner] + both_ref[earlier]
                return back_ref[earlier]

            lax.while_loop(lambda earlier: earlier >= 0, add, back_ref[partner])
            small = (both_ref[t] + both_ref[partner]).astype(F8)
            put(listed, skip, jnp.concatenate([small[:, :order].T, small[:, order:].T], axis=0))
            slot = slots_ref[t]
            place = rb_dev + ((slot - rb_dev) ^ central(slots - rb_dev))
            plan_ref[listed] = row | (jnp.where(slot < rb_dev, slot, place) << 8)

        return listed + closes

    def chunk(skip, c, listed):
        for copy in copies(c):
            copy.wait()
        for j in range(CHUNK):
            listed = one(skip, c * CHUNK + j, listed)
        return listed

    def pad(skip, listed):
        short = (UNROLL - listed % UNROLL) % UNROLL
        for j in range(UNROLL - 1):

            @pl.when(j < short)
            def _():
                put(listed + j, skip, jnp.zeros(small_ref.shape[1:], F8))
                plan_ref[listed + j] = slots << 8

        return listed + short

    near = pad(0, lax.fori_loop(0, near_count // CHUNK, functools.partial(chunk, 0), 0))
    skip = near + kept
    every = pad(skip, lax.fori_loop(near_count // CHUNK, chunks, functools.partial(chunk, skip), near))
    plan_ref[tiles] = near // UNROLL
    plan_ref[tiles + 1] = every // UNROLL
    plan_copy = pltpu.make_async_copy(plan_ref, plan_hbm, list_sems.at[2])
    plan_copy.start()

    ones = jnp.ones((8, order // 2), BF16)
    for r in range(rb_dev):
        degree = lax.dot_general(ones, present_ref[r], NT, preferred_element_type=F32)
        scale_ref[:, r * order : (r + 1) * order] = 1.0 / jnp.sqrt(jnp.maximum(degree, 1.0))

    def left(e, _):
        leave(e).wait()
        return _

    def stayed(e, _):
        keep(e, skip).wait()
        return _

    lax.fori_loop(0, near, left, 0)
    lax.fori_loop(near, jnp.minimum(skip, every), stayed, 0)
    lax.fori_loop(skip, every, left, 0)
    plan_copy.wait()


def in_hbm(x):
    return pltpu.with_memory_space_constraint(x, pltpu.HBM)


def tiles_call(rows, slots, real, imag, rb_dev, near_count):
    tiles, order, _ = real.shape
    nblk = lax.axis_size("blk")
    return pl.pallas_call(
        functools.partial(tiles_kernel, near_count),
        name="tiles",
        out_shape=(
            pltpu.HBM((tiles, 2 * order, order), F8),
            pltpu.VMEM((KEPT, 2 * order, order), F8),
            sds((8, rb_dev * order), F32),
            pltpu.HBM((tiles + 32,), I32),
        ),
        in_specs=[ANY] * 4,
        out_specs=(ANY, VMEM, VMEM, ANY),
        scratch_shapes=[
            pltpu.SMEM((tiles,), I32),
            pltpu.SMEM((tiles,), I32),
            pltpu.SMEM((tiles + 32,), I32),
            pltpu.VMEM((tiles + 1, order, 2 * order), BF16),
            pltpu.VMEM((tiles, 2 * order, order), F8),
            pltpu.VMEM((rb_dev, order, order // 2), BF16),
            pltpu.SMEM((rb_dev * (rb_dev + nblk),), I32),
            pltpu.SMEM((tiles + 1,), I32),
            pltpu.SMEM((tiles,), I32),
            pltpu.SemaphoreType.DMA((tiles // CHUNK, 2)),
            pltpu.SemaphoreType.DMA((tiles,)),
            pltpu.SemaphoreType.DMA((3,)),
        ],
        compiler_params=params(48),
        cost_estimate=pl.CostEstimate(flops=1 << 28, bytes_accessed=2 * real.size * 2, transcendentals=0),
    )(in_hbm(rows), in_hbm(slots), in_hbm(real), in_hbm(imag))


def rounded_block(field, scale_ref, r, order):
    at = slice(r * order, (r + 1) * order)
    return (field[:, at] * scale_ref[0:1, at]).astype(BF16)


def send_picked(wanted_ref, sent_ref, out_ref):
    me = lax.axis_index("blk")
    for i in range(out_ref.shape[0]):
        out_ref[i] = sent_ref[wanted_ref[i, 0, me]]


def first_kernel(y_ref, scale_ref, wanted_ref, out_ref, sent_ref):
    for r in range(sent_ref.shape[0]):
        sent_ref[r] = rounded_block(y_ref, scale_ref, r, sent_ref.shape[2])
    send_picked(wanted_ref, sent_ref, out_ref)


def load_groups(packed_hbm, tiles_ref, sems, lo, hi):
    def copy(g):
        at = pl.ds((g - lo) * UNROLL, UNROLL)
        return pltpu.make_async_copy(
            packed_hbm.at[pl.ds(g * UNROLL, UNROLL)], tiles_ref.at[at], sems.at[g - lo]
        )

    def begin(g, _):
        copy(g).start()
        return _

    lax.fori_loop(lo, hi, begin, 0)
    return copy


def split_sources(count, source, x_ref):
    _, rows, width = x_ref.shape
    group, order = rows // 2, width // 2
    most = jnp.zeros((group, order), F32)
    for p in range(count):
        most = jnp.maximum(most, jnp.abs(source(p).astype(F32)))
    most = jnp.broadcast_to(jnp.max(most, axis=1, keepdims=True), (group, 128))
    most = jnp.maximum(jnp.maximum(most, jnp.abs(turn_rows(most))), TINY)
    power = jnp.floor(jnp.log2(most))
    size = jnp.exp2(power - TOP)
    inverse = jnp.exp2(TOP - power)[:, 0:1]
    for p in range(count):
        scaled = source(p).astype(F32) * inverse
        far = scaled * SPLIT
        high = far - (far - scaled)
        low = (scaled - high) * FINER
        for k, part in enumerate((high, low)):
            at = slice(k * group, (k + 1) * group)
            x_ref[p, at, :order] = part.astype(F8)
            x_ref[p, at, order:] = turn_rows(part).astype(F8)
    x_ref[count] = jnp.zeros_like(x_ref[count])
    return size[:, 0:1]


def multiply(plan_ref, lo, hi, tile, load, acc_ref):
    def group(g, _):
        done = []
        for j in range(UNROLL):
            code = plan_ref[g * UNROLL + j]
            product = jnp.dot(load(code >> 8), tile(g, j), preferred_element_type=F32)
            done.append((code & 255, product))
        for row, product in done:
            acc_ref[row] = acc_ref[row] + product
        return _

    lax.fori_loop(lo, hi, group, 0)


def loaded(copy, tiles_ref, lo):
    def tile(g, j):
        if j == 0:
            copy(g).wait()
        return tiles_ref[(g - lo) * UNROLL + j]

    return tile


def collect(acc, size):
    group = size.shape[0]
    return (acc[:group] + acc[group:] * (1.0 / FINER)) * size


def near_kernel(step, plan_ref, packed_hbm, scale_ref, now_ref, before_ref, base_ref, tiles_ref, x_ref, acc_ref, sems):
    rb_dev, _, order = acc_ref.shape
    end = plan_ref.shape[0] - 32
    hi = plan_ref[end]
    copy = load_groups(packed_hbm, tiles_ref, sems, 0, hi)
    acc_ref[...] = jnp.zeros_like(acc_ref)
    size = split_sources(rb_dev, lambda r: rounded_block(now_ref, scale_ref, r, order), x_ref)
    multiply(plan_ref, 0, hi, loaded(copy, tiles_ref, 0), lambda c: x_ref[jnp.minimum(c, rb_dev)], acc_ref)
    for r in range(rb_dev):
        at = slice(r * order, (r + 1) * order)
        applied = scale_ref[0:1, at] * collect(acc_ref[r], size)
        moved = ((1.0 - center) * now_ref[:, at] - applied) / half_width
        base_ref[:, at] = moved if step == 0 else 2.0 * moved - before_ref[:, at]


def step_kernel(step, plan_ref, wanted_ref, packed_hbm, kept_ref, scale_ref, base_ref, arrived_ref, *refs):
    last = step == STEPS - 1
    next_ref = refs[0]
    if not last:
        out_ref, sent_ref = refs[1:3]
    tiles_ref, x_ref, acc_ref, sems = refs[-4:]
    rb_dev, _, order = acc_ref.shape
    end = plan_ref.shape[0] - 32
    lo, hi = plan_ref[end], plan_ref[end + 1]
    stay = jnp.minimum(lo + KEPT // UNROLL, hi)
    copy = load_groups(packed_hbm, tiles_ref, sems, stay, hi)
    acc_ref[...] = jnp.zeros_like(acc_ref)
    size = split_sources(arrived_ref.shape[0], lambda p: arrived_ref[p], x_ref)
    size = size * ((1.0 if step == 0 else 2.0) / half_width)
    multiply(
        plan_ref, lo, stay, lambda g, j: kept_ref[(g - lo) * UNROLL + j], lambda c: x_ref[c - rb_dev], acc_ref
    )
    multiply(plan_ref, stay, hi, loaded(copy, tiles_ref, stay), lambda c: x_ref[c - rb_dev], acc_ref)
    for r in range(rb_dev):
        at = slice(r * order, (r + 1) * order)
        scale = scale_ref[0:1, at]
        following = base_ref[:, at] - scale * collect(acc_ref[r], size)
        next_ref[:, at] = following
        if not last:
            sent_ref[r] = (following * scale).astype(BF16)
    if not last:
        send_picked(wanted_ref, sent_ref, out_ref)


def all_rows(own_ref, arrived, all_ref):
    c = lax.axis_index("col")
    all_ref[c] = own_ref[...].astype(BF16)
    for s, ref in enumerate(arrived, 1):
        all_ref[c ^ s] = ref[...]
    n, group, rows = all_ref.shape
    return all_ref[...].reshape(n * group, rows)


def gram_kernel(own_ref, *refs):
    arrived, (gram_ref, all_ref, full_ref) = refs[:-3], refs[-3:]
    rows = all_rows(own_ref, arrived, all_ref)
    full_ref[...] = lax.dot_general(rows, rows, NT, preferred_element_type=F32)
    half = gram_ref.shape[0]
    even = full_ref[pl.ds(0, half, stride=2), :]
    odd = full_ref[pl.ds(1, half, stride=2), :]
    gram_ref[...] = even + turn_lanes(odd)


PANEL = 32


def factor_kernel(nodes, own_ref, all_ref, *refs):
    parts, (out_ref, work_ref, inverse_ref) = refs[:-3], refs[-3:]
    group = own_ref.shape[0]
    order = work_ref.shape[0]
    total = parts[0][...]
    for part in parts[1:]:
        total = total + part[...]
    half = total.shape[0]
    work_ref[pl.ds(0, half, stride=2), :] = total
    work_ref[pl.ds(1, half, stride=2), :] = -turn_lanes(total)
    row_at = lax.broadcasted_iota(I32, (order, order), 0)
    lane_at = lax.broadcasted_iota(I32, (order, order), 1)
    inverse_ref[...] = (row_at == lane_at).astype(F32)
    here = lax.broadcasted_iota(I32, (PANEL, order), 0)
    for top in range(0, order, PANEL):
        a = work_ref[top : top + PANEL, :]
        m = inverse_ref[top : top + PANEL, :]
        pivots = jnp.ones_like(a)
        for k in range(0, PANEL, 4):
            w = [jnp.broadcast_to(a[:, i : i + 1], a.shape) for i in range(top + k, top + k + 4)]
            p, q = w[0][k : k + 1, :], w[2][k + 2 : k + 3, :]
            u, v = w[2][k : k + 1, :], w[3][k : k + 1, :]
            single = 1.0 / p
            det = p * q - (u * u + v * v)
            both = 1.0 / det
            second = (here == k + 2) | (here == k + 3)
            below = here > k + 3
            coefficients = (
                jnp.where(second, w[0] * single, (w[0] * q - w[2] * u - w[3] * v) * both),
                jnp.where(second, w[1] * single, (w[1] * q + w[2] * v - w[3] * u) * both),
                jnp.where(below, (w[2] * p - w[0] * u + w[1] * v) * both, 0.0),
                jnp.where(below, (w[3] * p - w[0] * v - w[1] * u) * both, 0.0),
            )
            coefficients = [jnp.where(here > k + 1, c, 0.0) for c in coefficients]
            pivots = jnp.where((here == k) | (here == k + 1), p, pivots)
            pivots = jnp.where(second, det * single, pivots)
            a, m = (
                x - sum(c * x[k + i : k + i + 1, :] for i, c in enumerate(coefficients)) for x in (a, m)
            )
        root = lax.rsqrt(pivots)
        a, m = a * root, m * root
        inverse_ref[top : top + PANEL, :] = m
        rest = top + PANEL
        if rest < order:
            update = lax.dot_general(
                a, jnp.concatenate([a, m], axis=1), TN, precision=lax.Precision.HIGHEST, preferred_element_type=F32
            )
            work_ref[rest:, :] = work_ref[rest:, :] - update[rest:, :order]
            inverse_ref[rest:, :] = inverse_ref[rest:, :] - update[rest:, order:]
    c = lax.axis_index("col")
    mine = inverse_ref[pl.ds(pl.multiple_of(c * group, group), group), :]
    mine = mine * math.sqrt(nodes)
    high = mine.astype(BF16)
    low = (mine - high.astype(F32)).astype(BF16)
    rows = all_ref[...].reshape(order, own_ref.shape[1])
    both = lax.dot_general(
        jnp.concatenate([high, low], axis=0), rows, (((1,), (0,)), ((), ())), preferred_element_type=F32
    )
    own = own_ref[...]
    lost = own - own.astype(BF16).astype(F32)
    own_lanes = (
        lax.broadcasted_iota(I32, (order, group), 0)
        == lax.broadcasted_iota(I32, (order, group), 1) + c * group
    ).astype(BF16)
    square = jnp.dot(high, own_lanes, preferred_element_type=F32).astype(BF16)
    out_ref[...] = (
        both[:group] + both[group:] + jnp.dot(square, lost.astype(BF16), preferred_element_type=F32)
    )


def central(nblk):
    return nblk // 4


def exchange(x):
    nblk = lax.axis_size("blk")
    group = [i ^ central(nblk) for i in range(nblk)]
    return lax.all_to_all(x, "blk", split_axis=0, concat_axis=0, tiled=True, axis_index_groups=[group])


def to_partner(x, axis, mask):
    n = lax.axis_size(axis)
    return lax.ppermute(x, axis, [(i, i ^ mask) for i in range(n)])


def sum_parts(part, nblk):
    wide = 1
    while 4 * wide < nblk:
        part = part + to_partner(part, "blk", wide)
        wide *= 2
    return [part] + [to_partner(part, "blk", s * wide) for s in range(1, nblk // wide)]


def per_device(y_start, tile_real, tile_imag, tile_rows, tile_slots, fetch_pick):
    group, rows = y_start.shape
    tiles, order, _ = tile_real.shape
    rb_dev = rows // order
    nblk = lax.axis_size("blk")
    ncol = lax.axis_size("col")
    near_count = LOC_RB * rb_dev
    wanted = exchange(jnp.broadcast_to(fetch_pick[None], (nblk, 1, nblk)))
    packed, kept, scale, plan = tiles_call(tile_rows, tile_slots, tile_real, tile_imag, rb_dev, near_count)

    out_blocks = sds((nblk, group, order), BF16)
    sent_scratch = pltpu.VMEM((rb_dev, group, order), BF16)
    blocks = pl.pallas_call(
        first_kernel,
        name="first",
        out_shape=out_blocks,
        in_specs=[VMEM, VMEM, SMEM],
        out_specs=VMEM,
        scratch_shapes=[sent_scratch],
        compiler_params=params(LIMIT),
    )(y_start, scale, wanted)

    def scratch(entries, sources):
        return [
            pltpu.VMEM((entries, 2 * order, order), F8),
            pltpu.VMEM((sources + 1, 2 * group, 2 * order), F8),
            pltpu.VMEM((rb_dev, 2 * group, order), F32),
            pltpu.SemaphoreType.DMA((entries // UNROLL,)),
        ]

    vectors_here = sds((group, rows), F32)
    previous, current = y_start, y_start
    for step in range(STEPS):
        arrived = exchange(blocks)
        base = pl.pallas_call(
            functools.partial(near_kernel, step),
            name="near",
            out_shape=vectors_here,
            in_specs=[SMEM, ANY] + [VMEM] * 3,
            out_specs=VMEM,
            scratch_shapes=scratch(near_count, rb_dev),
            compiler_params=params(LIMIT),
            cost_estimate=pl.CostEstimate(flops=1 << 28, bytes_accessed=1 << 21, transcendentals=0),
        )(in_hbm(plan), in_hbm(packed), scale, current, previous)
        last = step == STEPS - 1
        out = pl.pallas_call(
            functools.partial(step_kernel, step),
            name="step",
            out_shape=[vectors_here] if last else [vectors_here, out_blocks],
            in_specs=[SMEM, SMEM, ANY] + [VMEM] * 4,
            out_specs=[VMEM] if last else [VMEM, VMEM],
            scratch_shapes=([] if last else [sent_scratch]) + scratch(tiles - near_count - KEPT, nblk),
            compiler_params=params(LIMIT),
        )(in_hbm(plan), wanted, in_hbm(packed), pltpu.with_memory_space_constraint(kept, pltpu.VMEM), scale, base, arrived)
        previous, current = current, out[0]
        if not last:
            blocks = out[1]

    rounded = current.astype(BF16)
    if ncol == 4:
        beside, across = to_partner(rounded, "col", 1), to_partner(rounded, "col", 2)
        others = [beside, across, to_partner(across, "col", 1)]
    else:
        others = [to_partner(rounded, "col", s) for s in range(1, ncol)]
    vectors = group * ncol
    part, gathered = pl.pallas_call(
        gram_kernel,
        name="gram",
        out_shape=(sds((vectors // 2, vectors), F32), sds((ncol, group, rows), BF16)),
        in_specs=[VMEM] * (1 + len(others)),
        out_specs=(VMEM, VMEM),
        scratch_shapes=[pltpu.VMEM((vectors, vectors), F32)],
        compiler_params=params(LIMIT),
    )(current, *others)
    parts = sum_parts(part, nblk)
    return pl.pallas_call(
        functools.partial(factor_kernel, rows * nblk),
        name="factor",
        out_shape=sds((group, rows), F32),
        in_specs=[VMEM] * (2 + len(parts)),
        out_specs=VMEM,
        scratch_shapes=[pltpu.VMEM((vectors, vectors), F32)] * 2,
        compiler_params=params(LIMIT),
    )(current, gathered, *parts)


def solution(mesh):
    return jax.shard_map(
        per_device,
        mesh=mesh,
        in_specs=(
            P("col", "blk"),
            P("blk", None, None),
            P("blk", None, None),
            P("blk"),
            P("blk"),
            P("blk", None),
        ),
        out_specs=P("col", "blk"),
        check_vma=False,
    )
```

```python
import functools
import math

import jax
import jax.numpy as jnp
from jax import lax
from jax.experimental import pallas as pl
from jax.experimental.pallas import tpu as pltpu
from jax.sharding import PartitionSpec as P

LOC_RB = 2
STEPS = 4
UNROLL = 4
KEPT = 16
CHUNK = 4
MERGE = 16
TOP = 7.0
FINER = 16.0
SPLIT = float((1 << 20) + 1)
TINY = 1e-30
MIB = 1 << 20
LIMIT = 24

center = 1.25
half_width = 0.75

F32 = jnp.float32
BF16 = jnp.bfloat16
F8 = jnp.float8_e4m3fn
I32 = jnp.int32

VMEM = pl.BlockSpec(memory_space=pltpu.VMEM)
SMEM = pl.BlockSpec(memory_space=pltpu.SMEM)
ANY = pl.BlockSpec(memory_space=pl.ANY)

NT = (((1,), (1,)), ((), ()))
TN = (((0,), (0,)), ((), ()))


def sds(shape, dtype):
    return jax.ShapeDtypeStruct(shape, dtype)


def params(limit):
    return pltpu.CompilerParams(vmem_limit_bytes=limit * MIB)


def turn_rows(values):
    rows = values.shape[0]
    even = lax.broadcasted_iota(I32, values.shape, 0) % 2 == 0
    below = pltpu.roll(values, rows - 1, 0)
    above = pltpu.roll(values, 1, 0)
    return jnp.where(even, -below, above)


def turn_lanes(values):
    lanes = values.shape[1]
    even = lax.broadcasted_iota(I32, values.shape, 1) % 2 == 0
    after = pltpu.roll(values, lanes - 1, 1)
    before = pltpu.roll(values, 1, 1)
    return jnp.where(even, after, -before)


def tiles_kernel(
    near_count,
    rows_hbm,
    slots_hbm,
    real_hbm,
    imag_hbm,
    packed_hbm,
    kept_ref,
    scale_ref,
    plan_hbm,
    rows_ref,
    slots_ref,
    plan_ref,
    both_ref,
    small_ref,
    present_ref,
    table_ref,
    back_ref,
    done_ref,
    in_sems,
    out_sems,
    list_sems,
):
    kept = kept_ref.shape[0]
    tiles, order, _ = real_hbm.shape
    rb_dev = present_ref.shape[0]
    slots = rb_dev + lax.axis_size("blk")
    chunks = tiles // CHUNK

    def copies(c):
        at = pl.ds(c * CHUNK, CHUNK)
        return (
            pltpu.make_async_copy(real_hbm.at[at], both_ref.at[at, :, 0:order], in_sems.at[c, 0]),
            pltpu.make_async_copy(imag_hbm.at[at], both_ref.at[at, :, order : 2 * order], in_sems.at[c, 1]),
        )

    def leave(e):
        return pltpu.make_async_copy(small_ref.at[e], packed_hbm.at[e], out_sems.at[e])

    lists = (
        pltpu.make_async_copy(rows_hbm, rows_ref, list_sems.at[0]),
        pltpu.make_async_copy(slots_hbm, slots_ref, list_sems.at[1]),
    )
    for copy in lists:
        copy.start()
    for c in range(chunks):
        for copy in copies(c):
            copy.start()

    def clear(key, _):
        table_ref[key] = -1
        return _

    lax.fori_loop(0, rb_dev * slots, clear, 0)
    present_ref[...] = jnp.zeros_like(present_ref)
    both_ref[tiles] = jnp.zeros_like(both_ref[tiles])
    back_ref[tiles] = -1
    for copy in lists:
        copy.wait()

    def link(t, carry):
        key = rows_ref[t] * slots + slots_ref[t]
        seen = table_ref[key]
        before = seen & 255
        length = seen >> 8
        joins = (seen >= 0) & (length < MERGE)
        back_ref[t] = jnp.where(joins, before, -1)
        done_ref[t] = 1

        @pl.when(joins)
        def _():
            done_ref[before] = 0

        table_ref[key] = t | (jnp.where(joins, length + 1, 1) << 8)
        return carry

    lax.fori_loop(0, tiles, link, 0)

    def keep(e, skip):
        return pltpu.make_async_copy(small_ref.at[e], kept_ref.at[e - skip + kept], out_sems.at[e])

    def put(e, skip, value):
        small_ref[e] = value

        @pl.when(e < skip)
        def _():
            keep(e, skip).start()

        @pl.when(e >= skip)
        def _():
            leave(e).start()

    def one(skip, t, listed):
        row = rows_ref[t]
        both = both_ref[t]
        counted = both[:, :order] + jnp.abs(both[:, order:])
        present_ref[row] = present_ref[row] + (counted[:, : order // 2] + counted[:, order // 2 :])
        closes = done_ref[t]

        @pl.when(closes == 1)
        def _():
            prior = back_ref[t]
            partner = jnp.where(prior < 0, tiles, prior)

            def add(earlier):
                both_ref[partner] = both_ref[partner] + both_ref[earlier]
                return back_ref[earlier]

            lax.while_loop(lambda earlier: earlier >= 0, add, back_ref[partner])
            total = both_ref[t] + both_ref[partner]
            put(listed, skip, jnp.concatenate([total[:, :order].T, total[:, order:].T], axis=0).astype(F8))
            slot = slots_ref[t]
            place = rb_dev + ((slot - rb_dev) ^ central(slots - rb_dev))
            plan_ref[listed] = row | (jnp.where(slot < rb_dev, slot, place) << 8)

        return listed + closes

    def chunk(skip, c, listed):
        for copy in copies(c):
            copy.wait()
        for j in range(CHUNK):
            listed = one(skip, c * CHUNK + j, listed)
        return listed

    def pad(skip, listed):
        short = (UNROLL - listed % UNROLL) % UNROLL
        for j in range(UNROLL - 1):

            @pl.when(j < short)
            def _():
                put(listed + j, skip, jnp.zeros(small_ref.shape[1:], F8))
                plan_ref[listed + j] = slots << 8

        return listed + short

    near = pad(0, lax.fori_loop(0, near_count // CHUNK, functools.partial(chunk, 0), 0))
    skip = near + kept
    every = pad(skip, lax.fori_loop(near_count // CHUNK, chunks, functools.partial(chunk, skip), near))
    plan_ref[tiles] = near // UNROLL
    plan_ref[tiles + 1] = every // UNROLL
    plan_copy = pltpu.make_async_copy(plan_ref, plan_hbm, list_sems.at[2])
    plan_copy.start()

    ones = jnp.ones((8, order // 2), BF16)
    for r in range(rb_dev):
        degree = lax.dot_general(ones, present_ref[r], NT, preferred_element_type=F32)
        scale_ref[:, r * order : (r + 1) * order] = 1.0 / jnp.sqrt(jnp.maximum(degree, 1.0))

    def left(e, _):
        leave(e).wait()
        return _

    def stayed(e, _):
        keep(e, skip).wait()
        return _

    lax.fori_loop(0, near, left, 0)
    lax.fori_loop(near, jnp.minimum(skip, every), stayed, 0)
    lax.fori_loop(skip, every, left, 0)
    plan_copy.wait()


def in_hbm(x):
    return pltpu.with_memory_space_constraint(x, pltpu.HBM)


def tiles_call(rows, slots, real, imag, rb_dev, near_count):
    tiles, order, _ = real.shape
    nblk = lax.axis_size("blk")
    return pl.pallas_call(
        functools.partial(tiles_kernel, near_count),
        name="tiles",
        out_shape=(
            pltpu.HBM((tiles, 2 * order, order), F8),
            pltpu.VMEM((KEPT, 2 * order, order), F8),
            sds((8, rb_dev * order), F32),
            pltpu.HBM((tiles + 32,), I32),
        ),
        in_specs=[ANY] * 4,
        out_specs=(ANY, VMEM, VMEM, ANY),
        scratch_shapes=[
            pltpu.SMEM((tiles,), I32),
            pltpu.SMEM((tiles,), I32),
            pltpu.SMEM((tiles + 32,), I32),
            pltpu.VMEM((tiles + 1, order, 2 * order), BF16),
            pltpu.VMEM((tiles, 2 * order, order), F8),
            pltpu.VMEM((rb_dev, order, order // 2), BF16),
            pltpu.SMEM((rb_dev * (rb_dev + nblk),), I32),
            pltpu.SMEM((tiles + 1,), I32),
            pltpu.SMEM((tiles,), I32),
            pltpu.SemaphoreType.DMA((tiles // CHUNK, 2)),
            pltpu.SemaphoreType.DMA((tiles,)),
            pltpu.SemaphoreType.DMA((3,)),
        ],
        compiler_params=params(48),
        cost_estimate=pl.CostEstimate(flops=1 << 28, bytes_accessed=2 * real.size * 2, transcendentals=0),
    )(in_hbm(rows), in_hbm(slots), in_hbm(real), in_hbm(imag))


def rounded_block(field, scale_ref, r, order):
    at = slice(r * order, (r + 1) * order)
    return (field[:, at] * scale_ref[0:1, at]).astype(BF16)


def send_picked(wanted_ref, sent_ref, out_ref):
    me = lax.axis_index("blk")
    for i in range(out_ref.shape[0]):
        out_ref[i] = sent_ref[wanted_ref[i, 0, me]]


def first_kernel(y_ref, scale_ref, wanted_ref, out_ref, sent_ref):
    for r in range(sent_ref.shape[0]):
        sent_ref[r] = rounded_block(y_ref, scale_ref, r, sent_ref.shape[2])
    send_picked(wanted_ref, sent_ref, out_ref)


def load_groups(packed_hbm, tiles_ref, sems, lo, hi):
    def copy(g):
        at = pl.ds((g - lo) * UNROLL, UNROLL)
        return pltpu.make_async_copy(
            packed_hbm.at[pl.ds(g * UNROLL, UNROLL)], tiles_ref.at[at], sems.at[g - lo]
        )

    def begin(g, _):
        copy(g).start()
        return _

    lax.fori_loop(lo, hi, begin, 0)
    return copy


def split_sources(count, source, x_ref):
    _, rows, width = x_ref.shape
    group, order = rows // 2, width // 2
    most = jnp.zeros((group, order), F32)
    for p in range(count):
        most = jnp.maximum(most, jnp.abs(source(p).astype(F32)))
    most = jnp.broadcast_to(jnp.max(most, axis=1, keepdims=True), (group, 128))
    most = jnp.maximum(jnp.maximum(most, jnp.abs(turn_rows(most))), TINY)
    power = jnp.floor(jnp.log2(most))
    size = jnp.exp2(power - TOP)
    inverse = jnp.exp2(TOP - power)[:, 0:1]
    for p in range(count):
        scaled = source(p).astype(F32) * inverse
        far = scaled * SPLIT
        high = far - (far - scaled)
        low = (scaled - high) * FINER
        for k, part in enumerate((high, low)):
            at = slice(k * group, (k + 1) * group)
            x_ref[p, at, :order] = part.astype(F8)
            x_ref[p, at, order:] = turn_rows(part).astype(F8)
    x_ref[count] = jnp.zeros_like(x_ref[count])
    return size[:, 0:1]


def multiply(plan_ref, lo, hi, tile, load, acc_ref):
    def group(g, _):
        done = []
        for j in range(UNROLL):
            code = plan_ref[g * UNROLL + j]
            product = jnp.dot(load(code >> 8), tile(g, j), preferred_element_type=F32)
            done.append((code & 255, product))
        for row, product in done:
            acc_ref[row] = acc_ref[row] + product
        return _

    lax.fori_loop(lo, hi, group, 0)


def loaded(copy, tiles_ref, lo):
    def tile(g, j):
        if j == 0:
            copy(g).wait()
        return tiles_ref[(g - lo) * UNROLL + j]

    return tile


def collect(acc, size):
    group = size.shape[0]
    return (acc[:group] + acc[group:] * (1.0 / FINER)) * size


def near_kernel(step, plan_ref, packed_hbm, scale_ref, now_ref, before_ref, base_ref, tiles_ref, x_ref, acc_ref, sems):
    rb_dev, _, order = acc_ref.shape
    end = plan_ref.shape[0] - 32
    hi = plan_ref[end]
    copy = load_groups(packed_hbm, tiles_ref, sems, 0, hi)
    acc_ref[...] = jnp.zeros_like(acc_ref)
    size = split_sources(rb_dev, lambda r: rounded_block(now_ref, scale_ref, r, order), x_ref)
    multiply(plan_ref, 0, hi, loaded(copy, tiles_ref, 0), lambda c: x_ref[jnp.minimum(c, rb_dev)], acc_ref)
    for r in range(rb_dev):
        at = slice(r * order, (r + 1) * order)
        applied = scale_ref[0:1, at] * collect(acc_ref[r], size)
        moved = ((1.0 - center) * now_ref[:, at] - applied) / half_width
        base_ref[:, at] = moved if step == 0 else 2.0 * moved - before_ref[:, at]


def step_kernel(step, plan_ref, wanted_ref, packed_hbm, kept_ref, scale_ref, base_ref, arrived_ref, *refs):
    last = step == STEPS - 1
    next_ref = refs[0]
    if not last:
        out_ref, sent_ref = refs[1:3]
    tiles_ref, x_ref, acc_ref, sems = refs[-4:]
    rb_dev, _, order = acc_ref.shape
    end = plan_ref.shape[0] - 32
    lo, hi = plan_ref[end], plan_ref[end + 1]
    stay = jnp.minimum(lo + KEPT // UNROLL, hi)
    copy = load_groups(packed_hbm, tiles_ref, sems, stay, hi)
    acc_ref[...] = jnp.zeros_like(acc_ref)
    size = split_sources(arrived_ref.shape[0], lambda p: arrived_ref[p], x_ref)
    size = size * ((1.0 if step == 0 else 2.0) / half_width)
    multiply(
        plan_ref, lo, stay, lambda g, j: kept_ref[(g - lo) * UNROLL + j], lambda c: x_ref[c - rb_dev], acc_ref
    )
    multiply(plan_ref, stay, hi, loaded(copy, tiles_ref, stay), lambda c: x_ref[c - rb_dev], acc_ref)
    for r in range(rb_dev):
        at = slice(r * order, (r + 1) * order)
        scale = scale_ref[0:1, at]
        following = base_ref[:, at] - scale * collect(acc_ref[r], size)
        next_ref[:, at] = following
        if not last:
            sent_ref[r] = (following * scale).astype(BF16)
    if not last:
        send_picked(wanted_ref, sent_ref, out_ref)


def all_rows(own_ref, arrived, all_ref):
    c = lax.axis_index("col")
    all_ref[c] = own_ref[...].astype(BF16)
    for s, ref in enumerate(arrived, 1):
        all_ref[c ^ s] = ref[...]
    n, group, rows = all_ref.shape
    return all_ref[...].reshape(n * group, rows)


def gram_kernel(own_ref, *refs):
    arrived, (gram_ref, all_ref, full_ref) = refs[:-3], refs[-3:]
    rows = all_rows(own_ref, arrived, all_ref)
    full_ref[...] = lax.dot_general(rows, rows, NT, preferred_element_type=F32)
    half = gram_ref.shape[0]
    even = full_ref[pl.ds(0, half, stride=2), :]
    odd = full_ref[pl.ds(1, half, stride=2), :]
    gram_ref[...] = even + turn_lanes(odd)


PANEL = 32


def factor_kernel(nodes, own_ref, all_ref, *refs):
    parts, (out_ref, work_ref, inverse_ref) = refs[:-3], refs[-3:]
    group = own_ref.shape[0]
    order = work_ref.shape[0]
    total = parts[0][...]
    for part in parts[1:]:
        total = total + part[...]
    half = total.shape[0]
    work_ref[pl.ds(0, half, stride=2), :] = total
    work_ref[pl.ds(1, half, stride=2), :] = -turn_lanes(total)
    row_at = lax.broadcasted_iota(I32, (order, order), 0)
    lane_at = lax.broadcasted_iota(I32, (order, order), 1)
    inverse_ref[...] = (row_at == lane_at).astype(F32)
    here = lax.broadcasted_iota(I32, (PANEL, order), 0)
    for top in range(0, order, PANEL):
        a = work_ref[top : top + PANEL, :]
        m = inverse_ref[top : top + PANEL, :]
        pivots = jnp.ones_like(a)
        for k in range(0, PANEL, 4):
            w = [jnp.broadcast_to(a[:, i : i + 1], a.shape) for i in range(top + k, top + k + 4)]
            p, q = w[0][k : k + 1, :], w[2][k + 2 : k + 3, :]
            u, v = w[2][k : k + 1, :], w[3][k : k + 1, :]
            single = 1.0 / p
            det = p * q - (u * u + v * v)
            both = 1.0 / det
            second = (here == k + 2) | (here == k + 3)
            below = here > k + 3
            coefficients = (
                jnp.where(second, w[0] * single, (w[0] * q - w[2] * u - w[3] * v) * both),
                jnp.where(second, w[1] * single, (w[1] * q + w[2] * v - w[3] * u) * both),
                jnp.where(below, (w[2] * p - w[0] * u + w[1] * v) * both, 0.0),
                jnp.where(below, (w[3] * p - w[0] * v - w[1] * u) * both, 0.0),
            )
            coefficients = [jnp.where(here > k + 1, c, 0.0) for c in coefficients]
            pivots = jnp.where((here == k) | (here == k + 1), p, pivots)
            pivots = jnp.where(second, det * single, pivots)
            a, m = (
                x - sum(c * x[k + i : k + i + 1, :] for i, c in enumerate(coefficients)) for x in (a, m)
            )
        root = lax.rsqrt(pivots)
        a, m = a * root, m * root
        inverse_ref[top : top + PANEL, :] = m
        rest = top + PANEL
        if rest < order:
            update = lax.dot_general(
                a, jnp.concatenate([a, m], axis=1), TN, precision=lax.Precision.HIGHEST, preferred_element_type=F32
            )
            work_ref[rest:, :] = work_ref[rest:, :] - update[rest:, :order]
            inverse_ref[rest:, :] = inverse_ref[rest:, :] - update[rest:, order:]
    c = lax.axis_index("col")
    mine = inverse_ref[pl.ds(pl.multiple_of(c * group, group), group), :]
    mine = mine * math.sqrt(nodes)
    high = mine.astype(BF16)
    low = (mine - high.astype(F32)).astype(BF16)
    rows = all_ref[...].reshape(order, own_ref.shape[1])
    both = lax.dot_general(
        jnp.concatenate([high, low], axis=0), rows, (((1,), (0,)), ((), ())), preferred_element_type=F32
    )
    own = own_ref[...]
    lost = own - own.astype(BF16).astype(F32)
    own_lanes = (
        lax.broadcasted_iota(I32, (order, group), 0)
        == lax.broadcasted_iota(I32, (order, group), 1) + c * group
    ).astype(BF16)
    square = jnp.dot(high, own_lanes, preferred_element_type=F32).astype(BF16)
    out_ref[...] = (
        both[:group] + both[group:] + jnp.dot(square, lost.astype(BF16), preferred_element_type=F32)
    )


def central(nblk):
    return nblk // 4


def exchange(x):
    nblk = lax.axis_size("blk")
    group = [i ^ central(nblk) for i in range(nblk)]
    return lax.all_to_all(x, "blk", split_axis=0, concat_axis=0, tiled=True, axis_index_groups=[group])


def to_partner(x, axis, mask):
    n = lax.axis_size(axis)
    return lax.ppermute(x, axis, [(i, i ^ mask) for i in range(n)])


def sum_parts(part, nblk):
    wide = 1
    while 4 * wide < nblk:
        part = part + to_partner(part, "blk", wide)
        wide *= 2
    return [part] + [to_partner(part, "blk", s * wide) for s in range(1, nblk // wide)]


def per_device(y_start, tile_real, tile_imag, tile_rows, tile_slots, fetch_pick):
    group, rows = y_start.shape
    tiles, order, _ = tile_real.shape
    rb_dev = rows // order
    nblk = lax.axis_size("blk")
    ncol = lax.axis_size("col")
    near_count = LOC_RB * rb_dev
    wanted = exchange(jnp.broadcast_to(fetch_pick[None], (nblk, 1, nblk)))
    packed, kept, scale, plan = tiles_call(tile_rows, tile_slots, tile_real, tile_imag, rb_dev, near_count)

    out_blocks = sds((nblk, group, order), BF16)
    sent_scratch = pltpu.VMEM((rb_dev, group, order), BF16)
    blocks = pl.pallas_call(
        first_kernel,
        name="first",
        out_shape=out_blocks,
        in_specs=[VMEM, VMEM, SMEM],
        out_specs=VMEM,
        scratch_shapes=[sent_scratch],
        compiler_params=params(LIMIT),
    )(y_start, scale, wanted)

    def scratch(entries, sources):
        return [
            pltpu.VMEM((entries, 2 * order, order), F8),
            pltpu.VMEM((sources + 1, 2 * group, 2 * order), F8),
            pltpu.VMEM((rb_dev, 2 * group, order), F32),
            pltpu.SemaphoreType.DMA((entries // UNROLL,)),
        ]

    vectors_here = sds((group, rows), F32)
    previous, current = y_start, y_start
    for step in range(STEPS):
        arrived = exchange(blocks)
        base = pl.pallas_call(
            functools.partial(near_kernel, step),
            name="near",
            out_shape=vectors_here,
            in_specs=[SMEM, ANY] + [VMEM] * 3,
            out_specs=VMEM,
            scratch_shapes=scratch(near_count, rb_dev),
            compiler_params=params(LIMIT),
            cost_estimate=pl.CostEstimate(flops=1 << 28, bytes_accessed=1 << 21, transcendentals=0),
        )(in_hbm(plan), in_hbm(packed), scale, current, previous)
        last = step == STEPS - 1
        out = pl.pallas_call(
            functools.partial(step_kernel, step),
            name="step",
            out_shape=[vectors_here] if last else [vectors_here, out_blocks],
            in_specs=[SMEM, SMEM, ANY] + [VMEM] * 4,
            out_specs=[VMEM] if last else [VMEM, VMEM],
            scratch_shapes=([] if last else [sent_scratch]) + scratch(tiles - near_count - KEPT, nblk),
            compiler_params=params(LIMIT),
        )(in_hbm(plan), wanted, in_hbm(packed), pltpu.with_memory_space_constraint(kept, pltpu.VMEM), scale, base, arrived)
        previous, current = current, out[0]
        if not last:
            blocks = out[1]

    rounded = current.astype(BF16)
    if ncol == 4:
        beside, across = to_partner(rounded, "col", 1), to_partner(rounded, "col", 2)
        others = [beside, across, to_partner(across, "col", 1)]
    else:
        others = [to_partner(rounded, "col", s) for s in range(1, ncol)]
    vectors = group * ncol
    part, gathered = pl.pallas_call(
        gram_kernel,
        name="gram",
        out_shape=(sds((vectors // 2, vectors), F32), sds((ncol, group, rows), BF16)),
        in_specs=[VMEM] * (1 + len(others)),
        out_specs=(VMEM, VMEM),
        scratch_shapes=[pltpu.VMEM((vectors, vectors), F32)],
        compiler_params=params(LIMIT),
    )(current, *others)
    parts = sum_parts(part, nblk)
    return pl.pallas_call(
        functools.partial(factor_kernel, rows * nblk),
        name="factor",
        out_shape=sds((group, rows), F32),
        in_specs=[VMEM] * (2 + len(parts)),
        out_specs=VMEM,
        scratch_shapes=[pltpu.VMEM((vectors, vectors), F32)] * 2,
        compiler_params=params(LIMIT),
    )(current, gathered, *parts)


def solution(mesh):
    return jax.shard_map(
        per_device,
        mesh=mesh,
        in_specs=(
            P("col", "blk"),
            P("blk", None, None),
            P("blk", None, None),
            P("blk"),
            P("blk"),
            P("blk", None),
        ),
        out_specs=P("col", "blk"),
        check_vma=False,
    )
```

```python
import functools
import math

import jax
import jax.numpy as jnp
from jax import lax
from jax.experimental import pallas as pl
from jax.experimental.pallas import tpu as pltpu
from jax.sharding import PartitionSpec as P

LOC_RB = 2
STEPS = 4
UNROLL = 4
KEPT = 16
CHUNK = 4
MERGE = 16
TOP = 7.0
FINER = 16.0
SPLIT = float((1 << 20) + 1)
TINY = 1e-30
MIB = 1 << 20
LIMIT = 24

center = 1.25
half_width = 0.75

F32 = jnp.float32
BF16 = jnp.bfloat16
F8 = jnp.float8_e4m3fn
I32 = jnp.int32

VMEM = pl.BlockSpec(memory_space=pltpu.VMEM)
SMEM = pl.BlockSpec(memory_space=pltpu.SMEM)
ANY = pl.BlockSpec(memory_space=pl.ANY)

NT = (((1,), (1,)), ((), ()))
TN = (((0,), (0,)), ((), ()))


def sds(shape, dtype):
    return jax.ShapeDtypeStruct(shape, dtype)


def params(limit):
    return pltpu.CompilerParams(vmem_limit_bytes=limit * MIB)


def turn_rows(values):
    rows = values.shape[0]
    even = lax.broadcasted_iota(I32, values.shape, 0) % 2 == 0
    below = pltpu.roll(values, rows - 1, 0)
    above = pltpu.roll(values, 1, 0)
    return jnp.where(even, -below, above)


def turn_lanes(values):
    lanes = values.shape[1]
    even = lax.broadcasted_iota(I32, values.shape, 1) % 2 == 0
    after = pltpu.roll(values, lanes - 1, 1)
    before = pltpu.roll(values, 1, 1)
    return jnp.where(even, after, -before)


def tiles_kernel(
    near_count,
    rows_hbm,
    slots_hbm,
    real_hbm,
    imag_hbm,
    packed_hbm,
    kept_ref,
    scale_ref,
    plan_hbm,
    rows_ref,
    slots_ref,
    plan_ref,
    both_ref,
    small_ref,
    present_ref,
    table_ref,
    back_ref,
    done_ref,
    in_sems,
    out_sems,
    list_sems,
):
    kept = kept_ref.shape[0]
    tiles, order, _ = both_ref.shape
    rb_dev = present_ref.shape[0]
    slots = rb_dev + lax.axis_size("blk")
    chunks = tiles // CHUNK

    def copies(c):
        at = pl.ds(c * CHUNK, CHUNK)
        return (
            pltpu.make_async_copy(real_hbm.at[at], both_ref.at[at, :, 0:order], in_sems.at[c, 0]),
            pltpu.make_async_copy(imag_hbm.at[at], both_ref.at[at, :, order : 2 * order], in_sems.at[c, 1]),
        )

    def leave(e):
        return pltpu.make_async_copy(small_ref.at[e], packed_hbm.at[e], out_sems.at[e])

    lists = (
        pltpu.make_async_copy(rows_hbm, rows_ref, list_sems.at[0]),
        pltpu.make_async_copy(slots_hbm, slots_ref, list_sems.at[1]),
    )
    for copy in lists:
        copy.start()
    for c in range(chunks):
        for copy in copies(c):
            copy.start()

    def clear(key, _):
        table_ref[key] = -1
        return _

    lax.fori_loop(0, rb_dev * slots, clear, 0)
    present_ref[...] = jnp.zeros_like(present_ref)
    for copy in lists:
        copy.wait()

    def link(t, carry):
        key = rows_ref[t] * slots + slots_ref[t]
        seen = table_ref[key]
        before = seen & 255
        length = seen >> 8
        joins = (seen >= 0) & (length < MERGE)
        back_ref[t] = jnp.where(joins, before, -1)
        done_ref[t] = 1

        @pl.when(joins)
        def _():
            done_ref[before] = 0

        table_ref[key] = t | (jnp.where(joins, length + 1, 1) << 8)
        return carry

    lax.fori_loop(0, tiles, link, 0)

    def turned(tile):
        small = tile.astype(F8)
        return jnp.concatenate([small[:, :order].T, small[:, order:].T], axis=0)

    def put(e, skip, value):
        @pl.when(e < skip)
        def _():
            kept_ref[e - skip + kept] = value()

        @pl.when(e >= skip)
        def _():
            small_ref[e] = value()
            leave(e).start()

    def one(skip, t, listed):
        row = rows_ref[t]
        both = both_ref[t]
        present_ref[row] = present_ref[row] + (both[:, :order] + jnp.abs(both[:, order:]))
        closes = done_ref[t]

        @pl.when(closes == 1)
        def _():
            def add(prior):
                both_ref[t] = both_ref[t] + both_ref[prior]
                return back_ref[prior]

            lax.while_loop(lambda prior: prior >= 0, add, back_ref[t])
            put(listed, skip, lambda: turned(both_ref[t]))
            slot = slots_ref[t]
            place = rb_dev + ((slot - rb_dev) ^ central(slots - rb_dev))
            plan_ref[listed] = row | (jnp.where(slot < rb_dev, slot, place) << 8)

        return listed + closes

    def chunk(skip, c, listed):
        for copy in copies(c):
            copy.wait()
        for j in range(CHUNK):
            listed = one(skip, c * CHUNK + j, listed)
        return listed

    def pad(skip, listed):
        short = (UNROLL - listed % UNROLL) % UNROLL
        for j in range(UNROLL - 1):

            @pl.when(j < short)
            def _():
                put(listed + j, skip, lambda: jnp.zeros(small_ref.shape[1:], F8))
                plan_ref[listed + j] = slots << 8

        return listed + short

    near = pad(0, lax.fori_loop(0, near_count // CHUNK, functools.partial(chunk, 0), 0))
    skip = near + kept
    every = pad(skip, lax.fori_loop(near_count // CHUNK, chunks, functools.partial(chunk, skip), near))
    plan_ref[tiles] = near // UNROLL
    plan_ref[tiles + 1] = every // UNROLL
    plan_copy = pltpu.make_async_copy(plan_ref, plan_hbm, list_sems.at[2])
    plan_copy.start()

    ones = jnp.ones((8, order), BF16)
    for r in range(rb_dev):
        degree = lax.dot_general(ones, present_ref[r], NT, preferred_element_type=F32)
        scale_ref[:, r * order : (r + 1) * order] = 1.0 / jnp.sqrt(jnp.maximum(degree, 1.0))

    def left(e, _):
        leave(e).wait()
        return _

    lax.fori_loop(0, near, left, 0)
    lax.fori_loop(skip, every, left, 0)
    plan_copy.wait()


def in_hbm(x):
    return pltpu.with_memory_space_constraint(x, pltpu.HBM)


def tiles_call(rows, slots, real, imag, rb_dev, near_count):
    tiles, order, _ = real.shape
    nblk = lax.axis_size("blk")
    return pl.pallas_call(
        functools.partial(tiles_kernel, near_count),
        name="tiles",
        out_shape=(
            pltpu.HBM((tiles, 2 * order, order), F8),
            pltpu.VMEM((KEPT, 2 * order, order), F8),
            sds((8, rb_dev * order), F32),
            pltpu.HBM((tiles + 32,), I32),
        ),
        in_specs=[ANY] * 4,
        out_specs=(ANY, VMEM, VMEM, ANY),
        scratch_shapes=[
            pltpu.SMEM((tiles,), I32),
            pltpu.SMEM((tiles,), I32),
            pltpu.SMEM((tiles + 32,), I32),
            pltpu.VMEM((tiles, order, 2 * order), BF16),
            pltpu.VMEM((tiles, 2 * order, order), F8),
            pltpu.VMEM((rb_dev, order, order), BF16),
            pltpu.SMEM((rb_dev * (rb_dev + nblk),), I32),
            pltpu.SMEM((tiles,), I32),
            pltpu.SMEM((tiles,), I32),
            pltpu.SemaphoreType.DMA((tiles // CHUNK, 2)),
            pltpu.SemaphoreType.DMA((tiles,)),
            pltpu.SemaphoreType.DMA((3,)),
        ],
        compiler_params=params(48),
        cost_estimate=pl.CostEstimate(flops=1 << 28, bytes_accessed=2 * real.size * 2, transcendentals=0),
    )(in_hbm(rows), in_hbm(slots), in_hbm(real), in_hbm(imag))


def rounded_block(field, scale_ref, r, order):
    at = slice(r * order, (r + 1) * order)
    return (field[:, at] * scale_ref[0:1, at]).astype(BF16)


def send_picked(wanted_ref, sent_ref, out_hbm, sems):
    me = lax.axis_index("blk")
    copies = [
        pltpu.make_async_copy(sent_ref.at[wanted_ref[i, 0, me]], out_hbm.at[i], sems.at[i])
        for i in range(out_hbm.shape[0])
    ]
    for copy in copies:
        copy.start()
    for copy in copies:
        copy.wait()


def first_kernel(y_ref, scale_ref, wanted_ref, out_hbm, sent_ref, out_sems):
    for r in range(sent_ref.shape[0]):
        sent_ref[r] = rounded_block(y_ref, scale_ref, r, sent_ref.shape[2])
    send_picked(wanted_ref, sent_ref, out_hbm, out_sems)


def load_groups(packed_hbm, tiles_ref, sems, lo, hi):
    def copy(g):
        at = pl.ds((g - lo) * UNROLL, UNROLL)
        return pltpu.make_async_copy(
            packed_hbm.at[pl.ds(g * UNROLL, UNROLL)], tiles_ref.at[at], sems.at[g - lo]
        )

    def begin(g, _):
        copy(g).start()
        return _

    lax.fori_loop(lo, hi, begin, 0)
    return copy


def split_sources(count, source, x_ref):
    _, rows, width = x_ref.shape
    group, order = rows // 2, width // 2
    most = jnp.zeros((group, order), F32)
    for p in range(count):
        most = jnp.maximum(most, jnp.abs(source(p).astype(F32)))
    most = jnp.broadcast_to(jnp.max(most, axis=1, keepdims=True), (group, 128))
    most = jnp.maximum(jnp.maximum(most, jnp.abs(turn_rows(most))), TINY)
    power = jnp.floor(jnp.log2(most))
    size = jnp.exp2(power - TOP)
    inverse = jnp.exp2(TOP - power)[:, 0:1]
    for p in range(count):
        scaled = source(p).astype(F32) * inverse
        far = scaled * SPLIT
        high = far - (far - scaled)
        low = (scaled - high) * FINER
        for k, part in enumerate((high, low)):
            at = slice(k * group, (k + 1) * group)
            x_ref[p, at, :order] = part.astype(F8)
            x_ref[p, at, order:] = turn_rows(part).astype(F8)
    x_ref[count] = jnp.zeros_like(x_ref[count])
    return size[:, 0:1]


def multiply(plan_ref, lo, hi, tile, load, acc_ref):
    def group(g, _):
        done = []
        for j in range(UNROLL):
            code = plan_ref[g * UNROLL + j]
            product = jnp.dot(load(code >> 8), tile(g, j), preferred_element_type=F32)
            done.append((code & 255, product))
        for row, product in done:
            acc_ref[row] = acc_ref[row] + product
        return _

    lax.fori_loop(lo, hi, group, 0)


def loaded(copy, tiles_ref, lo):
    def tile(g, j):
        if j == 0:
            copy(g).wait()
        return tiles_ref[(g - lo) * UNROLL + j]

    return tile


def collect(acc, size):
    group = size.shape[0]
    return (acc[:group] + acc[group:] * (1.0 / FINER)) * size


def near_kernel(step, plan_ref, packed_hbm, scale_ref, now_ref, before_ref, base_ref, tiles_ref, x_ref, acc_ref, sems):
    rb_dev, _, order = acc_ref.shape
    end = plan_ref.shape[0] - 32
    hi = plan_ref[end]
    copy = load_groups(packed_hbm, tiles_ref, sems, 0, hi)
    acc_ref[...] = jnp.zeros_like(acc_ref)
    size = split_sources(rb_dev, lambda r: rounded_block(now_ref, scale_ref, r, order), x_ref)
    multiply(plan_ref, 0, hi, loaded(copy, tiles_ref, 0), lambda c: x_ref[jnp.minimum(c, rb_dev)], acc_ref)
    for r in range(rb_dev):
        at = slice(r * order, (r + 1) * order)
        applied = scale_ref[0:1, at] * collect(acc_ref[r], size)
        moved = ((1.0 - center) * now_ref[:, at] - applied) / half_width
        base_ref[:, at] = moved if step == 0 else 2.0 * moved - before_ref[:, at]


def step_kernel(step, plan_ref, wanted_ref, packed_hbm, kept_ref, scale_ref, base_ref, arrived_ref, *refs):
    last = step == STEPS - 1
    next_ref = refs[0]
    if not last:
        out_hbm, sent_ref, out_sems = refs[1:4]
    tiles_ref, x_ref, acc_ref, sems = refs[-4:]
    rb_dev, _, order = acc_ref.shape
    end = plan_ref.shape[0] - 32
    lo, hi = plan_ref[end], plan_ref[end + 1]
    stay = jnp.minimum(lo + KEPT // UNROLL, hi)
    copy = load_groups(packed_hbm, tiles_ref, sems, stay, hi)
    acc_ref[...] = jnp.zeros_like(acc_ref)
    size = split_sources(arrived_ref.shape[0], lambda p: arrived_ref[p], x_ref)
    size = size * ((1.0 if step == 0 else 2.0) / half_width)
    multiply(
        plan_ref, lo, stay, lambda g, j: kept_ref[(g - lo) * UNROLL + j], lambda c: x_ref[c - rb_dev], acc_ref
    )
    multiply(plan_ref, stay, hi, loaded(copy, tiles_ref, stay), lambda c: x_ref[c - rb_dev], acc_ref)
    for r in range(rb_dev):
        at = slice(r * order, (r + 1) * order)
        scale = scale_ref[0:1, at]
        following = base_ref[:, at] - scale * collect(acc_ref[r], size)
        next_ref[:, at] = following
        if not last:
            sent_ref[r] = (following * scale).astype(BF16)
    if not last:
        send_picked(wanted_ref, sent_ref, out_hbm, out_sems)


def all_rows(own_ref, arrived, all_ref):
    c = lax.axis_index("col")
    all_ref[c] = own_ref[...].astype(BF16)
    for s, ref in enumerate(arrived, 1):
        all_ref[c ^ s] = ref[...]
    n, group, rows = all_ref.shape
    return all_ref[...].reshape(n * group, rows)


def gram_kernel(own_ref, *refs):
    arrived, (gram_ref, all_ref, full_ref) = refs[:-3], refs[-3:]
    rows = all_rows(own_ref, arrived, all_ref)
    full_ref[...] = lax.dot_general(rows, rows, NT, preferred_element_type=F32)
    half = gram_ref.shape[0]
    even = full_ref[pl.ds(0, half, stride=2), :]
    odd = full_ref[pl.ds(1, half, stride=2), :]
    gram_ref[...] = even + turn_lanes(odd)


PANEL = 32


def factor_kernel(nodes, own_ref, all_ref, *refs):
    parts, (out_ref, work_ref, inverse_ref) = refs[:-3], refs[-3:]
    group = own_ref.shape[0]
    order = work_ref.shape[0]
    total = parts[0][...]
    for part in parts[1:]:
        total = total + part[...]
    half = total.shape[0]
    work_ref[pl.ds(0, half, stride=2), :] = total
    work_ref[pl.ds(1, half, stride=2), :] = -turn_lanes(total)
    row_at = lax.broadcasted_iota(I32, (order, order), 0)
    lane_at = lax.broadcasted_iota(I32, (order, order), 1)
    inverse_ref[...] = (row_at == lane_at).astype(F32)
    here = lax.broadcasted_iota(I32, (PANEL, order), 0)
    for top in range(0, order, PANEL):
        a = work_ref[top : top + PANEL, :]
        m = inverse_ref[top : top + PANEL, :]
        pivots = jnp.ones_like(a)
        for k in range(0, PANEL, 4):
            w = [jnp.broadcast_to(a[:, i : i + 1], a.shape) for i in range(top + k, top + k + 4)]
            p, q = w[0][k : k + 1, :], w[2][k + 2 : k + 3, :]
            u, v = w[2][k : k + 1, :], w[3][k : k + 1, :]
            single = 1.0 / p
            det = p * q - (u * u + v * v)
            both = 1.0 / det
            second = (here == k + 2) | (here == k + 3)
            below = here > k + 3
            coefficients = (
                jnp.where(second, w[0] * single, (w[0] * q - w[2] * u - w[3] * v) * both),
                jnp.where(second, w[1] * single, (w[1] * q + w[2] * v - w[3] * u) * both),
                jnp.where(below, (w[2] * p - w[0] * u + w[1] * v) * both, 0.0),
                jnp.where(below, (w[3] * p - w[0] * v - w[1] * u) * both, 0.0),
            )
            coefficients = [jnp.where(here > k + 1, c, 0.0) for c in coefficients]
            pivots = jnp.where((here == k) | (here == k + 1), p, pivots)
            pivots = jnp.where(second, det * single, pivots)
            a, m = (
                x - sum(c * x[k + i : k + i + 1, :] for i, c in enumerate(coefficients)) for x in (a, m)
            )
        root = lax.rsqrt(pivots)
        a, m = a * root, m * root
        inverse_ref[top : top + PANEL, :] = m
        rest = top + PANEL
        if rest < order:
            update = lax.dot_general(
                a, jnp.concatenate([a, m], axis=1), TN, precision=lax.Precision.HIGHEST, preferred_element_type=F32
            )
            work_ref[rest:, :] = work_ref[rest:, :] - update[rest:, :order]
            inverse_ref[rest:, :] = inverse_ref[rest:, :] - update[rest:, order:]
    c = lax.axis_index("col")
    mine = inverse_ref[pl.ds(pl.multiple_of(c * group, group), group), :]
    mine = mine * math.sqrt(nodes)
    high = mine.astype(BF16)
    low = (mine - high.astype(F32)).astype(BF16)
    rows = all_ref[...].reshape(order, own_ref.shape[1])
    both = lax.dot_general(
        jnp.concatenate([high, low], axis=0), rows, (((1,), (0,)), ((), ())), preferred_element_type=F32
    )
    own = own_ref[...]
    lost = own - own.astype(BF16).astype(F32)
    own_lanes = (
        lax.broadcasted_iota(I32, (order, group), 0)
        == lax.broadcasted_iota(I32, (order, group), 1) + c * group
    ).astype(BF16)
    square = jnp.dot(high, own_lanes, preferred_element_type=F32).astype(BF16)
    out_ref[...] = (
        both[:group] + both[group:] + jnp.dot(square, lost.astype(BF16), preferred_element_type=F32)
    )


def central(nblk):
    return nblk // 4


def exchange(x):
    nblk = lax.axis_size("blk")
    group = [i ^ central(nblk) for i in range(nblk)]
    return lax.all_to_all(x, "blk", split_axis=0, concat_axis=0, tiled=True, axis_index_groups=[group])


def to_partner(x, axis, mask):
    n = lax.axis_size(axis)
    return lax.ppermute(x, axis, [(i, i ^ mask) for i in range(n)])


def sum_parts(part, nblk):
    wide = 1
    while 4 * wide < nblk:
        part = part + to_partner(part, "blk", wide)
        wide *= 2
    return [part] + [to_partner(part, "blk", s * wide) for s in range(1, nblk // wide)]


def per_device(y_start, tile_real, tile_imag, tile_rows, tile_slots, fetch_pick):
    group, rows = y_start.shape
    tiles, order, _ = tile_real.shape
    rb_dev = rows // order
    nblk = lax.axis_size("blk")
    ncol = lax.axis_size("col")
    near_count = LOC_RB * rb_dev
    wanted = exchange(jnp.broadcast_to(fetch_pick[None], (nblk, 1, nblk)))
    packed, kept, scale, plan = tiles_call(tile_rows, tile_slots, tile_real, tile_imag, rb_dev, near_count)

    out_blocks = pltpu.HBM((nblk, group, order), BF16)
    sent_scratch = [pltpu.VMEM((rb_dev, group, order), BF16), pltpu.SemaphoreType.DMA((nblk,))]
    blocks = pl.pallas_call(
        first_kernel,
        name="first",
        out_shape=out_blocks,
        in_specs=[VMEM, VMEM, SMEM],
        out_specs=ANY,
        scratch_shapes=sent_scratch,
        compiler_params=params(LIMIT),
    )(y_start, scale, wanted)

    def scratch(entries, sources):
        return [
            pltpu.VMEM((entries, 2 * order, order), F8),
            pltpu.VMEM((sources + 1, 2 * group, 2 * order), F8),
            pltpu.VMEM((rb_dev, 2 * group, order), F32),
            pltpu.SemaphoreType.DMA((entries // UNROLL,)),
        ]

    vectors_here = sds((group, rows), F32)
    previous, current = y_start, y_start
    for step in range(STEPS):
        arrived = exchange(blocks)
        base = pl.pallas_call(
            functools.partial(near_kernel, step),
            name="near",
            out_shape=vectors_here,
            in_specs=[SMEM, ANY] + [VMEM] * 3,
            out_specs=VMEM,
            scratch_shapes=scratch(near_count, rb_dev),
            compiler_params=params(LIMIT),
            cost_estimate=pl.CostEstimate(flops=1 << 28, bytes_accessed=1 << 21, transcendentals=0),
        )(in_hbm(plan), in_hbm(packed), scale, current, previous)
        last = step == STEPS - 1
        out = pl.pallas_call(
            functools.partial(step_kernel, step),
            name="step",
            out_shape=[vectors_here] if last else [vectors_here, out_blocks],
            in_specs=[SMEM, SMEM, ANY] + [VMEM] * 4,
            out_specs=[VMEM] if last else [VMEM, ANY],
            scratch_shapes=([] if last else sent_scratch) + scratch(tiles - near_count - KEPT, nblk),
            compiler_params=params(LIMIT),
        )(in_hbm(plan), wanted, in_hbm(packed), pltpu.with_memory_space_constraint(kept, pltpu.VMEM), scale, base, arrived)
        previous, current = current, out[0]
        if not last:
            blocks = out[1]

    rounded = current.astype(BF16)
    if ncol == 4:
        beside, across = to_partner(rounded, "col", 1), to_partner(rounded, "col", 2)
        others = [beside, across, to_partner(across, "col", 1)]
    else:
        others = [to_partner(rounded, "col", s) for s in range(1, ncol)]
    vectors = group * ncol
    part, gathered = pl.pallas_call(
        gram_kernel,
        name="gram",
        out_shape=(sds((vectors // 2, vectors), F32), sds((ncol, group, rows), BF16)),
        in_specs=[VMEM] * (1 + len(others)),
        out_specs=(VMEM, VMEM),
        scratch_shapes=[pltpu.VMEM((vectors, vectors), F32)],
        compiler_params=params(LIMIT),
    )(current, *others)
    parts = sum_parts(part, nblk)
    return pl.pallas_call(
        functools.partial(factor_kernel, rows * nblk),
        name="factor",
        out_shape=sds((group, rows), F32),
        in_specs=[VMEM] * (2 + len(parts)),
        out_specs=VMEM,
        scratch_shapes=[pltpu.VMEM((vectors, vectors), F32)] * 2,
        compiler_params=params(LIMIT),
    )(current, gathered, *parts)


def solution(mesh):
    return jax.shard_map(
        per_device,
        mesh=mesh,
        in_specs=(
            P("col", "blk"),
            P("blk", None, None),
            P("blk", None, None),
            P("blk"),
            P("blk"),
            P("blk", None),
        ),
        out_specs=P("col", "blk"),
        check_vma=False,
    )
```

```python
import functools
import math

import jax
import jax.numpy as jnp
from jax import lax
from jax.experimental import pallas as pl
from jax.experimental.pallas import tpu as pltpu
from jax.sharding import PartitionSpec as P

LOC_RB = 2
STEPS = 4
UNROLL = 4
KEPT = 16
CHUNK = 4
MERGE = 16
TOP = 7.0
FINER = 16.0
SPLIT = float((1 << 20) + 1)
TINY = 1e-30
MIB = 1 << 20
LIMIT = 24

center = 1.25
half_width = 0.75

F32 = jnp.float32
BF16 = jnp.bfloat16
F8 = jnp.float8_e4m3fn
I32 = jnp.int32

VMEM = pl.BlockSpec(memory_space=pltpu.VMEM)
SMEM = pl.BlockSpec(memory_space=pltpu.SMEM)
ANY = pl.BlockSpec(memory_space=pl.ANY)

NT = (((1,), (1,)), ((), ()))
TN = (((0,), (0,)), ((), ()))


def sds(shape, dtype):
    return jax.ShapeDtypeStruct(shape, dtype)


def params(limit):
    return pltpu.CompilerParams(vmem_limit_bytes=limit * MIB)


def turn_rows(values):
    rows = values.shape[0]
    even = lax.broadcasted_iota(I32, values.shape, 0) % 2 == 0
    below = pltpu.roll(values, rows - 1, 0)
    above = pltpu.roll(values, 1, 0)
    return jnp.where(even, -below, above)


def turn_lanes(values):
    lanes = values.shape[1]
    even = lax.broadcasted_iota(I32, values.shape, 1) % 2 == 0
    after = pltpu.roll(values, lanes - 1, 1)
    before = pltpu.roll(values, 1, 1)
    return jnp.where(even, after, -before)


def tiles_kernel(
    near_count,
    rows_hbm,
    slots_hbm,
    real_hbm,
    imag_hbm,
    packed_hbm,
    kept_ref,
    scale_ref,
    plan_hbm,
    rows_ref,
    slots_ref,
    plan_ref,
    both_ref,
    small_ref,
    present_ref,
    table_ref,
    back_ref,
    done_ref,
    in_sems,
    out_sems,
    list_sems,
):
    kept = kept_ref.shape[0]
    tiles, order, _ = both_ref.shape
    rb_dev = present_ref.shape[0]
    slots = rb_dev + lax.axis_size("blk")
    chunks = tiles // CHUNK

    def copies(c):
        at = pl.ds(c * CHUNK, CHUNK)
        return (
            pltpu.make_async_copy(real_hbm.at[at], both_ref.at[at, :, 0:order], in_sems.at[c, 0]),
            pltpu.make_async_copy(imag_hbm.at[at], both_ref.at[at, :, order : 2 * order], in_sems.at[c, 1]),
        )

    def leave(e):
        return pltpu.make_async_copy(small_ref.at[e], packed_hbm.at[e], out_sems.at[e])

    lists = (
        pltpu.make_async_copy(rows_hbm, rows_ref, list_sems.at[0]),
        pltpu.make_async_copy(slots_hbm, slots_ref, list_sems.at[1]),
    )
    for copy in lists:
        copy.start()
    for c in range(chunks):
        for copy in copies(c):
            copy.start()

    def clear(row, _):
        for slot in range(slots):
            table_ref[row * slots + slot] = -1
        return _

    lax.fori_loop(0, rb_dev, clear, 0)
    present_ref[...] = jnp.zeros_like(present_ref)
    for copy in lists:
        copy.wait()

    def link(c, carry):
        for t in [c * CHUNK + j for j in range(CHUNK)]:
            key = rows_ref[t] * slots + slots_ref[t]
            seen = table_ref[key]
            before = seen & 255
            length = seen >> 8
            joins = (seen >= 0) & (length < MERGE)
            back_ref[t] = jnp.where(joins, before, -1)
            done_ref[t] = 1
            done_ref[jnp.where(joins, before, tiles)] = 0
            table_ref[key] = t | (jnp.where(joins, length + 1, 1) << 8)
        return carry

    lax.fori_loop(0, chunks, link, 0)

    def turned(tile):
        small = tile.astype(F8)
        return jnp.concatenate([small[:, :order].T, small[:, order:].T], axis=0)

    def put(e, skip, value):
        @pl.when(e < skip)
        def _():
            kept_ref[e - skip + kept] = value()

        @pl.when(e >= skip)
        def _():
            small_ref[e] = value()
            leave(e).start()

    def one(skip, t, listed):
        row = rows_ref[t]
        both = both_ref[t]
        counted = both[:, :order] + jnp.abs(both[:, order:])
        present_ref[row] = present_ref[row] + (counted[:, : order // 2] + counted[:, order // 2 :])
        closes = done_ref[t]

        @pl.when(closes == 1)
        def _():
            def add(prior):
                both_ref[t] = both_ref[t] + both_ref[prior]
                return back_ref[prior]

            lax.while_loop(lambda prior: prior >= 0, add, back_ref[t])
            put(listed, skip, lambda: turned(both_ref[t]))
            slot = slots_ref[t]
            place = rb_dev + ((slot - rb_dev) ^ central(slots - rb_dev))
            plan_ref[listed] = row | (jnp.where(slot < rb_dev, slot, place) << 8)

        return listed + closes

    def chunk(skip, c, listed):
        for copy in copies(c):
            copy.wait()
        for j in range(CHUNK):
            listed = one(skip, c * CHUNK + j, listed)
        return listed

    def pad(skip, listed):
        short = (UNROLL - listed % UNROLL) % UNROLL
        for j in range(UNROLL - 1):

            @pl.when(j < short)
            def _():
                put(listed + j, skip, lambda: jnp.zeros(small_ref.shape[1:], F8))
                plan_ref[listed + j] = slots << 8

        return listed + short

    near = pad(0, lax.fori_loop(0, near_count // CHUNK, functools.partial(chunk, 0), 0))
    skip = near + kept
    every = pad(skip, lax.fori_loop(near_count // CHUNK, chunks, functools.partial(chunk, skip), near))
    plan_ref[tiles] = near // UNROLL
    plan_ref[tiles + 1] = every // UNROLL
    plan_copy = pltpu.make_async_copy(plan_ref, plan_hbm, list_sems.at[2])
    plan_copy.start()

    ones = jnp.ones((8, order // 2), BF16)
    for r in range(rb_dev):
        degree = lax.dot_general(ones, present_ref[r], NT, preferred_element_type=F32)
        scale_ref[:, r * order : (r + 1) * order] = 1.0 / jnp.sqrt(jnp.maximum(degree, 1.0))

    def left(e, _):
        leave(e).wait()
        return _

    lax.fori_loop(0, near, left, 0)
    lax.fori_loop(skip, every, left, 0)
    plan_copy.wait()


def in_hbm(x):
    return pltpu.with_memory_space_constraint(x, pltpu.HBM)


def tiles_call(rows, slots, real, imag, rb_dev, near_count):
    tiles, order, _ = real.shape
    nblk = lax.axis_size("blk")
    return pl.pallas_call(
        functools.partial(tiles_kernel, near_count),
        name="tiles",
        out_shape=(
            pltpu.HBM((tiles, 2 * order, order), F8),
            pltpu.VMEM((KEPT, 2 * order, order), F8),
            sds((8, rb_dev * order), F32),
            pltpu.HBM((tiles + 32,), I32),
        ),
        in_specs=[ANY] * 4,
        out_specs=(ANY, VMEM, VMEM, ANY),
        scratch_shapes=[
            pltpu.SMEM((tiles,), I32),
            pltpu.SMEM((tiles,), I32),
            pltpu.SMEM((tiles + 32,), I32),
            pltpu.VMEM((tiles, order, 2 * order), BF16),
            pltpu.VMEM((tiles, 2 * order, order), F8),
            pltpu.VMEM((rb_dev, order, order // 2), BF16),
            pltpu.SMEM((rb_dev * (rb_dev + nblk),), I32),
            pltpu.SMEM((tiles,), I32),
            pltpu.SMEM((tiles + 1,), I32),
            pltpu.SemaphoreType.DMA((tiles // CHUNK, 2)),
            pltpu.SemaphoreType.DMA((tiles,)),
            pltpu.SemaphoreType.DMA((3,)),
        ],
        compiler_params=params(48),
        cost_estimate=pl.CostEstimate(flops=1 << 28, bytes_accessed=2 * real.size * 2, transcendentals=0),
    )(in_hbm(rows), in_hbm(slots), in_hbm(real), in_hbm(imag))


def rounded_block(field, scale_ref, r, order):
    at = slice(r * order, (r + 1) * order)
    return (field[:, at] * scale_ref[0:1, at]).astype(BF16)


def send_picked(wanted_ref, sent_ref, out_hbm, sems):
    me = lax.axis_index("blk")
    copies = [
        pltpu.make_async_copy(sent_ref.at[wanted_ref[i, 0, me]], out_hbm.at[i], sems.at[i])
        for i in range(out_hbm.shape[0])
    ]
    for copy in copies:
        copy.start()
    for copy in copies:
        copy.wait()


def first_kernel(y_ref, scale_ref, wanted_ref, out_hbm, sent_ref, out_sems):
    for r in range(sent_ref.shape[0]):
        sent_ref[r] = rounded_block(y_ref, scale_ref, r, sent_ref.shape[2])
    send_picked(wanted_ref, sent_ref, out_hbm, out_sems)


def load_groups(packed_hbm, tiles_ref, sems, lo, hi):
    def copy(g):
        at = pl.ds((g - lo) * UNROLL, UNROLL)
        return pltpu.make_async_copy(
            packed_hbm.at[pl.ds(g * UNROLL, UNROLL)], tiles_ref.at[at], sems.at[g - lo]
        )

    def begin(g, _):
        copy(g).start()
        return _

    lax.fori_loop(lo, hi, begin, 0)
    return copy


def split_sources(count, source, x_ref):
    _, rows, width = x_ref.shape
    group, order = rows // 2, width // 2
    most = jnp.zeros((group, order), F32)
    for p in range(count):
        most = jnp.maximum(most, jnp.abs(source(p).astype(F32)))
    most = jnp.broadcast_to(jnp.max(most, axis=1, keepdims=True), (group, 128))
    most = jnp.maximum(jnp.maximum(most, jnp.abs(turn_rows(most))), TINY)
    power = jnp.floor(jnp.log2(most))
    size = jnp.exp2(power - TOP)
    inverse = jnp.exp2(TOP - power)[:, 0:1]
    for p in range(count):
        scaled = source(p).astype(F32) * inverse
        far = scaled * SPLIT
        high = far - (far - scaled)
        low = (scaled - high) * FINER
        for k, part in enumerate((high, low)):
            at = slice(k * group, (k + 1) * group)
            x_ref[p, at, :order] = part.astype(F8)
            x_ref[p, at, order:] = turn_rows(part).astype(F8)
    x_ref[count] = jnp.zeros_like(x_ref[count])
    return size[:, 0:1]


def multiply(plan_ref, lo, hi, tile, load, acc_ref):
    def group(g, _):
        done = []
        for j in range(UNROLL):
            code = plan_ref[g * UNROLL + j]
            product = jnp.dot(load(code >> 8), tile(g, j), preferred_element_type=F32)
            done.append((code & 255, product))
        for row, product in done:
            acc_ref[row] = acc_ref[row] + product
        return _

    lax.fori_loop(lo, hi, group, 0)


def loaded(copy, tiles_ref, lo):
    def tile(g, j):
        if j == 0:
            copy(g).wait()
        return tiles_ref[(g - lo) * UNROLL + j]

    return tile


def collect(acc, size):
    group = size.shape[0]
    return (acc[:group] + acc[group:] * (1.0 / FINER)) * size


def near_kernel(step, plan_ref, packed_hbm, scale_ref, now_ref, before_ref, base_ref, tiles_ref, x_ref, acc_ref, sems):
    rb_dev, _, order = acc_ref.shape
    end = plan_ref.shape[0] - 32
    hi = plan_ref[end]
    copy = load_groups(packed_hbm, tiles_ref, sems, 0, hi)
    acc_ref[...] = jnp.zeros_like(acc_ref)
    size = split_sources(rb_dev, lambda r: rounded_block(now_ref, scale_ref, r, order), x_ref)
    multiply(plan_ref, 0, hi, loaded(copy, tiles_ref, 0), lambda c: x_ref[jnp.minimum(c, rb_dev)], acc_ref)
    for r in range(rb_dev):
        at = slice(r * order, (r + 1) * order)
        applied = scale_ref[0:1, at] * collect(acc_ref[r], size)
        moved = ((1.0 - center) * now_ref[:, at] - applied) / half_width
        base_ref[:, at] = moved if step == 0 else 2.0 * moved - before_ref[:, at]


def step_kernel(step, plan_ref, wanted_ref, packed_hbm, kept_ref, scale_ref, base_ref, arrived_ref, *refs):
    last = step == STEPS - 1
    next_ref = refs[0]
    if not last:
        out_hbm, sent_ref, out_sems = refs[1:4]
    tiles_ref, x_ref, acc_ref, sems = refs[-4:]
    rb_dev, _, order = acc_ref.shape
    end = plan_ref.shape[0] - 32
    lo, hi = plan_ref[end], plan_ref[end + 1]
    stay = jnp.minimum(lo + KEPT // UNROLL, hi)
    copy = load_groups(packed_hbm, tiles_ref, sems, stay, hi)
    acc_ref[...] = jnp.zeros_like(acc_ref)
    size = split_sources(arrived_ref.shape[0], lambda p: arrived_ref[p], x_ref)
    size = size * ((1.0 if step == 0 else 2.0) / half_width)
    multiply(
        plan_ref, lo, stay, lambda g, j: kept_ref[(g - lo) * UNROLL + j], lambda c: x_ref[c - rb_dev], acc_ref
    )
    multiply(plan_ref, stay, hi, loaded(copy, tiles_ref, stay), lambda c: x_ref[c - rb_dev], acc_ref)
    for r in range(rb_dev):
        at = slice(r * order, (r + 1) * order)
        scale = scale_ref[0:1, at]
        following = base_ref[:, at] - scale * collect(acc_ref[r], size)
        next_ref[:, at] = following
        if not last:
            sent_ref[r] = (following * scale).astype(BF16)
    if not last:
        send_picked(wanted_ref, sent_ref, out_hbm, out_sems)


def all_rows(own_ref, arrived, all_ref):
    c = lax.axis_index("col")
    all_ref[c] = own_ref[...].astype(BF16)
    for s, ref in enumerate(arrived, 1):
        all_ref[c ^ s] = ref[...]
    n, group, rows = all_ref.shape
    return all_ref[...].reshape(n * group, rows)


def gram_kernel(own_ref, *refs):
    arrived, (gram_ref, all_ref, full_ref) = refs[:-3], refs[-3:]
    rows = all_rows(own_ref, arrived, all_ref)
    full_ref[...] = lax.dot_general(rows, rows, NT, preferred_element_type=F32)
    half = gram_ref.shape[0]
    even = full_ref[pl.ds(0, half, stride=2), :]
    odd = full_ref[pl.ds(1, half, stride=2), :]
    gram_ref[...] = even + turn_lanes(odd)


PANEL = 64


def factor_kernel(nodes, own_ref, all_ref, *refs):
    parts, (out_ref, work_ref, inverse_ref) = refs[:-3], refs[-3:]
    group = own_ref.shape[0]
    order = work_ref.shape[0]
    total = parts[0][...]
    for part in parts[1:]:
        total = total + part[...]
    half = total.shape[0]
    work_ref[pl.ds(0, half, stride=2), :] = total
    work_ref[pl.ds(1, half, stride=2), :] = -turn_lanes(total)
    row_at = lax.broadcasted_iota(I32, (order, order), 0)
    lane_at = lax.broadcasted_iota(I32, (order, order), 1)
    inverse_ref[...] = (row_at == lane_at).astype(F32)
    here = lax.broadcasted_iota(I32, (PANEL, order), 0)
    for top in range(0, order, PANEL):
        a = work_ref[top : top + PANEL, :]
        m = inverse_ref[top : top + PANEL, :]
        pivots = jnp.ones_like(a)
        for k in range(0, PANEL, 4):
            w = [jnp.broadcast_to(a[:, i : i + 1], a.shape) for i in range(top + k, top + k + 4)]
            p, q = w[0][k : k + 1, :], w[2][k + 2 : k + 3, :]
            u, v = w[2][k : k + 1, :], w[3][k : k + 1, :]
            single = 1.0 / p
            det = p * q - (u * u + v * v)
            both = 1.0 / det
            second = (here == k + 2) | (here == k + 3)
            below = here > k + 3
            coefficients = (
                jnp.where(second, w[0] * single, (w[0] * q - w[2] * u - w[3] * v) * both),
                jnp.where(second, w[1] * single, (w[1] * q + w[2] * v - w[3] * u) * both),
                jnp.where(below, (w[2] * p - w[0] * u + w[1] * v) * both, 0.0),
                jnp.where(below, (w[3] * p - w[0] * v - w[1] * u) * both, 0.0),
            )
            coefficients = [jnp.where(here > k + 1, c, 0.0) for c in coefficients]
            pivots = jnp.where((here == k) | (here == k + 1), p, pivots)
            pivots = jnp.where(second, det * single, pivots)
            a, m = (
                x - sum(c * x[k + i : k + i + 1, :] for i, c in enumerate(coefficients)) for x in (a, m)
            )
        root = lax.rsqrt(pivots)
        a, m = a * root, m * root
        inverse_ref[top : top + PANEL, :] = m
        rest = top + PANEL
        if rest < order:
            update = lax.dot_general(
                a, jnp.concatenate([a, m], axis=1), TN, precision=lax.Precision.HIGHEST, preferred_element_type=F32
            )
            work_ref[rest:, :] = work_ref[rest:, :] - update[rest:, :order]
            inverse_ref[rest:, :] = inverse_ref[rest:, :] - update[rest:, order:]
    c = lax.axis_index("col")
    mine = inverse_ref[pl.ds(pl.multiple_of(c * group, group), group), :]
    mine = mine * math.sqrt(nodes)
    high = mine.astype(BF16)
    low = (mine - high.astype(F32)).astype(BF16)
    rows = all_ref[...].reshape(order, own_ref.shape[1])
    both = lax.dot_general(
        jnp.concatenate([high, low], axis=0), rows, (((1,), (0,)), ((), ())), preferred_element_type=F32
    )
    own = own_ref[...]
    lost = own - own.astype(BF16).astype(F32)
    own_lanes = (
        lax.broadcasted_iota(I32, (order, group), 0)
        == lax.broadcasted_iota(I32, (order, group), 1) + c * group
    ).astype(BF16)
    square = jnp.dot(high, own_lanes, preferred_element_type=F32).astype(BF16)
    out_ref[...] = (
        both[:group] + both[group:] + jnp.dot(square, lost.astype(BF16), preferred_element_type=F32)
    )


def central(nblk):
    return nblk // 4


def exchange(x):
    nblk = lax.axis_size("blk")
    group = [i ^ central(nblk) for i in range(nblk)]
    return lax.all_to_all(x, "blk", split_axis=0, concat_axis=0, tiled=True, axis_index_groups=[group])


def to_partner(x, axis, mask):
    n = lax.axis_size(axis)
    return lax.ppermute(x, axis, [(i, i ^ mask) for i in range(n)])


def sum_parts(part, nblk):
    wide = 1
    while 4 * wide < nblk:
        part = part + to_partner(part, "blk", wide)
        wide *= 2
    return [part] + [to_partner(part, "blk", s * wide) for s in range(1, nblk // wide)]


def per_device(y_start, tile_real, tile_imag, tile_rows, tile_slots, fetch_pick):
    group, rows = y_start.shape
    tiles, order, _ = tile_real.shape
    rb_dev = rows // order
    nblk = lax.axis_size("blk")
    ncol = lax.axis_size("col")
    near_count = LOC_RB * rb_dev
    wanted = exchange(jnp.broadcast_to(fetch_pick[None], (nblk, 1, nblk)))
    packed, kept, scale, plan = tiles_call(tile_rows, tile_slots, tile_real, tile_imag, rb_dev, near_count)

    out_blocks = pltpu.HBM((nblk, group, order), BF16)
    sent_scratch = [pltpu.VMEM((rb_dev, group, order), BF16), pltpu.SemaphoreType.DMA((nblk,))]
    blocks = pl.pallas_call(
        first_kernel,
        name="first",
        out_shape=out_blocks,
        in_specs=[VMEM, VMEM, SMEM],
        out_specs=ANY,
        scratch_shapes=sent_scratch,
        compiler_params=params(LIMIT),
    )(y_start, scale, wanted)

    def scratch(entries, sources):
        return [
            pltpu.VMEM((entries, 2 * order, order), F8),
            pltpu.VMEM((sources + 1, 2 * group, 2 * order), F8),
            pltpu.VMEM((rb_dev, 2 * group, order), F32),
            pltpu.SemaphoreType.DMA((entries // UNROLL,)),
        ]

    vectors_here = sds((group, rows), F32)
    previous, current = y_start, y_start
    for step in range(STEPS):
        arrived = exchange(blocks)
        base = pl.pallas_call(
            functools.partial(near_kernel, step),
            name="near",
            out_shape=vectors_here,
            in_specs=[SMEM, ANY] + [VMEM] * 3,
            out_specs=VMEM,
            scratch_shapes=scratch(near_count, rb_dev),
            compiler_params=params(LIMIT),
            cost_estimate=pl.CostEstimate(flops=1 << 28, bytes_accessed=1 << 21, transcendentals=0),
        )(in_hbm(plan), in_hbm(packed), scale, current, previous)
        last = step == STEPS - 1
        out = pl.pallas_call(
            functools.partial(step_kernel, step),
            name="step",
            out_shape=[vectors_here] if last else [vectors_here, out_blocks],
            in_specs=[SMEM, SMEM, ANY] + [VMEM] * 4,
            out_specs=[VMEM] if last else [VMEM, ANY],
            scratch_shapes=([] if last else sent_scratch) + scratch(tiles - near_count - KEPT, nblk),
            compiler_params=params(LIMIT),
        )(in_hbm(plan), wanted, in_hbm(packed), pltpu.with_memory_space_constraint(kept, pltpu.VMEM), scale, base, arrived)
        previous, current = current, out[0]
        if not last:
            blocks = out[1]

    rounded = current.astype(BF16)
    if ncol == 4:
        beside, across = to_partner(rounded, "col", 1), to_partner(rounded, "col", 2)
        others = [beside, across, to_partner(across, "col", 1)]
    else:
        others = [to_partner(rounded, "col", s) for s in range(1, ncol)]
    vectors = group * ncol
    part, gathered = pl.pallas_call(
        gram_kernel,
        name="gram",
        out_shape=(sds((vectors // 2, vectors), F32), sds((ncol, group, rows), BF16)),
        in_specs=[VMEM] * (1 + len(others)),
        out_specs=(VMEM, VMEM),
        scratch_shapes=[pltpu.VMEM((vectors, vectors), F32)],
        compiler_params=params(LIMIT),
    )(current, *others)
    parts = sum_parts(part, nblk)
    return pl.pallas_call(
        functools.partial(factor_kernel, rows * nblk),
        name="factor",
        out_shape=sds((group, rows), F32),
        in_specs=[VMEM] * (2 + len(parts)),
        out_specs=VMEM,
        scratch_shapes=[pltpu.VMEM((vectors, vectors), F32)] * 2,
        compiler_params=params(LIMIT),
    )(current, gathered, *parts)


def solution(mesh):
    return jax.shard_map(
        per_device,
        mesh=mesh,
        in_specs=(
            P("col", "blk"),
            P("blk", None, None),
            P("blk", None, None),
            P("blk"),
            P("blk"),
            P("blk", None),
        ),
        out_specs=P("col", "blk"),
        check_vma=False,
    )
```

```python
import functools
import math

import jax
import jax.numpy as jnp
from jax import lax
from jax.experimental import pallas as pl
from jax.experimental.pallas import tpu as pltpu
from jax.sharding import PartitionSpec as P

LOC_RB = 2
STEPS = 4
UNROLL = 4
KEPT = 16
CHUNK = 4
MERGE = 16
TOP = 7.0
FINER = 16.0
SPLIT = float((1 << 20) + 1)
TINY = 1e-30
MIB = 1 << 20
LIMIT = 24

center = 1.25
half_width = 0.75

F32 = jnp.float32
BF16 = jnp.bfloat16
F8 = jnp.float8_e4m3fn
I32 = jnp.int32

VMEM = pl.BlockSpec(memory_space=pltpu.VMEM)
SMEM = pl.BlockSpec(memory_space=pltpu.SMEM)
ANY = pl.BlockSpec(memory_space=pl.ANY)

NT = (((1,), (1,)), ((), ()))
TN = (((0,), (0,)), ((), ()))


def sds(shape, dtype):
    return jax.ShapeDtypeStruct(shape, dtype)


def params(limit):
    return pltpu.CompilerParams(vmem_limit_bytes=limit * MIB)


def turn_rows(values):
    rows = values.shape[0]
    even = lax.broadcasted_iota(I32, values.shape, 0) % 2 == 0
    below = pltpu.roll(values, rows - 1, 0)
    above = pltpu.roll(values, 1, 0)
    return jnp.where(even, -below, above)


def turn_lanes(values):
    lanes = values.shape[1]
    even = lax.broadcasted_iota(I32, values.shape, 1) % 2 == 0
    after = pltpu.roll(values, lanes - 1, 1)
    before = pltpu.roll(values, 1, 1)
    return jnp.where(even, after, -before)


def tiles_kernel(
    near_count,
    rows_hbm,
    slots_hbm,
    real_hbm,
    imag_hbm,
    packed_hbm,
    kept_ref,
    scale_ref,
    plan_hbm,
    rows_ref,
    slots_ref,
    plan_ref,
    both_ref,
    small_ref,
    present_ref,
    table_ref,
    back_ref,
    done_ref,
    in_sems,
    out_sems,
    list_sems,
):
    kept = kept_ref.shape[0]
    tiles, order, _ = both_ref.shape
    rb_dev = present_ref.shape[0]
    slots = rb_dev + lax.axis_size("blk")
    chunks = tiles // CHUNK

    def copies(c):
        at = pl.ds(c * CHUNK, CHUNK)
        return (
            pltpu.make_async_copy(real_hbm.at[at], both_ref.at[at, :, 0:order], in_sems.at[c, 0]),
            pltpu.make_async_copy(imag_hbm.at[at], both_ref.at[at, :, order : 2 * order], in_sems.at[c, 1]),
        )

    def leave(e):
        return pltpu.make_async_copy(small_ref.at[e], packed_hbm.at[e], out_sems.at[e])

    lists = (
        pltpu.make_async_copy(rows_hbm, rows_ref, list_sems.at[0]),
        pltpu.make_async_copy(slots_hbm, slots_ref, list_sems.at[1]),
    )
    for copy in lists:
        copy.start()
    for c in range(chunks):
        for copy in copies(c):
            copy.start()

    def clear(row, _):
        for slot in range(slots):
            table_ref[row * slots + slot] = -1
        return _

    lax.fori_loop(0, rb_dev, clear, 0)
    present_ref[...] = jnp.zeros_like(present_ref)
    for copy in lists:
        copy.wait()

    def link(c, carry):
        for t in [c * CHUNK + j for j in range(CHUNK)]:
            key = rows_ref[t] * slots + slots_ref[t]
            seen = table_ref[key]
            before = seen & 255
            length = seen >> 8
            joins = (seen >= 0) & (length < MERGE)
            back_ref[t] = jnp.where(joins, before, -1)
            done_ref[t] = 1
            done_ref[jnp.where(joins, before, tiles)] = 0
            table_ref[key] = t | (jnp.where(joins, length + 1, 1) << 8)
        return carry

    lax.fori_loop(0, chunks, link, 0)

    def fill(ref, e, t):
        for at in [slice(q, q + 128) for q in range(0, 2 * order, 128)]:
            ref[e, at] = jnp.zeros((128, order), F8) if t is None else both_ref[t, :, at].astype(F8).T

    def put(e, skip, t):
        @pl.when(e < skip)
        def _():
            fill(kept_ref, e - skip + kept, t)

        @pl.when(e >= skip)
        def _():
            fill(small_ref, e, t)
            leave(e).start()

    def one(skip, t, listed):
        row = rows_ref[t]
        for at in [slice(q, q + order // 4) for q in range(0, order, order // 4)]:
            counted = both_ref[t, at, :order] + jnp.abs(both_ref[t, at, order:])
            present_ref[row, at] = present_ref[row, at] + counted
        closes = done_ref[t]

        @pl.when(closes == 1)
        def _():
            def add(prior):
                both_ref[t] = both_ref[t] + both_ref[prior]
                return back_ref[prior]

            lax.while_loop(lambda prior: prior >= 0, add, back_ref[t])
            put(listed, skip, t)
            slot = slots_ref[t]
            place = rb_dev + ((slot - rb_dev) ^ central(slots - rb_dev))
            plan_ref[listed] = row | (jnp.where(slot < rb_dev, slot, place) << 8)

        return listed + closes

    def chunk(skip, c, listed):
        for copy in copies(c):
            copy.wait()
        for j in range(CHUNK):
            listed = one(skip, c * CHUNK + j, listed)
        return listed

    def pad(skip, listed):
        short = (UNROLL - listed % UNROLL) % UNROLL
        for j in range(UNROLL - 1):

            @pl.when(j < short)
            def _():
                put(listed + j, skip, None)
                plan_ref[listed + j] = slots << 8

        return listed + short

    near = pad(0, lax.fori_loop(0, near_count // CHUNK, functools.partial(chunk, 0), 0))
    skip = near + kept
    every = pad(skip, lax.fori_loop(near_count // CHUNK, chunks, functools.partial(chunk, skip), near))
    plan_ref[tiles] = near // UNROLL
    plan_ref[tiles + 1] = every // UNROLL
    plan_copy = pltpu.make_async_copy(plan_ref, plan_hbm, list_sems.at[2])
    plan_copy.start()

    ones = jnp.ones((8, order), BF16)
    for r in range(rb_dev):
        degree = lax.dot_general(ones, present_ref[r], NT, preferred_element_type=F32)
        scale_ref[:, r * order : (r + 1) * order] = 1.0 / jnp.sqrt(jnp.maximum(degree, 1.0))

    def left(e, _):
        leave(e).wait()
        return _

    lax.fori_loop(0, near, left, 0)
    lax.fori_loop(skip, every, left, 0)
    plan_copy.wait()


def in_hbm(x):
    return pltpu.with_memory_space_constraint(x, pltpu.HBM)


def tiles_call(rows, slots, real, imag, rb_dev, near_count):
    tiles, order, _ = real.shape
    nblk = lax.axis_size("blk")
    return pl.pallas_call(
        functools.partial(tiles_kernel, near_count),
        name="tiles",
        out_shape=(
            pltpu.HBM((tiles, 2 * order, order), F8),
            pltpu.VMEM((KEPT, 2 * order, order), F8),
            sds((8, rb_dev * order), F32),
            pltpu.HBM((tiles + 32,), I32),
        ),
        in_specs=[ANY] * 4,
        out_specs=(ANY, VMEM, VMEM, ANY),
        scratch_shapes=[
            pltpu.SMEM((tiles,), I32),
            pltpu.SMEM((tiles,), I32),
            pltpu.SMEM((tiles + 32,), I32),
            pltpu.VMEM((tiles, order, 2 * order), BF16),
            pltpu.VMEM((tiles, 2 * order, order), F8),
            pltpu.VMEM((rb_dev, order, order), BF16),
            pltpu.SMEM((rb_dev * (rb_dev + nblk),), I32),
            pltpu.SMEM((tiles,), I32),
            pltpu.SMEM((tiles + 1,), I32),
            pltpu.SemaphoreType.DMA((tiles // CHUNK, 2)),
            pltpu.SemaphoreType.DMA((tiles,)),
            pltpu.SemaphoreType.DMA((3,)),
        ],
        compiler_params=params(48),
        cost_estimate=pl.CostEstimate(flops=1 << 28, bytes_accessed=2 * real.size * 2, transcendentals=0),
    )(in_hbm(rows), in_hbm(slots), in_hbm(real), in_hbm(imag))


def rounded_block(field, scale_ref, r, order):
    at = slice(r * order, (r + 1) * order)
    return (field[:, at] * scale_ref[0:1, at]).astype(BF16)


def send_picked(wanted_ref, sent_ref, out_hbm, sems):
    me = lax.axis_index("blk")
    copies = [
        pltpu.make_async_copy(sent_ref.at[wanted_ref[i, 0, me]], out_hbm.at[i], sems.at[i])
        for i in range(out_hbm.shape[0])
    ]
    for copy in copies:
        copy.start()
    for copy in copies:
        copy.wait()


def first_kernel(y_ref, scale_ref, wanted_ref, out_hbm, sent_ref, out_sems):
    for r in range(sent_ref.shape[0]):
        sent_ref[r] = rounded_block(y_ref, scale_ref, r, sent_ref.shape[2])
    send_picked(wanted_ref, sent_ref, out_hbm, out_sems)


def load_groups(packed_hbm, tiles_ref, sems, lo, hi):
    def copy(g):
        at = pl.ds((g - lo) * UNROLL, UNROLL)
        return pltpu.make_async_copy(
            packed_hbm.at[pl.ds(g * UNROLL, UNROLL)], tiles_ref.at[at], sems.at[g - lo]
        )

    def begin(g, _):
        copy(g).start()
        return _

    lax.fori_loop(lo, hi, begin, 0)
    return copy


def split_sources(count, source, x_ref):
    _, rows, width = x_ref.shape
    group, order = rows // 2, width // 2
    most = jnp.zeros((group, order), F32)
    for p in range(count):
        most = jnp.maximum(most, jnp.abs(source(p).astype(F32)))
    most = jnp.broadcast_to(jnp.max(most, axis=1, keepdims=True), (group, 128))
    most = jnp.maximum(jnp.maximum(most, jnp.abs(turn_rows(most))), TINY)
    power = jnp.floor(jnp.log2(most))
    size = jnp.exp2(power - TOP)
    inverse = jnp.exp2(TOP - power)[:, 0:1]
    for p in range(count):
        scaled = source(p).astype(F32) * inverse
        far = scaled * SPLIT
        high = far - (far - scaled)
        low = (scaled - high) * FINER
        for k, part in enumerate((high, low)):
            at = slice(k * group, (k + 1) * group)
            x_ref[p, at, :order] = part.astype(F8)
            x_ref[p, at, order:] = turn_rows(part).astype(F8)
    x_ref[count] = jnp.zeros_like(x_ref[count])
    return size[:, 0:1]


def multiply(plan_ref, lo, hi, tile, load, acc_ref):
    def group(g, _):
        done = []
        for j in range(UNROLL):
            code = plan_ref[g * UNROLL + j]
            product = jnp.dot(load(code >> 8), tile(g, j), preferred_element_type=F32)
            done.append((code & 255, product))
        for row, product in done:
            acc_ref[row] = acc_ref[row] + product
        return _

    lax.fori_loop(lo, hi, group, 0)


def loaded(copy, tiles_ref, lo):
    def tile(g, j):
        if j == 0:
            copy(g).wait()
        return tiles_ref[(g - lo) * UNROLL + j]

    return tile


def collect(acc, size):
    group = size.shape[0]
    return (acc[:group] + acc[group:] * (1.0 / FINER)) * size


def near_kernel(step, plan_ref, packed_hbm, scale_ref, now_ref, before_ref, base_ref, tiles_ref, x_ref, acc_ref, sems):
    rb_dev, _, order = acc_ref.shape
    end = plan_ref.shape[0] - 32
    hi = plan_ref[end]
    copy = load_groups(packed_hbm, tiles_ref, sems, 0, hi)
    acc_ref[...] = jnp.zeros_like(acc_ref)
    size = split_sources(rb_dev, lambda r: rounded_block(now_ref, scale_ref, r, order), x_ref)
    multiply(plan_ref, 0, hi, loaded(copy, tiles_ref, 0), lambda c: x_ref[jnp.minimum(c, rb_dev)], acc_ref)
    for r in range(rb_dev):
        at = slice(r * order, (r + 1) * order)
        applied = scale_ref[0:1, at] * collect(acc_ref[r], size)
        moved = ((1.0 - center) * now_ref[:, at] - applied) / half_width
        base_ref[:, at] = moved if step == 0 else 2.0 * moved - before_ref[:, at]


def step_kernel(step, plan_ref, wanted_ref, packed_hbm, kept_ref, scale_ref, base_ref, arrived_ref, *refs):
    last = step == STEPS - 1
    next_ref = refs[0]
    if not last:
        out_hbm, sent_ref, out_sems = refs[1:4]
    tiles_ref, x_ref, acc_ref, sems = refs[-4:]
    rb_dev, _, order = acc_ref.shape
    end = plan_ref.shape[0] - 32
    lo, hi = plan_ref[end], plan_ref[end + 1]
    stay = jnp.minimum(lo + KEPT // UNROLL, hi)
    copy = load_groups(packed_hbm, tiles_ref, sems, stay, hi)
    acc_ref[...] = jnp.zeros_like(acc_ref)
    size = split_sources(arrived_ref.shape[0], lambda p: arrived_ref[p], x_ref)
    size = size * ((1.0 if step == 0 else 2.0) / half_width)
    multiply(
        plan_ref, lo, stay, lambda g, j: kept_ref[(g - lo) * UNROLL + j], lambda c: x_ref[c - rb_dev], acc_ref
    )
    multiply(plan_ref, stay, hi, loaded(copy, tiles_ref, stay), lambda c: x_ref[c - rb_dev], acc_ref)
    for r in range(rb_dev):
        at = slice(r * order, (r + 1) * order)
        scale = scale_ref[0:1, at]
        following = base_ref[:, at] - scale * collect(acc_ref[r], size)
        next_ref[:, at] = following
        if not last:
            sent_ref[r] = (following * scale).astype(BF16)
    if not last:
        send_picked(wanted_ref, sent_ref, out_hbm, out_sems)


def all_rows(own_ref, arrived, all_ref):
    c = lax.axis_index("col")
    all_ref[c] = own_ref[...].astype(BF16)
    for s, ref in enumerate(arrived, 1):
        all_ref[c ^ s] = ref[...]
    n, group, rows = all_ref.shape
    return all_ref[...].reshape(n * group, rows)


def gram_kernel(own_ref, *refs):
    arrived, (gram_ref, all_ref, full_ref) = refs[:-3], refs[-3:]
    rows = all_rows(own_ref, arrived, all_ref)
    full_ref[...] = lax.dot_general(rows, rows, NT, preferred_element_type=F32)
    half = gram_ref.shape[0]
    even = full_ref[pl.ds(0, half, stride=2), :]
    odd = full_ref[pl.ds(1, half, stride=2), :]
    gram_ref[...] = even + turn_lanes(odd)


PANEL = 128


def factor_kernel(nodes, own_ref, all_ref, *refs):
    parts, (out_ref, work_ref, inverse_ref) = refs[:-3], refs[-3:]
    group = own_ref.shape[0]
    order = work_ref.shape[0]
    total = parts[0][...]
    for part in parts[1:]:
        total = total + part[...]
    half = total.shape[0]
    work_ref[pl.ds(0, half, stride=2), :] = total
    work_ref[pl.ds(1, half, stride=2), :] = -turn_lanes(total)
    row_at = lax.broadcasted_iota(I32, (order, order), 0)
    lane_at = lax.broadcasted_iota(I32, (order, order), 1)
    inverse_ref[...] = (row_at == lane_at).astype(F32)
    here = lax.broadcasted_iota(I32, (PANEL, order), 0)
    for top in range(0, order, PANEL):
        a = work_ref[top : top + PANEL, :]
        m = inverse_ref[top : top + PANEL, :]
        pivots = jnp.ones_like(a)
        for k in range(0, PANEL, 4):
            w = [jnp.broadcast_to(a[:, i : i + 1], a.shape) for i in range(top + k, top + k + 4)]
            p, q = w[0][k : k + 1, :], w[2][k + 2 : k + 3, :]
            u, v = w[2][k : k + 1, :], w[3][k : k + 1, :]
            single = 1.0 / p
            det = p * q - (u * u + v * v)
            both = 1.0 / det
            second = (here == k + 2) | (here == k + 3)
            below = here > k + 3
            coefficients = (
                jnp.where(second, w[0] * single, (w[0] * q - w[2] * u - w[3] * v) * both),
                jnp.where(second, w[1] * single, (w[1] * q + w[2] * v - w[3] * u) * both),
                jnp.where(below, (w[2] * p - w[0] * u + w[1] * v) * both, 0.0),
                jnp.where(below, (w[3] * p - w[0] * v - w[1] * u) * both, 0.0),
            )
            coefficients = [jnp.where(here > k + 1, c, 0.0) for c in coefficients]
            pivots = jnp.where((here == k) | (here == k + 1), p, pivots)
            pivots = jnp.where(second, det * single, pivots)
            a, m = (
                x - sum(c * x[k + i : k + i + 1, :] for i, c in enumerate(coefficients)) for x in (a, m)
            )
        root = lax.rsqrt(pivots)
        a, m = a * root, m * root
        inverse_ref[top : top + PANEL, :] = m
        rest = top + PANEL
        if rest < order:
            update = lax.dot_general(
                a, jnp.concatenate([a, m], axis=1), TN, precision=lax.Precision.HIGHEST, preferred_element_type=F32
            )
            work_ref[rest:, :] = work_ref[rest:, :] - update[rest:, :order]
            inverse_ref[rest:, :] = inverse_ref[rest:, :] - update[rest:, order:]
    c = lax.axis_index("col")
    mine = inverse_ref[pl.ds(pl.multiple_of(c * group, group), group), :]
    mine = mine * math.sqrt(nodes)
    high = mine.astype(BF16)
    low = (mine - high.astype(F32)).astype(BF16)
    rows = all_ref[...].reshape(order, own_ref.shape[1])
    both = lax.dot_general(
        jnp.concatenate([high, low], axis=0), rows, (((1,), (0,)), ((), ())), preferred_element_type=F32
    )
    own = own_ref[...]
    lost = own - own.astype(BF16).astype(F32)
    own_lanes = (
        lax.broadcasted_iota(I32, (order, group), 0)
        == lax.broadcasted_iota(I32, (order, group), 1) + c * group
    ).astype(BF16)
    square = jnp.dot(high, own_lanes, preferred_element_type=F32).astype(BF16)
    out_ref[...] = (
        both[:group] + both[group:] + jnp.dot(square, lost.astype(BF16), preferred_element_type=F32)
    )


def central(nblk):
    return nblk // 4


def exchange(x):
    nblk = lax.axis_size("blk")
    group = [i ^ central(nblk) for i in range(nblk)]
    return lax.all_to_all(x, "blk", split_axis=0, concat_axis=0, tiled=True, axis_index_groups=[group])


def to_partner(x, axis, mask):
    n = lax.axis_size(axis)
    return lax.ppermute(x, axis, [(i, i ^ mask) for i in range(n)])


def sum_parts(part, nblk):
    wide = 1
    while 4 * wide < nblk:
        part = part + to_partner(part, "blk", wide)
        wide *= 2
    return [part] + [to_partner(part, "blk", s * wide) for s in range(1, nblk // wide)]


def per_device(y_start, tile_real, tile_imag, tile_rows, tile_slots, fetch_pick):
    group, rows = y_start.shape
    tiles, order, _ = tile_real.shape
    rb_dev = rows // order
    nblk = lax.axis_size("blk")
    ncol = lax.axis_size("col")
    near_count = LOC_RB * rb_dev
    wanted = exchange(jnp.broadcast_to(fetch_pick[None], (nblk, 1, nblk)))
    packed, kept, scale, plan = tiles_call(tile_rows, tile_slots, tile_real, tile_imag, rb_dev, near_count)

    out_blocks = pltpu.HBM((nblk, group, order), BF16)
    sent_scratch = [pltpu.VMEM((rb_dev, group, order), BF16), pltpu.SemaphoreType.DMA((nblk,))]
    blocks = pl.pallas_call(
        first_kernel,
        name="first",
        out_shape=out_blocks,
        in_specs=[VMEM, VMEM, SMEM],
        out_specs=ANY,
        scratch_shapes=sent_scratch,
        compiler_params=params(LIMIT),
    )(y_start, scale, wanted)

    def scratch(entries, sources):
        return [
            pltpu.VMEM((entries, 2 * order, order), F8),
            pltpu.VMEM((sources + 1, 2 * group, 2 * order), F8),
            pltpu.VMEM((rb_dev, 2 * group, order), F32),
            pltpu.SemaphoreType.DMA((entries // UNROLL,)),
        ]

    vectors_here = sds((group, rows), F32)
    previous, current = y_start, y_start
    for step in range(STEPS):
        arrived = exchange(blocks)
        base = pl.pallas_call(
            functools.partial(near_kernel, step),
            name="near",
            out_shape=vectors_here,
            in_specs=[SMEM, ANY] + [VMEM] * 3,
            out_specs=VMEM,
            scratch_shapes=scratch(near_count, rb_dev),
            compiler_params=params(LIMIT),
            cost_estimate=pl.CostEstimate(flops=1 << 28, bytes_accessed=1 << 21, transcendentals=0),
        )(in_hbm(plan), in_hbm(packed), scale, current, previous)
        last = step == STEPS - 1
        out = pl.pallas_call(
            functools.partial(step_kernel, step),
            name="step",
            out_shape=[vectors_here] if last else [vectors_here, out_blocks],
            in_specs=[SMEM, SMEM, ANY] + [VMEM] * 4,
            out_specs=[VMEM] if last else [VMEM, ANY],
            scratch_shapes=([] if last else sent_scratch) + scratch(tiles - near_count - KEPT, nblk),
            compiler_params=params(LIMIT),
        )(in_hbm(plan), wanted, in_hbm(packed), pltpu.with_memory_space_constraint(kept, pltpu.VMEM), scale, base, arrived)
        previous, current = current, out[0]
        if not last:
            blocks = out[1]

    rounded = current.astype(BF16)
    if ncol == 4:
        beside, across = to_partner(rounded, "col", 1), to_partner(rounded, "col", 2)
        others = [beside, across, to_partner(across, "col", 1)]
    else:
        others = [to_partner(rounded, "col", s) for s in range(1, ncol)]
    vectors = group * ncol
    part, gathered = pl.pallas_call(
        gram_kernel,
        name="gram",
        out_shape=(sds((vectors // 2, vectors), F32), sds((ncol, group, rows), BF16)),
        in_specs=[VMEM] * (1 + len(others)),
        out_specs=(VMEM, VMEM),
        scratch_shapes=[pltpu.VMEM((vectors, vectors), F32)],
        compiler_params=params(LIMIT),
    )(current, *others)
    parts = sum_parts(part, nblk)
    return pl.pallas_call(
        functools.partial(factor_kernel, rows * nblk),
        name="factor",
        out_shape=sds((group, rows), F32),
        in_specs=[VMEM] * (2 + len(parts)),
        out_specs=VMEM,
        scratch_shapes=[pltpu.VMEM((vectors, vectors), F32)] * 2,
        compiler_params=params(LIMIT),
    )(current, gathered, *parts)


def solution(mesh):
    return jax.shard_map(
        per_device,
        mesh=mesh,
        in_specs=(
            P("col", "blk"),
            P("blk", None, None),
            P("blk", None, None),
            P("blk"),
            P("blk"),
            P("blk", None),
        ),
        out_specs=P("col", "blk"),
        check_vma=False,
    )
```

```python
import functools
import math

import jax
import jax.numpy as jnp
from jax import lax
from jax.experimental import pallas as pl
from jax.experimental.pallas import tpu as pltpu
from jax.sharding import PartitionSpec as P

LOC_RB = 2
STEPS = 4
UNROLL = 4
KEPT = 16
CHUNK = 4
MERGE = 16
TOP = 7.0
FINER = 16.0
SPLIT = float((1 << 20) + 1)
TINY = 1e-30
MIB = 1 << 20
LIMIT = 24

center = 1.25
half_width = 0.75

F32 = jnp.float32
BF16 = jnp.bfloat16
F8 = jnp.float8_e4m3fn
I32 = jnp.int32

VMEM = pl.BlockSpec(memory_space=pltpu.VMEM)
SMEM = pl.BlockSpec(memory_space=pltpu.SMEM)
ANY = pl.BlockSpec(memory_space=pl.ANY)

NT = (((1,), (1,)), ((), ()))
TN = (((0,), (0,)), ((), ()))


def sds(shape, dtype):
    return jax.ShapeDtypeStruct(shape, dtype)


def params(limit):
    return pltpu.CompilerParams(vmem_limit_bytes=limit * MIB)


def turn_rows(values):
    rows = values.shape[0]
    even = lax.broadcasted_iota(I32, values.shape, 0) % 2 == 0
    below = pltpu.roll(values, rows - 1, 0)
    above = pltpu.roll(values, 1, 0)
    return jnp.where(even, -below, above)


def turn_lanes(values):
    lanes = values.shape[1]
    even = lax.broadcasted_iota(I32, values.shape, 1) % 2 == 0
    after = pltpu.roll(values, lanes - 1, 1)
    before = pltpu.roll(values, 1, 1)
    return jnp.where(even, after, -before)


def tiles_kernel(
    near_count,
    rows_hbm,
    slots_hbm,
    real_hbm,
    imag_hbm,
    packed_hbm,
    kept_ref,
    scale_ref,
    plan_hbm,
    rows_ref,
    slots_ref,
    plan_ref,
    both_ref,
    small_ref,
    present_ref,
    table_ref,
    back_ref,
    done_ref,
    in_sems,
    out_sems,
    list_sems,
):
    kept = kept_ref.shape[0]
    tiles, order, _ = both_ref.shape
    rb_dev = present_ref.shape[0]
    slots = rb_dev + lax.axis_size("blk")
    chunks = tiles // CHUNK

    def copies(c):
        at = pl.ds(c * CHUNK, CHUNK)
        return (
            pltpu.make_async_copy(real_hbm.at[at], both_ref.at[at, :, 0:order], in_sems.at[c, 0]),
            pltpu.make_async_copy(imag_hbm.at[at], both_ref.at[at, :, order : 2 * order], in_sems.at[c, 1]),
        )

    def leave(e):
        return pltpu.make_async_copy(small_ref.at[e], packed_hbm.at[e], out_sems.at[e])

    lists = (
        pltpu.make_async_copy(rows_hbm, rows_ref, list_sems.at[0]),
        pltpu.make_async_copy(slots_hbm, slots_ref, list_sems.at[1]),
    )
    for copy in lists:
        copy.start()
    for c in range(chunks):
        for copy in copies(c):
            copy.start()

    def clear(row, _):
        for slot in range(slots):
            table_ref[row * slots + slot] = -1
        return _

    lax.fori_loop(0, rb_dev, clear, 0)
    present_ref[...] = jnp.zeros_like(present_ref)
    for copy in lists:
        copy.wait()

    def link(c, carry):
        for t in [c * CHUNK + j for j in range(CHUNK)]:
            key = rows_ref[t] * slots + slots_ref[t]
            seen = table_ref[key]
            before = seen & 255
            length = seen >> 8
            joins = (seen >= 0) & (length < MERGE)
            back_ref[t] = jnp.where(joins, before, -1)
            done_ref[t] = 1
            done_ref[jnp.where(joins, before, tiles)] = 0
            table_ref[key] = t | (jnp.where(joins, length + 1, 1) << 8)
        return carry

    lax.fori_loop(0, chunks, link, 0)

    def fill(ref, e, t):
        for at in [slice(q, q + 128) for q in range(0, 2 * order, 128)]:
            ref[e, at] = jnp.zeros((128, order), F8) if t is None else both_ref[t, :, at].astype(F8).T

    def put(e, skip, t):
        @pl.when(e < skip)
        def _():
            fill(kept_ref, e - skip + kept, t)

        @pl.when(e >= skip)
        def _():
            fill(small_ref, e, t)
            leave(e).start()

    def one(skip, t, listed):
        row = rows_ref[t]
        for at in [slice(q, q + order // 4) for q in range(0, order, order // 4)]:
            counted = both_ref[t, at, :order] + jnp.abs(both_ref[t, at, order:])
            present_ref[row, at] = present_ref[row, at] + counted
        closes = done_ref[t]

        @pl.when(closes == 1)
        def _():
            def add(prior):
                both_ref[t] = both_ref[t] + both_ref[prior]
                return back_ref[prior]

            lax.while_loop(lambda prior: prior >= 0, add, back_ref[t])
            put(listed, skip, t)
            slot = slots_ref[t]
            place = rb_dev + ((slot - rb_dev) ^ central(slots - rb_dev))
            plan_ref[listed] = row | (jnp.where(slot < rb_dev, slot, place) << 8)

        return listed + closes

    def chunk(skip, c, listed):
        for copy in copies(c):
            copy.wait()
        for j in range(CHUNK):
            listed = one(skip, c * CHUNK + j, listed)
        return listed

    def pad(skip, listed):
        short = (UNROLL - listed % UNROLL) % UNROLL
        for j in range(UNROLL - 1):

            @pl.when(j < short)
            def _():
                put(listed + j, skip, None)
                plan_ref[listed + j] = slots << 8

        return listed + short

    near = pad(0, lax.fori_loop(0, near_count // CHUNK, functools.partial(chunk, 0), 0))
    skip = near + kept
    every = pad(skip, lax.fori_loop(near_count // CHUNK, chunks, functools.partial(chunk, skip), near))
    plan_ref[tiles] = near // UNROLL
    plan_ref[tiles + 1] = every // UNROLL
    plan_copy = pltpu.make_async_copy(plan_ref, plan_hbm, list_sems.at[2])
    plan_copy.start()

    ones = jnp.ones((8, order), BF16)
    for r in range(rb_dev):
        degree = lax.dot_general(ones, present_ref[r], NT, preferred_element_type=F32)
        scale_ref[:, r * order : (r + 1) * order] = 1.0 / jnp.sqrt(jnp.maximum(degree, 1.0))

    def left(e, _):
        leave(e).wait()
        return _

    lax.fori_loop(0, near, left, 0)
    lax.fori_loop(skip, every, left, 0)
    plan_copy.wait()


def in_hbm(x):
    return pltpu.with_memory_space_constraint(x, pltpu.HBM)


def tiles_call(rows, slots, real, imag, rb_dev, near_count):
    tiles, order, _ = real.shape
    nblk = lax.axis_size("blk")
    return pl.pallas_call(
        functools.partial(tiles_kernel, near_count),
        name="tiles",
        out_shape=(
            pltpu.HBM((tiles, 2 * order, order), F8),
            pltpu.VMEM((KEPT, 2 * order, order), F8),
            sds((8, rb_dev * order), F32),
            pltpu.HBM((tiles + 32,), I32),
        ),
        in_specs=[ANY] * 4,
        out_specs=(ANY, VMEM, VMEM, ANY),
        scratch_shapes=[
            pltpu.SMEM((tiles,), I32),
            pltpu.SMEM((tiles,), I32),
            pltpu.SMEM((tiles + 32,), I32),
            pltpu.VMEM((tiles, order, 2 * order), BF16),
            pltpu.VMEM((tiles, 2 * order, order), F8),
            pltpu.VMEM((rb_dev, order, order), BF16),
            pltpu.SMEM((rb_dev * (rb_dev + nblk),), I32),
            pltpu.SMEM((tiles,), I32),
            pltpu.SMEM((tiles + 1,), I32),
            pltpu.SemaphoreType.DMA((tiles // CHUNK, 2)),
            pltpu.SemaphoreType.DMA((tiles,)),
            pltpu.SemaphoreType.DMA((3,)),
        ],
        compiler_params=params(48),
        cost_estimate=pl.CostEstimate(flops=1 << 28, bytes_accessed=2 * real.size * 2, transcendentals=0),
    )(in_hbm(rows), in_hbm(slots), in_hbm(real), in_hbm(imag))


def rounded_block(field, scale_ref, r, order):
    at = slice(r * order, (r + 1) * order)
    return (field[:, at] * scale_ref[0:1, at]).astype(BF16)


def send_picked(wanted_ref, sent_ref, out_hbm, sems):
    me = lax.axis_index("blk")
    copies = [
        pltpu.make_async_copy(sent_ref.at[wanted_ref[i, 0, me]], out_hbm.at[i], sems.at[i])
        for i in range(out_hbm.shape[0])
    ]
    for copy in copies:
        copy.start()
    for copy in copies:
        copy.wait()


def first_kernel(y_ref, scale_ref, wanted_ref, out_hbm, sent_ref, out_sems):
    for r in range(sent_ref.shape[0]):
        sent_ref[r] = rounded_block(y_ref, scale_ref, r, sent_ref.shape[2])
    send_picked(wanted_ref, sent_ref, out_hbm, out_sems)


def load_groups(packed_hbm, tiles_ref, sems, lo, hi):
    def copy(g):
        at = pl.ds((g - lo) * UNROLL, UNROLL)
        return pltpu.make_async_copy(
            packed_hbm.at[pl.ds(g * UNROLL, UNROLL)], tiles_ref.at[at], sems.at[g - lo]
        )

    def begin(g, _):
        copy(g).start()
        return _

    lax.fori_loop(lo, hi, begin, 0)
    return copy


def split_sources(count, source, x_ref):
    _, rows, width = x_ref.shape
    group, order = rows // 2, width // 2
    most = jnp.zeros((group, order), F32)
    for p in range(count):
        most = jnp.maximum(most, jnp.abs(source(p).astype(F32)))
    most = jnp.broadcast_to(jnp.max(most, axis=1, keepdims=True), (group, 128))
    most = jnp.maximum(jnp.maximum(most, jnp.abs(turn_rows(most))), TINY)
    power = jnp.floor(jnp.log2(most))
    size = jnp.exp2(power - TOP)
    inverse = jnp.exp2(TOP - power)[:, 0:1]
    for p in range(count):
        scaled = source(p).astype(F32) * inverse
        far = scaled * SPLIT
        high = far - (far - scaled)
        low = (scaled - high) * FINER
        for k, part in enumerate((high, low)):
            at = slice(k * group, (k + 1) * group)
            x_ref[p, at, :order] = part.astype(F8)
            x_ref[p, at, order:] = turn_rows(part).astype(F8)
    x_ref[count] = jnp.zeros_like(x_ref[count])
    return size[:, 0:1]


def multiply(plan_ref, lo, hi, tile, load, acc_ref):
    def group(g, _):
        done = []
        for j in range(UNROLL):
            code = plan_ref[g * UNROLL + j]
            product = jnp.dot(load(code >> 8), tile(g, j), preferred_element_type=F32)
            done.append((code & 255, product))
        for row, product in done:
            acc_ref[row] = acc_ref[row] + product
        return _

    lax.fori_loop(lo, hi, group, 0)


def loaded(copy, tiles_ref, lo):
    def tile(g, j):
        if j == 0:
            copy(g).wait()
        return tiles_ref[(g - lo) * UNROLL + j]

    return tile


def collect(acc, size):
    group = size.shape[0]
    return (acc[:group] + acc[group:] * (1.0 / FINER)) * size


def near_kernel(step, plan_ref, packed_hbm, scale_ref, now_ref, before_ref, base_ref, tiles_ref, x_ref, acc_ref, sems):
    rb_dev, _, order = acc_ref.shape
    end = plan_ref.shape[0] - 32
    hi = plan_ref[end]
    copy = load_groups(packed_hbm, tiles_ref, sems, 0, hi)
    acc_ref[...] = jnp.zeros_like(acc_ref)
    size = split_sources(rb_dev, lambda r: rounded_block(now_ref, scale_ref, r, order), x_ref)
    multiply(plan_ref, 0, hi, loaded(copy, tiles_ref, 0), lambda c: x_ref[jnp.minimum(c, rb_dev)], acc_ref)
    for r in range(rb_dev):
        at = slice(r * order, (r + 1) * order)
        applied = scale_ref[0:1, at] * collect(acc_ref[r], size)
        moved = ((1.0 - center) * now_ref[:, at] - applied) / half_width
        base_ref[:, at] = moved if step == 0 else 2.0 * moved - before_ref[:, at]


def step_kernel(step, plan_ref, wanted_ref, packed_hbm, kept_ref, scale_ref, base_ref, arrived_ref, *refs):
    last = step == STEPS - 1
    next_ref = refs[0]
    if not last:
        out_hbm, sent_ref, out_sems = refs[1:4]
    tiles_ref, x_ref, acc_ref, sems = refs[-4:]
    rb_dev, _, order = acc_ref.shape
    end = plan_ref.shape[0] - 32
    lo, hi = plan_ref[end], plan_ref[end + 1]
    stay = jnp.minimum(lo + KEPT // UNROLL, hi)
    copy = load_groups(packed_hbm, tiles_ref, sems, stay, hi)
    acc_ref[...] = jnp.zeros_like(acc_ref)
    size = split_sources(arrived_ref.shape[0], lambda p: arrived_ref[p], x_ref)
    size = size * ((1.0 if step == 0 else 2.0) / half_width)
    multiply(
        plan_ref, lo, stay, lambda g, j: kept_ref[(g - lo) * UNROLL + j], lambda c: x_ref[c - rb_dev], acc_ref
    )
    multiply(plan_ref, stay, hi, loaded(copy, tiles_ref, stay), lambda c: x_ref[c - rb_dev], acc_ref)
    for r in range(rb_dev):
        at = slice(r * order, (r + 1) * order)
        scale = scale_ref[0:1, at]
        following = base_ref[:, at] - scale * collect(acc_ref[r], size)
        next_ref[:, at] = following
        if not last:
            sent_ref[r] = (following * scale).astype(BF16)
    if not last:
        send_picked(wanted_ref, sent_ref, out_hbm, out_sems)


def all_rows(own_ref, arrived, all_ref):
    c = lax.axis_index("col")
    all_ref[c] = own_ref[...].astype(BF16)
    for s, ref in enumerate(arrived, 1):
        all_ref[c ^ s] = ref[...]
    n, group, rows = all_ref.shape
    return all_ref[...].reshape(n * group, rows)


def gram_kernel(own_ref, *refs):
    arrived, (gram_ref, all_ref, full_ref) = refs[:-3], refs[-3:]
    rows = all_rows(own_ref, arrived, all_ref)
    full_ref[...] = lax.dot_general(rows, rows, NT, preferred_element_type=F32)
    half = gram_ref.shape[0]
    even = full_ref[pl.ds(0, half, stride=2), :]
    odd = full_ref[pl.ds(1, half, stride=2), :]
    gram_ref[...] = even + turn_lanes(odd)


PANEL = 64
SUB = 8


def eliminate(a, m, top):
    shape = a[0].shape
    here = lax.broadcasted_iota(I32, shape, 0)
    pivots = [None] * len(a)

    def column(rows, lane):
        return jnp.broadcast_to(rows[:, lane : lane + 1], shape)

    for step in range(0, len(a) * SUB, 4):
        own, k = divmod(step, SUB)
        head = [column(a[own], top + step + i) for i in range(4)]
        p, q = head[0][k : k + 1, :], head[2][k + 2 : k + 3, :]
        u, v = head[2][k : k + 1, :], head[3][k : k + 1, :]
        single = 1.0 / p
        det = p * q - (u * u + v * v)
        both = 1.0 / det
        pq, ub, vb, pb = q * both, u * both, v * both, p * both
        second = (here == k + 2) | (here == k + 3)
        last = det * single
        pivot = jnp.where(second, last, jnp.broadcast_to(p, shape))
        pivots[own] = pivot if k == 0 else jnp.where(here < k, pivots[own], pivot)
        rows = [[x[own][k + i : k + i + 1, :] for i in range(4)] for x in (a, m)]
        for g in range(own, len(a)):
            w = head if g == own else [column(a[g], top + step + i) for i in range(4)]
            c = [
                w[0] * pq - w[2] * ub - w[3] * vb,
                w[1] * pq + w[2] * vb - w[3] * ub,
                w[2] * pb - w[0] * ub + w[1] * vb,
                w[3] * pb - w[0] * vb - w[1] * ub,
            ]
            if g == own:
                below = here > k + 3
                c = [jnp.where(below, x, 0.0) for x in c]
                c[0] = jnp.where(second, w[0] * single, c[0])
                c[1] = jnp.where(second, w[1] * single, c[1])
            a[g], m[g] = (
                x[g] - (c[0] * r[0] + c[1] * r[1] + c[2] * r[2] + c[3] * r[3]) for x, r in zip((a, m), rows)
            )
    roots = [lax.rsqrt(x) for x in pivots]
    return [x * r for x, r in zip(a, roots)], [x * r for x, r in zip(m, roots)]


def factor_kernel(nodes, own_ref, all_ref, *refs):
    parts, (out_ref, work_ref, inverse_ref) = refs[:-3], refs[-3:]
    group = own_ref.shape[0]
    order = work_ref.shape[0]
    total = parts[0][...]
    for part in parts[1:]:
        total = total + part[...]
    half = total.shape[0]
    work_ref[pl.ds(0, half, stride=2), :] = total
    work_ref[pl.ds(1, half, stride=2), :] = -turn_lanes(total)
    row_at = lax.broadcasted_iota(I32, (order, order), 0)
    lane_at = lax.broadcasted_iota(I32, (order, order), 1)
    inverse_ref[...] = (row_at == lane_at).astype(F32)
    for top in range(0, order, PANEL):
        tops = range(top, top + PANEL, SUB)
        a, m = ([ref[r : r + SUB, :] for r in tops] for ref in (work_ref, inverse_ref))
        a, m = eliminate(a, m, top)
        a, m = jnp.concatenate(a, axis=0), jnp.concatenate(m, axis=0)
        inverse_ref[top : top + PANEL, :] = m
        rest = top + PANEL
        if rest < order:
            update = lax.dot_general(
                a, jnp.concatenate([a, m], axis=1), TN, precision=lax.Precision.HIGHEST, preferred_element_type=F32
            )
            work_ref[rest:, :] = work_ref[rest:, :] - update[rest:, :order]
            inverse_ref[rest:, :] = inverse_ref[rest:, :] - update[rest:, order:]
    c = lax.axis_index("col")
    mine = inverse_ref[pl.ds(pl.multiple_of(c * group, group), group), :]
    mine = mine * math.sqrt(nodes)
    high = mine.astype(BF16)
    low = (mine - high.astype(F32)).astype(BF16)
    rows = all_ref[...].reshape(order, own_ref.shape[1])
    both = lax.dot_general(
        jnp.concatenate([high, low], axis=0), rows, (((1,), (0,)), ((), ())), preferred_element_type=F32
    )
    own = own_ref[...]
    lost = own - own.astype(BF16).astype(F32)
    own_lanes = (
        lax.broadcasted_iota(I32, (order, group), 0)
        == lax.broadcasted_iota(I32, (order, group), 1) + c * group
    ).astype(BF16)
    square = jnp.dot(high, own_lanes, preferred_element_type=F32).astype(BF16)
    out_ref[...] = (
        both[:group] + both[group:] + jnp.dot(square, lost.astype(BF16), preferred_element_type=F32)
    )


def central(nblk):
    return nblk // 4


def exchange(x):
    nblk = lax.axis_size("blk")
    group = [i ^ central(nblk) for i in range(nblk)]
    return lax.all_to_all(x, "blk", split_axis=0, concat_axis=0, tiled=True, axis_index_groups=[group])


def to_partner(x, axis, mask):
    n = lax.axis_size(axis)
    return lax.ppermute(x, axis, [(i, i ^ mask) for i in range(n)])


def sum_parts(part, nblk):
    wide = 1
    while 4 * wide < nblk:
        part = part + to_partner(part, "blk", wide)
        wide *= 2
    return [part] + [to_partner(part, "blk", s * wide) for s in range(1, nblk // wide)]


def per_device(y_start, tile_real, tile_imag, tile_rows, tile_slots, fetch_pick):
    group, rows = y_start.shape
    tiles, order, _ = tile_real.shape
    rb_dev = rows // order
    nblk = lax.axis_size("blk")
    ncol = lax.axis_size("col")
    near_count = LOC_RB * rb_dev
    wanted = exchange(jnp.broadcast_to(fetch_pick[None], (nblk, 1, nblk)))
    packed, kept, scale, plan = tiles_call(tile_rows, tile_slots, tile_real, tile_imag, rb_dev, near_count)

    out_blocks = pltpu.HBM((nblk, group, order), BF16)
    sent_scratch = [pltpu.VMEM((rb_dev, group, order), BF16), pltpu.SemaphoreType.DMA((nblk,))]
    blocks = pl.pallas_call(
        first_kernel,
        name="first",
        out_shape=out_blocks,
        in_specs=[VMEM, VMEM, SMEM],
        out_specs=ANY,
        scratch_shapes=sent_scratch,
        compiler_params=params(LIMIT),
    )(y_start, scale, wanted)

    def scratch(entries, sources):
        return [
            pltpu.VMEM((entries, 2 * order, order), F8),
            pltpu.VMEM((sources + 1, 2 * group, 2 * order), F8),
            pltpu.VMEM((rb_dev, 2 * group, order), F32),
            pltpu.SemaphoreType.DMA((entries // UNROLL,)),
        ]

    vectors_here = sds((group, rows), F32)
    previous, current = y_start, y_start
    for step in range(STEPS):
        arrived = exchange(blocks)
        base = pl.pallas_call(
            functools.partial(near_kernel, step),
            name="near",
            out_shape=vectors_here,
            in_specs=[SMEM, ANY] + [VMEM] * 3,
            out_specs=VMEM,
            scratch_shapes=scratch(near_count, rb_dev),
            compiler_params=params(LIMIT),
            cost_estimate=pl.CostEstimate(flops=1 << 28, bytes_accessed=1 << 21, transcendentals=0),
        )(in_hbm(plan), in_hbm(packed), scale, current, previous)
        last = step == STEPS - 1
        out = pl.pallas_call(
            functools.partial(step_kernel, step),
            name="step",
            out_shape=[vectors_here] if last else [vectors_here, out_blocks],
            in_specs=[SMEM, SMEM, ANY] + [VMEM] * 4,
            out_specs=[VMEM] if last else [VMEM, ANY],
            scratch_shapes=([] if last else sent_scratch) + scratch(tiles - near_count - KEPT, nblk),
            compiler_params=params(LIMIT),
        )(in_hbm(plan), wanted, in_hbm(packed), pltpu.with_memory_space_constraint(kept, pltpu.VMEM), scale, base, arrived)
        previous, current = current, out[0]
        if not last:
            blocks = out[1]

    rounded = current.astype(BF16)
    if ncol == 4:
        beside, across = to_partner(rounded, "col", 1), to_partner(rounded, "col", 2)
        others = [beside, across, to_partner(across, "col", 1)]
    else:
        others = [to_partner(rounded, "col", s) for s in range(1, ncol)]
    vectors = group * ncol
    part, gathered = pl.pallas_call(
        gram_kernel,
        name="gram",
        out_shape=(sds((vectors // 2, vectors), F32), sds((ncol, group, rows), BF16)),
        in_specs=[VMEM] * (1 + len(others)),
        out_specs=(VMEM, VMEM),
        scratch_shapes=[pltpu.VMEM((vectors, vectors), F32)],
        compiler_params=params(LIMIT),
    )(current, *others)
    parts = sum_parts(part, nblk)
    return pl.pallas_call(
        functools.partial(factor_kernel, rows * nblk),
        name="factor",
        out_shape=sds((group, rows), F32),
        in_specs=[VMEM] * (2 + len(parts)),
        out_specs=VMEM,
        scratch_shapes=[pltpu.VMEM((vectors, vectors), F32)] * 2,
        compiler_params=params(LIMIT),
    )(current, gathered, *parts)


def solution(mesh):
    return jax.shard_map(
        per_device,
        mesh=mesh,
        in_specs=(
            P("col", "blk"),
            P("blk", None, None),
            P("blk", None, None),
            P("blk"),
            P("blk"),
            P("blk", None),
        ),
        out_specs=P("col", "blk"),
        check_vma=False,
    )
```

```python
import functools
import math

import jax
import jax.numpy as jnp
from jax import lax
from jax.experimental import pallas as pl
from jax.experimental.pallas import tpu as pltpu
from jax.sharding import PartitionSpec as P

LOC_RB = 2
STEPS = 4
UNROLL = 4
KEPT = 16
CHUNK = 4
MERGE = 16
TOP = 7.0
FINER = 16.0
SPLIT = float((1 << 20) + 1)
TINY = 1e-30
MIB = 1 << 20
LIMIT = 24

center = 1.25
half_width = 0.75

F32 = jnp.float32
BF16 = jnp.bfloat16
F8 = jnp.float8_e4m3fn
I32 = jnp.int32

VMEM = pl.BlockSpec(memory_space=pltpu.VMEM)
SMEM = pl.BlockSpec(memory_space=pltpu.SMEM)
ANY = pl.BlockSpec(memory_space=pl.ANY)

NT = (((1,), (1,)), ((), ()))
TN = (((0,), (0,)), ((), ()))


def sds(shape, dtype):
    return jax.ShapeDtypeStruct(shape, dtype)


def params(limit):
    return pltpu.CompilerParams(vmem_limit_bytes=limit * MIB)


def turn_rows(values):
    rows = values.shape[0]
    even = lax.broadcasted_iota(I32, values.shape, 0) % 2 == 0
    below = pltpu.roll(values, rows - 1, 0)
    above = pltpu.roll(values, 1, 0)
    return jnp.where(even, -below, above)


def turn_lanes(values):
    lanes = values.shape[1]
    even = lax.broadcasted_iota(I32, values.shape, 1) % 2 == 0
    after = pltpu.roll(values, lanes - 1, 1)
    before = pltpu.roll(values, 1, 1)
    return jnp.where(even, after, -before)


def tiles_kernel(
    near_count,
    rows_hbm,
    slots_hbm,
    real_hbm,
    imag_hbm,
    packed_hbm,
    kept_ref,
    scale_ref,
    plan_hbm,
    rows_ref,
    slots_ref,
    plan_ref,
    both_ref,
    small_ref,
    present_ref,
    table_ref,
    back_ref,
    done_ref,
    in_sems,
    out_sems,
    list_sems,
):
    kept = kept_ref.shape[0]
    tiles, order, _ = both_ref.shape
    rb_dev = present_ref.shape[0]
    slots = rb_dev + lax.axis_size("blk")
    chunks = tiles // CHUNK

    def copies(c):
        at = pl.ds(c * CHUNK, CHUNK)
        return (
            pltpu.make_async_copy(real_hbm.at[at], both_ref.at[at, :, 0:order], in_sems.at[c, 0]),
            pltpu.make_async_copy(imag_hbm.at[at], both_ref.at[at, :, order : 2 * order], in_sems.at[c, 1]),
        )

    def leave(e):
        return pltpu.make_async_copy(small_ref.at[e], packed_hbm.at[e], out_sems.at[e])

    lists = (
        pltpu.make_async_copy(rows_hbm, rows_ref, list_sems.at[0]),
        pltpu.make_async_copy(slots_hbm, slots_ref, list_sems.at[1]),
    )
    for copy in lists:
        copy.start()
    for c in range(chunks):
        for copy in copies(c):
            copy.start()

    def clear(row, _):
        for slot in range(slots):
            table_ref[row * slots + slot] = -1
        return _

    lax.fori_loop(0, rb_dev, clear, 0)
    present_ref[...] = jnp.zeros_like(present_ref)
    for copy in lists:
        copy.wait()

    def link(c, carry):
        for t in [c * CHUNK + j for j in range(CHUNK)]:
            key = rows_ref[t] * slots + slots_ref[t]
            seen = table_ref[key]
            before = seen & 255
            length = seen >> 8
            joins = (seen >= 0) & (length < MERGE)
            back_ref[t] = jnp.where(joins, before, -1)
            done_ref[t] = 1
            done_ref[jnp.where(joins, before, tiles)] = 0
            table_ref[key] = t | (jnp.where(joins, length + 1, 1) << 8)
        return carry

    lax.fori_loop(near_count // CHUNK, chunks, link, 0)

    def fill(ref, e, t):
        for at in [slice(q, q + 128) for q in range(0, 2 * order, 128)]:
            ref[e, at] = jnp.zeros((128, order), F8) if t is None else both_ref[t, :, at].astype(F8).T

    def put(e, t):
        @pl.when(e < kept)
        def _():
            fill(kept_ref, e, t)

        @pl.when(e >= kept)
        def _():
            fill(small_ref, e - kept, t)
            leave(e - kept).start()

    def count(t):
        row = rows_ref[t]
        for at in [slice(q, q + order // 4) for q in range(0, order, order // 4)]:
            counted = both_ref[t, at, :order] + jnp.abs(both_ref[t, at, order:])
            present_ref[row, at] = present_ref[row, at] + counted

    def one(t, listed):
        count(t)
        closes = done_ref[t]

        @pl.when(closes == 1)
        def _():
            def add(prior):
                both_ref[t] = both_ref[t] + both_ref[prior]
                return back_ref[prior]

            lax.while_loop(lambda prior: prior >= 0, add, back_ref[t])
            put(listed, t)
            place = (slots_ref[t] - rb_dev) ^ central(slots - rb_dev)
            plan_ref[listed] = rows_ref[t] | (place << 8)

        return listed + closes

    def near_chunk(c, carry):
        for copy in copies(c):
            copy.wait()
        for j in range(CHUNK):
            count(c * CHUNK + j)
        return carry

    def far_chunk(c, listed):
        for copy in copies(c):
            copy.wait()
        for j in range(CHUNK):
            listed = one(c * CHUNK + j, listed)
        return listed

    lax.fori_loop(0, near_count // CHUNK, near_chunk, 0)
    listed = lax.fori_loop(near_count // CHUNK, chunks, far_chunk, 0)
    short = (UNROLL - listed % UNROLL) % UNROLL
    for j in range(UNROLL - 1):

        @pl.when(j < short)
        def _():
            put(listed + j, None)
            plan_ref[listed + j] = (slots - rb_dev) << 8

    every = listed + short
    plan_ref[tiles] = every // UNROLL
    plan_copy = pltpu.make_async_copy(plan_ref, plan_hbm, list_sems.at[2])
    plan_copy.start()

    ones = jnp.ones((8, order), BF16)
    for r in range(rb_dev):
        degree = lax.dot_general(ones, present_ref[r], NT, preferred_element_type=F32)
        scale_ref[:, r * order : (r + 1) * order] = 1.0 / jnp.sqrt(jnp.maximum(degree, 1.0))

    def left(e, _):
        leave(e - kept).wait()
        return _

    lax.fori_loop(kept, every, left, 0)
    plan_copy.wait()


def in_hbm(x):
    return pltpu.with_memory_space_constraint(x, pltpu.HBM)


def tiles_call(rows, slots, real, imag, rb_dev, near_count):
    tiles, order, _ = real.shape
    nblk = lax.axis_size("blk")
    return pl.pallas_call(
        functools.partial(tiles_kernel, near_count),
        name="tiles",
        out_shape=(
            pltpu.HBM((tiles - near_count - KEPT, 2 * order, order), F8),
            pltpu.VMEM((KEPT, 2 * order, order), F8),
            sds((8, rb_dev * order), F32),
            pltpu.HBM((tiles + 32,), I32),
        ),
        in_specs=[ANY] * 4,
        out_specs=(ANY, VMEM, VMEM, ANY),
        scratch_shapes=[
            pltpu.SMEM((tiles,), I32),
            pltpu.SMEM((tiles,), I32),
            pltpu.SMEM((tiles + 32,), I32),
            pltpu.VMEM((tiles, order, 2 * order), BF16),
            pltpu.VMEM((tiles - near_count - KEPT, 2 * order, order), F8),
            pltpu.VMEM((rb_dev, order, order), BF16),
            pltpu.SMEM((rb_dev * (rb_dev + nblk),), I32),
            pltpu.SMEM((tiles,), I32),
            pltpu.SMEM((tiles + 1,), I32),
            pltpu.SemaphoreType.DMA((tiles // CHUNK, 2)),
            pltpu.SemaphoreType.DMA((tiles,)),
            pltpu.SemaphoreType.DMA((3,)),
        ],
        compiler_params=params(48),
        cost_estimate=pl.CostEstimate(flops=1 << 28, bytes_accessed=2 * real.size * 2, transcendentals=0),
    )(in_hbm(rows), in_hbm(slots), in_hbm(real), in_hbm(imag))


def rounded_block(field, scale_ref, r, order):
    at = slice(r * order, (r + 1) * order)
    return (field[:, at] * scale_ref[0:1, at]).astype(BF16)


def send_picked(wanted_ref, sent_ref, out_hbm, sems):
    me = lax.axis_index("blk")
    copies = [
        pltpu.make_async_copy(sent_ref.at[wanted_ref[i, 0, me]], out_hbm.at[i], sems.at[i])
        for i in range(out_hbm.shape[0])
    ]
    for copy in copies:
        copy.start()
    for copy in copies:
        copy.wait()


def first_kernel(y_ref, scale_ref, wanted_ref, out_hbm, sent_ref, out_sems):
    for r in range(sent_ref.shape[0]):
        sent_ref[r] = rounded_block(y_ref, scale_ref, r, sent_ref.shape[2])
    send_picked(wanted_ref, sent_ref, out_hbm, out_sems)


def load_groups(packed_hbm, tiles_ref, sems, count):
    def copy(g):
        at = pl.ds(g * UNROLL, UNROLL)
        return pltpu.make_async_copy(packed_hbm.at[at], tiles_ref.at[at], sems.at[g])

    def begin(g, _):
        copy(g).start()
        return _

    lax.fori_loop(0, count, begin, 0)
    return copy


def split_sources(count, source, x_ref):
    _, rows, width = x_ref.shape
    group, order = rows // 2, width // 2
    most = jnp.zeros((group, order), F32)
    for p in range(count):
        most = jnp.maximum(most, jnp.abs(source(p).astype(F32)))
    most = jnp.broadcast_to(jnp.max(most, axis=1, keepdims=True), (group, 128))
    most = jnp.maximum(jnp.maximum(most, jnp.abs(turn_rows(most))), TINY)
    power = jnp.floor(jnp.log2(most))
    size = jnp.exp2(power - TOP)
    inverse = jnp.exp2(TOP - power)[:, 0:1]
    for p in range(count):
        scaled = source(p).astype(F32) * inverse
        far = scaled * SPLIT
        high = far - (far - scaled)
        low = (scaled - high) * FINER
        for k, part in enumerate((high, low)):
            at = slice(k * group, (k + 1) * group)
            x_ref[p, at, :order] = part.astype(F8)
            x_ref[p, at, order:] = turn_rows(part).astype(F8)
    x_ref[count] = jnp.zeros_like(x_ref[count])
    return size[:, 0:1]


def multiply(plan_ref, lo, hi, tile, load, acc_ref):
    def group(g, _):
        done = []
        for j in range(UNROLL):
            code = plan_ref[g * UNROLL + j]
            product = jnp.dot(load(code >> 8), tile(g, j), preferred_element_type=F32)
            done.append((code & 255, product))
        for row, product in done:
            acc_ref[row] = acc_ref[row] + product
        return _

    lax.fori_loop(lo, hi, group, 0)


def collect(acc, size):
    group = size.shape[0]
    return (acc[:group] + acc[group:] * (1.0 / FINER)) * size


def near_kernel(
    step, rows_ref, slots_ref, real_hbm, imag_hbm, scale_ref, now_ref, before_ref, base_ref, tiles_ref, x_ref, acc_ref, sems
):
    rb_dev, _, order = x_ref.shape
    groups = sems.shape[0]

    def copies(g):
        at = pl.ds(g * UNROLL, UNROLL)
        return [
            pltpu.make_async_copy(hbm.at[at], tiles_ref.at[i, at], sems.at[g, i])
            for i, hbm in enumerate((real_hbm, imag_hbm))
        ]

    for g in range(groups):
        for copy in copies(g):
            copy.start()
    acc_ref[...] = jnp.zeros_like(acc_ref)
    for r in range(rb_dev):
        x_ref[r] = rounded_block(now_ref, scale_ref, r, order)

    def group(g, _):
        for copy in copies(g):
            copy.wait()
        done = []
        for t in [g * UNROLL + j for j in range(UNROLL)]:
            x = x_ref[slots_ref[t]]
            done.append([lax.dot_general(x, tiles_ref[i, t], NT, preferred_element_type=F32) for i in range(2)])
        for j, products in enumerate(done):
            row = rows_ref[g * UNROLL + j]
            for i, product in enumerate(products):
                acc_ref[i, row] = acc_ref[i, row] + product
        return _

    lax.fori_loop(0, groups, group, 0)
    for r in range(rb_dev):
        at = slice(r * order, (r + 1) * order)
        applied = scale_ref[0:1, at] * (acc_ref[0, r] + turn_rows(acc_ref[1, r]))
        moved = ((1.0 - center) * now_ref[:, at] - applied) / half_width
        base_ref[:, at] = moved if step == 0 else 2.0 * moved - before_ref[:, at]


def step_kernel(step, plan_ref, wanted_ref, packed_hbm, kept_ref, scale_ref, base_ref, arrived_ref, *refs):
    last = step == STEPS - 1
    next_ref = refs[0]
    if not last:
        out_hbm, sent_ref, out_sems = refs[1:4]
    tiles_ref, x_ref, acc_ref, sems = refs[-4:]
    rb_dev, _, order = acc_ref.shape
    stay = KEPT // UNROLL
    groups = plan_ref[plan_ref.shape[0] - 32]
    copy = load_groups(packed_hbm, tiles_ref, sems, groups - stay)
    acc_ref[...] = jnp.zeros_like(acc_ref)
    size = split_sources(arrived_ref.shape[0], lambda p: arrived_ref[p], x_ref)
    size = size * ((1.0 if step == 0 else 2.0) / half_width)

    def loaded(g, j):
        if j == 0:
            copy(g - stay).wait()
        return tiles_ref[(g - stay) * UNROLL + j]

    def load(place):
        return x_ref[place]

    multiply(plan_ref, 0, jnp.minimum(stay, groups), lambda g, j: kept_ref[g * UNROLL + j], load, acc_ref)
    multiply(plan_ref, stay, groups, loaded, load, acc_ref)
    for r in range(rb_dev):
        at = slice(r * order, (r + 1) * order)
        scale = scale_ref[0:1, at]
        following = base_ref[:, at] - scale * collect(acc_ref[r], size)
        next_ref[:, at] = following
        if not last:
            sent_ref[r] = (following * scale).astype(BF16)
    if not last:
        send_picked(wanted_ref, sent_ref, out_hbm, out_sems)


def all_rows(own_ref, arrived, all_ref):
    c = lax.axis_index("col")
    all_ref[c] = own_ref[...].astype(BF16)
    for s, ref in enumerate(arrived, 1):
        all_ref[c ^ s] = ref[...]
    n, group, rows = all_ref.shape
    return all_ref[...].reshape(n * group, rows)


def gram_kernel(own_ref, *refs):
    arrived, (gram_ref, all_ref, full_ref) = refs[:-3], refs[-3:]
    rows = all_rows(own_ref, arrived, all_ref)
    full_ref[...] = lax.dot_general(rows, rows, NT, preferred_element_type=F32)
    half = gram_ref.shape[0]
    even = full_ref[pl.ds(0, half, stride=2), :]
    odd = full_ref[pl.ds(1, half, stride=2), :]
    gram_ref[...] = even + turn_lanes(odd)


PANEL = 64
PIECES = 4
SUB = 8


def eliminate(a, m, top):
    shape = a[0].shape
    here = lax.broadcasted_iota(I32, shape, 0)
    pivots = [None] * len(a)

    def column(rows, lane):
        return jnp.broadcast_to(rows[:, lane : lane + 1], shape)

    for step in range(0, len(a) * SUB, 4):
        own, k = divmod(step, SUB)
        head = [column(a[own], top + step + i) for i in range(4)]
        p, q = head[0][k : k + 1, :], head[2][k + 2 : k + 3, :]
        u, v = head[2][k : k + 1, :], head[3][k : k + 1, :]
        single = 1.0 / p
        det = p * q - (u * u + v * v)
        both = 1.0 / det
        pq, ub, vb, pb = q * both, u * both, v * both, p * both
        second = (here == k + 2) | (here == k + 3)
        last = det * single
        pivot = jnp.where(second, last, jnp.broadcast_to(p, shape))
        pivots[own] = pivot if k == 0 else jnp.where(here < k, pivots[own], pivot)
        rows = [[x[own][k + i : k + i + 1, :] for i in range(4)] for x in (a, m)]
        for g in range(own, len(a)):
            w = head if g == own else [column(a[g], top + step + i) for i in range(4)]
            c = [
                w[0] * pq - w[2] * ub - w[3] * vb,
                w[1] * pq + w[2] * vb - w[3] * ub,
                w[2] * pb - w[0] * ub + w[1] * vb,
                w[3] * pb - w[0] * vb - w[1] * ub,
            ]
            if g == own:
                below = here > k + 3
                c = [jnp.where(below, x, 0.0) for x in c]
                c[0] = jnp.where(second, w[0] * single, c[0])
                c[1] = jnp.where(second, w[1] * single, c[1])
            a[g], m[g] = (
                x[g] - (c[0] * r[0] + c[1] * r[1] + c[2] * r[2] + c[3] * r[3]) for x, r in zip((a, m), rows)
            )
    roots = [lax.rsqrt(x) for x in pivots]
    return [x * r for x, r in zip(a, roots)], [x * r for x, r in zip(m, roots)]


def factor_kernel(nodes, own_ref, all_ref, *refs):
    parts, (out_hbm, work_ref, inverse_ref, piece_ref, sems) = refs[:-5], refs[-5:]
    group = own_ref.shape[0]
    order = work_ref.shape[0]
    total = parts[0][...]
    for part in parts[1:]:
        total = total + part[...]
    half = total.shape[0]
    work_ref[pl.ds(0, half, stride=2), :] = total
    work_ref[pl.ds(1, half, stride=2), :] = -turn_lanes(total)
    row_at = lax.broadcasted_iota(I32, (order, order), 0)
    lane_at = lax.broadcasted_iota(I32, (order, order), 1)
    inverse_ref[...] = (row_at == lane_at).astype(F32)
    for top in range(0, order, PANEL):
        tops = range(top, top + PANEL, SUB)
        a, m = ([ref[r : r + SUB, :] for r in tops] for ref in (work_ref, inverse_ref))
        a, m = eliminate(a, m, top)
        a, m = jnp.concatenate(a, axis=0), jnp.concatenate(m, axis=0)
        inverse_ref[top : top + PANEL, :] = m
        rest = top + PANEL
        if rest < order:
            update = lax.dot_general(
                a, jnp.concatenate([a, m], axis=1), TN, precision=lax.Precision.HIGHEST, preferred_element_type=F32
            )
            work_ref[rest:, :] = work_ref[rest:, :] - update[rest:, :order]
            inverse_ref[rest:, :] = inverse_ref[rest:, :] - update[rest:, order:]
    c = lax.axis_index("col")
    mine = inverse_ref[pl.ds(pl.multiple_of(c * group, group), group), :]
    mine = mine * math.sqrt(nodes)
    high = mine.astype(BF16)
    low = (mine - high.astype(F32)).astype(BF16)
    own_lanes = (
        lax.broadcasted_iota(I32, (order, group), 0)
        == lax.broadcasted_iota(I32, (order, group), 1) + c * group
    ).astype(BF16)
    square = jnp.dot(high, own_lanes, preferred_element_type=F32).astype(BF16)
    left = jnp.concatenate([high, low], axis=0)
    width = own_ref.shape[1] // PIECES
    copies = []
    for i in range(PIECES):
        at = slice(i * width, (i + 1) * width)
        rows = all_ref[:, :, at].reshape(order, width)
        both = jnp.dot(left, rows, preferred_element_type=F32)
        own = own_ref[:, at]
        lost = (own - own.astype(BF16).astype(F32)).astype(BF16)
        piece_ref[i] = both[:group] + both[group:] + jnp.dot(square, lost, preferred_element_type=F32)
        copies.append(pltpu.make_async_copy(piece_ref.at[i], out_hbm.at[:, at], sems.at[i]))
        copies[-1].start()
    for copy in copies:
        copy.wait()


def central(nblk):
    return nblk // 4


def exchange(x):
    nblk = lax.axis_size("blk")
    group = [i ^ central(nblk) for i in range(nblk)]
    return lax.all_to_all(x, "blk", split_axis=0, concat_axis=0, tiled=True, axis_index_groups=[group])


def to_partner(x, axis, mask):
    n = lax.axis_size(axis)
    return lax.ppermute(x, axis, [(i, i ^ mask) for i in range(n)])


def sum_parts(part, nblk):
    wide = 1
    while 4 * wide < nblk:
        part = part + to_partner(part, "blk", wide)
        wide *= 2
    return [part] + [to_partner(part, "blk", s * wide) for s in range(1, nblk // wide)]


def per_device(y_start, tile_real, tile_imag, tile_rows, tile_slots, fetch_pick):
    group, rows = y_start.shape
    tiles, order, _ = tile_real.shape
    rb_dev = rows // order
    nblk = lax.axis_size("blk")
    ncol = lax.axis_size("col")
    near_count = LOC_RB * rb_dev
    wanted = exchange(jnp.broadcast_to(fetch_pick[None], (nblk, 1, nblk)))
    packed, kept, scale, plan = tiles_call(tile_rows, tile_slots, tile_real, tile_imag, rb_dev, near_count)

    out_blocks = pltpu.HBM((nblk, group, order), BF16)
    sent_scratch = [pltpu.VMEM((rb_dev, group, order), BF16), pltpu.SemaphoreType.DMA((nblk,))]
    blocks = pl.pallas_call(
        first_kernel,
        name="first",
        out_shape=out_blocks,
        in_specs=[VMEM, VMEM, SMEM],
        out_specs=ANY,
        scratch_shapes=sent_scratch,
        compiler_params=params(LIMIT),
    )(y_start, scale, wanted)

    vectors_here = sds((group, rows), F32)
    previous, current = y_start, y_start
    for step in range(STEPS):
        arrived = exchange(blocks)
        base = pl.pallas_call(
            functools.partial(near_kernel, step),
            name="near",
            out_shape=vectors_here,
            in_specs=[SMEM, SMEM, ANY, ANY] + [VMEM] * 3,
            out_specs=VMEM,
            scratch_shapes=[
                pltpu.VMEM((2, near_count, order, order), BF16),
                pltpu.VMEM((rb_dev, group, order), BF16),
                pltpu.VMEM((2, rb_dev, group, order), F32),
                pltpu.SemaphoreType.DMA((near_count // UNROLL, 2)),
            ],
            compiler_params=params(LIMIT),
            cost_estimate=pl.CostEstimate(flops=1 << 28, bytes_accessed=1 << 21, transcendentals=0),
        )(in_hbm(tile_rows), in_hbm(tile_slots), in_hbm(tile_real), in_hbm(tile_imag), scale, current, previous)
        last = step == STEPS - 1
        out = pl.pallas_call(
            functools.partial(step_kernel, step),
            name="step",
            out_shape=[vectors_here] if last else [vectors_here, out_blocks],
            in_specs=[SMEM, SMEM, ANY] + [VMEM] * 4,
            out_specs=[VMEM] if last else [VMEM, ANY],
            scratch_shapes=([] if last else sent_scratch)
            + [
                pltpu.VMEM(packed.shape, F8),
                pltpu.VMEM((nblk + 1, 2 * group, 2 * order), F8),
                pltpu.VMEM((rb_dev, 2 * group, order), F32),
                pltpu.SemaphoreType.DMA((packed.shape[0] // UNROLL,)),
            ],
            compiler_params=params(LIMIT),
        )(in_hbm(plan), wanted, in_hbm(packed), pltpu.with_memory_space_constraint(kept, pltpu.VMEM), scale, base, arrived)
        previous, current = current, out[0]
        if not last:
            blocks = out[1]

    rounded = current.astype(BF16)
    if ncol == 4:
        beside, across = to_partner(rounded, "col", 1), to_partner(rounded, "col", 2)
        others = [beside, across, to_partner(across, "col", 1)]
    else:
        others = [to_partner(rounded, "col", s) for s in range(1, ncol)]
    vectors = group * ncol
    part, gathered = pl.pallas_call(
        gram_kernel,
        name="gram",
        out_shape=(sds((vectors // 2, vectors), F32), sds((ncol, group, rows), BF16)),
        in_specs=[VMEM] * (1 + len(others)),
        out_specs=(VMEM, VMEM),
        scratch_shapes=[pltpu.VMEM((vectors, vectors), F32)],
        compiler_params=params(LIMIT),
    )(current, *others)
    parts = sum_parts(part, nblk)
    return pl.pallas_call(
        functools.partial(factor_kernel, rows * nblk),
        name="factor",
        out_shape=pltpu.HBM((group, rows), F32),
        in_specs=[VMEM] * (2 + len(parts)),
        out_specs=ANY,
        scratch_shapes=[pltpu.VMEM((vectors, vectors), F32)] * 2
        + [pltpu.VMEM((PIECES, group, rows // PIECES), F32), pltpu.SemaphoreType.DMA((PIECES,))],
        compiler_params=params(LIMIT),
    )(current, gathered, *parts)


def solution(mesh):
    return jax.shard_map(
        per_device,
        mesh=mesh,
        in_specs=(
            P("col", "blk"),
            P("blk", None, None),
            P("blk", None, None),
            P("blk"),
            P("blk"),
            P("blk", None),
        ),
        out_specs=P("col", "blk"),
        check_vma=False,
    )
```

```python
import functools
import math

import jax
import jax.numpy as jnp
from jax import lax
from jax.experimental import pallas as pl
from jax.experimental.pallas import tpu as pltpu
from jax.sharding import PartitionSpec as P

LOC_RB = 2
STEPS = 4
UNROLL = 8
NEAR_UNROLL = 4
KEPT = 16
CHUNK = 4
MERGE = 16
TOP = 7.0
FINER = 16.0
SPLIT = float((1 << 20) + 1)
TINY = 1e-30
MIB = 1 << 20
LIMIT = 24

center = 1.25
half_width = 0.75

F32 = jnp.float32
BF16 = jnp.bfloat16
F8 = jnp.float8_e4m3fn
I32 = jnp.int32

VMEM = pl.BlockSpec(memory_space=pltpu.VMEM)
SMEM = pl.BlockSpec(memory_space=pltpu.SMEM)
ANY = pl.BlockSpec(memory_space=pl.ANY)

NT = (((1,), (1,)), ((), ()))
TN = (((0,), (0,)), ((), ()))


def sds(shape, dtype):
    return jax.ShapeDtypeStruct(shape, dtype)


def params(limit):
    return pltpu.CompilerParams(vmem_limit_bytes=limit * MIB)


def turn_rows(values):
    rows = values.shape[0]
    even = lax.broadcasted_iota(I32, values.shape, 0) % 2 == 0
    below = pltpu.roll(values, rows - 1, 0)
    above = pltpu.roll(values, 1, 0)
    return jnp.where(even, -below, above)


def turn_lanes(values):
    lanes = values.shape[1]
    even = lax.broadcasted_iota(I32, values.shape, 1) % 2 == 0
    after = pltpu.roll(values, lanes - 1, 1)
    before = pltpu.roll(values, 1, 1)
    return jnp.where(even, after, -before)


def tiles_kernel(
    near_count,
    rows_hbm,
    slots_hbm,
    real_hbm,
    imag_hbm,
    packed_hbm,
    kept_ref,
    scale_ref,
    plan_hbm,
    rows_ref,
    slots_ref,
    plan_ref,
    both_ref,
    small_ref,
    present_ref,
    table_ref,
    back_ref,
    done_ref,
    in_sems,
    out_sems,
    list_sems,
):
    kept = kept_ref.shape[0]
    tiles, order, _ = both_ref.shape
    rb_dev = present_ref.shape[0]
    slots = rb_dev + lax.axis_size("blk")
    chunks = tiles // CHUNK

    def copies(c):
        at = pl.ds(c * CHUNK, CHUNK)
        return (
            pltpu.make_async_copy(real_hbm.at[at], both_ref.at[at, :, 0:order], in_sems.at[c, 0]),
            pltpu.make_async_copy(imag_hbm.at[at], both_ref.at[at, :, order : 2 * order], in_sems.at[c, 1]),
        )

    def leave(e):
        return pltpu.make_async_copy(small_ref.at[e], packed_hbm.at[e], out_sems.at[e])

    lists = (
        pltpu.make_async_copy(rows_hbm, rows_ref, list_sems.at[0]),
        pltpu.make_async_copy(slots_hbm, slots_ref, list_sems.at[1]),
    )
    for copy in lists:
        copy.start()
    for c in range(chunks):
        for copy in copies(c):
            copy.start()

    def clear(row, _):
        for slot in range(slots):
            table_ref[row * slots + slot] = -1
        return _

    lax.fori_loop(0, rb_dev, clear, 0)
    present_ref[...] = jnp.zeros_like(present_ref)
    for copy in lists:
        copy.wait()

    def link(c, carry):
        for t in [c * CHUNK + j for j in range(CHUNK)]:
            key = rows_ref[t] * slots + slots_ref[t]
            seen = table_ref[key]
            before = seen & 255
            length = seen >> 8
            joins = (seen >= 0) & (length < MERGE)
            back_ref[t] = jnp.where(joins, before, -1)
            done_ref[t] = 1
            done_ref[jnp.where(joins, before, tiles)] = 0
            table_ref[key] = t | (jnp.where(joins, length + 1, 1) << 8)
        return carry

    lax.fori_loop(near_count // CHUNK, chunks, link, 0)

    def fill(ref, e, t):
        for at in [slice(q, q + 128) for q in range(0, 2 * order, 128)]:
            ref[e, at] = jnp.zeros((128, order), F8) if t is None else both_ref[t, :, at].astype(F8).T

    def put(e, t):
        @pl.when(e < kept)
        def _():
            fill(kept_ref, e, t)

        @pl.when(e >= kept)
        def _():
            fill(small_ref, e - kept, t)
            leave(e - kept).start()

    def count(t):
        row = rows_ref[t]
        for at in [slice(q, q + order // 4) for q in range(0, order, order // 4)]:
            counted = both_ref[t, at, :order] + jnp.abs(both_ref[t, at, order:])
            present_ref[row, at] = present_ref[row, at] + counted

    def one(t, listed):
        count(t)
        closes = done_ref[t]

        @pl.when(closes == 1)
        def _():
            def add(prior):
                both_ref[t] = both_ref[t] + both_ref[prior]
                return back_ref[prior]

            lax.while_loop(lambda prior: prior >= 0, add, back_ref[t])
            put(listed, t)
            place = (slots_ref[t] - rb_dev) ^ central(slots - rb_dev)
            plan_ref[listed] = rows_ref[t] | (place << 8)

        return listed + closes

    def near_chunk(c, carry):
        for copy in copies(c):
            copy.wait()
        for j in range(CHUNK):
            count(c * CHUNK + j)
        return carry

    def far_chunk(c, listed):
        for copy in copies(c):
            copy.wait()
        for j in range(CHUNK):
            listed = one(c * CHUNK + j, listed)
        return listed

    lax.fori_loop(0, near_count // CHUNK, near_chunk, 0)
    listed = lax.fori_loop(near_count // CHUNK, chunks, far_chunk, 0)
    short = (UNROLL - listed % UNROLL) % UNROLL
    for j in range(UNROLL - 1):

        @pl.when(j < short)
        def _():
            put(listed + j, None)
            plan_ref[listed + j] = (slots - rb_dev) << 8

    every = listed + short
    plan_ref[tiles] = every // UNROLL
    plan_copy = pltpu.make_async_copy(plan_ref, plan_hbm, list_sems.at[2])
    plan_copy.start()

    ones = jnp.ones((8, order), BF16)
    for r in range(rb_dev):
        degree = lax.dot_general(ones, present_ref[r], NT, preferred_element_type=F32)
        scale_ref[:, r * order : (r + 1) * order] = 1.0 / jnp.sqrt(jnp.maximum(degree, 1.0))

    def left(e, _):
        leave(e - kept).wait()
        return _

    lax.fori_loop(kept, every, left, 0)
    plan_copy.wait()


def in_hbm(x):
    return pltpu.with_memory_space_constraint(x, pltpu.HBM)


def tiles_call(rows, slots, real, imag, rb_dev, near_count):
    tiles, order, _ = real.shape
    nblk = lax.axis_size("blk")
    return pl.pallas_call(
        functools.partial(tiles_kernel, near_count),
        name="tiles",
        out_shape=(
            pltpu.HBM((tiles - near_count - KEPT, 2 * order, order), F8),
            pltpu.VMEM((KEPT, 2 * order, order), F8),
            sds((8, rb_dev * order), F32),
            pltpu.HBM((tiles + 32,), I32),
        ),
        in_specs=[ANY] * 4,
        out_specs=(ANY, VMEM, VMEM, ANY),
        scratch_shapes=[
            pltpu.SMEM((tiles,), I32),
            pltpu.SMEM((tiles,), I32),
            pltpu.SMEM((tiles + 32,), I32),
            pltpu.VMEM((tiles, order, 2 * order), BF16),
            pltpu.VMEM((tiles - near_count - KEPT, 2 * order, order), F8),
            pltpu.VMEM((rb_dev, order, order), BF16),
            pltpu.SMEM((rb_dev * (rb_dev + nblk),), I32),
            pltpu.SMEM((tiles,), I32),
            pltpu.SMEM((tiles + 1,), I32),
            pltpu.SemaphoreType.DMA((tiles // CHUNK, 2)),
            pltpu.SemaphoreType.DMA((tiles,)),
            pltpu.SemaphoreType.DMA((3,)),
        ],
        compiler_params=params(48),
        cost_estimate=pl.CostEstimate(flops=1 << 28, bytes_accessed=2 * real.size * 2, transcendentals=0),
    )(in_hbm(rows), in_hbm(slots), in_hbm(real), in_hbm(imag))


def rounded_block(field, scale_ref, r, order):
    at = slice(r * order, (r + 1) * order)
    return (field[:, at] * scale_ref[0:1, at]).astype(BF16)


def send_picked(wanted_ref, sent_ref, out_hbm, sems):
    me = lax.axis_index("blk")
    copies = [
        pltpu.make_async_copy(sent_ref.at[wanted_ref[i, 0, me]], out_hbm.at[i], sems.at[i])
        for i in range(out_hbm.shape[0])
    ]
    for copy in copies:
        copy.start()
    for copy in copies:
        copy.wait()


def first_kernel(y_ref, scale_ref, wanted_ref, out_hbm, sent_ref, out_sems):
    for r in range(sent_ref.shape[0]):
        sent_ref[r] = rounded_block(y_ref, scale_ref, r, sent_ref.shape[2])
    send_picked(wanted_ref, sent_ref, out_hbm, out_sems)


def load_groups(packed_hbm, tiles_ref, sems, count):
    def copy(g):
        at = pl.ds(g * UNROLL, UNROLL)
        return pltpu.make_async_copy(packed_hbm.at[at], tiles_ref.at[at], sems.at[g])

    def begin(g, _):
        copy(g).start()
        return _

    lax.fori_loop(0, count, begin, 0)
    return copy


def split_sources(count, source, x_ref):
    _, rows, width = x_ref.shape
    group, order = rows // 2, width // 2
    most = jnp.zeros((group, order), F32)
    for p in range(count):
        most = jnp.maximum(most, jnp.abs(source(p).astype(F32)))
    most = jnp.broadcast_to(jnp.max(most, axis=1, keepdims=True), (group, 128))
    most = jnp.maximum(jnp.maximum(most, jnp.abs(turn_rows(most))), TINY)
    power = jnp.floor(jnp.log2(most))
    size = jnp.exp2(power - TOP)
    inverse = jnp.exp2(TOP - power)[:, 0:1]
    for p in range(count):
        scaled = source(p).astype(F32) * inverse
        far = scaled * SPLIT
        high = far - (far - scaled)
        low = (scaled - high) * FINER
        for k, part in enumerate((high, low)):
            at = slice(k * group, (k + 1) * group)
            x_ref[p, at, :order] = part.astype(F8)
            x_ref[p, at, order:] = turn_rows(part).astype(F8)
    x_ref[count] = jnp.zeros_like(x_ref[count])
    return size[:, 0:1]


def multiply(plan_ref, lo, hi, tile, load, acc_ref):
    def group(g, _):
        done = []
        for j in range(UNROLL):
            code = plan_ref[g * UNROLL + j]
            product = jnp.dot(load(code >> 8), tile(g, j), preferred_element_type=F32)
            done.append((code & 255, product))
        for row, product in done:
            acc_ref[row] = acc_ref[row] + product
        return _

    lax.fori_loop(lo, hi, group, 0)


def collect(acc, size):
    group = size.shape[0]
    return (acc[:group] + acc[group:] * (1.0 / FINER)) * size


def near_kernel(
    step, rows_ref, slots_ref, real_hbm, imag_hbm, scale_ref, now_ref, before_ref, base_ref, tiles_ref, x_ref, acc_ref, sems
):
    rb_dev, _, order = x_ref.shape
    groups = sems.shape[0]

    def copies(g):
        at = pl.ds(g * NEAR_UNROLL, NEAR_UNROLL)
        return [
            pltpu.make_async_copy(hbm.at[at], tiles_ref.at[i, at], sems.at[g, i])
            for i, hbm in enumerate((real_hbm, imag_hbm))
        ]

    for g in range(groups):
        for copy in copies(g):
            copy.start()
    acc_ref[...] = jnp.zeros_like(acc_ref)
    for r in range(rb_dev):
        x_ref[r] = rounded_block(now_ref, scale_ref, r, order)

    def group(g, _):
        for copy in copies(g):
            copy.wait()
        done = []
        for t in [g * NEAR_UNROLL + j for j in range(NEAR_UNROLL)]:
            x = x_ref[slots_ref[t]]
            done.append([lax.dot_general(x, tiles_ref[i, t], NT, preferred_element_type=F32) for i in range(2)])
        for j, products in enumerate(done):
            row = rows_ref[g * NEAR_UNROLL + j]
            for i, product in enumerate(products):
                acc_ref[i, row] = acc_ref[i, row] + product
        return _

    lax.fori_loop(0, groups, group, 0)
    for r in range(rb_dev):
        at = slice(r * order, (r + 1) * order)
        applied = scale_ref[0:1, at] * (acc_ref[0, r] + turn_rows(acc_ref[1, r]))
        moved = ((1.0 - center) * now_ref[:, at] - applied) / half_width
        base_ref[:, at] = moved if step == 0 else 2.0 * moved - before_ref[:, at]


def step_kernel(step, plan_ref, wanted_ref, packed_hbm, kept_ref, scale_ref, base_ref, arrived_ref, *refs):
    last = step == STEPS - 1
    next_ref = refs[0]
    if not last:
        out_hbm, sent_ref, out_sems = refs[1:4]
    tiles_ref, x_ref, acc_ref, sems = refs[-4:]
    rb_dev, _, order = acc_ref.shape
    stay = KEPT // UNROLL
    groups = plan_ref[plan_ref.shape[0] - 32]
    copy = load_groups(packed_hbm, tiles_ref, sems, groups - stay)
    acc_ref[...] = jnp.zeros_like(acc_ref)
    size = split_sources(arrived_ref.shape[0], lambda p: arrived_ref[p], x_ref)
    size = size * ((1.0 if step == 0 else 2.0) / half_width)

    def loaded(g, j):
        if j == 0:
            copy(g - stay).wait()
        return tiles_ref[(g - stay) * UNROLL + j]

    def load(place):
        return x_ref[place]

    multiply(plan_ref, 0, jnp.minimum(stay, groups), lambda g, j: kept_ref[g * UNROLL + j], load, acc_ref)
    multiply(plan_ref, stay, groups, loaded, load, acc_ref)
    for r in range(rb_dev):
        at = slice(r * order, (r + 1) * order)
        scale = scale_ref[0:1, at]
        following = base_ref[:, at] - scale * collect(acc_ref[r], size)
        next_ref[:, at] = following
        if not last:
            sent_ref[r] = (following * scale).astype(BF16)
    if not last:
        send_picked(wanted_ref, sent_ref, out_hbm, out_sems)


def all_rows(own_ref, arrived, all_ref):
    c = lax.axis_index("col")
    all_ref[c] = own_ref[...].astype(BF16)
    for s, ref in enumerate(arrived, 1):
        all_ref[c ^ s] = ref[...]
    n, group, rows = all_ref.shape
    return all_ref[...].reshape(n * group, rows)


def gram_kernel(own_ref, *refs):
    arrived, (gram_ref, all_ref, full_ref) = refs[:-3], refs[-3:]
    rows = all_rows(own_ref, arrived, all_ref)
    full_ref[...] = lax.dot_general(rows, rows, NT, preferred_element_type=F32)
    half = gram_ref.shape[0]
    even = full_ref[pl.ds(0, half, stride=2), :]
    odd = full_ref[pl.ds(1, half, stride=2), :]
    gram_ref[...] = even + turn_lanes(odd)


PANEL = 64
PIECES = 4
SUB = 8


def eliminate(a, m, top):
    shape = a[0].shape
    here = lax.broadcasted_iota(I32, shape, 0)
    pivots = [None] * len(a)

    def column(rows, lane):
        return jnp.broadcast_to(rows[:, lane : lane + 1], shape)

    for step in range(0, len(a) * SUB, 4):
        own, k = divmod(step, SUB)
        head = [column(a[own], top + step + i) for i in range(4)]
        p, q = head[0][k : k + 1, :], head[2][k + 2 : k + 3, :]
        u, v = head[2][k : k + 1, :], head[3][k : k + 1, :]
        single = 1.0 / p
        det = p * q - (u * u + v * v)
        both = 1.0 / det
        pq, ub, vb, pb = q * both, u * both, v * both, p * both
        second = (here == k + 2) | (here == k + 3)
        last = det * single
        pivot = jnp.where(second, last, jnp.broadcast_to(p, shape))
        pivots[own] = pivot if k == 0 else jnp.where(here < k, pivots[own], pivot)
        rows = [[x[own][k + i : k + i + 1, :] for i in range(4)] for x in (a, m)]
        for g in range(own, len(a)):
            w = head if g == own else [column(a[g], top + step + i) for i in range(4)]
            c = [
                w[0] * pq - w[2] * ub - w[3] * vb,
                w[1] * pq + w[2] * vb - w[3] * ub,
                w[2] * pb - w[0] * ub + w[1] * vb,
                w[3] * pb - w[0] * vb - w[1] * ub,
            ]
            if g == own:
                below = here > k + 3
                c = [jnp.where(below, x, 0.0) for x in c]
                c[0] = jnp.where(second, w[0] * single, c[0])
                c[1] = jnp.where(second, w[1] * single, c[1])
            a[g], m[g] = (
                x[g] - (c[0] * r[0] + c[1] * r[1] + c[2] * r[2] + c[3] * r[3]) for x, r in zip((a, m), rows)
            )
    roots = [lax.rsqrt(x) for x in pivots]
    return [x * r for x, r in zip(a, roots)], [x * r for x, r in zip(m, roots)]


def factor_kernel(nodes, own_ref, all_ref, *refs):
    parts, (out_hbm, work_ref, inverse_ref, piece_ref, sems) = refs[:-5], refs[-5:]
    group = own_ref.shape[0]
    order = work_ref.shape[0]
    total = parts[0][...]
    for part in parts[1:]:
        total = total + part[...]
    half = total.shape[0]
    work_ref[pl.ds(0, half, stride=2), :] = total
    work_ref[pl.ds(1, half, stride=2), :] = -turn_lanes(total)
    row_at = lax.broadcasted_iota(I32, (order, order), 0)
    lane_at = lax.broadcasted_iota(I32, (order, order), 1)
    inverse_ref[...] = (row_at == lane_at).astype(F32)
    for top in range(0, order, PANEL):
        tops = range(top, top + PANEL, SUB)
        a, m = ([ref[r : r + SUB, :] for r in tops] for ref in (work_ref, inverse_ref))
        a, m = eliminate(a, m, top)
        a, m = jnp.concatenate(a, axis=0), jnp.concatenate(m, axis=0)
        inverse_ref[top : top + PANEL, :] = m
        rest = top + PANEL
        if rest < order:
            update = lax.dot_general(
                a, jnp.concatenate([a, m], axis=1), TN, precision=lax.Precision.HIGHEST, preferred_element_type=F32
            )
            work_ref[rest:, :] = work_ref[rest:, :] - update[rest:, :order]
            inverse_ref[rest:, :] = inverse_ref[rest:, :] - update[rest:, order:]
    c = lax.axis_index("col")
    mine = inverse_ref[pl.ds(pl.multiple_of(c * group, group), group), :]
    mine = mine * math.sqrt(nodes)
    high = mine.astype(BF16)
    low = (mine - high.astype(F32)).astype(BF16)
    own_lanes = (
        lax.broadcasted_iota(I32, (order, group), 0)
        == lax.broadcasted_iota(I32, (order, group), 1) + c * group
    ).astype(BF16)
    square = jnp.dot(high, own_lanes, preferred_element_type=F32).astype(BF16)
    left = jnp.concatenate([high, low], axis=0)
    width = own_ref.shape[1] // PIECES
    copies = []
    for i in range(PIECES):
        at = slice(i * width, (i + 1) * width)
        rows = all_ref[:, :, at].reshape(order, width)
        both = jnp.dot(left, rows, preferred_element_type=F32)
        own = own_ref[:, at]
        lost = (own - own.astype(BF16).astype(F32)).astype(BF16)
        piece_ref[i] = both[:group] + both[group:] + jnp.dot(square, lost, preferred_element_type=F32)
        copies.append(pltpu.make_async_copy(piece_ref.at[i], out_hbm.at[:, at], sems.at[i]))
        copies[-1].start()
    for copy in copies:
        copy.wait()


def central(nblk):
    return nblk // 4


def exchange(x):
    nblk = lax.axis_size("blk")
    group = [i ^ central(nblk) for i in range(nblk)]
    return lax.all_to_all(x, "blk", split_axis=0, concat_axis=0, tiled=True, axis_index_groups=[group])


def to_partner(x, axis, mask):
    n = lax.axis_size(axis)
    return lax.ppermute(x, axis, [(i, i ^ mask) for i in range(n)])


def sum_parts(part, nblk):
    wide = 1
    while 4 * wide < nblk:
        part = part + to_partner(part, "blk", wide)
        wide *= 2
    return [part] + [to_partner(part, "blk", s * wide) for s in range(1, nblk // wide)]


def per_device(y_start, tile_real, tile_imag, tile_rows, tile_slots, fetch_pick):
    group, rows = y_start.shape
    tiles, order, _ = tile_real.shape
    rb_dev = rows // order
    nblk = lax.axis_size("blk")
    ncol = lax.axis_size("col")
    near_count = LOC_RB * rb_dev
    wanted = exchange(jnp.broadcast_to(fetch_pick[None], (nblk, 1, nblk)))
    packed, kept, scale, plan = tiles_call(tile_rows, tile_slots, tile_real, tile_imag, rb_dev, near_count)

    out_blocks = pltpu.HBM((nblk, group, order), BF16)
    sent_scratch = [pltpu.VMEM((rb_dev, group, order), BF16), pltpu.SemaphoreType.DMA((nblk,))]
    blocks = pl.pallas_call(
        first_kernel,
        name="first",
        out_shape=out_blocks,
        in_specs=[VMEM, VMEM, SMEM],
        out_specs=ANY,
        scratch_shapes=sent_scratch,
        compiler_params=params(LIMIT),
    )(y_start, scale, wanted)

    vectors_here = sds((group, rows), F32)
    previous, current = y_start, y_start
    for step in range(STEPS):
        arrived = exchange(blocks)
        base = pl.pallas_call(
            functools.partial(near_kernel, step),
            name="near",
            out_shape=vectors_here,
            in_specs=[SMEM, SMEM, ANY, ANY] + [VMEM] * 3,
            out_specs=VMEM,
            scratch_shapes=[
                pltpu.VMEM((2, near_count, order, order), BF16),
                pltpu.VMEM((rb_dev, group, order), BF16),
                pltpu.VMEM((2, rb_dev, group, order), F32),
                pltpu.SemaphoreType.DMA((near_count // NEAR_UNROLL, 2)),
            ],
            compiler_params=params(LIMIT),
            cost_estimate=pl.CostEstimate(flops=1 << 28, bytes_accessed=1 << 21, transcendentals=0),
        )(in_hbm(tile_rows), in_hbm(tile_slots), in_hbm(tile_real), in_hbm(tile_imag), scale, current, previous)
        last = step == STEPS - 1
        out = pl.pallas_call(
            functools.partial(step_kernel, step),
            name="step",
            out_shape=[vectors_here] if last else [vectors_here, out_blocks],
            in_specs=[SMEM, SMEM, ANY] + [VMEM] * 4,
            out_specs=[VMEM] if last else [VMEM, ANY],
            scratch_shapes=([] if last else sent_scratch)
            + [
                pltpu.VMEM(packed.shape, F8),
                pltpu.VMEM((nblk + 1, 2 * group, 2 * order), F8),
                pltpu.VMEM((rb_dev, 2 * group, order), F32),
                pltpu.SemaphoreType.DMA((packed.shape[0] // UNROLL,)),
            ],
            compiler_params=params(LIMIT),
        )(in_hbm(plan), wanted, in_hbm(packed), pltpu.with_memory_space_constraint(kept, pltpu.VMEM), scale, base, arrived)
        previous, current = current, out[0]
        if not last:
            blocks = out[1]

    rounded = current.astype(BF16)
    if ncol == 4:
        beside, across = to_partner(rounded, "col", 1), to_partner(rounded, "col", 2)
        others = [beside, across, to_partner(across, "col", 1)]
    else:
        others = [to_partner(rounded, "col", s) for s in range(1, ncol)]
    vectors = group * ncol
    part, gathered = pl.pallas_call(
        gram_kernel,
        name="gram",
        out_shape=(sds((vectors // 2, vectors), F32), sds((ncol, group, rows), BF16)),
        in_specs=[VMEM] * (1 + len(others)),
        out_specs=(VMEM, VMEM),
        scratch_shapes=[pltpu.VMEM((vectors, vectors), F32)],
        compiler_params=params(LIMIT),
    )(current, *others)
    parts = sum_parts(part, nblk)
    return pl.pallas_call(
        functools.partial(factor_kernel, rows * nblk),
        name="factor",
        out_shape=pltpu.HBM((group, rows), F32),
        in_specs=[VMEM] * (2 + len(parts)),
        out_specs=ANY,
        scratch_shapes=[pltpu.VMEM((vectors, vectors), F32)] * 2
        + [pltpu.VMEM((PIECES, group, rows // PIECES), F32), pltpu.SemaphoreType.DMA((PIECES,))],
        compiler_params=params(LIMIT),
    )(current, gathered, *parts)


def solution(mesh):
    return jax.shard_map(
        per_device,
        mesh=mesh,
        in_specs=(
            P("col", "blk"),
            P("blk", None, None),
            P("blk", None, None),
            P("blk"),
            P("blk"),
            P("blk", None),
        ),
        out_specs=P("col", "blk"),
        check_vma=False,
    )
```

```python
import functools
import math

import jax
import jax.numpy as jnp
from jax import lax
from jax.experimental import pallas as pl
from jax.experimental.pallas import tpu as pltpu
from jax.sharding import PartitionSpec as P

LOC_RB = 2
STEPS = 4
UNROLL = 16
LOAD = 8
NEAR_UNROLL = 4
KEPT = 16
CHUNK = 4
MERGE = 16
TOP = 7.0
FINER = 16.0
SPLIT = float((1 << 20) + 1)
TINY = 1e-30
MIB = 1 << 20
LIMIT = 24

center = 1.25
half_width = 0.75

F32 = jnp.float32
BF16 = jnp.bfloat16
F8 = jnp.float8_e4m3fn
I32 = jnp.int32

VMEM = pl.BlockSpec(memory_space=pltpu.VMEM)
SMEM = pl.BlockSpec(memory_space=pltpu.SMEM)
ANY = pl.BlockSpec(memory_space=pl.ANY)

NT = (((1,), (1,)), ((), ()))
TN = (((0,), (0,)), ((), ()))


def sds(shape, dtype):
    return jax.ShapeDtypeStruct(shape, dtype)


def params(limit):
    return pltpu.CompilerParams(vmem_limit_bytes=limit * MIB)


def turn_rows(values):
    rows = values.shape[0]
    even = lax.broadcasted_iota(I32, values.shape, 0) % 2 == 0
    below = pltpu.roll(values, rows - 1, 0)
    above = pltpu.roll(values, 1, 0)
    return jnp.where(even, -below, above)


def turn_lanes(values):
    lanes = values.shape[1]
    even = lax.broadcasted_iota(I32, values.shape, 1) % 2 == 0
    after = pltpu.roll(values, lanes - 1, 1)
    before = pltpu.roll(values, 1, 1)
    return jnp.where(even, after, -before)


def tiles_kernel(
    near_count,
    rows_hbm,
    slots_hbm,
    real_hbm,
    imag_hbm,
    packed_hbm,
    kept_ref,
    scale_ref,
    plan_hbm,
    rows_ref,
    slots_ref,
    plan_ref,
    both_ref,
    small_ref,
    present_ref,
    table_ref,
    back_ref,
    done_ref,
    in_sems,
    out_sems,
    list_sems,
):
    kept = kept_ref.shape[0]
    tiles, order, _ = both_ref.shape
    rb_dev = present_ref.shape[0]
    slots = rb_dev + lax.axis_size("blk")
    chunks = tiles // CHUNK

    def copies(c):
        at = pl.ds(c * CHUNK, CHUNK)
        return (
            pltpu.make_async_copy(real_hbm.at[at], both_ref.at[at, :, 0:order], in_sems.at[c, 0]),
            pltpu.make_async_copy(imag_hbm.at[at], both_ref.at[at, :, order : 2 * order], in_sems.at[c, 1]),
        )

    def leave(e):
        return pltpu.make_async_copy(small_ref.at[e], packed_hbm.at[e], out_sems.at[e])

    lists = (
        pltpu.make_async_copy(rows_hbm, rows_ref, list_sems.at[0]),
        pltpu.make_async_copy(slots_hbm, slots_ref, list_sems.at[1]),
    )
    for copy in lists:
        copy.start()
    for c in range(chunks):
        for copy in copies(c):
            copy.start()

    def clear(row, _):
        for slot in range(slots):
            table_ref[row * slots + slot] = -1
        return _

    lax.fori_loop(0, rb_dev, clear, 0)
    present_ref[...] = jnp.zeros_like(present_ref)
    for copy in lists:
        copy.wait()

    def link(c, carry):
        for t in [c * CHUNK + j for j in range(CHUNK)]:
            key = rows_ref[t] * slots + slots_ref[t]
            seen = table_ref[key]
            before = seen & 255
            length = seen >> 8
            joins = (seen >= 0) & (length < MERGE)
            back_ref[t] = jnp.where(joins, before, -1)
            done_ref[t] = 1
            done_ref[jnp.where(joins, before, tiles)] = 0
            table_ref[key] = t | (jnp.where(joins, length + 1, 1) << 8)
        return carry

    lax.fori_loop(near_count // CHUNK, chunks, link, 0)

    def fill(ref, e, t):
        for at in [slice(q, q + 128) for q in range(0, 2 * order, 128)]:
            ref[e, at] = jnp.zeros((128, order), F8) if t is None else both_ref[t, :, at].astype(F8).T

    def put(e, t):
        @pl.when(e < kept)
        def _():
            fill(kept_ref, e, t)

        @pl.when(e >= kept)
        def _():
            fill(small_ref, e - kept, t)
            leave(e - kept).start()

    def count(t):
        row = rows_ref[t]
        for at in [slice(q, q + order // 4) for q in range(0, order, order // 4)]:
            counted = both_ref[t, at, :order] + jnp.abs(both_ref[t, at, order:])
            present_ref[row, at] = present_ref[row, at] + counted

    def one(t, listed):
        count(t)
        closes = done_ref[t]

        @pl.when(closes == 1)
        def _():
            def add(prior):
                both_ref[t] = both_ref[t] + both_ref[prior]
                return back_ref[prior]

            lax.while_loop(lambda prior: prior >= 0, add, back_ref[t])
            put(listed, t)
            place = place_of(slots_ref[t] - rb_dev, slots - rb_dev)
            plan_ref[listed] = rows_ref[t] | (place << 8)

        return listed + closes

    def near_chunk(c, carry):
        for copy in copies(c):
            copy.wait()
        for j in range(CHUNK):
            count(c * CHUNK + j)
        return carry

    def far_chunk(c, listed):
        for copy in copies(c):
            copy.wait()
        for j in range(CHUNK):
            listed = one(c * CHUNK + j, listed)
        return listed

    lax.fori_loop(0, near_count // CHUNK, near_chunk, 0)
    listed = lax.fori_loop(near_count // CHUNK, chunks, far_chunk, 0)
    short = (UNROLL - listed % UNROLL) % UNROLL
    for j in range(UNROLL - 1):

        @pl.when(j < short)
        def _():
            put(listed + j, None)
            plan_ref[listed + j] = (slots - rb_dev) << 8

    every = listed + short
    plan_ref[tiles] = every // UNROLL
    plan_copy = pltpu.make_async_copy(plan_ref, plan_hbm, list_sems.at[2])
    plan_copy.start()

    ones = jnp.ones((8, order), BF16)
    for r in range(rb_dev):
        degree = lax.dot_general(ones, present_ref[r], NT, preferred_element_type=F32)
        scale_ref[:, r * order : (r + 1) * order] = 1.0 / jnp.sqrt(jnp.maximum(degree, 1.0))

    def left(e, _):
        leave(e - kept).wait()
        return _

    lax.fori_loop(kept, every, left, 0)
    plan_copy.wait()


def in_hbm(x):
    return pltpu.with_memory_space_constraint(x, pltpu.HBM)


def tiles_call(rows, slots, real, imag, rb_dev, near_count):
    tiles, order, _ = real.shape
    nblk = lax.axis_size("blk")
    return pl.pallas_call(
        functools.partial(tiles_kernel, near_count),
        name="tiles",
        out_shape=(
            pltpu.HBM((tiles - near_count - KEPT, 2 * order, order), F8),
            pltpu.VMEM((KEPT, 2 * order, order), F8),
            sds((8, rb_dev * order), F32),
            pltpu.HBM((tiles + 32,), I32),
        ),
        in_specs=[ANY] * 4,
        out_specs=(ANY, VMEM, VMEM, ANY),
        scratch_shapes=[
            pltpu.SMEM((tiles,), I32),
            pltpu.SMEM((tiles,), I32),
            pltpu.SMEM((tiles + 32,), I32),
            pltpu.VMEM((tiles, order, 2 * order), BF16),
            pltpu.VMEM((tiles - near_count - KEPT, 2 * order, order), F8),
            pltpu.VMEM((rb_dev, order, order), BF16),
            pltpu.SMEM((rb_dev * (rb_dev + nblk),), I32),
            pltpu.SMEM((tiles,), I32),
            pltpu.SMEM((tiles + 1,), I32),
            pltpu.SemaphoreType.DMA((tiles // CHUNK, 2)),
            pltpu.SemaphoreType.DMA((tiles,)),
            pltpu.SemaphoreType.DMA((3,)),
        ],
        compiler_params=params(48),
        cost_estimate=pl.CostEstimate(flops=1 << 28, bytes_accessed=2 * real.size * 2, transcendentals=0),
    )(in_hbm(rows), in_hbm(slots), in_hbm(real), in_hbm(imag))


def rounded_block(field, scale_ref, r, order):
    at = slice(r * order, (r + 1) * order)
    return (field[:, at] * scale_ref[0:1, at]).astype(BF16)


def send_picked(wanted_ref, sent_ref, out_hbm, sems):
    me = lax.axis_index("blk")
    copies = [
        pltpu.make_async_copy(sent_ref.at[wanted_ref[i, 0, me]], out_hbm.at[i], sems.at[i])
        for i in range(out_hbm.shape[0])
    ]
    for copy in copies:
        copy.start()
    for copy in copies:
        copy.wait()


def first_kernel(y_ref, scale_ref, wanted_ref, out_hbm, sent_ref, out_sems):
    for r in range(sent_ref.shape[0]):
        sent_ref[r] = rounded_block(y_ref, scale_ref, r, sent_ref.shape[2])
    send_picked(wanted_ref, sent_ref, out_hbm, out_sems)


def load_tiles(packed_hbm, tiles_ref, sems, count):
    def copy(part):
        at = pl.ds(part * LOAD, LOAD)
        return pltpu.make_async_copy(packed_hbm.at[at], tiles_ref.at[at], sems.at[part])

    def begin(part, _):
        copy(part).start()
        return _

    lax.fori_loop(0, count, begin, 0)
    return copy


def split_sources(count, source, x_ref):
    _, rows, width = x_ref.shape
    group, order = rows // 2, width // 2
    most = jnp.zeros((group, order), F32)
    for p in range(count):
        most = jnp.maximum(most, jnp.abs(source(p).astype(F32)))
    most = jnp.broadcast_to(jnp.max(most, axis=1, keepdims=True), (group, 128))
    most = jnp.maximum(jnp.maximum(most, jnp.abs(turn_rows(most))), TINY)
    power = jnp.floor(jnp.log2(most))
    size = jnp.exp2(power - TOP)
    inverse = jnp.exp2(TOP - power)[:, 0:1]
    for p in range(count):
        scaled = source(p).astype(F32) * inverse
        far = scaled * SPLIT
        high = far - (far - scaled)
        low = (scaled - high) * FINER
        for k, part in enumerate((high, low)):
            at = slice(k * group, (k + 1) * group)
            x_ref[p, at, :order] = part.astype(F8)
            x_ref[p, at, order:] = turn_rows(part).astype(F8)
    x_ref[count] = jnp.zeros_like(x_ref[count])
    return size[:, 0:1]


def multiply(plan_ref, lo, hi, tile, load, acc_ref):
    def group(g, _):
        done = []
        for j in range(UNROLL):
            code = plan_ref[g * UNROLL + j]
            product = jnp.dot(load(code >> 8), tile(g, j), preferred_element_type=F32)
            done.append((code & 255, product))
        for row, product in done:
            acc_ref[row] = acc_ref[row] + product
        return _

    lax.fori_loop(lo, hi, group, 0)


def collect(acc, size):
    group = size.shape[0]
    return (acc[:group] + acc[group:] * (1.0 / FINER)) * size


def near_kernel(
    step, rows_ref, slots_ref, real_hbm, imag_hbm, scale_ref, now_ref, before_ref, base_ref, tiles_ref, x_ref, acc_ref, sems
):
    rb_dev, _, order = x_ref.shape
    groups = sems.shape[0]

    def copies(g):
        at = pl.ds(g * NEAR_UNROLL, NEAR_UNROLL)
        return [
            pltpu.make_async_copy(hbm.at[at], tiles_ref.at[i, at], sems.at[g, i])
            for i, hbm in enumerate((real_hbm, imag_hbm))
        ]

    for g in range(groups):
        for copy in copies(g):
            copy.start()
    acc_ref[...] = jnp.zeros_like(acc_ref)
    for r in range(rb_dev):
        x_ref[r] = rounded_block(now_ref, scale_ref, r, order)

    def group(g, _):
        for copy in copies(g):
            copy.wait()
        done = []
        for t in [g * NEAR_UNROLL + j for j in range(NEAR_UNROLL)]:
            x = x_ref[slots_ref[t]]
            done.append([lax.dot_general(x, tiles_ref[i, t], NT, preferred_element_type=F32) for i in range(2)])
        for j, products in enumerate(done):
            row = rows_ref[g * NEAR_UNROLL + j]
            for i, product in enumerate(products):
                acc_ref[i, row] = acc_ref[i, row] + product
        return _

    lax.fori_loop(0, groups, group, 0)
    for r in range(rb_dev):
        at = slice(r * order, (r + 1) * order)
        applied = scale_ref[0:1, at] * (acc_ref[0, r] + turn_rows(acc_ref[1, r]))
        moved = ((1.0 - center) * now_ref[:, at] - applied) / half_width
        base_ref[:, at] = moved if step == 0 else 2.0 * moved - before_ref[:, at]


def step_kernel(step, plan_ref, wanted_ref, packed_hbm, kept_ref, scale_ref, base_ref, arrived_ref, *refs):
    last = step == STEPS - 1
    next_ref = refs[0]
    if not last:
        out_hbm, sent_ref, out_sems = refs[1:4]
    tiles_ref, x_ref, acc_ref, sems = refs[-4:]
    rb_dev, _, order = acc_ref.shape
    stay = KEPT // UNROLL
    groups = plan_ref[plan_ref.shape[0] - 32]
    copy = load_tiles(packed_hbm, tiles_ref, sems, (groups - stay) * (UNROLL // LOAD))
    acc_ref[...] = jnp.zeros_like(acc_ref)
    size = split_sources(arrived_ref.shape[0], lambda p: arrived_ref[p], x_ref)
    size = size * ((1.0 if step == 0 else 2.0) / half_width)

    def loaded(g, j):
        if j % LOAD == 0:
            copy(((g - stay) * UNROLL + j) // LOAD).wait()
        return tiles_ref[(g - stay) * UNROLL + j]

    def load(place):
        return x_ref[place]

    multiply(plan_ref, 0, jnp.minimum(stay, groups), lambda g, j: kept_ref[g * UNROLL + j], load, acc_ref)
    multiply(plan_ref, stay, groups, loaded, load, acc_ref)
    for r in range(rb_dev):
        at = slice(r * order, (r + 1) * order)
        scale = scale_ref[0:1, at]
        following = base_ref[:, at] - scale * collect(acc_ref[r], size)
        next_ref[:, at] = following
        if not last:
            sent_ref[r] = (following * scale).astype(BF16)
    if not last:
        send_picked(wanted_ref, sent_ref, out_hbm, out_sems)


def all_rows(own_ref, arrived, all_ref):
    c = lax.axis_index("col")
    all_ref[c] = own_ref[...].astype(BF16)
    for s, ref in enumerate(arrived, 1):
        all_ref[c ^ s] = ref[...]
    n, group, rows = all_ref.shape
    return all_ref[...].reshape(n * group, rows)


def gram_kernel(own_ref, *refs):
    arrived, (gram_ref, all_ref, full_ref) = refs[:-3], refs[-3:]
    rows = all_rows(own_ref, arrived, all_ref)
    full_ref[...] = lax.dot_general(rows, rows, NT, preferred_element_type=F32)
    half = gram_ref.shape[0]
    even = full_ref[pl.ds(0, half, stride=2), :]
    odd = full_ref[pl.ds(1, half, stride=2), :]
    gram_ref[...] = even + turn_lanes(odd)


PANEL = 64
PIECES = 4
SUB = 8


def eliminate(a, m, top):
    shape = a[0].shape
    here = lax.broadcasted_iota(I32, shape, 0)
    pivots = [None] * len(a)

    def column(rows, lane):
        return jnp.broadcast_to(rows[:, lane : lane + 1], shape)

    for step in range(0, len(a) * SUB, 4):
        own, k = divmod(step, SUB)
        head = [column(a[own], top + step + i) for i in range(4)]
        p, q = head[0][k : k + 1, :], head[2][k + 2 : k + 3, :]
        u, v = head[2][k : k + 1, :], head[3][k : k + 1, :]
        single = 1.0 / p
        det = p * q - (u * u + v * v)
        both = 1.0 / det
        pq, ub, vb, pb = q * both, u * both, v * both, p * both
        second = (here == k + 2) | (here == k + 3)
        last = det * single
        pivot = jnp.where(second, last, jnp.broadcast_to(p, shape))
        pivots[own] = pivot if k == 0 else jnp.where(here < k, pivots[own], pivot)
        rows = [[x[own][k + i : k + i + 1, :] for i in range(4)] for x in (a, m)]
        for g in range(own, len(a)):
            w = head if g == own else [column(a[g], top + step + i) for i in range(4)]
            c = [
                w[0] * pq - w[2] * ub - w[3] * vb,
                w[1] * pq + w[2] * vb - w[3] * ub,
                w[2] * pb - w[0] * ub + w[1] * vb,
                w[3] * pb - w[0] * vb - w[1] * ub,
            ]
            if g == own:
                below = here > k + 3
                c = [jnp.where(below, x, 0.0) for x in c]
                c[0] = jnp.where(second, w[0] * single, c[0])
                c[1] = jnp.where(second, w[1] * single, c[1])
            a[g], m[g] = (
                x[g] - (c[0] * r[0] + c[1] * r[1] + c[2] * r[2] + c[3] * r[3]) for x, r in zip((a, m), rows)
            )
    roots = [lax.rsqrt(x) for x in pivots]
    return [x * r for x, r in zip(a, roots)], [x * r for x, r in zip(m, roots)]


def factor_kernel(nodes, own_ref, all_ref, *refs):
    parts, (out_hbm, work_ref, inverse_ref, piece_ref, sems) = refs[:-5], refs[-5:]
    group = own_ref.shape[0]
    order = work_ref.shape[0]
    total = parts[0][...]
    for part in parts[1:]:
        total = total + part[...]
    half = total.shape[0]
    work_ref[pl.ds(0, half, stride=2), :] = total
    work_ref[pl.ds(1, half, stride=2), :] = -turn_lanes(total)
    row_at = lax.broadcasted_iota(I32, (order, order), 0)
    lane_at = lax.broadcasted_iota(I32, (order, order), 1)
    inverse_ref[...] = (row_at == lane_at).astype(F32)
    for top in range(0, order, PANEL):
        tops = range(top, top + PANEL, SUB)
        a, m = ([ref[r : r + SUB, :] for r in tops] for ref in (work_ref, inverse_ref))
        a, m = eliminate(a, m, top)
        a, m = jnp.concatenate(a, axis=0), jnp.concatenate(m, axis=0)
        inverse_ref[top : top + PANEL, :] = m
        rest = top + PANEL
        if rest < order:
            update = lax.dot_general(
                a, jnp.concatenate([a, m], axis=1), TN, precision=lax.Precision.HIGHEST, preferred_element_type=F32
            )
            work_ref[rest:, :] = work_ref[rest:, :] - update[rest:, :order]
            inverse_ref[rest:, :] = inverse_ref[rest:, :] - update[rest:, order:]
    c = lax.axis_index("col")
    mine = inverse_ref[pl.ds(pl.multiple_of(c * group, group), group), :]
    mine = mine * math.sqrt(nodes)
    high = mine.astype(BF16)
    low = (mine - high.astype(F32)).astype(BF16)
    own_lanes = (
        lax.broadcasted_iota(I32, (order, group), 0)
        == lax.broadcasted_iota(I32, (order, group), 1) + c * group
    ).astype(BF16)
    square = jnp.dot(high, own_lanes, preferred_element_type=F32).astype(BF16)
    left = jnp.concatenate([high, low], axis=0)
    width = own_ref.shape[1] // PIECES
    copies = []
    for i in range(PIECES):
        at = slice(i * width, (i + 1) * width)
        rows = all_ref[:, :, at].reshape(order, width)
        both = jnp.dot(left, rows, preferred_element_type=F32)
        own = own_ref[:, at]
        lost = (own - own.astype(BF16).astype(F32)).astype(BF16)
        piece_ref[i] = both[:group] + both[group:] + jnp.dot(square, lost, preferred_element_type=F32)
        copies.append(pltpu.make_async_copy(piece_ref.at[i], out_hbm.at[:, at], sems.at[i]))
        copies[-1].start()
    for copy in copies:
        copy.wait()


def place_of(device, nblk):
    if nblk != 8:
        return device ^ (nblk // 4)
    z, y = device >> 1, device & 1
    half = z >> 1
    outer = (z & 1) ^ 1 ^ half
    return half | (y << 1) | (outer << 2)


def exchange(x):
    nblk = lax.axis_size("blk")
    group = sorted(range(nblk), key=lambda device: place_of(device, nblk))
    return lax.all_to_all(x, "blk", split_axis=0, concat_axis=0, tiled=True, axis_index_groups=[group])


def to_partner(x, axis, mask):
    n = lax.axis_size(axis)
    return lax.ppermute(x, axis, [(i, i ^ mask) for i in range(n)])


def sum_parts(part, nblk):
    wide = 1
    while 4 * wide < nblk:
        part = part + to_partner(part, "blk", wide)
        wide *= 2
    return [part] + [to_partner(part, "blk", s * wide) for s in range(1, nblk // wide)]


def per_device(y_start, tile_real, tile_imag, tile_rows, tile_slots, fetch_pick):
    group, rows = y_start.shape
    tiles, order, _ = tile_real.shape
    rb_dev = rows // order
    nblk = lax.axis_size("blk")
    ncol = lax.axis_size("col")
    near_count = LOC_RB * rb_dev
    wanted = exchange(jnp.broadcast_to(fetch_pick[None], (nblk, 1, nblk)))
    packed, kept, scale, plan = tiles_call(tile_rows, tile_slots, tile_real, tile_imag, rb_dev, near_count)

    out_blocks = pltpu.HBM((nblk, group, order), BF16)
    sent_scratch = [pltpu.VMEM((rb_dev, group, order), BF16), pltpu.SemaphoreType.DMA((nblk,))]
    blocks = pl.pallas_call(
        first_kernel,
        name="first",
        out_shape=out_blocks,
        in_specs=[VMEM, VMEM, SMEM],
        out_specs=ANY,
        scratch_shapes=sent_scratch,
        compiler_params=params(LIMIT),
    )(y_start, scale, wanted)

    vectors_here = sds((group, rows), F32)
    previous, current = y_start, y_start
    for step in range(STEPS):
        arrived = exchange(blocks)
        base = pl.pallas_call(
            functools.partial(near_kernel, step),
            name="near",
            out_shape=vectors_here,
            in_specs=[SMEM, SMEM, ANY, ANY] + [VMEM] * 3,
            out_specs=VMEM,
            scratch_shapes=[
                pltpu.VMEM((2, near_count, order, order), BF16),
                pltpu.VMEM((rb_dev, group, order), BF16),
                pltpu.VMEM((2, rb_dev, group, order), F32),
                pltpu.SemaphoreType.DMA((near_count // NEAR_UNROLL, 2)),
            ],
            compiler_params=params(LIMIT),
            cost_estimate=pl.CostEstimate(flops=1 << 28, bytes_accessed=1 << 21, transcendentals=0),
        )(in_hbm(tile_rows), in_hbm(tile_slots), in_hbm(tile_real), in_hbm(tile_imag), scale, current, previous)
        last = step == STEPS - 1
        out = pl.pallas_call(
            functools.partial(step_kernel, step),
            name="step",
            out_shape=[vectors_here] if last else [vectors_here, out_blocks],
            in_specs=[SMEM, SMEM, ANY] + [VMEM] * 4,
            out_specs=[VMEM] if last else [VMEM, ANY],
            scratch_shapes=([] if last else sent_scratch)
            + [
                pltpu.VMEM(packed.shape, F8),
                pltpu.VMEM((nblk + 1, 2 * group, 2 * order), F8),
                pltpu.VMEM((rb_dev, 2 * group, order), F32),
                pltpu.SemaphoreType.DMA((packed.shape[0] // LOAD,)),
            ],
            compiler_params=params(LIMIT),
        )(in_hbm(plan), wanted, in_hbm(packed), pltpu.with_memory_space_constraint(kept, pltpu.VMEM), scale, base, arrived)
        previous, current = current, out[0]
        if not last:
            blocks = out[1]

    rounded = current.astype(BF16)
    if ncol == 4:
        beside, across = to_partner(rounded, "col", 1), to_partner(rounded, "col", 2)
        others = [beside, across, to_partner(across, "col", 1)]
    else:
        others = [to_partner(rounded, "col", s) for s in range(1, ncol)]
    vectors = group * ncol
    part, gathered = pl.pallas_call(
        gram_kernel,
        name="gram",
        out_shape=(sds((vectors // 2, vectors), F32), sds((ncol, group, rows), BF16)),
        in_specs=[VMEM] * (1 + len(others)),
        out_specs=(VMEM, VMEM),
        scratch_shapes=[pltpu.VMEM((vectors, vectors), F32)],
        compiler_params=params(LIMIT),
    )(current, *others)
    parts = sum_parts(part, nblk)
    return pl.pallas_call(
        functools.partial(factor_kernel, rows * nblk),
        name="factor",
        out_shape=pltpu.HBM((group, rows), F32),
        in_specs=[VMEM] * (2 + len(parts)),
        out_specs=ANY,
        scratch_shapes=[pltpu.VMEM((vectors, vectors), F32)] * 2
        + [pltpu.VMEM((PIECES, group, rows // PIECES), F32), pltpu.SemaphoreType.DMA((PIECES,))],
        compiler_params=params(LIMIT),
    )(current, gathered, *parts)


def solution(mesh):
    return jax.shard_map(
        per_device,
        mesh=mesh,
        in_specs=(
            P("col", "blk"),
            P("blk", None, None),
            P("blk", None, None),
            P("blk"),
            P("blk"),
            P("blk", None),
        ),
        out_specs=P("col", "blk"),
        check_vma=False,
    )
```

```python
import functools
import math

import jax
import jax.numpy as jnp
from jax import lax
from jax.experimental import pallas as pl
from jax.experimental.pallas import tpu as pltpu
from jax.sharding import PartitionSpec as P

LOC_RB = 2
STEPS = 4
UNROLL = 8
NEAR_UNROLL = 4
KEPT = 16
CHUNK = 4
MERGE = 16
TOP = 7.0
FINER = 16.0
SPLIT = float((1 << 20) + 1)
TINY = 1e-30
MIB = 1 << 20
LIMIT = 24

center = 1.25
half_width = 0.75

F32 = jnp.float32
BF16 = jnp.bfloat16
F8 = jnp.float8_e4m3fn
I32 = jnp.int32

VMEM = pl.BlockSpec(memory_space=pltpu.VMEM)
SMEM = pl.BlockSpec(memory_space=pltpu.SMEM)
ANY = pl.BlockSpec(memory_space=pl.ANY)

NT = (((1,), (1,)), ((), ()))
TN = (((0,), (0,)), ((), ()))


def sds(shape, dtype):
    return jax.ShapeDtypeStruct(shape, dtype)


def params(limit):
    return pltpu.CompilerParams(vmem_limit_bytes=limit * MIB)


def turn_rows(values):
    rows = values.shape[0]
    even = lax.broadcasted_iota(I32, values.shape, 0) % 2 == 0
    below = pltpu.roll(values, rows - 1, 0)
    above = pltpu.roll(values, 1, 0)
    return jnp.where(even, -below, above)


def turn_lanes(values):
    lanes = values.shape[1]
    even = lax.broadcasted_iota(I32, values.shape, 1) % 2 == 0
    after = pltpu.roll(values, lanes - 1, 1)
    before = pltpu.roll(values, 1, 1)
    return jnp.where(even, after, -before)


def tiles_kernel(
    near_count,
    rows_hbm,
    slots_hbm,
    real_hbm,
    imag_hbm,
    packed_hbm,
    kept_ref,
    scale_ref,
    plan_hbm,
    rows_ref,
    slots_ref,
    plan_ref,
    both_ref,
    small_ref,
    present_ref,
    table_ref,
    back_ref,
    done_ref,
    in_sems,
    out_sems,
    list_sems,
):
    kept = kept_ref.shape[0]
    tiles, order, _ = both_ref.shape
    rb_dev = present_ref.shape[0]
    slots = rb_dev + lax.axis_size("blk")
    chunks = tiles // CHUNK

    def copies(c):
        at = pl.ds(c * CHUNK, CHUNK)
        return (
            pltpu.make_async_copy(real_hbm.at[at], both_ref.at[at, :, 0:order], in_sems.at[c, 0]),
            pltpu.make_async_copy(imag_hbm.at[at], both_ref.at[at, :, order : 2 * order], in_sems.at[c, 1]),
        )

    def leave(e):
        return pltpu.make_async_copy(small_ref.at[e], packed_hbm.at[e], out_sems.at[e])

    lists = (
        pltpu.make_async_copy(rows_hbm, rows_ref, list_sems.at[0]),
        pltpu.make_async_copy(slots_hbm, slots_ref, list_sems.at[1]),
    )
    for copy in lists:
        copy.start()
    for c in range(chunks):
        for copy in copies(c):
            copy.start()

    def clear(row, _):
        for slot in range(slots):
            table_ref[row * slots + slot] = -1
        return _

    lax.fori_loop(0, rb_dev, clear, 0)
    present_ref[...] = jnp.zeros_like(present_ref)
    for copy in lists:
        copy.wait()

    def link(c, carry):
        for t in [c * CHUNK + j for j in range(CHUNK)]:
            key = rows_ref[t] * slots + slots_ref[t]
            seen = table_ref[key]
            before = seen & 255
            length = seen >> 8
            joins = (seen >= 0) & (length < MERGE)
            back_ref[t] = jnp.where(joins, before, -1)
            done_ref[t] = 1
            done_ref[jnp.where(joins, before, tiles)] = 0
            table_ref[key] = t | (jnp.where(joins, length + 1, 1) << 8)
        return carry

    lax.fori_loop(near_count // CHUNK, chunks, link, 0)

    def fill(ref, e, t):
        for at in [slice(q, q + 128) for q in range(0, 2 * order, 128)]:
            ref[e, at] = jnp.zeros((128, order), F8) if t is None else both_ref[t, :, at].astype(F8).T

    def put(e, t):
        @pl.when(e < kept)
        def _():
            fill(kept_ref, e, t)

        @pl.when(e >= kept)
        def _():
            fill(small_ref, e - kept, t)
            leave(e - kept).start()

    def count(t):
        row = rows_ref[t]
        for at in [slice(q, q + order // 4) for q in range(0, order, order // 4)]:
            counted = both_ref[t, at, :order] + jnp.abs(both_ref[t, at, order:])
            present_ref[row, at] = present_ref[row, at] + counted

    def one(t, listed):
        count(t)
        closes = done_ref[t]

        @pl.when(closes == 1)
        def _():
            def add(prior):
                both_ref[t] = both_ref[t] + both_ref[prior]
                return back_ref[prior]

            lax.while_loop(lambda prior: prior >= 0, add, back_ref[t])
            put(listed, t)
            place = place_of(slots_ref[t] - rb_dev, slots - rb_dev)
            plan_ref[listed] = rows_ref[t] | (place << 8)

        return listed + closes

    def near_chunk(c, carry):
        for copy in copies(c):
            copy.wait()
        for j in range(CHUNK):
            count(c * CHUNK + j)
        return carry

    def far_chunk(c, listed):
        for copy in copies(c):
            copy.wait()
        for j in range(CHUNK):
            listed = one(c * CHUNK + j, listed)
        return listed

    lax.fori_loop(0, near_count // CHUNK, near_chunk, 0)
    listed = lax.fori_loop(near_count // CHUNK, chunks, far_chunk, 0)
    short = (UNROLL - listed % UNROLL) % UNROLL
    for j in range(UNROLL - 1):

        @pl.when(j < short)
        def _():
            put(listed + j, None)
            plan_ref[listed + j] = (slots - rb_dev) << 8

    every = listed + short
    plan_ref[tiles] = every // UNROLL
    plan_copy = pltpu.make_async_copy(plan_ref, plan_hbm, list_sems.at[2])
    plan_copy.start()

    ones = jnp.ones((8, order), BF16)
    for r in range(rb_dev):
        degree = lax.dot_general(ones, present_ref[r], NT, preferred_element_type=F32)
        scale_ref[:, r * order : (r + 1) * order] = 1.0 / jnp.sqrt(jnp.maximum(degree, 1.0))

    def left(e, _):
        leave(e - kept).wait()
        return _

    lax.fori_loop(kept, every, left, 0)
    plan_copy.wait()


def in_hbm(x):
    return pltpu.with_memory_space_constraint(x, pltpu.HBM)


def tiles_call(rows, slots, real, imag, rb_dev, near_count):
    tiles, order, _ = real.shape
    nblk = lax.axis_size("blk")
    return pl.pallas_call(
        functools.partial(tiles_kernel, near_count),
        name="tiles",
        out_shape=(
            pltpu.HBM((tiles - near_count - KEPT, 2 * order, order), F8),
            pltpu.VMEM((KEPT, 2 * order, order), F8),
            sds((8, rb_dev * order), F32),
            pltpu.HBM((tiles + 32,), I32),
        ),
        in_specs=[ANY] * 4,
        out_specs=(ANY, VMEM, VMEM, ANY),
        scratch_shapes=[
            pltpu.SMEM((tiles,), I32),
            pltpu.SMEM((tiles,), I32),
            pltpu.SMEM((tiles + 32,), I32),
            pltpu.VMEM((tiles, order, 2 * order), BF16),
            pltpu.VMEM((tiles - near_count - KEPT, 2 * order, order), F8),
            pltpu.VMEM((rb_dev, order, order), BF16),
            pltpu.SMEM((rb_dev * (rb_dev + nblk),), I32),
            pltpu.SMEM((tiles,), I32),
            pltpu.SMEM((tiles + 1,), I32),
            pltpu.SemaphoreType.DMA((tiles // CHUNK, 2)),
            pltpu.SemaphoreType.DMA((tiles,)),
            pltpu.SemaphoreType.DMA((3,)),
        ],
        compiler_params=params(48),
        cost_estimate=pl.CostEstimate(flops=1 << 28, bytes_accessed=2 * real.size * 2, transcendentals=0),
    )(in_hbm(rows), in_hbm(slots), in_hbm(real), in_hbm(imag))


def rounded_block(field, scale_ref, r, order):
    at = slice(r * order, (r + 1) * order)
    return (field[:, at] * scale_ref[0:1, at]).astype(BF16)


def send_picked(wanted_ref, sent_ref, out_hbm, sems):
    me = lax.axis_index("blk")
    copies = [
        pltpu.make_async_copy(sent_ref.at[wanted_ref[i, 0, me]], out_hbm.at[i], sems.at[i])
        for i in range(out_hbm.shape[0])
    ]
    for copy in copies:
        copy.start()
    for copy in copies:
        copy.wait()


def first_kernel(y_ref, scale_ref, wanted_ref, out_hbm, sent_ref, out_sems):
    for r in range(sent_ref.shape[0]):
        sent_ref[r] = rounded_block(y_ref, scale_ref, r, sent_ref.shape[2])
    send_picked(wanted_ref, sent_ref, out_hbm, out_sems)


def load_groups(packed_hbm, tiles_ref, sems, count):
    def copy(g):
        at = pl.ds(g * UNROLL, UNROLL)
        return pltpu.make_async_copy(packed_hbm.at[at], tiles_ref.at[at], sems.at[g])

    def begin(g, _):
        copy(g).start()
        return _

    lax.fori_loop(0, count, begin, 0)
    return copy


def split_sources(count, source, x_ref):
    _, rows, width = x_ref.shape
    group, order = rows // 2, width // 2
    most = jnp.zeros((group, order), F32)
    for p in range(count):
        most = jnp.maximum(most, jnp.abs(source(p).astype(F32)))
    most = jnp.broadcast_to(jnp.max(most, axis=1, keepdims=True), (group, 128))
    most = jnp.maximum(jnp.maximum(most, jnp.abs(turn_rows(most))), TINY)
    power = jnp.floor(jnp.log2(most))
    size = jnp.exp2(power - TOP)
    inverse = jnp.exp2(TOP - power)[:, 0:1]
    for p in range(count):
        scaled = source(p).astype(F32) * inverse
        far = scaled * SPLIT
        high = far - (far - scaled)
        low = (scaled - high) * FINER
        for k, part in enumerate((high, low)):
            at = slice(k * group, (k + 1) * group)
            x_ref[p, at, :order] = part.astype(F8)
            x_ref[p, at, order:] = turn_rows(part).astype(F8)
    x_ref[count] = jnp.zeros_like(x_ref[count])
    return size[:, 0:1]


def multiply(plan_ref, lo, hi, tile, load, acc_ref):
    def group(g, _):
        done = []
        for j in range(UNROLL):
            code = plan_ref[g * UNROLL + j]
            product = jnp.dot(load(code >> 8), tile(g, j), preferred_element_type=F32)
            done.append((code & 255, product))
        for row, product in done:
            acc_ref[row] = acc_ref[row] + product
        return _

    lax.fori_loop(lo, hi, group, 0)


def collect(acc, size):
    group = size.shape[0]
    return (acc[:group] + acc[group:] * (1.0 / FINER)) * size


def near_kernel(
    step, rows_ref, slots_ref, real_hbm, imag_hbm, scale_ref, now_ref, before_ref, base_ref, tiles_ref, x_ref, acc_ref, sems
):
    rb_dev, _, order = x_ref.shape
    groups = sems.shape[0]

    def copies(g):
        at = pl.ds(g * NEAR_UNROLL, NEAR_UNROLL)
        return [
            pltpu.make_async_copy(hbm.at[at], tiles_ref.at[i, at], sems.at[g, i])
            for i, hbm in enumerate((real_hbm, imag_hbm))
        ]

    for g in range(groups):
        for copy in copies(g):
            copy.start()
    acc_ref[...] = jnp.zeros_like(acc_ref)
    for r in range(rb_dev):
        x_ref[r] = rounded_block(now_ref, scale_ref, r, order)

    def group(g, _):
        for copy in copies(g):
            copy.wait()
        done = []
        for t in [g * NEAR_UNROLL + j for j in range(NEAR_UNROLL)]:
            x = x_ref[slots_ref[t]]
            done.append([lax.dot_general(x, tiles_ref[i, t], NT, preferred_element_type=F32) for i in range(2)])
        for j, products in enumerate(done):
            row = rows_ref[g * NEAR_UNROLL + j]
            for i, product in enumerate(products):
                acc_ref[i, row] = acc_ref[i, row] + product
        return _

    lax.fori_loop(0, groups, group, 0)
    for r in range(rb_dev):
        at = slice(r * order, (r + 1) * order)
        applied = scale_ref[0:1, at] * (acc_ref[0, r] + turn_rows(acc_ref[1, r]))
        moved = ((1.0 - center) * now_ref[:, at] - applied) / half_width
        base_ref[:, at] = moved if step == 0 else 2.0 * moved - before_ref[:, at]


def step_kernel(step, plan_ref, wanted_ref, packed_hbm, kept_ref, scale_ref, base_ref, arrived_ref, *refs):
    last = step == STEPS - 1
    next_ref = refs[0]
    if not last:
        out_hbm, sent_ref, out_sems = refs[1:4]
    tiles_ref, x_ref, acc_ref, sems = refs[-4:]
    rb_dev, _, order = acc_ref.shape
    stay = KEPT // UNROLL
    groups = plan_ref[plan_ref.shape[0] - 32]
    copy = load_groups(packed_hbm, tiles_ref, sems, groups - stay)
    acc_ref[...] = jnp.zeros_like(acc_ref)
    size = split_sources(arrived_ref.shape[0], lambda p: arrived_ref[p], x_ref)
    size = size * ((1.0 if step == 0 else 2.0) / half_width)

    def loaded(g, j):
        if j == 0:
            copy(g - stay).wait()
        return tiles_ref[(g - stay) * UNROLL + j]

    def load(place):
        return x_ref[place]

    multiply(plan_ref, 0, jnp.minimum(stay, groups), lambda g, j: kept_ref[g * UNROLL + j], load, acc_ref)
    multiply(plan_ref, stay, groups, loaded, load, acc_ref)
    for r in range(rb_dev):
        at = slice(r * order, (r + 1) * order)
        scale = scale_ref[0:1, at]
        following = base_ref[:, at] - scale * collect(acc_ref[r], size)
        next_ref[:, at] = following
        if not last:
            sent_ref[r] = (following * scale).astype(BF16)
    if not last:
        send_picked(wanted_ref, sent_ref, out_hbm, out_sems)


def all_rows(own_ref, arrived, all_ref):
    c = lax.axis_index("col")
    all_ref[c] = own_ref[...].astype(BF16)
    for s, ref in enumerate(arrived, 1):
        all_ref[c ^ s] = ref[...]
    n, group, rows = all_ref.shape
    return all_ref[...].reshape(n * group, rows)


def gram_kernel(own_ref, *refs):
    arrived, (gram_ref, all_ref, full_ref) = refs[:-3], refs[-3:]
    rows = all_rows(own_ref, arrived, all_ref)
    full_ref[...] = lax.dot_general(rows, rows, NT, preferred_element_type=F32)
    half = gram_ref.shape[0]
    even = full_ref[pl.ds(0, half, stride=2), :]
    odd = full_ref[pl.ds(1, half, stride=2), :]
    gram_ref[...] = even + turn_lanes(odd)


PANEL = 64
PIECES = 4
SUB = 8


def eliminate(a, m, top):
    shape = a[0].shape
    here = lax.broadcasted_iota(I32, shape, 0)
    pivots = [None] * len(a)

    def column(rows, lane):
        return jnp.broadcast_to(rows[:, lane : lane + 1], shape)

    for step in range(0, len(a) * SUB, 4):
        own, k = divmod(step, SUB)
        head = [column(a[own], top + step + i) for i in range(4)]
        p, q = head[0][k : k + 1, :], head[2][k + 2 : k + 3, :]
        u, v = head[2][k : k + 1, :], head[3][k : k + 1, :]
        single = 1.0 / p
        det = p * q - (u * u + v * v)
        both = 1.0 / det
        pq, ub, vb, pb = q * both, u * both, v * both, p * both
        second = (here == k + 2) | (here == k + 3)
        last = det * single
        pivot = jnp.where(second, last, jnp.broadcast_to(p, shape))
        pivots[own] = pivot if k == 0 else jnp.where(here < k, pivots[own], pivot)
        rows = [[x[own][k + i : k + i + 1, :] for i in range(4)] for x in (a, m)]
        for g in range(own, len(a)):
            w = head if g == own else [column(a[g], top + step + i) for i in range(4)]
            c = [
                w[0] * pq - w[2] * ub - w[3] * vb,
                w[1] * pq + w[2] * vb - w[3] * ub,
                w[2] * pb - w[0] * ub + w[1] * vb,
                w[3] * pb - w[0] * vb - w[1] * ub,
            ]
            if g == own:
                below = here > k + 3
                c = [jnp.where(below, x, 0.0) for x in c]
                c[0] = jnp.where(second, w[0] * single, c[0])
                c[1] = jnp.where(second, w[1] * single, c[1])
            a[g], m[g] = (
                x[g] - (c[0] * r[0] + c[1] * r[1] + c[2] * r[2] + c[3] * r[3]) for x, r in zip((a, m), rows)
            )
    roots = [lax.rsqrt(x) for x in pivots]
    return [x * r for x, r in zip(a, roots)], [x * r for x, r in zip(m, roots)]


def factor_kernel(nodes, own_ref, all_ref, *refs):
    parts, (out_hbm, work_ref, inverse_ref, piece_ref, sems) = refs[:-5], refs[-5:]
    group = own_ref.shape[0]
    order = work_ref.shape[0]
    total = parts[0][...]
    for part in parts[1:]:
        total = total + part[...]
    half = total.shape[0]
    work_ref[pl.ds(0, half, stride=2), :] = total
    work_ref[pl.ds(1, half, stride=2), :] = -turn_lanes(total)
    row_at = lax.broadcasted_iota(I32, (order, order), 0)
    lane_at = lax.broadcasted_iota(I32, (order, order), 1)
    inverse_ref[...] = (row_at == lane_at).astype(F32)
    for top in range(0, order, PANEL):
        tops = range(top, top + PANEL, SUB)
        a, m = ([ref[r : r + SUB, :] for r in tops] for ref in (work_ref, inverse_ref))
        a, m = eliminate(a, m, top)
        a, m = jnp.concatenate(a, axis=0), jnp.concatenate(m, axis=0)
        inverse_ref[top : top + PANEL, :] = m
        rest = top + PANEL
        if rest < order:
            update = lax.dot_general(
                a, jnp.concatenate([a, m], axis=1), TN, precision=lax.Precision.HIGHEST, preferred_element_type=F32
            )
            work_ref[rest:, :] = work_ref[rest:, :] - update[rest:, :order]
            inverse_ref[rest:, :] = inverse_ref[rest:, :] - update[rest:, order:]
    c = lax.axis_index("col")
    mine = inverse_ref[pl.ds(pl.multiple_of(c * group, group), group), :]
    mine = mine * math.sqrt(nodes)
    high = mine.astype(BF16)
    low = (mine - high.astype(F32)).astype(BF16)
    own_lanes = (
        lax.broadcasted_iota(I32, (order, group), 0)
        == lax.broadcasted_iota(I32, (order, group), 1) + c * group
    ).astype(BF16)
    square = jnp.dot(high, own_lanes, preferred_element_type=F32).astype(BF16)
    left = jnp.concatenate([high, low], axis=0)
    width = own_ref.shape[1] // PIECES
    copies = []
    for i in range(PIECES):
        at = slice(i * width, (i + 1) * width)
        rows = all_ref[:, :, at].reshape(order, width)
        both = jnp.dot(left, rows, preferred_element_type=F32)
        own = own_ref[:, at]
        lost = (own - own.astype(BF16).astype(F32)).astype(BF16)
        piece_ref[i] = both[:group] + both[group:] + jnp.dot(square, lost, preferred_element_type=F32)
        copies.append(pltpu.make_async_copy(piece_ref.at[i], out_hbm.at[:, at], sems.at[i]))
        copies[-1].start()
    for copy in copies:
        copy.wait()


def place_of(device, nblk):
    if nblk != 8:
        return device ^ (nblk // 4)
    z, y = device >> 1, device & 1
    half = z >> 1
    outer = (z & 1) ^ 1 ^ half
    return y | (outer << 1) | (half << 2)


def exchange(x):
    nblk = lax.axis_size("blk")
    group = sorted(range(nblk), key=lambda device: place_of(device, nblk))
    return lax.all_to_all(x, "blk", split_axis=0, concat_axis=0, tiled=True, axis_index_groups=[group])


def to_partner(x, axis, mask):
    n = lax.axis_size(axis)
    return lax.ppermute(x, axis, [(i, i ^ mask) for i in range(n)])


def sum_parts(part, nblk):
    wide = 1
    while 4 * wide < nblk:
        part = part + to_partner(part, "blk", wide)
        wide *= 2
    return [part] + [to_partner(part, "blk", s * wide) for s in range(1, nblk // wide)]


def per_device(y_start, tile_real, tile_imag, tile_rows, tile_slots, fetch_pick):
    group, rows = y_start.shape
    tiles, order, _ = tile_real.shape
    rb_dev = rows // order
    nblk = lax.axis_size("blk")
    ncol = lax.axis_size("col")
    near_count = LOC_RB * rb_dev
    wanted = exchange(jnp.broadcast_to(fetch_pick[None], (nblk, 1, nblk)))
    packed, kept, scale, plan = tiles_call(tile_rows, tile_slots, tile_real, tile_imag, rb_dev, near_count)

    out_blocks = pltpu.HBM((nblk, group, order), BF16)
    sent_scratch = [pltpu.VMEM((rb_dev, group, order), BF16), pltpu.SemaphoreType.DMA((nblk,))]
    blocks = pl.pallas_call(
        first_kernel,
        name="first",
        out_shape=out_blocks,
        in_specs=[VMEM, VMEM, SMEM],
        out_specs=ANY,
        scratch_shapes=sent_scratch,
        compiler_params=params(LIMIT),
    )(y_start, scale, wanted)

    vectors_here = sds((group, rows), F32)
    previous, current = y_start, y_start
    for step in range(STEPS):
        arrived = exchange(blocks)
        base = pl.pallas_call(
            functools.partial(near_kernel, step),
            name="near",
            out_shape=vectors_here,
            in_specs=[SMEM, SMEM, ANY, ANY] + [VMEM] * 3,
            out_specs=VMEM,
            scratch_shapes=[
                pltpu.VMEM((2, near_count, order, order), BF16),
                pltpu.VMEM((rb_dev, group, order), BF16),
                pltpu.VMEM((2, rb_dev, group, order), F32),
                pltpu.SemaphoreType.DMA((near_count // NEAR_UNROLL, 2)),
            ],
            compiler_params=params(LIMIT),
            cost_estimate=pl.CostEstimate(flops=1 << 28, bytes_accessed=1 << 21, transcendentals=0),
        )(in_hbm(tile_rows), in_hbm(tile_slots), in_hbm(tile_real), in_hbm(tile_imag), scale, current, previous)
        last = step == STEPS - 1
        out = pl.pallas_call(
            functools.partial(step_kernel, step),
            name="step",
            out_shape=[vectors_here] if last else [vectors_here, out_blocks],
            in_specs=[SMEM, SMEM, ANY] + [VMEM] * 4,
            out_specs=[VMEM] if last else [VMEM, ANY],
            scratch_shapes=([] if last else sent_scratch)
            + [
                pltpu.VMEM(packed.shape, F8),
                pltpu.VMEM((nblk + 1, 2 * group, 2 * order), F8),
                pltpu.VMEM((rb_dev, 2 * group, order), F32),
                pltpu.SemaphoreType.DMA((packed.shape[0] // UNROLL,)),
            ],
            compiler_params=params(LIMIT),
        )(in_hbm(plan), wanted, in_hbm(packed), pltpu.with_memory_space_constraint(kept, pltpu.VMEM), scale, base, arrived)
        previous, current = current, out[0]
        if not last:
            blocks = out[1]

    rounded = current.astype(BF16)
    if ncol == 4:
        beside, across = to_partner(rounded, "col", 1), to_partner(rounded, "col", 2)
        others = [beside, across, to_partner(across, "col", 1)]
    else:
        others = [to_partner(rounded, "col", s) for s in range(1, ncol)]
    vectors = group * ncol
    part, gathered = pl.pallas_call(
        gram_kernel,
        name="gram",
        out_shape=(sds((vectors // 2, vectors), F32), sds((ncol, group, rows), BF16)),
        in_specs=[VMEM] * (1 + len(others)),
        out_specs=(VMEM, VMEM),
        scratch_shapes=[pltpu.VMEM((vectors, vectors), F32)],
        compiler_params=params(LIMIT),
    )(current, *others)
    parts = sum_parts(part, nblk)
    return pl.pallas_call(
        functools.partial(factor_kernel, rows * nblk),
        name="factor",
        out_shape=pltpu.HBM((group, rows), F32),
        in_specs=[VMEM] * (2 + len(parts)),
        out_specs=ANY,
        scratch_shapes=[pltpu.VMEM((vectors, vectors), F32)] * 2
        + [pltpu.VMEM((PIECES, group, rows // PIECES), F32), pltpu.SemaphoreType.DMA((PIECES,))],
        compiler_params=params(LIMIT),
    )(current, gathered, *parts)


def solution(mesh):
    return jax.shard_map(
        per_device,
        mesh=mesh,
        in_specs=(
            P("col", "blk"),
            P("blk", None, None),
            P("blk", None, None),
            P("blk"),
            P("blk"),
            P("blk", None),
        ),
        out_specs=P("col", "blk"),
        check_vma=False,
    )
```

```python
import functools
import math

import jax
import jax.numpy as jnp
from jax import lax
from jax.experimental import pallas as pl
from jax.experimental.pallas import tpu as pltpu
from jax.sharding import PartitionSpec as P

LOC_RB = 2
STEPS = 4
UNROLL = 8
NEAR_UNROLL = 4
KEPT = 16
CHUNK = 4
MERGE = 16
TOP = 7.0
FINER = 16.0
SPLIT = float((1 << 20) + 1)
TINY = 1e-30
MIB = 1 << 20
LIMIT = 24

center = 1.25
half_width = 0.75

F32 = jnp.float32
BF16 = jnp.bfloat16
F8 = jnp.float8_e4m3fn
I32 = jnp.int32

VMEM = pl.BlockSpec(memory_space=pltpu.VMEM)
SMEM = pl.BlockSpec(memory_space=pltpu.SMEM)
ANY = pl.BlockSpec(memory_space=pl.ANY)

NT = (((1,), (1,)), ((), ()))
TN = (((0,), (0,)), ((), ()))


def sds(shape, dtype):
    return jax.ShapeDtypeStruct(shape, dtype)


def params(limit):
    return pltpu.CompilerParams(vmem_limit_bytes=limit * MIB)


def turn_rows(values):
    rows = values.shape[0]
    even = lax.broadcasted_iota(I32, values.shape, 0) % 2 == 0
    below = pltpu.roll(values, rows - 1, 0)
    above = pltpu.roll(values, 1, 0)
    return jnp.where(even, -below, above)


def turn_lanes(values):
    lanes = values.shape[1]
    even = lax.broadcasted_iota(I32, values.shape, 1) % 2 == 0
    after = pltpu.roll(values, lanes - 1, 1)
    before = pltpu.roll(values, 1, 1)
    return jnp.where(even, after, -before)


def tiles_kernel(
    near_count,
    rows_hbm,
    slots_hbm,
    real_hbm,
    imag_hbm,
    packed_hbm,
    kept_ref,
    scale_ref,
    plan_hbm,
    rows_ref,
    slots_ref,
    plan_ref,
    both_ref,
    small_ref,
    present_ref,
    table_ref,
    back_ref,
    done_ref,
    in_sems,
    out_sems,
    list_sems,
):
    kept = kept_ref.shape[0]
    tiles, order, _ = both_ref.shape
    rb_dev = present_ref.shape[0]
    slots = rb_dev + lax.axis_size("blk")
    chunks = tiles // CHUNK

    def copies(c):
        at = pl.ds(c * CHUNK, CHUNK)
        return (
            pltpu.make_async_copy(real_hbm.at[at], both_ref.at[at, :, 0:order], in_sems.at[c, 0]),
            pltpu.make_async_copy(imag_hbm.at[at], both_ref.at[at, :, order : 2 * order], in_sems.at[c, 1]),
        )

    def leave(e):
        return pltpu.make_async_copy(small_ref.at[e], packed_hbm.at[e], out_sems.at[e])

    lists = (
        pltpu.make_async_copy(rows_hbm, rows_ref, list_sems.at[0]),
        pltpu.make_async_copy(slots_hbm, slots_ref, list_sems.at[1]),
    )
    for copy in lists:
        copy.start()
    for c in range(chunks):
        for copy in copies(c):
            copy.start()

    def clear(row, _):
        for slot in range(slots):
            table_ref[row * slots + slot] = -1
        return _

    lax.fori_loop(0, rb_dev, clear, 0)
    present_ref[...] = jnp.zeros_like(present_ref)
    for copy in lists:
        copy.wait()

    def link(c, carry):
        for t in [c * CHUNK + j for j in range(CHUNK)]:
            key = rows_ref[t] * slots + slots_ref[t]
            seen = table_ref[key]
            before = seen & 255
            length = seen >> 8
            joins = (seen >= 0) & (length < MERGE)
            back_ref[t] = jnp.where(joins, before, -1)
            done_ref[t] = 1
            done_ref[jnp.where(joins, before, tiles)] = 0
            table_ref[key] = t | (jnp.where(joins, length + 1, 1) << 8)
        return carry

    lax.fori_loop(near_count // CHUNK, chunks, link, 0)

    def fill(ref, e, t):
        for at in [slice(q, q + 128) for q in range(0, 2 * order, 128)]:
            ref[e, at] = jnp.zeros((128, order), F8) if t is None else both_ref[t, :, at].astype(F8).T

    def put(e, t):
        @pl.when(e < kept)
        def _():
            fill(kept_ref, e, t)

        @pl.when(e >= kept)
        def _():
            fill(small_ref, e - kept, t)
            leave(e - kept).start()

    def count(t):
        row = rows_ref[t]
        for at in [slice(q, q + order // 4) for q in range(0, order, order // 4)]:
            counted = both_ref[t, at, :order] + jnp.abs(both_ref[t, at, order:])
            present_ref[row, at] = present_ref[row, at] + counted

    def one(t, listed):
        count(t)
        closes = done_ref[t]

        @pl.when(closes == 1)
        def _():
            def add(prior):
                both_ref[t] = both_ref[t] + both_ref[prior]
                return back_ref[prior]

            lax.while_loop(lambda prior: prior >= 0, add, back_ref[t])
            put(listed, t)
            place = place_of(slots_ref[t] - rb_dev, slots - rb_dev)
            plan_ref[listed] = rows_ref[t] | (place << 8)

        return listed + closes

    def near_chunk(c, carry):
        for copy in copies(c):
            copy.wait()
        for j in range(CHUNK):
            count(c * CHUNK + j)
        return carry

    def far_chunk(c, listed):
        for copy in copies(c):
            copy.wait()
        for j in range(CHUNK):
            listed = one(c * CHUNK + j, listed)
        return listed

    lax.fori_loop(0, near_count // CHUNK, near_chunk, 0)
    listed = lax.fori_loop(near_count // CHUNK, chunks, far_chunk, 0)
    short = (UNROLL - listed % UNROLL) % UNROLL
    for j in range(UNROLL - 1):

        @pl.when(j < short)
        def _():
            put(listed + j, None)
            plan_ref[listed + j] = (slots - rb_dev) << 8

    every = listed + short
    plan_ref[tiles] = every // UNROLL
    plan_copy = pltpu.make_async_copy(plan_ref, plan_hbm, list_sems.at[2])
    plan_copy.start()

    ones = jnp.ones((8, order), BF16)
    for r in range(rb_dev):
        degree = lax.dot_general(ones, present_ref[r], NT, preferred_element_type=F32)
        scale_ref[:, r * order : (r + 1) * order] = 1.0 / jnp.sqrt(jnp.maximum(degree, 1.0))

    def left(e, _):
        leave(e - kept).wait()
        return _

    lax.fori_loop(kept, every, left, 0)
    plan_copy.wait()


def in_hbm(x):
    return pltpu.with_memory_space_constraint(x, pltpu.HBM)


def tiles_call(rows, slots, real, imag, rb_dev, near_count):
    tiles, order, _ = real.shape
    nblk = lax.axis_size("blk")
    return pl.pallas_call(
        functools.partial(tiles_kernel, near_count),
        name="tiles",
        out_shape=(
            pltpu.HBM((tiles - near_count - KEPT, 2 * order, order), F8),
            pltpu.VMEM((KEPT, 2 * order, order), F8),
            sds((8, rb_dev * order), F32),
            pltpu.HBM((tiles + 32,), I32),
        ),
        in_specs=[ANY] * 4,
        out_specs=(ANY, VMEM, VMEM, ANY),
        scratch_shapes=[
            pltpu.SMEM((tiles,), I32),
            pltpu.SMEM((tiles,), I32),
            pltpu.SMEM((tiles + 32,), I32),
            pltpu.VMEM((tiles, order, 2 * order), BF16),
            pltpu.VMEM((tiles - near_count - KEPT, 2 * order, order), F8),
            pltpu.VMEM((rb_dev, order, order), BF16),
            pltpu.SMEM((rb_dev * (rb_dev + nblk),), I32),
            pltpu.SMEM((tiles,), I32),
            pltpu.SMEM((tiles + 1,), I32),
            pltpu.SemaphoreType.DMA((tiles // CHUNK, 2)),
            pltpu.SemaphoreType.DMA((tiles,)),
            pltpu.SemaphoreType.DMA((3,)),
        ],
        compiler_params=params(48),
        cost_estimate=pl.CostEstimate(flops=1 << 28, bytes_accessed=2 * real.size * 2, transcendentals=0),
    )(in_hbm(rows), in_hbm(slots), in_hbm(real), in_hbm(imag))


def rounded_block(field, scale_ref, r, order):
    at = slice(r * order, (r + 1) * order)
    return (field[:, at] * scale_ref[0:1, at]).astype(BF16)


def send_picked(wanted_ref, sent_ref, out_hbm, sems):
    me = lax.axis_index("blk")
    copies = [
        pltpu.make_async_copy(sent_ref.at[wanted_ref[i, 0, me]], out_hbm.at[i], sems.at[i])
        for i in range(out_hbm.shape[0])
    ]
    for copy in copies:
        copy.start()
    for copy in copies:
        copy.wait()


def first_kernel(y_ref, scale_ref, wanted_ref, out_hbm, sent_ref, out_sems):
    for r in range(sent_ref.shape[0]):
        sent_ref[r] = rounded_block(y_ref, scale_ref, r, sent_ref.shape[2])
    send_picked(wanted_ref, sent_ref, out_hbm, out_sems)


def load_groups(packed_hbm, tiles_ref, sems, count):
    def copy(g):
        at = pl.ds(g * UNROLL, UNROLL)
        return pltpu.make_async_copy(packed_hbm.at[at], tiles_ref.at[at], sems.at[g])

    def begin(g, _):
        copy(g).start()
        return _

    lax.fori_loop(0, count, begin, 0)
    return copy


def split_sources(count, source, x_ref):
    _, rows, width = x_ref.shape
    group, order = rows // 2, width // 2
    most = jnp.zeros((group, order), F32)
    for p in range(count):
        most = jnp.maximum(most, jnp.abs(source(p).astype(F32)))
    most = jnp.broadcast_to(jnp.max(most, axis=1, keepdims=True), (group, 128))
    most = jnp.maximum(jnp.maximum(most, jnp.abs(turn_rows(most))), TINY)
    power = jnp.floor(jnp.log2(most))
    size = jnp.exp2(power - TOP)
    inverse = jnp.exp2(TOP - power)[:, 0:1]
    for p in range(count):
        scaled = source(p).astype(F32) * inverse
        far = scaled * SPLIT
        high = far - (far - scaled)
        low = (scaled - high) * FINER
        for k, part in enumerate((high, low)):
            at = slice(k * group, (k + 1) * group)
            x_ref[p, at, :order] = part.astype(F8)
            x_ref[p, at, order:] = turn_rows(part).astype(F8)
    x_ref[count] = jnp.zeros_like(x_ref[count])
    return size[:, 0:1]


def multiply(plan_ref, lo, hi, tile, load, acc_ref):
    def group(g, _):
        done = []
        for j in range(UNROLL):
            code = plan_ref[g * UNROLL + j]
            product = jnp.dot(load(code >> 8), tile(g, j), preferred_element_type=F32)
            done.append((code & 255, product))
        for row, product in done:
            acc_ref[row] = acc_ref[row] + product
        return _

    lax.fori_loop(lo, hi, group, 0)


def collect(acc, size):
    group = size.shape[0]
    return (acc[:group] + acc[group:] * (1.0 / FINER)) * size


def near_kernel(
    step, rows_ref, slots_ref, real_hbm, imag_hbm, scale_ref, now_ref, before_ref, base_ref, tiles_ref, x_ref, acc_ref, sems
):
    rb_dev, _, order = x_ref.shape
    groups = sems.shape[0]

    def copies(g):
        at = pl.ds(g * NEAR_UNROLL, NEAR_UNROLL)
        return [
            pltpu.make_async_copy(hbm.at[at], tiles_ref.at[i, at], sems.at[g, i])
            for i, hbm in enumerate((real_hbm, imag_hbm))
        ]

    for g in range(groups):
        for copy in copies(g):
            copy.start()
    acc_ref[...] = jnp.zeros_like(acc_ref)
    for r in range(rb_dev):
        x_ref[r] = rounded_block(now_ref, scale_ref, r, order)

    def group(g, _):
        for copy in copies(g):
            copy.wait()
        done = []
        for t in [g * NEAR_UNROLL + j for j in range(NEAR_UNROLL)]:
            x = x_ref[slots_ref[t]]
            done.append([lax.dot_general(x, tiles_ref[i, t], NT, preferred_element_type=F32) for i in range(2)])
        for j, products in enumerate(done):
            row = rows_ref[g * NEAR_UNROLL + j]
            for i, product in enumerate(products):
                acc_ref[i, row] = acc_ref[i, row] + product
        return _

    lax.fori_loop(0, groups, group, 0)
    for r in range(rb_dev):
        at = slice(r * order, (r + 1) * order)
        applied = scale_ref[0:1, at] * (acc_ref[0, r] + turn_rows(acc_ref[1, r]))
        moved = ((1.0 - center) * now_ref[:, at] - applied) / half_width
        base_ref[:, at] = moved if step == 0 else 2.0 * moved - before_ref[:, at]


def step_kernel(step, plan_ref, wanted_ref, packed_hbm, kept_ref, scale_ref, base_ref, arrived_ref, *refs):
    last = step == STEPS - 1
    next_ref = refs[0]
    if not last:
        out_hbm, sent_ref, out_sems = refs[1:4]
    tiles_ref, x_ref, acc_ref, sems = refs[-4:]
    rb_dev, _, order = acc_ref.shape
    stay = KEPT // UNROLL
    groups = plan_ref[plan_ref.shape[0] - 32]
    copy = load_groups(packed_hbm, tiles_ref, sems, groups - stay)
    acc_ref[...] = jnp.zeros_like(acc_ref)
    size = split_sources(arrived_ref.shape[0], lambda p: arrived_ref[p], x_ref)
    size = size * ((1.0 if step == 0 else 2.0) / half_width)

    def loaded(g, j):
        if j == 0:
            copy(g - stay).wait()
        return tiles_ref[(g - stay) * UNROLL + j]

    def load(place):
        return x_ref[place]

    multiply(plan_ref, 0, jnp.minimum(stay, groups), lambda g, j: kept_ref[g * UNROLL + j], load, acc_ref)
    multiply(plan_ref, stay, groups, loaded, load, acc_ref)
    for r in range(rb_dev):
        at = slice(r * order, (r + 1) * order)
        scale = scale_ref[0:1, at]
        following = base_ref[:, at] - scale * collect(acc_ref[r], size)
        next_ref[:, at] = following
        if not last:
            sent_ref[r] = (following * scale).astype(BF16)
    if not last:
        send_picked(wanted_ref, sent_ref, out_hbm, out_sems)


def all_rows(own_ref, arrived, all_ref):
    c = lax.axis_index("col")
    all_ref[c] = own_ref[...].astype(BF16)
    for s, ref in enumerate(arrived, 1):
        all_ref[c ^ s] = ref[...]
    n, group, rows = all_ref.shape
    return all_ref[...].reshape(n * group, rows)


def gram_kernel(own_ref, *refs):
    arrived, (gram_ref, all_ref, full_ref) = refs[:-3], refs[-3:]
    rows = all_rows(own_ref, arrived, all_ref)
    full_ref[...] = lax.dot_general(rows, rows, NT, preferred_element_type=F32)
    half = gram_ref.shape[0]
    even = full_ref[pl.ds(0, half, stride=2), :]
    odd = full_ref[pl.ds(1, half, stride=2), :]
    gram_ref[...] = even + turn_lanes(odd)


PANEL = 64
PIECES = 4
SUB = 8


def eliminate(a, m, top):
    shape = a[0].shape
    here = lax.broadcasted_iota(I32, shape, 0)
    pivots = [None] * len(a)

    def column(rows, lane):
        return jnp.broadcast_to(rows[:, lane : lane + 1], shape)

    for step in range(0, len(a) * SUB, 4):
        own, k = divmod(step, SUB)
        head = [column(a[own], top + step + i) for i in range(4)]
        p, q = head[0][k : k + 1, :], head[2][k + 2 : k + 3, :]
        u, v = head[2][k : k + 1, :], head[3][k : k + 1, :]
        single = 1.0 / p
        det = p * q - (u * u + v * v)
        both = 1.0 / det
        pq, ub, vb, pb = q * both, u * both, v * both, p * both
        second = (here == k + 2) | (here == k + 3)
        last = det * single
        pivot = jnp.where(second, last, jnp.broadcast_to(p, shape))
        pivots[own] = pivot if k == 0 else jnp.where(here < k, pivots[own], pivot)
        rows = [[x[own][k + i : k + i + 1, :] for i in range(4)] for x in (a, m)]
        for g in range(own, len(a)):
            w = head if g == own else [column(a[g], top + step + i) for i in range(4)]
            c = [
                w[0] * pq - w[2] * ub - w[3] * vb,
                w[1] * pq + w[2] * vb - w[3] * ub,
                w[2] * pb - w[0] * ub + w[1] * vb,
                w[3] * pb - w[0] * vb - w[1] * ub,
            ]
            if g == own:
                below = here > k + 3
                c = [jnp.where(below, x, 0.0) for x in c]
                c[0] = jnp.where(second, w[0] * single, c[0])
                c[1] = jnp.where(second, w[1] * single, c[1])
            a[g], m[g] = (
                x[g] - (c[0] * r[0] + c[1] * r[1] + c[2] * r[2] + c[3] * r[3]) for x, r in zip((a, m), rows)
            )
    roots = [lax.rsqrt(x) for x in pivots]
    return [x * r for x, r in zip(a, roots)], [x * r for x, r in zip(m, roots)]


def factor_kernel(nodes, own_ref, all_ref, *refs):
    parts, (out_hbm, work_ref, inverse_ref, piece_ref, sems) = refs[:-5], refs[-5:]
    group = own_ref.shape[0]
    order = work_ref.shape[0]
    total = parts[0][...]
    for part in parts[1:]:
        total = total + part[...]
    half = total.shape[0]
    work_ref[pl.ds(0, half, stride=2), :] = total
    work_ref[pl.ds(1, half, stride=2), :] = -turn_lanes(total)
    row_at = lax.broadcasted_iota(I32, (order, order), 0)
    lane_at = lax.broadcasted_iota(I32, (order, order), 1)
    inverse_ref[...] = (row_at == lane_at).astype(F32)
    for top in range(0, order, PANEL):
        tops = range(top, top + PANEL, SUB)
        a, m = ([ref[r : r + SUB, :] for r in tops] for ref in (work_ref, inverse_ref))
        a, m = eliminate(a, m, top)
        a, m = jnp.concatenate(a, axis=0), jnp.concatenate(m, axis=0)
        inverse_ref[top : top + PANEL, :] = m
        rest = top + PANEL
        if rest < order:
            update = lax.dot_general(
                a, jnp.concatenate([a, m], axis=1), TN, precision=lax.Precision.HIGHEST, preferred_element_type=F32
            )
            work_ref[rest:, :] = work_ref[rest:, :] - update[rest:, :order]
            inverse_ref[rest:, :] = inverse_ref[rest:, :] - update[rest:, order:]
    c = lax.axis_index("col")
    mine = inverse_ref[pl.ds(pl.multiple_of(c * group, group), group), :]
    mine = mine * math.sqrt(nodes)
    high = mine.astype(BF16)
    low = (mine - high.astype(F32)).astype(BF16)
    own_lanes = (
        lax.broadcasted_iota(I32, (order, group), 0)
        == lax.broadcasted_iota(I32, (order, group), 1) + c * group
    ).astype(BF16)
    square = jnp.dot(high, own_lanes, preferred_element_type=F32).astype(BF16)
    left = jnp.concatenate([high, low], axis=0)
    width = own_ref.shape[1] // PIECES
    copies = []
    for i in range(PIECES):
        at = slice(i * width, (i + 1) * width)
        rows = all_ref[:, :, at].reshape(order, width)
        both = jnp.dot(left, rows, preferred_element_type=F32)
        own = own_ref[:, at]
        lost = (own - own.astype(BF16).astype(F32)).astype(BF16)
        piece_ref[i] = both[:group] + both[group:] + jnp.dot(square, lost, preferred_element_type=F32)
        copies.append(pltpu.make_async_copy(piece_ref.at[i], out_hbm.at[:, at], sems.at[i]))
        copies[-1].start()
    for copy in copies:
        copy.wait()


PLACES = 0x12365047


def place_of(device, nblk):
    return (PLACES >> (4 * device)) & 15 if nblk == 8 else device ^ (nblk // 4)


def exchange(x):
    nblk = lax.axis_size("blk")
    group = sorted(range(nblk), key=lambda device: place_of(device, nblk))
    return lax.all_to_all(x, "blk", split_axis=0, concat_axis=0, tiled=True, axis_index_groups=[group])


def to_partner(x, axis, mask):
    n = lax.axis_size(axis)
    return lax.ppermute(x, axis, [(i, i ^ mask) for i in range(n)])


def sum_parts(part, nblk):
    wide = 1
    while 4 * wide < nblk:
        part = part + to_partner(part, "blk", wide)
        wide *= 2
    return [part] + [to_partner(part, "blk", s * wide) for s in range(1, nblk // wide)]


def per_device(y_start, tile_real, tile_imag, tile_rows, tile_slots, fetch_pick):
    group, rows = y_start.shape
    tiles, order, _ = tile_real.shape
    rb_dev = rows // order
    nblk = lax.axis_size("blk")
    ncol = lax.axis_size("col")
    near_count = LOC_RB * rb_dev
    wanted = exchange(jnp.broadcast_to(fetch_pick[None], (nblk, 1, nblk)))
    packed, kept, scale, plan = tiles_call(tile_rows, tile_slots, tile_real, tile_imag, rb_dev, near_count)

    out_blocks = pltpu.HBM((nblk, group, order), BF16)
    sent_scratch = [pltpu.VMEM((rb_dev, group, order), BF16), pltpu.SemaphoreType.DMA((nblk,))]
    blocks = pl.pallas_call(
        first_kernel,
        name="first",
        out_shape=out_blocks,
        in_specs=[VMEM, VMEM, SMEM],
        out_specs=ANY,
        scratch_shapes=sent_scratch,
        compiler_params=params(LIMIT),
    )(y_start, scale, wanted)

    vectors_here = sds((group, rows), F32)
    previous, current = y_start, y_start
    for step in range(STEPS):
        arrived = exchange(blocks)
        base = pl.pallas_call(
            functools.partial(near_kernel, step),
            name="near",
            out_shape=vectors_here,
            in_specs=[SMEM, SMEM, ANY, ANY] + [VMEM] * 3,
            out_specs=VMEM,
            scratch_shapes=[
                pltpu.VMEM((2, near_count, order, order), BF16),
                pltpu.VMEM((rb_dev, group, order), BF16),
                pltpu.VMEM((2, rb_dev, group, order), F32),
                pltpu.SemaphoreType.DMA((near_count // NEAR_UNROLL, 2)),
            ],
            compiler_params=params(LIMIT),
            cost_estimate=pl.CostEstimate(flops=1 << 28, bytes_accessed=1 << 21, transcendentals=0),
        )(in_hbm(tile_rows), in_hbm(tile_slots), in_hbm(tile_real), in_hbm(tile_imag), scale, current, previous)
        last = step == STEPS - 1
        out = pl.pallas_call(
            functools.partial(step_kernel, step),
            name="step",
            out_shape=[vectors_here] if last else [vectors_here, out_blocks],
            in_specs=[SMEM, SMEM, ANY] + [VMEM] * 4,
            out_specs=[VMEM] if last else [VMEM, ANY],
            scratch_shapes=([] if last else sent_scratch)
            + [
                pltpu.VMEM(packed.shape, F8),
                pltpu.VMEM((nblk + 1, 2 * group, 2 * order), F8),
                pltpu.VMEM((rb_dev, 2 * group, order), F32),
                pltpu.SemaphoreType.DMA((packed.shape[0] // UNROLL,)),
            ],
            compiler_params=params(LIMIT),
        )(in_hbm(plan), wanted, in_hbm(packed), pltpu.with_memory_space_constraint(kept, pltpu.VMEM), scale, base, arrived)
        previous, current = current, out[0]
        if not last:
            blocks = out[1]

    rounded = current.astype(BF16)
    if ncol == 4:
        beside, across = to_partner(rounded, "col", 1), to_partner(rounded, "col", 2)
        others = [beside, across, to_partner(across, "col", 1)]
    else:
        others = [to_partner(rounded, "col", s) for s in range(1, ncol)]
    vectors = group * ncol
    part, gathered = pl.pallas_call(
        gram_kernel,
        name="gram",
        out_shape=(sds((vectors // 2, vectors), F32), sds((ncol, group, rows), BF16)),
        in_specs=[VMEM] * (1 + len(others)),
        out_specs=(VMEM, VMEM),
        scratch_shapes=[pltpu.VMEM((vectors, vectors), F32)],
        compiler_params=params(LIMIT),
    )(current, *others)
    parts = sum_parts(part, nblk)
    return pl.pallas_call(
        functools.partial(factor_kernel, rows * nblk),
        name="factor",
        out_shape=pltpu.HBM((group, rows), F32),
        in_specs=[VMEM] * (2 + len(parts)),
        out_specs=ANY,
        scratch_shapes=[pltpu.VMEM((vectors, vectors), F32)] * 2
        + [pltpu.VMEM((PIECES, group, rows // PIECES), F32), pltpu.SemaphoreType.DMA((PIECES,))],
        compiler_params=params(LIMIT),
    )(current, gathered, *parts)


def solution(mesh):
    return jax.shard_map(
        per_device,
        mesh=mesh,
        in_specs=(
            P("col", "blk"),
            P("blk", None, None),
            P("blk", None, None),
            P("blk"),
            P("blk"),
            P("blk", None),
        ),
        out_specs=P("col", "blk"),
        check_vma=False,
    )
```

```python
import functools
import math

import jax
import jax.numpy as jnp
from jax import lax
from jax.experimental import pallas as pl
from jax.experimental.pallas import tpu as pltpu
from jax.sharding import PartitionSpec as P

LOC_RB = 2
STEPS = 4
UNROLL = 8
NEAR_UNROLL = 4
KEPT = 16
CHUNK = 4
MERGE = 16
TOP = 7.0
FINER = 16.0
SPLIT = float((1 << 20) + 1)
TINY = 1e-30
MIB = 1 << 20
LIMIT = 24

center = 1.25
half_width = 0.75

F32 = jnp.float32
BF16 = jnp.bfloat16
F8 = jnp.float8_e4m3fn
I32 = jnp.int32

VMEM = pl.BlockSpec(memory_space=pltpu.VMEM)
SMEM = pl.BlockSpec(memory_space=pltpu.SMEM)
ANY = pl.BlockSpec(memory_space=pl.ANY)

NT = (((1,), (1,)), ((), ()))
TN = (((0,), (0,)), ((), ()))


def sds(shape, dtype):
    return jax.ShapeDtypeStruct(shape, dtype)


def params(limit):
    return pltpu.CompilerParams(vmem_limit_bytes=limit * MIB)


def turn_rows(values):
    rows = values.shape[0]
    even = lax.broadcasted_iota(I32, values.shape, 0) % 2 == 0
    below = pltpu.roll(values, rows - 1, 0)
    above = pltpu.roll(values, 1, 0)
    return jnp.where(even, -below, above)


def turn_lanes(values):
    lanes = values.shape[1]
    even = lax.broadcasted_iota(I32, values.shape, 1) % 2 == 0
    after = pltpu.roll(values, lanes - 1, 1)
    before = pltpu.roll(values, 1, 1)
    return jnp.where(even, after, -before)


def tiles_kernel(
    near_count,
    rows_hbm,
    slots_hbm,
    real_hbm,
    imag_hbm,
    packed_hbm,
    kept_ref,
    scale_ref,
    plan_hbm,
    rows_ref,
    slots_ref,
    plan_ref,
    both_ref,
    small_ref,
    present_ref,
    table_ref,
    back_ref,
    done_ref,
    in_sems,
    out_sems,
    list_sems,
):
    kept = kept_ref.shape[0]
    tiles, order, _ = both_ref.shape
    rb_dev = present_ref.shape[0]
    slots = rb_dev + lax.axis_size("blk")
    chunks = tiles // CHUNK

    def copies(c):
        at = pl.ds(c * CHUNK, CHUNK)
        return (
            pltpu.make_async_copy(real_hbm.at[at], both_ref.at[at, :, 0:order], in_sems.at[c, 0]),
            pltpu.make_async_copy(imag_hbm.at[at], both_ref.at[at, :, order : 2 * order], in_sems.at[c, 1]),
        )

    def leave(e):
        return pltpu.make_async_copy(small_ref.at[e], packed_hbm.at[e], out_sems.at[e])

    lists = (
        pltpu.make_async_copy(rows_hbm, rows_ref, list_sems.at[0]),
        pltpu.make_async_copy(slots_hbm, slots_ref, list_sems.at[1]),
    )
    for copy in lists:
        copy.start()
    for c in range(chunks):
        for copy in copies(c):
            copy.start()

    def clear(row, _):
        for slot in range(slots):
            table_ref[row * slots + slot] = -1
        return _

    lax.fori_loop(0, rb_dev, clear, 0)
    present_ref[...] = jnp.zeros_like(present_ref)
    for copy in lists:
        copy.wait()

    def link(c, entries):
        for t in [c * CHUNK + j for j in range(CHUNK)]:
            key = rows_ref[t] * slots + slots_ref[t]
            seen = table_ref[key]
            before = seen & 255
            length = seen >> 8
            joins = (seen >= 0) & (length < MERGE)
            back_ref[t] = jnp.where(joins, before, -1)
            done_ref[t] = 1
            done_ref[jnp.where(joins, before, tiles)] = 0
            table_ref[key] = t | (jnp.where(joins, length + 1, 1) << 8)
            entries = entries + jnp.where(joins, 0, 1)
        return entries

    entries = lax.fori_loop(near_count // CHUNK, chunks, link, 0)

    def fill(ref, e, t):
        for at in [slice(q, q + 128) for q in range(0, 2 * order, 128)]:
            ref[e, at] = jnp.zeros((128, order), F8) if t is None else both_ref[t, :, at].astype(F8).T

    def put(e, t):
        @pl.when(e < kept)
        def _():
            fill(kept_ref, e, t)

        @pl.when(e >= kept)
        def _():
            fill(small_ref, e - kept, t)
            leave(e - kept).start()

    def count(t):
        row = rows_ref[t]
        for at in [slice(q, q + order // 4) for q in range(0, order, order // 4)]:
            counted = both_ref[t, at, :order] + jnp.abs(both_ref[t, at, order:])
            present_ref[row, at] = present_ref[row, at] + counted

    def one(t, listed):
        count(t)
        closes = done_ref[t]

        @pl.when(closes == 1)
        def _():
            def add(prior):
                both_ref[t] = both_ref[t] + both_ref[prior]
                return back_ref[prior]

            lax.while_loop(lambda prior: prior >= 0, add, back_ref[t])
            put(listed, t)
            place = (slots_ref[t] - rb_dev) ^ central(slots - rb_dev)
            plan_ref[listed] = rows_ref[t] | (place << 8)

        return listed + closes

    def near_chunk(c, carry):
        for copy in copies(c):
            copy.wait()
        for j in range(CHUNK):
            count(c * CHUNK + j)
        return carry

    def far_chunk(c, listed):
        for copy in copies(c):
            copy.wait()
        for j in range(CHUNK):
            listed = one(c * CHUNK + j, listed)
        return listed

    short = (UNROLL - entries % UNROLL) % UNROLL
    for j in range(UNROLL - 1):

        @pl.when(j < short)
        def _():
            put(entries + j, None)
            plan_ref[entries + j] = (slots - rb_dev) << 8

    every = entries + short
    plan_ref[tiles] = every // UNROLL
    lax.fori_loop(0, near_count // CHUNK, near_chunk, 0)
    lax.fori_loop(near_count // CHUNK, chunks, far_chunk, 0)
    plan_copy = pltpu.make_async_copy(plan_ref, plan_hbm, list_sems.at[2])
    plan_copy.start()

    ones = jnp.ones((8, order), BF16)
    for r in range(rb_dev):
        degree = lax.dot_general(ones, present_ref[r], NT, preferred_element_type=F32)
        scale_ref[:, r * order : (r + 1) * order] = 1.0 / jnp.sqrt(jnp.maximum(degree, 1.0))

    def left(e, _):
        leave(e - kept).wait()
        return _

    lax.fori_loop(kept, every, left, 0)
    plan_copy.wait()


def in_hbm(x):
    return pltpu.with_memory_space_constraint(x, pltpu.HBM)


def tiles_call(rows, slots, real, imag, rb_dev, near_count):
    tiles, order, _ = real.shape
    nblk = lax.axis_size("blk")
    return pl.pallas_call(
        functools.partial(tiles_kernel, near_count),
        name="tiles",
        out_shape=(
            pltpu.HBM((tiles - near_count - KEPT, 2 * order, order), F8),
            pltpu.VMEM((KEPT, 2 * order, order), F8),
            sds((8, rb_dev * order), F32),
            pltpu.HBM((tiles + 32,), I32),
        ),
        in_specs=[ANY] * 4,
        out_specs=(ANY, VMEM, VMEM, ANY),
        scratch_shapes=[
            pltpu.SMEM((tiles,), I32),
            pltpu.SMEM((tiles,), I32),
            pltpu.SMEM((tiles + 32,), I32),
            pltpu.VMEM((tiles, order, 2 * order), BF16),
            pltpu.VMEM((tiles - near_count - KEPT, 2 * order, order), F8),
            pltpu.VMEM((rb_dev, order, order), BF16),
            pltpu.SMEM((rb_dev * (rb_dev + nblk),), I32),
            pltpu.SMEM((tiles,), I32),
            pltpu.SMEM((tiles + 1,), I32),
            pltpu.SemaphoreType.DMA((tiles // CHUNK, 2)),
            pltpu.SemaphoreType.DMA((tiles,)),
            pltpu.SemaphoreType.DMA((3,)),
        ],
        compiler_params=params(48),
        cost_estimate=pl.CostEstimate(flops=1 << 28, bytes_accessed=2 * real.size * 2, transcendentals=0),
    )(in_hbm(rows), in_hbm(slots), in_hbm(real), in_hbm(imag))


def rounded_block(field, scale_ref, r, order):
    at = slice(r * order, (r + 1) * order)
    return (field[:, at] * scale_ref[0:1, at]).astype(BF16)


def send_picked(wanted_ref, sent_ref, out_hbm, sems):
    me = lax.axis_index("blk")
    copies = [
        pltpu.make_async_copy(sent_ref.at[wanted_ref[i, 0, me]], out_hbm.at[i], sems.at[i])
        for i in range(out_hbm.shape[0])
    ]
    for copy in copies:
        copy.start()
    for copy in copies:
        copy.wait()


def spread_kernel(picks_hbm, out_hbm, sems):
    copies = [pltpu.make_async_copy(picks_hbm, out_hbm.at[i], sems.at[i]) for i in range(out_hbm.shape[0])]
    for copy in copies:
        copy.start()
    for copy in copies:
        copy.wait()


def first_kernel(y_ref, scale_ref, wanted_ref, out_hbm, sent_ref, out_sems):
    for r in range(sent_ref.shape[0]):
        sent_ref[r] = rounded_block(y_ref, scale_ref, r, sent_ref.shape[2])
    send_picked(wanted_ref, sent_ref, out_hbm, out_sems)


def load_groups(packed_hbm, tiles_ref, sems, count):
    def copy(g):
        at = pl.ds(g * UNROLL, UNROLL)
        return pltpu.make_async_copy(packed_hbm.at[at], tiles_ref.at[at], sems.at[g])

    def begin(g, _):
        copy(g).start()
        return _

    lax.fori_loop(0, count, begin, 0)
    return copy


def split_sources(count, source, x_ref):
    _, rows, width = x_ref.shape
    group, order = rows // 2, width // 2
    most = jnp.zeros((group, order), F32)
    for p in range(count):
        most = jnp.maximum(most, jnp.abs(source(p).astype(F32)))
    most = jnp.broadcast_to(jnp.max(most, axis=1, keepdims=True), (group, 128))
    most = jnp.maximum(jnp.maximum(most, jnp.abs(turn_rows(most))), TINY)
    power = jnp.floor(jnp.log2(most))
    size = jnp.exp2(power - TOP)
    inverse = jnp.exp2(TOP - power)[:, 0:1]
    for p in range(count):
        scaled = source(p).astype(F32) * inverse
        far = scaled * SPLIT
        high = far - (far - scaled)
        low = (scaled - high) * FINER
        for k, part in enumerate((high, low)):
            at = slice(k * group, (k + 1) * group)
            x_ref[p, at, :order] = part.astype(F8)
            x_ref[p, at, order:] = turn_rows(part).astype(F8)
    x_ref[count] = jnp.zeros_like(x_ref[count])
    return size[:, 0:1]


def multiply(plan_ref, lo, hi, tile, load, acc_ref):
    def group(g, _):
        done = []
        for j in range(UNROLL):
            code = plan_ref[g * UNROLL + j]
            product = jnp.dot(load(code >> 8), tile(g, j), preferred_element_type=F32)
            done.append((code & 255, product))
        for row, product in done:
            acc_ref[row] = acc_ref[row] + product
        return _

    lax.fori_loop(lo, hi, group, 0)


def collect(acc, size):
    group = size.shape[0]
    return (acc[:group] + acc[group:] * (1.0 / FINER)) * size


def near_kernel(
    step, rows_ref, slots_ref, real_hbm, imag_hbm, scale_ref, now_ref, before_ref, base_ref, tiles_ref, x_ref, acc_ref, sems
):
    rb_dev, _, order = x_ref.shape
    groups = sems.shape[0]

    def copies(g):
        at = pl.ds(g * NEAR_UNROLL, NEAR_UNROLL)
        return [
            pltpu.make_async_copy(hbm.at[at], tiles_ref.at[i, at], sems.at[g, i])
            for i, hbm in enumerate((real_hbm, imag_hbm))
        ]

    for g in range(groups):
        for copy in copies(g):
            copy.start()
    acc_ref[...] = jnp.zeros_like(acc_ref)
    for r in range(rb_dev):
        x_ref[r] = rounded_block(now_ref, scale_ref, r, order)

    def group(g, _):
        for copy in copies(g):
            copy.wait()
        done = []
        for t in [g * NEAR_UNROLL + j for j in range(NEAR_UNROLL)]:
            x = x_ref[slots_ref[t]]
            done.append([lax.dot_general(x, tiles_ref[i, t], NT, preferred_element_type=F32) for i in range(2)])
        for j, products in enumerate(done):
            row = rows_ref[g * NEAR_UNROLL + j]
            for i, product in enumerate(products):
                acc_ref[i, row] = acc_ref[i, row] + product
        return _

    lax.fori_loop(0, groups, group, 0)
    for r in range(rb_dev):
        at = slice(r * order, (r + 1) * order)
        applied = scale_ref[0:1, at] * (acc_ref[0, r] + turn_rows(acc_ref[1, r]))
        moved = ((1.0 - center) * now_ref[:, at] - applied) / half_width
        base_ref[:, at] = moved if step == 0 else 2.0 * moved - before_ref[:, at]


def step_kernel(step, plan_ref, wanted_ref, packed_hbm, kept_ref, scale_ref, base_ref, arrived_ref, *refs):
    last = step == STEPS - 1
    next_ref = refs[0]
    if not last:
        out_hbm, sent_ref, out_sems = refs[1:4]
    tiles_ref, x_ref, acc_ref, sems = refs[-4:]
    rb_dev, _, order = acc_ref.shape
    stay = KEPT // UNROLL
    groups = plan_ref[plan_ref.shape[0] - 32]
    copy = load_groups(packed_hbm, tiles_ref, sems, groups - stay)
    acc_ref[...] = jnp.zeros_like(acc_ref)
    size = split_sources(arrived_ref.shape[0], lambda p: arrived_ref[p], x_ref)
    size = size * ((1.0 if step == 0 else 2.0) / half_width)

    def loaded(g, j):
        if j == 0:
            copy(g - stay).wait()
        return tiles_ref[(g - stay) * UNROLL + j]

    def load(place):
        return x_ref[place]

    multiply(plan_ref, 0, jnp.minimum(stay, groups), lambda g, j: kept_ref[g * UNROLL + j], load, acc_ref)
    multiply(plan_ref, stay, groups, loaded, load, acc_ref)
    for r in range(rb_dev):
        at = slice(r * order, (r + 1) * order)
        scale = scale_ref[0:1, at]
        following = base_ref[:, at] - scale * collect(acc_ref[r], size)
        next_ref[:, at] = following
        if not last:
            sent_ref[r] = (following * scale).astype(BF16)
    if not last:
        send_picked(wanted_ref, sent_ref, out_hbm, out_sems)


def all_rows(own_ref, arrived, all_ref):
    c = lax.axis_index("col")
    all_ref[c] = own_ref[...].astype(BF16)
    for s, ref in enumerate(arrived, 1):
        all_ref[c ^ s] = ref[...]
    n, group, rows = all_ref.shape
    return all_ref[...].reshape(n * group, rows)


def gram_kernel(own_ref, *refs):
    arrived, (gram_ref, all_ref, full_ref) = refs[:-3], refs[-3:]
    rows = all_rows(own_ref, arrived, all_ref)
    full_ref[...] = lax.dot_general(rows, rows, NT, preferred_element_type=F32)
    half = gram_ref.shape[0]
    even = full_ref[pl.ds(0, half, stride=2), :]
    odd = full_ref[pl.ds(1, half, stride=2), :]
    gram_ref[...] = even + turn_lanes(odd)


PANEL = 64
PIECES = 4
SUB = 8


def eliminate(a, m, top):
    shape = a[0].shape
    here = lax.broadcasted_iota(I32, shape, 0)
    pivots = [None] * len(a)

    def column(rows, lane):
        return jnp.broadcast_to(rows[:, lane : lane + 1], shape)

    for step in range(0, len(a) * SUB, 4):
        own, k = divmod(step, SUB)
        head = [column(a[own], top + step + i) for i in range(4)]
        p, q = head[0][k : k + 1, :], head[2][k + 2 : k + 3, :]
        u, v = head[2][k : k + 1, :], head[3][k : k + 1, :]
        single = 1.0 / p
        det = p * q - (u * u + v * v)
        both = 1.0 / det
        pq, ub, vb, pb = q * both, u * both, v * both, p * both
        second = (here == k + 2) | (here == k + 3)
        last = det * single
        pivot = jnp.where(second, last, jnp.broadcast_to(p, shape))
        pivots[own] = pivot if k == 0 else jnp.where(here < k, pivots[own], pivot)
        rows = [[x[own][k + i : k + i + 1, :] for i in range(4)] for x in (a, m)]
        for g in range(own, len(a)):
            w = head if g == own else [column(a[g], top + step + i) for i in range(4)]
            c = [
                w[0] * pq - w[2] * ub - w[3] * vb,
                w[1] * pq + w[2] * vb - w[3] * ub,
                w[2] * pb - w[0] * ub + w[1] * vb,
                w[3] * pb - w[0] * vb - w[1] * ub,
            ]
            if g == own:
                below = here > k + 3
                c = [jnp.where(below, x, 0.0) for x in c]
                c[0] = jnp.where(second, w[0] * single, c[0])
                c[1] = jnp.where(second, w[1] * single, c[1])
            a[g], m[g] = (
                x[g] - (c[0] * r[0] + c[1] * r[1] + c[2] * r[2] + c[3] * r[3]) for x, r in zip((a, m), rows)
            )
    roots = [lax.rsqrt(x) for x in pivots]
    return [x * r for x, r in zip(a, roots)], [x * r for x, r in zip(m, roots)]


def factor_kernel(nodes, own_ref, all_ref, *refs):
    parts, (out_hbm, work_ref, inverse_ref, piece_ref, sems) = refs[:-5], refs[-5:]
    group = own_ref.shape[0]
    order = work_ref.shape[0]
    total = parts[0][...]
    for part in parts[1:]:
        total = total + part[...]
    half = total.shape[0]
    work_ref[pl.ds(0, half, stride=2), :] = total
    work_ref[pl.ds(1, half, stride=2), :] = -turn_lanes(total)
    row_at = lax.broadcasted_iota(I32, (order, order), 0)
    lane_at = lax.broadcasted_iota(I32, (order, order), 1)
    inverse_ref[...] = (row_at == lane_at).astype(F32)
    for top in range(0, order, PANEL):
        tops = range(top, top + PANEL, SUB)
        a, m = ([ref[r : r + SUB, :] for r in tops] for ref in (work_ref, inverse_ref))
        a, m = eliminate(a, m, top)
        a, m = jnp.concatenate(a, axis=0), jnp.concatenate(m, axis=0)
        inverse_ref[top : top + PANEL, :] = m
        rest = top + PANEL
        if rest < order:
            update = lax.dot_general(
                a, jnp.concatenate([a, m], axis=1), TN, precision=lax.Precision.HIGHEST, preferred_element_type=F32
            )
            work_ref[rest:, :] = work_ref[rest:, :] - update[rest:, :order]
            inverse_ref[rest:, :] = inverse_ref[rest:, :] - update[rest:, order:]
    c = lax.axis_index("col")
    mine = inverse_ref[pl.ds(pl.multiple_of(c * group, group), group), :]
    mine = mine * math.sqrt(nodes)
    high = mine.astype(BF16)
    low = (mine - high.astype(F32)).astype(BF16)
    own_lanes = (
        lax.broadcasted_iota(I32, (order, group), 0)
        == lax.broadcasted_iota(I32, (order, group), 1) + c * group
    ).astype(BF16)
    square = jnp.dot(high, own_lanes, preferred_element_type=F32).astype(BF16)
    left = jnp.concatenate([high, low], axis=0)
    width = own_ref.shape[1] // PIECES
    copies = []
    for i in range(PIECES):
        at = slice(i * width, (i + 1) * width)
        rows = all_ref[:, :, at].reshape(order, width)
        both = jnp.dot(left, rows, preferred_element_type=F32)
        own = own_ref[:, at]
        lost = (own - own.astype(BF16).astype(F32)).astype(BF16)
        piece_ref[i] = both[:group] + both[group:] + jnp.dot(square, lost, preferred_element_type=F32)
        copies.append(pltpu.make_async_copy(piece_ref.at[i], out_hbm.at[:, at], sems.at[i]))
        copies[-1].start()
    for copy in copies:
        copy.wait()


def central(nblk):
    return nblk // 4


def exchange(x):
    nblk = lax.axis_size("blk")
    group = [i ^ central(nblk) for i in range(nblk)]
    return lax.all_to_all(x, "blk", split_axis=0, concat_axis=0, tiled=True, axis_index_groups=[group])


def to_partner(x, axis, mask):
    n = lax.axis_size(axis)
    return lax.ppermute(x, axis, [(i, i ^ mask) for i in range(n)])


def sum_parts(part, nblk):
    wide = 1
    while 4 * wide < nblk:
        part = part + to_partner(part, "blk", wide)
        wide *= 2
    return [part] + [to_partner(part, "blk", s * wide) for s in range(1, nblk // wide)]


def per_device(y_start, tile_real, tile_imag, tile_rows, tile_slots, fetch_pick):
    group, rows = y_start.shape
    tiles, order, _ = tile_real.shape
    rb_dev = rows // order
    nblk = lax.axis_size("blk")
    ncol = lax.axis_size("col")
    near_count = LOC_RB * rb_dev
    asked = pl.pallas_call(
        spread_kernel,
        name="spread",
        out_shape=pltpu.HBM((nblk, 1, nblk), I32),
        in_specs=[ANY],
        out_specs=ANY,
        scratch_shapes=[pltpu.SemaphoreType.DMA((nblk,))],
        compiler_params=params(LIMIT),
    )(in_hbm(fetch_pick))
    wanted = exchange(asked)
    packed, kept, scale, plan = tiles_call(tile_rows, tile_slots, tile_real, tile_imag, rb_dev, near_count)

    out_blocks = pltpu.HBM((nblk, group, order), BF16)
    sent_scratch = [pltpu.VMEM((rb_dev, group, order), BF16), pltpu.SemaphoreType.DMA((nblk,))]
    blocks = pl.pallas_call(
        first_kernel,
        name="first",
        out_shape=out_blocks,
        in_specs=[VMEM, VMEM, SMEM],
        out_specs=ANY,
        scratch_shapes=sent_scratch,
        compiler_params=params(LIMIT),
    )(y_start, scale, wanted)

    vectors_here = sds((group, rows), F32)
    previous, current = y_start, y_start
    for step in range(STEPS):
        arrived = exchange(blocks)
        base = pl.pallas_call(
            functools.partial(near_kernel, step),
            name="near",
            out_shape=vectors_here,
            in_specs=[SMEM, SMEM, ANY, ANY] + [VMEM] * 3,
            out_specs=VMEM,
            scratch_shapes=[
                pltpu.VMEM((2, near_count, order, order), BF16),
                pltpu.VMEM((rb_dev, group, order), BF16),
                pltpu.VMEM((2, rb_dev, group, order), F32),
                pltpu.SemaphoreType.DMA((near_count // NEAR_UNROLL, 2)),
            ],
            compiler_params=params(LIMIT),
            cost_estimate=pl.CostEstimate(flops=1 << 28, bytes_accessed=1 << 21, transcendentals=0),
        )(in_hbm(tile_rows), in_hbm(tile_slots), in_hbm(tile_real), in_hbm(tile_imag), scale, current, previous)
        last = step == STEPS - 1
        out = pl.pallas_call(
            functools.partial(step_kernel, step),
            name="step",
            out_shape=[vectors_here] if last else [vectors_here, out_blocks],
            in_specs=[SMEM, SMEM, ANY] + [VMEM] * 4,
            out_specs=[VMEM] if last else [VMEM, ANY],
            scratch_shapes=([] if last else sent_scratch)
            + [
                pltpu.VMEM(packed.shape, F8),
                pltpu.VMEM((nblk + 1, 2 * group, 2 * order), F8),
                pltpu.VMEM((rb_dev, 2 * group, order), F32),
                pltpu.SemaphoreType.DMA((packed.shape[0] // UNROLL,)),
            ],
            compiler_params=params(LIMIT),
        )(in_hbm(plan), wanted, in_hbm(packed), pltpu.with_memory_space_constraint(kept, pltpu.VMEM), scale, base, arrived)
        previous, current = current, out[0]
        if not last:
            blocks = out[1]

    rounded = current.astype(BF16)
    if ncol == 4:
        beside, across = to_partner(rounded, "col", 1), to_partner(rounded, "col", 2)
        others = [beside, across, to_partner(across, "col", 1)]
    else:
        others = [to_partner(rounded, "col", s) for s in range(1, ncol)]
    vectors = group * ncol
    part, gathered = pl.pallas_call(
        gram_kernel,
        name="gram",
        out_shape=(sds((vectors // 2, vectors), F32), sds((ncol, group, rows), BF16)),
        in_specs=[VMEM] * (1 + len(others)),
        out_specs=(VMEM, VMEM),
        scratch_shapes=[pltpu.VMEM((vectors, vectors), F32)],
        compiler_params=params(LIMIT),
    )(current, *others)
    parts = sum_parts(part, nblk)
    return pl.pallas_call(
        functools.partial(factor_kernel, rows * nblk),
        name="factor",
        out_shape=pltpu.HBM((group, rows), F32),
        in_specs=[VMEM] * (2 + len(parts)),
        out_specs=ANY,
        scratch_shapes=[pltpu.VMEM((vectors, vectors), F32)] * 2
        + [pltpu.VMEM((PIECES, group, rows // PIECES), F32), pltpu.SemaphoreType.DMA((PIECES,))],
        compiler_params=params(LIMIT),
    )(current, gathered, *parts)


def solution(mesh):
    return jax.shard_map(
        per_device,
        mesh=mesh,
        in_specs=(
            P("col", "blk"),
            P("blk", None, None),
            P("blk", None, None),
            P("blk"),
            P("blk"),
            P("blk", None),
        ),
        out_specs=P("col", "blk"),
        check_vma=False,
    )
```

```python
import functools
import math

import jax
import jax.numpy as jnp
from jax import lax
from jax.experimental import pallas as pl
from jax.experimental.pallas import tpu as pltpu
from jax.sharding import PartitionSpec as P

LOC_RB = 2
STEPS = 4
UNROLL = 8
NEAR_UNROLL = 4
KEPT = 16
CHUNK = 4
MERGE = 16
TOP = 7.0
FINER = 16.0
SPLIT = float((1 << 20) + 1)
TINY = 1e-30
MIB = 1 << 20
LIMIT = 24

center = 1.25
half_width = 0.75

F32 = jnp.float32
BF16 = jnp.bfloat16
F8 = jnp.float8_e4m3fn
I32 = jnp.int32

VMEM = pl.BlockSpec(memory_space=pltpu.VMEM)
SMEM = pl.BlockSpec(memory_space=pltpu.SMEM)
ANY = pl.BlockSpec(memory_space=pl.ANY)

NT = (((1,), (1,)), ((), ()))
TN = (((0,), (0,)), ((), ()))


def sds(shape, dtype):
    return jax.ShapeDtypeStruct(shape, dtype)


def params(limit):
    return pltpu.CompilerParams(vmem_limit_bytes=limit * MIB)


def turn_rows(values):
    rows = values.shape[0]
    even = lax.broadcasted_iota(I32, values.shape, 0) % 2 == 0
    below = pltpu.roll(values, rows - 1, 0)
    above = pltpu.roll(values, 1, 0)
    return jnp.where(even, -below, above)


def turn_lanes(values):
    lanes = values.shape[1]
    even = lax.broadcasted_iota(I32, values.shape, 1) % 2 == 0
    after = pltpu.roll(values, lanes - 1, 1)
    before = pltpu.roll(values, 1, 1)
    return jnp.where(even, after, -before)


def tiles_kernel(
    near_count,
    rows_hbm,
    slots_hbm,
    real_hbm,
    imag_hbm,
    packed_hbm,
    kept_ref,
    scale_ref,
    plan_hbm,
    rows_ref,
    slots_ref,
    plan_ref,
    both_ref,
    small_ref,
    present_ref,
    table_ref,
    back_ref,
    done_ref,
    in_sems,
    out_sems,
    list_sems,
):
    kept = kept_ref.shape[0]
    tiles, order, _ = both_ref.shape
    rb_dev = present_ref.shape[0]
    slots = rb_dev + lax.axis_size("blk")
    chunks = tiles // CHUNK

    def copies(c):
        at = pl.ds(c * CHUNK, CHUNK)
        return (
            pltpu.make_async_copy(real_hbm.at[at], both_ref.at[at, :, 0:order], in_sems.at[c, 0]),
            pltpu.make_async_copy(imag_hbm.at[at], both_ref.at[at, :, order : 2 * order], in_sems.at[c, 1]),
        )

    def leave(e):
        return pltpu.make_async_copy(small_ref.at[e], packed_hbm.at[e], out_sems.at[e])

    lists = (
        pltpu.make_async_copy(rows_hbm, rows_ref, list_sems.at[0]),
        pltpu.make_async_copy(slots_hbm, slots_ref, list_sems.at[1]),
    )
    for copy in lists:
        copy.start()
    for c in range(chunks):
        for copy in copies(c):
            copy.start()

    def clear(row, _):
        for slot in range(slots):
            table_ref[row * slots + slot] = -1
        return _

    lax.fori_loop(0, rb_dev, clear, 0)
    present_ref[...] = jnp.zeros_like(present_ref)
    for copy in lists:
        copy.wait()

    def link(c, entries):
        for t in [c * CHUNK + j for j in range(CHUNK)]:
            key = rows_ref[t] * slots + slots_ref[t]
            seen = table_ref[key]
            before = seen & 255
            length = seen >> 8
            joins = (seen >= 0) & (length < MERGE)
            back_ref[t] = jnp.where(joins, before, -1)
            done_ref[t] = 1
            done_ref[jnp.where(joins, before, tiles)] = 0
            table_ref[key] = t | (jnp.where(joins, length + 1, 1) << 8)
            entries = entries + jnp.where(joins, 0, 1)
        return entries

    entries = lax.fori_loop(near_count // CHUNK, chunks, link, 0)

    def fill(ref, e, t):
        for at in [slice(q, q + 128) for q in range(0, 2 * order, 128)]:
            ref[e, at] = jnp.zeros((128, order), F8) if t is None else both_ref[t, :, at].astype(F8).T

    def put(e, t):
        @pl.when(e < kept)
        def _():
            fill(kept_ref, e, t)

        @pl.when(e >= kept)
        def _():
            fill(small_ref, e - kept, t)
            leave(e - kept).start()

    def count(t):
        row = rows_ref[t]
        for at in [slice(q, q + order // 4) for q in range(0, order, order // 4)]:
            counted = both_ref[t, at, :order] + jnp.abs(both_ref[t, at, order:])
            present_ref[row, at] = present_ref[row, at] + counted

    def one(t, listed):
        count(t)
        closes = done_ref[t]

        @pl.when(closes == 1)
        def _():
            def add(prior):
                both_ref[t] = both_ref[t] + both_ref[prior]
                return back_ref[prior]

            lax.while_loop(lambda prior: prior >= 0, add, back_ref[t])
            put(listed, t)
            place = (slots_ref[t] - rb_dev) ^ central(slots - rb_dev)
            plan_ref[listed] = rows_ref[t] | (place << 8)

        return listed + closes

    def near_chunk(c, carry):
        for copy in copies(c):
            copy.wait()
        for j in range(CHUNK):
            count(c * CHUNK + j)
        return carry

    def far_chunk(c, listed):
        for copy in copies(c):
            copy.wait()
        for j in range(CHUNK):
            listed = one(c * CHUNK + j, listed)
        return listed

    short = (UNROLL - entries % UNROLL) % UNROLL
    for j in range(UNROLL - 1):

        @pl.when(j < short)
        def _():
            put(entries + j, None)
            plan_ref[entries + j] = (slots - rb_dev) << 8

    every = entries + short
    plan_ref[tiles] = every // UNROLL
    lax.fori_loop(0, near_count // CHUNK, near_chunk, 0)
    lax.fori_loop(near_count // CHUNK, chunks, far_chunk, 0)
    plan_copy = pltpu.make_async_copy(plan_ref, plan_hbm, list_sems.at[2])
    plan_copy.start()

    ones = jnp.ones((8, order), BF16)
    for r in range(rb_dev):
        degree = lax.dot_general(ones, present_ref[r], NT, preferred_element_type=F32)
        scale_ref[:, r * order : (r + 1) * order] = 1.0 / jnp.sqrt(jnp.maximum(degree, 1.0))

    def left(e, _):
        leave(e - kept).wait()
        return _

    lax.fori_loop(kept, every, left, 0)
    plan_copy.wait()


def in_hbm(x):
    return pltpu.with_memory_space_constraint(x, pltpu.HBM)


def tiles_call(rows, slots, real, imag, rb_dev, near_count):
    tiles, order, _ = real.shape
    nblk = lax.axis_size("blk")
    return pl.pallas_call(
        functools.partial(tiles_kernel, near_count),
        name="tiles",
        out_shape=(
            pltpu.HBM((tiles - near_count - KEPT, 2 * order, order), F8),
            pltpu.VMEM((KEPT, 2 * order, order), F8),
            sds((8, rb_dev * order), F32),
            pltpu.HBM((tiles + 32,), I32),
        ),
        in_specs=[ANY] * 4,
        out_specs=(ANY, VMEM, VMEM, ANY),
        scratch_shapes=[
            pltpu.SMEM((tiles,), I32),
            pltpu.SMEM((tiles,), I32),
            pltpu.SMEM((tiles + 32,), I32),
            pltpu.VMEM((tiles, order, 2 * order), BF16),
            pltpu.VMEM((tiles - near_count - KEPT, 2 * order, order), F8),
            pltpu.VMEM((rb_dev, order, order), BF16),
            pltpu.SMEM((rb_dev * (rb_dev + nblk),), I32),
            pltpu.SMEM((tiles,), I32),
            pltpu.SMEM((tiles + 1,), I32),
            pltpu.SemaphoreType.DMA((tiles // CHUNK, 2)),
            pltpu.SemaphoreType.DMA((tiles,)),
            pltpu.SemaphoreType.DMA((3,)),
        ],
        compiler_params=params(48),
        cost_estimate=pl.CostEstimate(flops=1 << 28, bytes_accessed=2 * real.size * 2, transcendentals=0),
    )(in_hbm(rows), in_hbm(slots), in_hbm(real), in_hbm(imag))


def rounded_block(field, scale_ref, r, order):
    at = slice(r * order, (r + 1) * order)
    return (field[:, at] * scale_ref[0:1, at]).astype(BF16)


def send_picked(wanted_ref, sent_ref, out_hbm, sems):
    me = lax.axis_index("blk")
    copies = [
        pltpu.make_async_copy(sent_ref.at[wanted_ref[i, 0, me]], out_hbm.at[i], sems.at[i])
        for i in range(out_hbm.shape[0])
    ]
    for copy in copies:
        copy.start()
    for copy in copies:
        copy.wait()


def first_kernel(y_ref, scale_ref, wanted_ref, out_hbm, sent_ref, out_sems):
    for r in range(sent_ref.shape[0]):
        sent_ref[r] = rounded_block(y_ref, scale_ref, r, sent_ref.shape[2])
    send_picked(wanted_ref, sent_ref, out_hbm, out_sems)


def load_groups(packed_hbm, tiles_ref, sems, count):
    def copy(g):
        at = pl.ds(g * UNROLL, UNROLL)
        return pltpu.make_async_copy(packed_hbm.at[at], tiles_ref.at[at], sems.at[g])

    def begin(g, _):
        copy(g).start()
        return _

    lax.fori_loop(0, count, begin, 0)
    return copy


def split_sources(count, source, x_ref):
    _, rows, width = x_ref.shape
    group, order = rows // 2, width // 2
    most = jnp.zeros((group, order), F32)
    for p in range(count):
        most = jnp.maximum(most, jnp.abs(source(p).astype(F32)))
    most = jnp.broadcast_to(jnp.max(most, axis=1, keepdims=True), (group, 128))
    most = jnp.maximum(jnp.maximum(most, jnp.abs(turn_rows(most))), TINY)
    power = jnp.floor(jnp.log2(most))
    size = jnp.exp2(power - TOP)
    inverse = jnp.exp2(TOP - power)[:, 0:1]
    for p in range(count):
        scaled = source(p).astype(F32) * inverse
        far = scaled * SPLIT
        high = far - (far - scaled)
        low = (scaled - high) * FINER
        for k, part in enumerate((high, low)):
            at = slice(k * group, (k + 1) * group)
            x_ref[p, at, :order] = part.astype(F8)
            x_ref[p, at, order:] = turn_rows(part).astype(F8)
    x_ref[count] = jnp.zeros_like(x_ref[count])
    return size[:, 0:1]


def multiply(plan_ref, lo, hi, tile, load, acc_ref):
    def group(g, _):
        done = []
        for j in range(UNROLL):
            code = plan_ref[g * UNROLL + j]
            product = jnp.dot(load(code >> 8), tile(g, j), preferred_element_type=F32)
            done.append((code & 255, product))
        for row, product in done:
            acc_ref[row] = acc_ref[row] + product
        return _

    lax.fori_loop(lo, hi, group, 0)


def collect(acc, size):
    group = size.shape[0]
    return (acc[:group] + acc[group:] * (1.0 / FINER)) * size


def near_kernel(
    step, rows_ref, slots_ref, real_hbm, imag_hbm, scale_ref, now_ref, before_ref, base_ref, tiles_ref, x_ref, acc_ref, sems
):
    rb_dev, _, order = x_ref.shape
    groups = sems.shape[0]

    def copies(g):
        at = pl.ds(g * NEAR_UNROLL, NEAR_UNROLL)
        return [
            pltpu.make_async_copy(hbm.at[at], tiles_ref.at[i, at], sems.at[g, i])
            for i, hbm in enumerate((real_hbm, imag_hbm))
        ]

    for g in range(groups):
        for copy in copies(g):
            copy.start()
    acc_ref[...] = jnp.zeros_like(acc_ref)
    for r in range(rb_dev):
        x_ref[r] = rounded_block(now_ref, scale_ref, r, order)

    def group(g, _):
        for copy in copies(g):
            copy.wait()
        done = []
        for t in [g * NEAR_UNROLL + j for j in range(NEAR_UNROLL)]:
            x = x_ref[slots_ref[t]]
            done.append([lax.dot_general(x, tiles_ref[i, t], NT, preferred_element_type=F32) for i in range(2)])
        for j, products in enumerate(done):
            row = rows_ref[g * NEAR_UNROLL + j]
            for i, product in enumerate(products):
                acc_ref[i, row] = acc_ref[i, row] + product
        return _

    lax.fori_loop(0, groups, group, 0)
    for r in range(rb_dev):
        at = slice(r * order, (r + 1) * order)
        applied = scale_ref[0:1, at] * (acc_ref[0, r] + turn_rows(acc_ref[1, r]))
        moved = ((1.0 - center) * now_ref[:, at] - applied) / half_width
        base_ref[:, at] = moved if step == 0 else 2.0 * moved - before_ref[:, at]


def step_kernel(step, plan_ref, wanted_ref, packed_hbm, kept_ref, scale_ref, base_ref, arrived_ref, *refs):
    last = step == STEPS - 1
    next_ref = refs[0]
    if not last:
        out_hbm, sent_ref, out_sems = refs[1:4]
    tiles_ref, x_ref, acc_ref, sems = refs[-4:]
    rb_dev, _, order = acc_ref.shape
    stay = KEPT // UNROLL
    groups = plan_ref[plan_ref.shape[0] - 32]
    copy = load_groups(packed_hbm, tiles_ref, sems, groups - stay)
    acc_ref[...] = jnp.zeros_like(acc_ref)
    size = split_sources(arrived_ref.shape[0], lambda p: arrived_ref[p], x_ref)
    size = size * ((1.0 if step == 0 else 2.0) / half_width)

    def loaded(g, j):
        if j == 0:
            copy(g - stay).wait()
        return tiles_ref[(g - stay) * UNROLL + j]

    def load(place):
        return x_ref[place]

    multiply(plan_ref, 0, jnp.minimum(stay, groups), lambda g, j: kept_ref[g * UNROLL + j], load, acc_ref)
    multiply(plan_ref, stay, groups, loaded, load, acc_ref)
    for r in range(rb_dev):
        at = slice(r * order, (r + 1) * order)
        scale = scale_ref[0:1, at]
        following = base_ref[:, at] - scale * collect(acc_ref[r], size)
        next_ref[:, at] = following
        if not last:
            sent_ref[r] = (following * scale).astype(BF16)
    if not last:
        send_picked(wanted_ref, sent_ref, out_hbm, out_sems)


def all_rows(own_ref, arrived, all_ref):
    c = lax.axis_index("col")
    all_ref[c] = own_ref[...].astype(BF16)
    for s, ref in enumerate(arrived, 1):
        all_ref[c ^ s] = ref[...]
    n, group, rows = all_ref.shape
    return all_ref[...].reshape(n * group, rows)


def gram_kernel(own_ref, *refs):
    arrived, (gram_ref, all_ref, full_ref) = refs[:-3], refs[-3:]
    rows = all_rows(own_ref, arrived, all_ref)
    full_ref[...] = lax.dot_general(rows, rows, NT, preferred_element_type=F32)
    half = gram_ref.shape[0]
    even = full_ref[pl.ds(0, half, stride=2), :]
    odd = full_ref[pl.ds(1, half, stride=2), :]
    gram_ref[...] = even + turn_lanes(odd)


PANEL = 64
PIECES = 4
SUB = 8


def eliminate(a, m, top):
    shape = a[0].shape
    here = lax.broadcasted_iota(I32, shape, 0)
    pivots = [None] * len(a)

    def column(rows, lane):
        return jnp.broadcast_to(rows[:, lane : lane + 1], shape)

    for step in range(0, len(a) * SUB, 4):
        own, k = divmod(step, SUB)
        head = [column(a[own], top + step + i) for i in range(4)]
        p, q = head[0][k : k + 1, :], head[2][k + 2 : k + 3, :]
        u, v = head[2][k : k + 1, :], head[3][k : k + 1, :]
        single = 1.0 / p
        det = p * q - (u * u + v * v)
        both = 1.0 / det
        pq, ub, vb, pb = q * both, u * both, v * both, p * both
        second = (here == k + 2) | (here == k + 3)
        last = det * single
        pivot = jnp.where(second, last, jnp.broadcast_to(p, shape))
        pivots[own] = pivot if k == 0 else jnp.where(here < k, pivots[own], pivot)
        rows = [[x[own][k + i : k + i + 1, :] for i in range(4)] for x in (a, m)]
        for g in range(own, len(a)):
            w = head if g == own else [column(a[g], top + step + i) for i in range(4)]
            c = [
                w[0] * pq - w[2] * ub - w[3] * vb,
                w[1] * pq + w[2] * vb - w[3] * ub,
                w[2] * pb - w[0] * ub + w[1] * vb,
                w[3] * pb - w[0] * vb - w[1] * ub,
            ]
            if g == own:
                below = here > k + 3
                c = [jnp.where(below, x, 0.0) for x in c]
                c[0] = jnp.where(second, w[0] * single, c[0])
                c[1] = jnp.where(second, w[1] * single, c[1])
            a[g], m[g] = (
                x[g] - (c[0] * r[0] + c[1] * r[1] + c[2] * r[2] + c[3] * r[3]) for x, r in zip((a, m), rows)
            )
    roots = [lax.rsqrt(x) for x in pivots]
    return [x * r for x, r in zip(a, roots)], [x * r for x, r in zip(m, roots)]


def factor_kernel(nodes, own_ref, all_ref, *refs):
    parts, (out_hbm, work_ref, inverse_ref, piece_ref, sems) = refs[:-5], refs[-5:]
    group = own_ref.shape[0]
    order = work_ref.shape[0]
    total = parts[0][...]
    for part in parts[1:]:
        total = total + part[...]
    half = total.shape[0]
    work_ref[pl.ds(0, half, stride=2), :] = total
    work_ref[pl.ds(1, half, stride=2), :] = -turn_lanes(total)
    row_at = lax.broadcasted_iota(I32, (order, order), 0)
    lane_at = lax.broadcasted_iota(I32, (order, order), 1)
    inverse_ref[...] = (row_at == lane_at).astype(F32)
    for top in range(0, order, PANEL):
        tops = range(top, top + PANEL, SUB)
        a, m = ([ref[r : r + SUB, :] for r in tops] for ref in (work_ref, inverse_ref))
        a, m = eliminate(a, m, top)
        a, m = jnp.concatenate(a, axis=0), jnp.concatenate(m, axis=0)
        inverse_ref[top : top + PANEL, :] = m
        rest = top + PANEL
        if rest < order:
            update = lax.dot_general(
                a, jnp.concatenate([a, m], axis=1), TN, precision=lax.Precision.HIGHEST, preferred_element_type=F32
            )
            work_ref[rest:, :] = work_ref[rest:, :] - update[rest:, :order]
            inverse_ref[rest:, :] = inverse_ref[rest:, :] - update[rest:, order:]
    c = lax.axis_index("col")
    mine = inverse_ref[pl.ds(pl.multiple_of(c * group, group), group), :]
    mine = mine * math.sqrt(nodes)
    high = mine.astype(BF16)
    low = (mine - high.astype(F32)).astype(BF16)
    own_lanes = (
        lax.broadcasted_iota(I32, (order, group), 0)
        == lax.broadcasted_iota(I32, (order, group), 1) + c * group
    ).astype(BF16)
    square = jnp.dot(high, own_lanes, preferred_element_type=F32).astype(BF16)
    left = jnp.concatenate([high, low], axis=0)
    width = own_ref.shape[1] // PIECES
    copies = []
    for i in range(PIECES):
        at = slice(i * width, (i + 1) * width)
        rows = all_ref[:, :, at].reshape(order, width)
        both = jnp.dot(left, rows, preferred_element_type=F32)
        own = own_ref[:, at]
        lost = (own - own.astype(BF16).astype(F32)).astype(BF16)
        piece_ref[i] = both[:group] + both[group:] + jnp.dot(square, lost, preferred_element_type=F32)
        copies.append(pltpu.make_async_copy(piece_ref.at[i], out_hbm.at[:, at], sems.at[i]))
        copies[-1].start()
    for copy in copies:
        copy.wait()


def central(nblk):
    return nblk // 2 + nblk // 8


def exchange(x):
    nblk = lax.axis_size("blk")
    group = [i ^ central(nblk) for i in range(nblk)]
    return lax.all_to_all(x, "blk", split_axis=0, concat_axis=0, tiled=True, axis_index_groups=[group])


def to_partner(x, axis, mask):
    n = lax.axis_size(axis)
    return lax.ppermute(x, axis, [(i, i ^ mask) for i in range(n)])


def sum_parts(part, nblk):
    wide = 1
    while 4 * wide < nblk:
        part = part + to_partner(part, "blk", wide)
        wide *= 2
    return [part] + [to_partner(part, "blk", s * wide) for s in range(1, nblk // wide)]


def per_device(y_start, tile_real, tile_imag, tile_rows, tile_slots, fetch_pick):
    group, rows = y_start.shape
    tiles, order, _ = tile_real.shape
    rb_dev = rows // order
    nblk = lax.axis_size("blk")
    ncol = lax.axis_size("col")
    near_count = LOC_RB * rb_dev
    wanted = exchange(jnp.broadcast_to(fetch_pick[None], (nblk, 1, nblk)))
    packed, kept, scale, plan = tiles_call(tile_rows, tile_slots, tile_real, tile_imag, rb_dev, near_count)

    out_blocks = pltpu.HBM((nblk, group, order), BF16)
    sent_scratch = [pltpu.VMEM((rb_dev, group, order), BF16), pltpu.SemaphoreType.DMA((nblk,))]
    blocks = pl.pallas_call(
        first_kernel,
        name="first",
        out_shape=out_blocks,
        in_specs=[VMEM, VMEM, SMEM],
        out_specs=ANY,
        scratch_shapes=sent_scratch,
        compiler_params=params(LIMIT),
    )(y_start, scale, wanted)

    vectors_here = sds((group, rows), F32)
    previous, current = y_start, y_start
    for step in range(STEPS):
        arrived = exchange(blocks)
        base = pl.pallas_call(
            functools.partial(near_kernel, step),
            name="near",
            out_shape=vectors_here,
            in_specs=[SMEM, SMEM, ANY, ANY] + [VMEM] * 3,
            out_specs=VMEM,
            scratch_shapes=[
                pltpu.VMEM((2, near_count, order, order), BF16),
                pltpu.VMEM((rb_dev, group, order), BF16),
                pltpu.VMEM((2, rb_dev, group, order), F32),
                pltpu.SemaphoreType.DMA((near_count // NEAR_UNROLL, 2)),
            ],
            compiler_params=params(LIMIT),
            cost_estimate=pl.CostEstimate(flops=1 << 28, bytes_accessed=1 << 21, transcendentals=0),
        )(in_hbm(tile_rows), in_hbm(tile_slots), in_hbm(tile_real), in_hbm(tile_imag), scale, current, previous)
        last = step == STEPS - 1
        out = pl.pallas_call(
            functools.partial(step_kernel, step),
            name="step",
            out_shape=[vectors_here] if last else [vectors_here, out_blocks],
            in_specs=[SMEM, SMEM, ANY] + [VMEM] * 4,
            out_specs=[VMEM] if last else [VMEM, ANY],
            scratch_shapes=([] if last else sent_scratch)
            + [
                pltpu.VMEM(packed.shape, F8),
                pltpu.VMEM((nblk + 1, 2 * group, 2 * order), F8),
                pltpu.VMEM((rb_dev, 2 * group, order), F32),
                pltpu.SemaphoreType.DMA((packed.shape[0] // UNROLL,)),
            ],
            compiler_params=params(LIMIT),
        )(in_hbm(plan), wanted, in_hbm(packed), pltpu.with_memory_space_constraint(kept, pltpu.VMEM), scale, base, arrived)
        previous, current = current, out[0]
        if not last:
            blocks = out[1]

    rounded = current.astype(BF16)
    if ncol == 4:
        beside, across = to_partner(rounded, "col", 1), to_partner(rounded, "col", 2)
        others = [beside, across, to_partner(across, "col", 1)]
    else:
        others = [to_partner(rounded, "col", s) for s in range(1, ncol)]
    vectors = group * ncol
    part, gathered = pl.pallas_call(
        gram_kernel,
        name="gram",
        out_shape=(sds((vectors // 2, vectors), F32), sds((ncol, group, rows), BF16)),
        in_specs=[VMEM] * (1 + len(others)),
        out_specs=(VMEM, VMEM),
        scratch_shapes=[pltpu.VMEM((vectors, vectors), F32)],
        compiler_params=params(LIMIT),
    )(current, *others)
    parts = sum_parts(part, nblk)
    return pl.pallas_call(
        functools.partial(factor_kernel, rows * nblk),
        name="factor",
        out_shape=pltpu.HBM((group, rows), F32),
        in_specs=[VMEM] * (2 + len(parts)),
        out_specs=ANY,
        scratch_shapes=[pltpu.VMEM((vectors, vectors), F32)] * 2
        + [pltpu.VMEM((PIECES, group, rows // PIECES), F32), pltpu.SemaphoreType.DMA((PIECES,))],
        compiler_params=params(LIMIT),
    )(current, gathered, *parts)


def solution(mesh):
    return jax.shard_map(
        per_device,
        mesh=mesh,
        in_specs=(
            P("col", "blk"),
            P("blk", None, None),
            P("blk", None, None),
            P("blk"),
            P("blk"),
            P("blk", None),
        ),
        out_specs=P("col", "blk"),
        check_vma=False,
    )
```

```python
import functools
import math

import jax
import jax.numpy as jnp
from jax import lax
from jax.experimental import pallas as pl
from jax.experimental.pallas import tpu as pltpu
from jax.sharding import PartitionSpec as P

LOC_RB = 2
STEPS = 4
UNROLL = 8
NEAR_UNROLL = 4
KEPT = 16
CHUNK = 4
MERGE = 16
TOP = 7.0
FINER = 16.0
SPLIT = float((1 << 20) + 1)
TINY = 1e-30
MIB = 1 << 20
LIMIT = 24

center = 1.25
half_width = 0.75

F32 = jnp.float32
BF16 = jnp.bfloat16
F8 = jnp.float8_e4m3fn
I32 = jnp.int32

VMEM = pl.BlockSpec(memory_space=pltpu.VMEM)
SMEM = pl.BlockSpec(memory_space=pltpu.SMEM)
ANY = pl.BlockSpec(memory_space=pl.ANY)

NT = (((1,), (1,)), ((), ()))
TN = (((0,), (0,)), ((), ()))


def sds(shape, dtype):
    return jax.ShapeDtypeStruct(shape, dtype)


def params(limit):
    return pltpu.CompilerParams(vmem_limit_bytes=limit * MIB)


def turn_rows(values):
    rows = values.shape[0]
    even = lax.broadcasted_iota(I32, values.shape, 0) % 2 == 0
    below = pltpu.roll(values, rows - 1, 0)
    above = pltpu.roll(values, 1, 0)
    return jnp.where(even, -below, above)


def turn_lanes(values):
    lanes = values.shape[1]
    even = lax.broadcasted_iota(I32, values.shape, 1) % 2 == 0
    after = pltpu.roll(values, lanes - 1, 1)
    before = pltpu.roll(values, 1, 1)
    return jnp.where(even, after, -before)


def tiles_kernel(
    near_count,
    rows_hbm,
    slots_hbm,
    real_hbm,
    imag_hbm,
    packed_hbm,
    kept_ref,
    scale_ref,
    plan_hbm,
    rows_ref,
    slots_ref,
    plan_ref,
    both_ref,
    small_ref,
    present_ref,
    table_ref,
    back_ref,
    done_ref,
    in_sems,
    out_sems,
    list_sems,
):
    kept = kept_ref.shape[0]
    tiles, order, _ = both_ref.shape
    rb_dev = present_ref.shape[0]
    slots = rb_dev + lax.axis_size("blk")
    chunks = tiles // CHUNK

    def copies(c):
        at = pl.ds(c * CHUNK, CHUNK)
        return (
            pltpu.make_async_copy(real_hbm.at[at], both_ref.at[at, :, 0:order], in_sems.at[c, 0]),
            pltpu.make_async_copy(imag_hbm.at[at], both_ref.at[at, :, order : 2 * order], in_sems.at[c, 1]),
        )

    def leave(e):
        return pltpu.make_async_copy(small_ref.at[e], packed_hbm.at[e], out_sems.at[e])

    lists = (
        pltpu.make_async_copy(rows_hbm, rows_ref, list_sems.at[0]),
        pltpu.make_async_copy(slots_hbm, slots_ref, list_sems.at[1]),
    )
    for copy in lists:
        copy.start()
    first_far = near_count // CHUNK
    for c in [*range(first_far, chunks), *range(first_far)]:
        for copy in copies(c):
            copy.start()

    def clear(row, _):
        for slot in range(slots):
            table_ref[row * slots + slot] = -1
        return _

    lax.fori_loop(0, rb_dev, clear, 0)
    present_ref[...] = jnp.zeros_like(present_ref)
    for copy in lists:
        copy.wait()

    def link(c, entries):
        for t in [c * CHUNK + j for j in range(CHUNK)]:
            key = rows_ref[t] * slots + slots_ref[t]
            seen = table_ref[key]
            before = seen & 255
            length = seen >> 8
            joins = (seen >= 0) & (length < MERGE)
            back_ref[t] = jnp.where(joins, before, -1)
            done_ref[t] = 1
            done_ref[jnp.where(joins, before, tiles)] = 0
            table_ref[key] = t | (jnp.where(joins, length + 1, 1) << 8)
            entries = entries + jnp.where(joins, 0, 1)
        return entries

    entries = lax.fori_loop(first_far, chunks, link, 0)

    def fill(ref, e, t):
        for at in [slice(q, q + 128) for q in range(0, 2 * order, 128)]:
            ref[e, at] = jnp.zeros((128, order), F8) if t is None else both_ref[t, :, at].astype(F8).T

    def put(e, t):
        @pl.when(e < kept)
        def _():
            fill(kept_ref, e, t)

        @pl.when(e >= kept)
        def _():
            fill(small_ref, e - kept, t)
            leave(e - kept).start()

    def count(t):
        row = rows_ref[t]
        for at in [slice(q, q + order // 4) for q in range(0, order, order // 4)]:
            counted = both_ref[t, at, :order] + jnp.abs(both_ref[t, at, order:])
            present_ref[row, at] = present_ref[row, at] + counted

    def one(t, listed):
        count(t)
        closes = done_ref[t]

        @pl.when(closes == 1)
        def _():
            def add(prior):
                both_ref[t] = both_ref[t] + both_ref[prior]
                return back_ref[prior]

            lax.while_loop(lambda prior: prior >= 0, add, back_ref[t])
            put(listed, t)
            place = (slots_ref[t] - rb_dev) ^ central(slots - rb_dev)
            plan_ref[listed] = rows_ref[t] | (place << 8)

        return listed + closes

    def near_chunk(c, carry):
        for copy in copies(c):
            copy.wait()
        for j in range(CHUNK):
            count(c * CHUNK + j)
        return carry

    def far_chunk(c, listed):
        for copy in copies(c):
            copy.wait()
        for j in range(CHUNK):
            listed = one(c * CHUNK + j, listed)
        return listed

    short = (UNROLL - entries % UNROLL) % UNROLL
    for j in range(UNROLL - 1):

        @pl.when(j < short)
        def _():
            put(entries + j, None)
            plan_ref[entries + j] = (slots - rb_dev) << 8

    every = entries + short
    plan_ref[tiles] = every // UNROLL
    lax.fori_loop(first_far, chunks, far_chunk, 0)
    lax.fori_loop(0, first_far, near_chunk, 0)
    plan_copy = pltpu.make_async_copy(plan_ref, plan_hbm, list_sems.at[2])
    plan_copy.start()

    ones = jnp.ones((8, order), BF16)
    for r in range(rb_dev):
        degree = lax.dot_general(ones, present_ref[r], NT, preferred_element_type=F32)
        scale_ref[:, r * order : (r + 1) * order] = 1.0 / jnp.sqrt(jnp.maximum(degree, 1.0))

    def left(e, _):
        leave(e - kept).wait()
        return _

    lax.fori_loop(kept, every, left, 0)
    plan_copy.wait()


def in_hbm(x):
    return pltpu.with_memory_space_constraint(x, pltpu.HBM)


def tiles_call(rows, slots, real, imag, rb_dev, near_count):
    tiles, order, _ = real.shape
    nblk = lax.axis_size("blk")
    return pl.pallas_call(
        functools.partial(tiles_kernel, near_count),
        name="tiles",
        out_shape=(
            pltpu.HBM((tiles - near_count - KEPT, 2 * order, order), F8),
            pltpu.VMEM((KEPT, 2 * order, order), F8),
            sds((8, rb_dev * order), F32),
            pltpu.HBM((tiles + 32,), I32),
        ),
        in_specs=[ANY] * 4,
        out_specs=(ANY, VMEM, VMEM, ANY),
        scratch_shapes=[
            pltpu.SMEM((tiles,), I32),
            pltpu.SMEM((tiles,), I32),
            pltpu.SMEM((tiles + 32,), I32),
            pltpu.VMEM((tiles, order, 2 * order), BF16),
            pltpu.VMEM((tiles - near_count - KEPT, 2 * order, order), F8),
            pltpu.VMEM((rb_dev, order, order), BF16),
            pltpu.SMEM((rb_dev * (rb_dev + nblk),), I32),
            pltpu.SMEM((tiles,), I32),
            pltpu.SMEM((tiles + 1,), I32),
            pltpu.SemaphoreType.DMA((tiles // CHUNK, 2)),
            pltpu.SemaphoreType.DMA((tiles,)),
            pltpu.SemaphoreType.DMA((3,)),
        ],
        compiler_params=params(48),
        cost_estimate=pl.CostEstimate(flops=1 << 28, bytes_accessed=2 * real.size * 2, transcendentals=0),
    )(in_hbm(rows), in_hbm(slots), in_hbm(real), in_hbm(imag))


def rounded_block(field, scale_ref, r, order):
    at = slice(r * order, (r + 1) * order)
    return (field[:, at] * scale_ref[0:1, at]).astype(BF16)


def send_picked(wanted_ref, sent_ref, out_hbm, sems):
    me = lax.axis_index("blk")
    copies = [
        pltpu.make_async_copy(sent_ref.at[wanted_ref[i, 0, me]], out_hbm.at[i], sems.at[i])
        for i in range(out_hbm.shape[0])
    ]
    for copy in copies:
        copy.start()
    for copy in copies:
        copy.wait()


def first_kernel(y_ref, scale_ref, wanted_ref, out_hbm, sent_ref, out_sems):
    for r in range(sent_ref.shape[0]):
        sent_ref[r] = rounded_block(y_ref, scale_ref, r, sent_ref.shape[2])
    send_picked(wanted_ref, sent_ref, out_hbm, out_sems)


def load_groups(packed_hbm, tiles_ref, sems, count):
    def copy(g):
        at = pl.ds(g * UNROLL, UNROLL)
        return pltpu.make_async_copy(packed_hbm.at[at], tiles_ref.at[at], sems.at[g])

    def begin(g, _):
        copy(g).start()
        return _

    lax.fori_loop(0, count, begin, 0)
    return copy


def split_sources(count, source, x_ref):
    _, rows, width = x_ref.shape
    group, order = rows // 2, width // 2
    most = jnp.zeros((group, order), F32)
    for p in range(count):
        most = jnp.maximum(most, jnp.abs(source(p).astype(F32)))
    most = jnp.broadcast_to(jnp.max(most, axis=1, keepdims=True), (group, 128))
    most = jnp.maximum(jnp.maximum(most, jnp.abs(turn_rows(most))), TINY)
    power = jnp.floor(jnp.log2(most))
    size = jnp.exp2(power - TOP)
    inverse = jnp.exp2(TOP - power)[:, 0:1]
    for p in range(count):
        scaled = source(p).astype(F32) * inverse
        far = scaled * SPLIT
        high = far - (far - scaled)
        low = (scaled - high) * FINER
        for k, part in enumerate((high, low)):
            at = slice(k * group, (k + 1) * group)
            x_ref[p, at, :order] = part.astype(F8)
            x_ref[p, at, order:] = turn_rows(part).astype(F8)
    x_ref[count] = jnp.zeros_like(x_ref[count])
    return size[:, 0:1]


def multiply(plan_ref, lo, hi, tile, load, acc_ref):
    def group(g, _):
        done = []
        for j in range(UNROLL):
            code = plan_ref[g * UNROLL + j]
            product = jnp.dot(load(code >> 8), tile(g, j), preferred_element_type=F32)
            done.append((code & 255, product))
        for row, product in done:
            acc_ref[row] = acc_ref[row] + product
        return _

    lax.fori_loop(lo, hi, group, 0)


def collect(acc, size):
    group = size.shape[0]
    return (acc[:group] + acc[group:] * (1.0 / FINER)) * size


def near_kernel(
    step, rows_ref, slots_ref, real_hbm, imag_hbm, scale_ref, now_ref, before_ref, base_ref, tiles_ref, x_ref, acc_ref, sems
):
    rb_dev, _, order = x_ref.shape
    groups = sems.shape[0]

    def copies(g):
        at = pl.ds(g * NEAR_UNROLL, NEAR_UNROLL)
        return [
            pltpu.make_async_copy(hbm.at[at], tiles_ref.at[i, at], sems.at[g, i])
            for i, hbm in enumerate((real_hbm, imag_hbm))
        ]

    for g in range(groups):
        for copy in copies(g):
            copy.start()
    acc_ref[...] = jnp.zeros_like(acc_ref)
    for r in range(rb_dev):
        x_ref[r] = rounded_block(now_ref, scale_ref, r, order)

    def group(g, _):
        for copy in copies(g):
            copy.wait()
        done = []
        for t in [g * NEAR_UNROLL + j for j in range(NEAR_UNROLL)]:
            x = x_ref[slots_ref[t]]
            done.append([lax.dot_general(x, tiles_ref[i, t], NT, preferred_element_type=F32) for i in range(2)])
        for j, products in enumerate(done):
            row = rows_ref[g * NEAR_UNROLL + j]
            for i, product in enumerate(products):
                acc_ref[i, row] = acc_ref[i, row] + product
        return _

    lax.fori_loop(0, groups, group, 0)
    for r in range(rb_dev):
        at = slice(r * order, (r + 1) * order)
        applied = scale_ref[0:1, at] * (acc_ref[0, r] + turn_rows(acc_ref[1, r]))
        moved = ((1.0 - center) * now_ref[:, at] - applied) / half_width
        base_ref[:, at] = moved if step == 0 else 2.0 * moved - before_ref[:, at]


def step_kernel(step, plan_ref, wanted_ref, packed_hbm, kept_ref, scale_ref, base_ref, arrived_ref, *refs):
    last = step == STEPS - 1
    next_ref = refs[0]
    if not last:
        out_hbm, sent_ref, out_sems = refs[1:4]
    tiles_ref, x_ref, acc_ref, sems = refs[-4:]
    rb_dev, _, order = acc_ref.shape
    stay = KEPT // UNROLL
    groups = plan_ref[plan_ref.shape[0] - 32]
    copy = load_groups(packed_hbm, tiles_ref, sems, groups - stay)
    acc_ref[...] = jnp.zeros_like(acc_ref)
    size = split_sources(arrived_ref.shape[0], lambda p: arrived_ref[p], x_ref)
    size = size * ((1.0 if step == 0 else 2.0) / half_width)

    def loaded(g, j):
        if j == 0:
            copy(g - stay).wait()
        return tiles_ref[(g - stay) * UNROLL + j]

    def load(place):
        return x_ref[place]

    multiply(plan_ref, 0, jnp.minimum(stay, groups), lambda g, j: kept_ref[g * UNROLL + j], load, acc_ref)
    multiply(plan_ref, stay, groups, loaded, load, acc_ref)
    for r in range(rb_dev):
        at = slice(r * order, (r + 1) * order)
        scale = scale_ref[0:1, at]
        following = base_ref[:, at] - scale * collect(acc_ref[r], size)
        next_ref[:, at] = following
        if not last:
            sent_ref[r] = (following * scale).astype(BF16)
    if not last:
        send_picked(wanted_ref, sent_ref, out_hbm, out_sems)


def all_rows(own_ref, arrived, all_ref):
    c = lax.axis_index("col")
    all_ref[c] = own_ref[...].astype(BF16)
    for s, ref in enumerate(arrived, 1):
        all_ref[c ^ s] = ref[...]
    n, group, rows = all_ref.shape
    return all_ref[...].reshape(n * group, rows)


def gram_kernel(own_ref, *refs):
    arrived, (gram_ref, all_ref, full_ref) = refs[:-3], refs[-3:]
    rows = all_rows(own_ref, arrived, all_ref)
    full_ref[...] = lax.dot_general(rows, rows, NT, preferred_element_type=F32)
    half = gram_ref.shape[0]
    even = full_ref[pl.ds(0, half, stride=2), :]
    odd = full_ref[pl.ds(1, half, stride=2), :]
    gram_ref[...] = even + turn_lanes(odd)


PANEL = 64
PIECES = 4
SUB = 8


def eliminate(a, m, top):
    shape = a[0].shape
    here = lax.broadcasted_iota(I32, shape, 0)
    pivots = [None] * len(a)

    def column(rows, lane):
        return jnp.broadcast_to(rows[:, lane : lane + 1], shape)

    for step in range(0, len(a) * SUB, 4):
        own, k = divmod(step, SUB)
        head = [column(a[own], top + step + i) for i in range(4)]
        p, q = head[0][k : k + 1, :], head[2][k + 2 : k + 3, :]
        u, v = head[2][k : k + 1, :], head[3][k : k + 1, :]
        single = 1.0 / p
        det = p * q - (u * u + v * v)
        both = 1.0 / det
        pq, ub, vb, pb = q * both, u * both, v * both, p * both
        second = (here == k + 2) | (here == k + 3)
        last = det * single
        pivot = jnp.where(second, last, jnp.broadcast_to(p, shape))
        pivots[own] = pivot if k == 0 else jnp.where(here < k, pivots[own], pivot)
        rows = [[x[own][k + i : k + i + 1, :] for i in range(4)] for x in (a, m)]
        for g in range(own, len(a)):
            w = head if g == own else [column(a[g], top + step + i) for i in range(4)]
            c = [
                w[0] * pq - w[2] * ub - w[3] * vb,
                w[1] * pq + w[2] * vb - w[3] * ub,
                w[2] * pb - w[0] * ub + w[1] * vb,
                w[3] * pb - w[0] * vb - w[1] * ub,
            ]
            if g == own:
                below = here > k + 3
                c = [jnp.where(below, x, 0.0) for x in c]
                c[0] = jnp.where(second, w[0] * single, c[0])
                c[1] = jnp.where(second, w[1] * single, c[1])
            a[g], m[g] = (
                x[g] - (c[0] * r[0] + c[1] * r[1] + c[2] * r[2] + c[3] * r[3]) for x, r in zip((a, m), rows)
            )
    roots = [lax.rsqrt(x) for x in pivots]
    return [x * r for x, r in zip(a, roots)], [x * r for x, r in zip(m, roots)]


def factor_kernel(nodes, own_ref, all_ref, *refs):
    parts, (out_hbm, work_ref, inverse_ref, piece_ref, sems) = refs[:-5], refs[-5:]
    group = own_ref.shape[0]
    order = work_ref.shape[0]
    total = parts[0][...]
    for part in parts[1:]:
        total = total + part[...]
    half = total.shape[0]
    work_ref[pl.ds(0, half, stride=2), :] = total
    work_ref[pl.ds(1, half, stride=2), :] = -turn_lanes(total)
    row_at = lax.broadcasted_iota(I32, (order, order), 0)
    lane_at = lax.broadcasted_iota(I32, (order, order), 1)
    inverse_ref[...] = (row_at == lane_at).astype(F32)
    for top in range(0, order, PANEL):
        tops = range(top, top + PANEL, SUB)
        a, m = ([ref[r : r + SUB, :] for r in tops] for ref in (work_ref, inverse_ref))
        a, m = eliminate(a, m, top)
        a, m = jnp.concatenate(a, axis=0), jnp.concatenate(m, axis=0)
        inverse_ref[top : top + PANEL, :] = m
        rest = top + PANEL
        if rest < order:
            update = lax.dot_general(
                a, jnp.concatenate([a, m], axis=1), TN, precision=lax.Precision.HIGHEST, preferred_element_type=F32
            )
            work_ref[rest:, :] = work_ref[rest:, :] - update[rest:, :order]
            inverse_ref[rest:, :] = inverse_ref[rest:, :] - update[rest:, order:]
    c = lax.axis_index("col")
    mine = inverse_ref[pl.ds(pl.multiple_of(c * group, group), group), :]
    mine = mine * math.sqrt(nodes)
    high = mine.astype(BF16)
    low = (mine - high.astype(F32)).astype(BF16)
    own_lanes = (
        lax.broadcasted_iota(I32, (order, group), 0)
        == lax.broadcasted_iota(I32, (order, group), 1) + c * group
    ).astype(BF16)
    square = jnp.dot(high, own_lanes, preferred_element_type=F32).astype(BF16)
    left = jnp.concatenate([high, low], axis=0)
    width = own_ref.shape[1] // PIECES
    copies = []
    for i in range(PIECES):
        at = slice(i * width, (i + 1) * width)
        rows = all_ref[:, :, at].reshape(order, width)
        both = jnp.dot(left, rows, preferred_element_type=F32)
        own = own_ref[:, at]
        lost = (own - own.astype(BF16).astype(F32)).astype(BF16)
        piece_ref[i] = both[:group] + both[group:] + jnp.dot(square, lost, preferred_element_type=F32)
        copies.append(pltpu.make_async_copy(piece_ref.at[i], out_hbm.at[:, at], sems.at[i]))
        copies[-1].start()
    for copy in copies:
        copy.wait()


def central(nblk):
    return nblk // 2 + nblk // 8


def exchange(x):
    nblk = lax.axis_size("blk")
    group = [i ^ central(nblk) for i in range(nblk)]
    return lax.all_to_all(x, "blk", split_axis=0, concat_axis=0, tiled=True, axis_index_groups=[group])


def to_partner(x, axis, mask):
    n = lax.axis_size(axis)
    return lax.ppermute(x, axis, [(i, i ^ mask) for i in range(n)])


def sum_parts(part, nblk):
    wide = 1
    while 4 * wide < nblk:
        part = part + to_partner(part, "blk", wide)
        wide *= 2
    return [part] + [to_partner(part, "blk", s * wide) for s in range(1, nblk // wide)]


def per_device(y_start, tile_real, tile_imag, tile_rows, tile_slots, fetch_pick):
    group, rows = y_start.shape
    tiles, order, _ = tile_real.shape
    rb_dev = rows // order
    nblk = lax.axis_size("blk")
    ncol = lax.axis_size("col")
    near_count = LOC_RB * rb_dev
    wanted = exchange(jnp.broadcast_to(fetch_pick[None], (nblk, 1, nblk)))
    packed, kept, scale, plan = tiles_call(tile_rows, tile_slots, tile_real, tile_imag, rb_dev, near_count)

    out_blocks = pltpu.HBM((nblk, group, order), BF16)
    sent_scratch = [pltpu.VMEM((rb_dev, group, order), BF16), pltpu.SemaphoreType.DMA((nblk,))]
    blocks = pl.pallas_call(
        first_kernel,
        name="first",
        out_shape=out_blocks,
        in_specs=[VMEM, VMEM, SMEM],
        out_specs=ANY,
        scratch_shapes=sent_scratch,
        compiler_params=params(LIMIT),
    )(y_start, scale, wanted)

    vectors_here = sds((group, rows), F32)
    previous, current = y_start, y_start
    for step in range(STEPS):
        arrived = exchange(blocks)
        base = pl.pallas_call(
            functools.partial(near_kernel, step),
            name="near",
            out_shape=vectors_here,
            in_specs=[SMEM, SMEM, ANY, ANY] + [VMEM] * 3,
            out_specs=VMEM,
            scratch_shapes=[
                pltpu.VMEM((2, near_count, order, order), BF16),
                pltpu.VMEM((rb_dev, group, order), BF16),
                pltpu.VMEM((2, rb_dev, group, order), F32),
                pltpu.SemaphoreType.DMA((near_count // NEAR_UNROLL, 2)),
            ],
            compiler_params=params(LIMIT),
            cost_estimate=pl.CostEstimate(flops=1 << 28, bytes_accessed=1 << 21, transcendentals=0),
        )(in_hbm(tile_rows), in_hbm(tile_slots), in_hbm(tile_real), in_hbm(tile_imag), scale, current, previous)
        last = step == STEPS - 1
        out = pl.pallas_call(
            functools.partial(step_kernel, step),
            name="step",
            out_shape=[vectors_here] if last else [vectors_here, out_blocks],
            in_specs=[SMEM, SMEM, ANY] + [VMEM] * 4,
            out_specs=[VMEM] if last else [VMEM, ANY],
            scratch_shapes=([] if last else sent_scratch)
            + [
                pltpu.VMEM(packed.shape, F8),
                pltpu.VMEM((nblk + 1, 2 * group, 2 * order), F8),
                pltpu.VMEM((rb_dev, 2 * group, order), F32),
                pltpu.SemaphoreType.DMA((packed.shape[0] // UNROLL,)),
            ],
            compiler_params=params(LIMIT),
        )(in_hbm(plan), wanted, in_hbm(packed), pltpu.with_memory_space_constraint(kept, pltpu.VMEM), scale, base, arrived)
        previous, current = current, out[0]
        if not last:
            blocks = out[1]

    rounded = current.astype(BF16)
    if ncol == 4:
        beside, across = to_partner(rounded, "col", 1), to_partner(rounded, "col", 2)
        others = [beside, across, to_partner(across, "col", 1)]
    else:
        others = [to_partner(rounded, "col", s) for s in range(1, ncol)]
    vectors = group * ncol
    part, gathered = pl.pallas_call(
        gram_kernel,
        name="gram",
        out_shape=(sds((vectors // 2, vectors), F32), sds((ncol, group, rows), BF16)),
        in_specs=[VMEM] * (1 + len(others)),
        out_specs=(VMEM, VMEM),
        scratch_shapes=[pltpu.VMEM((vectors, vectors), F32)],
        compiler_params=params(LIMIT),
    )(current, *others)
    parts = sum_parts(part, nblk)
    return pl.pallas_call(
        functools.partial(factor_kernel, rows * nblk),
        name="factor",
        out_shape=pltpu.HBM((group, rows), F32),
        in_specs=[VMEM] * (2 + len(parts)),
        out_specs=ANY,
        scratch_shapes=[pltpu.VMEM((vectors, vectors), F32)] * 2
        + [pltpu.VMEM((PIECES, group, rows // PIECES), F32), pltpu.SemaphoreType.DMA((PIECES,))],
        compiler_params=params(LIMIT),
    )(current, gathered, *parts)


def solution(mesh):
    return jax.shard_map(
        per_device,
        mesh=mesh,
        in_specs=(
            P("col", "blk"),
            P("blk", None, None),
            P("blk", None, None),
            P("blk"),
            P("blk"),
            P("blk", None),
        ),
        out_specs=P("col", "blk"),
        check_vma=False,
    )
```

```python
import functools
import math

import jax
import jax.numpy as jnp
from jax import lax
from jax.experimental import pallas as pl
from jax.experimental.pallas import tpu as pltpu
from jax.sharding import PartitionSpec as P

LOC_RB = 2
STEPS = 4
UNROLL = 8
NEAR_UNROLL = 4
KEPT = 16
CHUNK = 4
MERGE = 16
TOP = 7.0
FINER = 16.0
SPLIT = float((1 << 20) + 1)
TINY = 1e-30
MIB = 1 << 20
LIMIT = 24

center = 1.25
half_width = 0.75

F32 = jnp.float32
BF16 = jnp.bfloat16
F8 = jnp.float8_e4m3fn
I32 = jnp.int32

VMEM = pl.BlockSpec(memory_space=pltpu.VMEM)
SMEM = pl.BlockSpec(memory_space=pltpu.SMEM)
ANY = pl.BlockSpec(memory_space=pl.ANY)

NT = (((1,), (1,)), ((), ()))
TN = (((0,), (0,)), ((), ()))


def sds(shape, dtype):
    return jax.ShapeDtypeStruct(shape, dtype)


def params(limit):
    return pltpu.CompilerParams(vmem_limit_bytes=limit * MIB)


def turn_rows(values):
    rows = values.shape[0]
    even = lax.broadcasted_iota(I32, values.shape, 0) % 2 == 0
    below = pltpu.roll(values, rows - 1, 0)
    above = pltpu.roll(values, 1, 0)
    return jnp.where(even, -below, above)


def turn_lanes(values):
    lanes = values.shape[1]
    even = lax.broadcasted_iota(I32, values.shape, 1) % 2 == 0
    after = pltpu.roll(values, lanes - 1, 1)
    before = pltpu.roll(values, 1, 1)
    return jnp.where(even, after, -before)


def tiles_kernel(
    near_count,
    rows_hbm,
    slots_hbm,
    real_hbm,
    imag_hbm,
    packed_hbm,
    kept_ref,
    scale_ref,
    plan_hbm,
    rows_ref,
    slots_ref,
    plan_ref,
    both_ref,
    small_ref,
    present_ref,
    table_ref,
    back_ref,
    done_ref,
    in_sems,
    out_sems,
    list_sems,
):
    kept = kept_ref.shape[0]
    tiles, order, _ = both_ref.shape
    rb_dev = present_ref.shape[0]
    slots = rb_dev + lax.axis_size("blk")
    chunks = tiles // CHUNK

    def copies(c):
        at = pl.ds(c * CHUNK, CHUNK)
        return (
            pltpu.make_async_copy(real_hbm.at[at], both_ref.at[at, :, 0:order], in_sems.at[c, 0]),
            pltpu.make_async_copy(imag_hbm.at[at], both_ref.at[at, :, order : 2 * order], in_sems.at[c, 1]),
        )

    def leave(e):
        return pltpu.make_async_copy(small_ref.at[e], packed_hbm.at[e], out_sems.at[e])

    lists = (
        pltpu.make_async_copy(rows_hbm, rows_ref, list_sems.at[0]),
        pltpu.make_async_copy(slots_hbm, slots_ref, list_sems.at[1]),
    )
    for copy in lists:
        copy.start()
    first_far = near_count // CHUNK
    for c in [*range(first_far, chunks), *range(first_far)]:
        for copy in copies(c):
            copy.start()

    def clear(row, _):
        for slot in range(slots):
            table_ref[row * slots + slot] = -1
        return _

    lax.fori_loop(0, rb_dev, clear, 0)
    present_ref[...] = jnp.zeros_like(present_ref)
    for copy in lists:
        copy.wait()

    def link(c, entries):
        for t in [c * CHUNK + j for j in range(CHUNK)]:
            key = rows_ref[t] * slots + slots_ref[t]
            seen = table_ref[key]
            before = seen & 255
            length = seen >> 8
            joins = (seen >= 0) & (length < MERGE)
            back_ref[t] = jnp.where(joins, before, -1)
            done_ref[t] = 1
            done_ref[jnp.where(joins, before, tiles)] = 0
            table_ref[key] = t | (jnp.where(joins, length + 1, 1) << 8)
            entries = entries + jnp.where(joins, 0, 1)
        return entries

    entries = lax.fori_loop(first_far, chunks, link, 0)

    def fill(ref, e, t):
        for at in [slice(q, q + 128) for q in range(0, 2 * order, 128)]:
            ref[e, at] = jnp.zeros((128, order), F8) if t is None else both_ref[t, :, at].astype(F8).T

    def put(e, t):
        @pl.when(e < kept)
        def _():
            fill(kept_ref, e, t)

        @pl.when(e >= kept)
        def _():
            fill(small_ref, e - kept, t)
            leave(e - kept).start()

    def count(t):
        row = rows_ref[t]
        for at in [slice(q, q + order // 4) for q in range(0, order, order // 4)]:
            counted = both_ref[t, at, :order] + jnp.abs(both_ref[t, at, order:])
            present_ref[row, at] = present_ref[row, at] + counted

    def one(t, listed):
        count(t)
        closes = done_ref[t]

        @pl.when(closes == 1)
        def _():
            def add(prior):
                both_ref[t] = both_ref[t] + both_ref[prior]
                return back_ref[prior]

            lax.while_loop(lambda prior: prior >= 0, add, back_ref[t])
            put(listed, t)
            place = (slots_ref[t] - rb_dev) ^ central(slots - rb_dev)
            plan_ref[listed] = rows_ref[t] | (place << 8)

        return listed + closes

    def near_chunk(c, carry):
        for copy in copies(c):
            copy.wait()
        for j in range(CHUNK):
            count(c * CHUNK + j)
        return carry

    def far_chunk(c, listed):
        for copy in copies(c):
            copy.wait()
        for j in range(CHUNK):
            listed = one(c * CHUNK + j, listed)
        return listed

    short = (UNROLL - entries % UNROLL) % UNROLL
    for j in range(UNROLL - 1):

        @pl.when(j < short)
        def _():
            put(entries + j, None)
            plan_ref[entries + j] = (slots - rb_dev) << 8

    every = entries + short
    plan_ref[tiles] = every // UNROLL
    lax.fori_loop(first_far, chunks, far_chunk, 0)
    lax.fori_loop(0, first_far, near_chunk, 0)
    plan_copy = pltpu.make_async_copy(plan_ref, plan_hbm, list_sems.at[2])
    plan_copy.start()

    ones = jnp.ones((8, order), BF16)
    for r in range(rb_dev):
        degree = lax.dot_general(ones, present_ref[r], NT, preferred_element_type=F32)
        scale_ref[:, r * order : (r + 1) * order] = 1.0 / jnp.sqrt(jnp.maximum(degree, 1.0))

    def left(e, _):
        leave(e - kept).wait()
        return _

    lax.fori_loop(kept, every, left, 0)
    plan_copy.wait()


def in_hbm(x):
    return pltpu.with_memory_space_constraint(x, pltpu.HBM)


def tiles_call(rows, slots, real, imag, rb_dev, near_count):
    tiles, order, _ = real.shape
    nblk = lax.axis_size("blk")
    return pl.pallas_call(
        functools.partial(tiles_kernel, near_count),
        name="tiles",
        out_shape=(
            pltpu.HBM((tiles - near_count - KEPT, 2 * order, order), F8),
            pltpu.VMEM((KEPT, 2 * order, order), F8),
            sds((8, rb_dev * order), F32),
            pltpu.HBM((tiles + 32,), I32),
        ),
        in_specs=[ANY] * 4,
        out_specs=(ANY, VMEM, VMEM, ANY),
        scratch_shapes=[
            pltpu.SMEM((tiles,), I32),
            pltpu.SMEM((tiles,), I32),
            pltpu.SMEM((tiles + 32,), I32),
            pltpu.VMEM((tiles, order, 2 * order), BF16),
            pltpu.VMEM((tiles - near_count - KEPT, 2 * order, order), F8),
            pltpu.VMEM((rb_dev, order, order), BF16),
            pltpu.SMEM((rb_dev * (rb_dev + nblk),), I32),
            pltpu.SMEM((tiles,), I32),
            pltpu.SMEM((tiles + 1,), I32),
            pltpu.SemaphoreType.DMA((tiles // CHUNK, 2)),
            pltpu.SemaphoreType.DMA((tiles,)),
            pltpu.SemaphoreType.DMA((3,)),
        ],
        compiler_params=params(48),
        cost_estimate=pl.CostEstimate(flops=1 << 28, bytes_accessed=2 * real.size * 2, transcendentals=0),
    )(in_hbm(rows), in_hbm(slots), in_hbm(real), in_hbm(imag))


def rounded_block(field, scale_ref, r, order):
    at = slice(r * order, (r + 1) * order)
    return (field[:, at] * scale_ref[0:1, at]).astype(BF16)


def send_picked(wanted_ref, sent_ref, out_hbm, sems):
    me = lax.axis_index("blk")
    copies = [
        pltpu.make_async_copy(sent_ref.at[wanted_ref[i, 0, me]], out_hbm.at[i], sems.at[i])
        for i in range(out_hbm.shape[0])
    ]
    for copy in copies:
        copy.start()
    for copy in copies:
        copy.wait()


def first_kernel(y_ref, scale_ref, wanted_ref, out_hbm, sent_ref, out_sems):
    for r in range(sent_ref.shape[0]):
        sent_ref[r] = rounded_block(y_ref, scale_ref, r, sent_ref.shape[2])
    send_picked(wanted_ref, sent_ref, out_hbm, out_sems)


def load_groups(packed_hbm, tiles_ref, sems, count):
    def copy(g):
        at = pl.ds(g * UNROLL, UNROLL)
        return pltpu.make_async_copy(packed_hbm.at[at], tiles_ref.at[at], sems.at[g])

    def begin(g, _):
        copy(g).start()
        return _

    lax.fori_loop(0, count, begin, 0)
    return copy


def split_sources(count, source, x_ref):
    _, rows, width = x_ref.shape
    group, order = rows // 2, width // 2
    most = jnp.zeros((group, order), F32)
    for p in range(count):
        most = jnp.maximum(most, jnp.abs(source(p).astype(F32)))
    most = jnp.broadcast_to(jnp.max(most, axis=1, keepdims=True), (group, 128))
    most = jnp.maximum(jnp.maximum(most, jnp.abs(turn_rows(most))), TINY)
    power = jnp.floor(jnp.log2(most))
    size = jnp.exp2(power - TOP)
    inverse = jnp.exp2(TOP - power)[:, 0:1]
    for p in range(count):
        scaled = source(p).astype(F32) * inverse
        far = scaled * SPLIT
        high = far - (far - scaled)
        low = (scaled - high) * FINER
        for k, part in enumerate((high, low)):
            at = slice(k * group, (k + 1) * group)
            x_ref[p, at, :order] = part.astype(F8)
            x_ref[p, at, order:] = turn_rows(part).astype(F8)
    x_ref[count] = jnp.zeros_like(x_ref[count])
    return size[:, 0:1]


def multiply(plan_ref, lo, hi, tile, load, acc_ref):
    def group(g, _):
        done = []
        for j in range(UNROLL):
            code = plan_ref[g * UNROLL + j]
            product = jnp.dot(load(code >> 8), tile(g, j), preferred_element_type=F32)
            done.append((code & 255, product))
        for row, product in done:
            acc_ref[row] = acc_ref[row] + product
        return _

    lax.fori_loop(lo, hi, group, 0)


def collect(acc, size):
    group = size.shape[0]
    return (acc[:group] + acc[group:] * (1.0 / FINER)) * size


def near_kernel(
    step, rows_ref, slots_ref, real_hbm, imag_hbm, scale_ref, now_ref, before_ref, base_ref, tiles_ref, x_ref, acc_ref, sems
):
    rb_dev, _, order = x_ref.shape
    groups = sems.shape[0]

    def copies(g):
        at = pl.ds(g * NEAR_UNROLL, NEAR_UNROLL)
        return [
            pltpu.make_async_copy(hbm.at[at], tiles_ref.at[i, at], sems.at[g, i])
            for i, hbm in enumerate((real_hbm, imag_hbm))
        ]

    for g in range(groups):
        for copy in copies(g):
            copy.start()
    acc_ref[...] = jnp.zeros_like(acc_ref)
    for r in range(rb_dev):
        x_ref[r] = rounded_block(now_ref, scale_ref, r, order)

    def group(g, _):
        for copy in copies(g):
            copy.wait()
        done = []
        for t in [g * NEAR_UNROLL + j for j in range(NEAR_UNROLL)]:
            x = x_ref[slots_ref[t]]
            done.append([lax.dot_general(x, tiles_ref[i, t], NT, preferred_element_type=F32) for i in range(2)])
        for j, products in enumerate(done):
            row = rows_ref[g * NEAR_UNROLL + j]
            for i, product in enumerate(products):
                acc_ref[i, row] = acc_ref[i, row] + product
        return _

    lax.fori_loop(0, groups, group, 0)
    for r in range(rb_dev):
        at = slice(r * order, (r + 1) * order)
        applied = scale_ref[0:1, at] * (acc_ref[0, r] + turn_rows(acc_ref[1, r]))
        moved = ((1.0 - center) * now_ref[:, at] - applied) / half_width
        base_ref[:, at] = moved if step == 0 else 2.0 * moved - before_ref[:, at]


def step_kernel(step, plan_ref, wanted_ref, packed_hbm, kept_ref, scale_ref, base_ref, arrived_ref, *refs):
    last = step == STEPS - 1
    next_ref = refs[0]
    if not last:
        out_hbm, sent_ref, out_sems = refs[1:4]
    tiles_ref, x_ref, acc_ref, sems = refs[-4:]
    rb_dev, _, order = acc_ref.shape
    stay = KEPT // UNROLL
    groups = plan_ref[plan_ref.shape[0] - 32]
    copy = load_groups(packed_hbm, tiles_ref, sems, groups - stay)
    acc_ref[...] = jnp.zeros_like(acc_ref)
    size = split_sources(arrived_ref.shape[0], lambda p: arrived_ref[p], x_ref)
    size = size * ((1.0 if step == 0 else 2.0) / half_width)

    def loaded(g, j):
        if j == 0:
            copy(g - stay).wait()
        return tiles_ref[(g - stay) * UNROLL + j]

    def load(place):
        return x_ref[place]

    multiply(plan_ref, 0, jnp.minimum(stay, groups), lambda g, j: kept_ref[g * UNROLL + j], load, acc_ref)
    multiply(plan_ref, stay, groups, loaded, load, acc_ref)
    for r in range(rb_dev):
        at = slice(r * order, (r + 1) * order)
        scale = scale_ref[0:1, at]
        following = base_ref[:, at] - scale * collect(acc_ref[r], size)
        next_ref[:, at] = following
        if not last:
            sent_ref[r] = (following * scale).astype(BF16)
    if not last:
        send_picked(wanted_ref, sent_ref, out_hbm, out_sems)


def all_rows(own_ref, arrived, all_ref):
    c = lax.axis_index("col")
    all_ref[c] = own_ref[...].astype(BF16)
    for s, ref in enumerate(arrived, 1):
        all_ref[c ^ s] = ref[...]
    n, group, rows = all_ref.shape
    return all_ref[...].reshape(n * group, rows)


def gram_kernel(own_ref, *refs):
    arrived, (gram_ref, all_ref, full_ref) = refs[:-3], refs[-3:]
    rows = all_rows(own_ref, arrived, all_ref)
    full_ref[...] = lax.dot_general(rows, rows, NT, preferred_element_type=F32)
    half = gram_ref.shape[0]
    even = full_ref[pl.ds(0, half, stride=2), :]
    odd = full_ref[pl.ds(1, half, stride=2), :]
    gram_ref[...] = even + turn_lanes(odd)


PANEL = 64
PIECES = 4
SUB = 8


def eliminate(a, m, top):
    shape = a[0].shape
    here = lax.broadcasted_iota(I32, shape, 0)
    pivots = [None] * len(a)

    def column(rows, lane):
        return jnp.broadcast_to(rows[:, lane : lane + 1], shape)

    for step in range(0, len(a) * SUB, 4):
        own, k = divmod(step, SUB)
        head = [column(a[own], top + step + i) for i in range(4)]
        p, q = head[0][k : k + 1, :], head[2][k + 2 : k + 3, :]
        u, v = head[2][k : k + 1, :], head[3][k : k + 1, :]
        single = 1.0 / p
        det = p * q - (u * u + v * v)
        both = 1.0 / det
        pq, ub, vb, pb = q * both, u * both, v * both, p * both
        second = (here == k + 2) | (here == k + 3)
        last = det * single
        pivot = jnp.where(second, last, jnp.broadcast_to(p, shape))
        pivots[own] = pivot if k == 0 else jnp.where(here < k, pivots[own], pivot)
        rows = [[x[own][k + i : k + i + 1, :] for i in range(4)] for x in (a, m)]
        for g in range(own, len(a)):
            w = head if g == own else [column(a[g], top + step + i) for i in range(4)]
            c = [
                w[0] * pq - w[2] * ub - w[3] * vb,
                w[1] * pq + w[2] * vb - w[3] * ub,
                w[2] * pb - w[0] * ub + w[1] * vb,
                w[3] * pb - w[0] * vb - w[1] * ub,
            ]
            if g == own:
                below = here > k + 3
                c = [jnp.where(below, x, 0.0) for x in c]
                c[0] = jnp.where(second, w[0] * single, c[0])
                c[1] = jnp.where(second, w[1] * single, c[1])
            a[g], m[g] = (
                x[g] - (c[0] * r[0] + c[1] * r[1] + c[2] * r[2] + c[3] * r[3]) for x, r in zip((a, m), rows)
            )
    roots = [lax.rsqrt(x) for x in pivots]
    return [x * r for x, r in zip(a, roots)], [x * r for x, r in zip(m, roots)]


def factor_kernel(nodes, own_ref, all_ref, *refs):
    parts, (out_hbm, work_ref, inverse_ref, piece_ref, sems) = refs[:-5], refs[-5:]
    group = own_ref.shape[0]
    order = work_ref.shape[0]
    total = parts[0][...]
    for part in parts[1:]:
        total = total + part[...]
    half = total.shape[0]
    work_ref[pl.ds(0, half, stride=2), :] = total
    work_ref[pl.ds(1, half, stride=2), :] = -turn_lanes(total)
    row_at = lax.broadcasted_iota(I32, (order, order), 0)
    lane_at = lax.broadcasted_iota(I32, (order, order), 1)
    inverse_ref[...] = (row_at == lane_at).astype(F32)
    for top in range(0, order, PANEL):
        tops = range(top, top + PANEL, SUB)
        a, m = ([ref[r : r + SUB, :] for r in tops] for ref in (work_ref, inverse_ref))
        a, m = eliminate(a, m, top)
        a, m = jnp.concatenate(a, axis=0), jnp.concatenate(m, axis=0)
        inverse_ref[top : top + PANEL, :] = m
        rest = top + PANEL
        if rest < order:
            update = lax.dot_general(
                a, jnp.concatenate([a, m], axis=1), TN, precision=lax.Precision.HIGHEST, preferred_element_type=F32
            )
            work_ref[rest:, :] = work_ref[rest:, :] - update[rest:, :order]
            inverse_ref[rest:, :] = inverse_ref[rest:, :] - update[rest:, order:]
    c = lax.axis_index("col")
    mine = inverse_ref[pl.ds(pl.multiple_of(c * group, group), group), :]
    mine = mine * math.sqrt(nodes)
    high = mine.astype(BF16)
    low = (mine - high.astype(F32)).astype(BF16)
    own_lanes = (
        lax.broadcasted_iota(I32, (order, group), 0)
        == lax.broadcasted_iota(I32, (order, group), 1) + c * group
    ).astype(BF16)
    square = jnp.dot(high, own_lanes, preferred_element_type=F32).astype(BF16)
    left = jnp.concatenate([high, low], axis=0)
    width = own_ref.shape[1] // PIECES
    copies = []
    for i in range(PIECES):
        at = slice(i * width, (i + 1) * width)
        rows = all_ref[:, :, at].reshape(order, width)
        both = jnp.dot(left, rows, preferred_element_type=F32)
        own = own_ref[:, at]
        lost = (own - own.astype(BF16).astype(F32)).astype(BF16)
        piece_ref[i] = both[:group] + both[group:] + jnp.dot(square, lost, preferred_element_type=F32)
        copies.append(pltpu.make_async_copy(piece_ref.at[i], out_hbm.at[:, at], sems.at[i]))
        copies[-1].start()
    for copy in copies:
        copy.wait()


def central(nblk):
    return nblk // 2


def exchange(x):
    nblk = lax.axis_size("blk")
    group = [i ^ central(nblk) for i in range(nblk)]
    return lax.all_to_all(x, "blk", split_axis=0, concat_axis=0, tiled=True, axis_index_groups=[group])


def to_partner(x, axis, mask):
    n = lax.axis_size(axis)
    return lax.ppermute(x, axis, [(i, i ^ mask) for i in range(n)])


def sum_parts(part, nblk):
    wide = 1
    while 4 * wide < nblk:
        part = part + to_partner(part, "blk", wide)
        wide *= 2
    return [part] + [to_partner(part, "blk", s * wide) for s in range(1, nblk // wide)]


def per_device(y_start, tile_real, tile_imag, tile_rows, tile_slots, fetch_pick):
    group, rows = y_start.shape
    tiles, order, _ = tile_real.shape
    rb_dev = rows // order
    nblk = lax.axis_size("blk")
    ncol = lax.axis_size("col")
    near_count = LOC_RB * rb_dev
    wanted = exchange(jnp.broadcast_to(fetch_pick[None], (nblk, 1, nblk)))
    packed, kept, scale, plan = tiles_call(tile_rows, tile_slots, tile_real, tile_imag, rb_dev, near_count)

    out_blocks = pltpu.HBM((nblk, group, order), BF16)
    sent_scratch = [pltpu.VMEM((rb_dev, group, order), BF16), pltpu.SemaphoreType.DMA((nblk,))]
    blocks = pl.pallas_call(
        first_kernel,
        name="first",
        out_shape=out_blocks,
        in_specs=[VMEM, VMEM, SMEM],
        out_specs=ANY,
        scratch_shapes=sent_scratch,
        compiler_params=params(LIMIT),
    )(y_start, scale, wanted)

    vectors_here = sds((group, rows), F32)
    previous, current = y_start, y_start
    for step in range(STEPS):
        arrived = exchange(blocks)
        base = pl.pallas_call(
            functools.partial(near_kernel, step),
            name="near",
            out_shape=vectors_here,
            in_specs=[SMEM, SMEM, ANY, ANY] + [VMEM] * 3,
            out_specs=VMEM,
            scratch_shapes=[
                pltpu.VMEM((2, near_count, order, order), BF16),
                pltpu.VMEM((rb_dev, group, order), BF16),
                pltpu.VMEM((2, rb_dev, group, order), F32),
                pltpu.SemaphoreType.DMA((near_count // NEAR_UNROLL, 2)),
            ],
            compiler_params=params(LIMIT),
            cost_estimate=pl.CostEstimate(flops=1 << 28, bytes_accessed=1 << 21, transcendentals=0),
        )(in_hbm(tile_rows), in_hbm(tile_slots), in_hbm(tile_real), in_hbm(tile_imag), scale, current, previous)
        last = step == STEPS - 1
        out = pl.pallas_call(
            functools.partial(step_kernel, step),
            name="step",
            out_shape=[vectors_here] if last else [vectors_here, out_blocks],
            in_specs=[SMEM, SMEM, ANY] + [VMEM] * 4,
            out_specs=[VMEM] if last else [VMEM, ANY],
            scratch_shapes=([] if last else sent_scratch)
            + [
                pltpu.VMEM(packed.shape, F8),
                pltpu.VMEM((nblk + 1, 2 * group, 2 * order), F8),
                pltpu.VMEM((rb_dev, 2 * group, order), F32),
                pltpu.SemaphoreType.DMA((packed.shape[0] // UNROLL,)),
            ],
            compiler_params=params(LIMIT),
        )(in_hbm(plan), wanted, in_hbm(packed), pltpu.with_memory_space_constraint(kept, pltpu.VMEM), scale, base, arrived)
        previous, current = current, out[0]
        if not last:
            blocks = out[1]

    rounded = current.astype(BF16)
    if ncol == 4:
        beside, across = to_partner(rounded, "col", 1), to_partner(rounded, "col", 2)
        others = [beside, across, to_partner(across, "col", 1)]
    else:
        others = [to_partner(rounded, "col", s) for s in range(1, ncol)]
    vectors = group * ncol
    part, gathered = pl.pallas_call(
        gram_kernel,
        name="gram",
        out_shape=(sds((vectors // 2, vectors), F32), sds((ncol, group, rows), BF16)),
        in_specs=[VMEM] * (1 + len(others)),
        out_specs=(VMEM, VMEM),
        scratch_shapes=[pltpu.VMEM((vectors, vectors), F32)],
        compiler_params=params(LIMIT),
    )(current, *others)
    parts = sum_parts(part, nblk)
    return pl.pallas_call(
        functools.partial(factor_kernel, rows * nblk),
        name="factor",
        out_shape=pltpu.HBM((group, rows), F32),
        in_specs=[VMEM] * (2 + len(parts)),
        out_specs=ANY,
        scratch_shapes=[pltpu.VMEM((vectors, vectors), F32)] * 2
        + [pltpu.VMEM((PIECES, group, rows // PIECES), F32), pltpu.SemaphoreType.DMA((PIECES,))],
        compiler_params=params(LIMIT),
    )(current, gathered, *parts)


def solution(mesh):
    return jax.shard_map(
        per_device,
        mesh=mesh,
        in_specs=(
            P("col", "blk"),
            P("blk", None, None),
            P("blk", None, None),
            P("blk"),
            P("blk"),
            P("blk", None),
        ),
        out_specs=P("col", "blk"),
        check_vma=False,
    )
```

```python
import functools
import math

import jax
import jax.numpy as jnp
from jax import lax
from jax.experimental import pallas as pl
from jax.experimental.pallas import tpu as pltpu
from jax.sharding import PartitionSpec as P

LOC_RB = 2
STEPS = 4
UNROLL = 8
NEAR_UNROLL = 8
KEPT = 16
CHUNK = 4
MERGE = 16
TOP = 7.0
FINER = 16.0
SPLIT = float((1 << 20) + 1)
TINY = 1e-30
MIB = 1 << 20
LIMIT = 24

center = 1.25
half_width = 0.75

F32 = jnp.float32
BF16 = jnp.bfloat16
F8 = jnp.float8_e4m3fn
I32 = jnp.int32

VMEM = pl.BlockSpec(memory_space=pltpu.VMEM)
SMEM = pl.BlockSpec(memory_space=pltpu.SMEM)
ANY = pl.BlockSpec(memory_space=pl.ANY)

NT = (((1,), (1,)), ((), ()))
TN = (((0,), (0,)), ((), ()))


def sds(shape, dtype):
    return jax.ShapeDtypeStruct(shape, dtype)


def params(limit):
    return pltpu.CompilerParams(vmem_limit_bytes=limit * MIB)


def turn_rows(values):
    rows = values.shape[0]
    even = lax.broadcasted_iota(I32, values.shape, 0) % 2 == 0
    below = pltpu.roll(values, rows - 1, 0)
    above = pltpu.roll(values, 1, 0)
    return jnp.where(even, -below, above)


def turn_lanes(values):
    lanes = values.shape[1]
    even = lax.broadcasted_iota(I32, values.shape, 1) % 2 == 0
    after = pltpu.roll(values, lanes - 1, 1)
    before = pltpu.roll(values, 1, 1)
    return jnp.where(even, after, -before)


def tiles_kernel(
    near_count,
    rows_hbm,
    slots_hbm,
    real_hbm,
    imag_hbm,
    packed_hbm,
    kept_ref,
    scale_ref,
    plan_hbm,
    rows_ref,
    slots_ref,
    plan_ref,
    both_ref,
    small_ref,
    present_ref,
    table_ref,
    back_ref,
    done_ref,
    in_sems,
    out_sems,
    list_sems,
):
    kept = kept_ref.shape[0]
    tiles, order, _ = both_ref.shape
    rb_dev = present_ref.shape[0]
    slots = rb_dev + lax.axis_size("blk")
    chunks = tiles // CHUNK

    def copies(c):
        at = pl.ds(c * CHUNK, CHUNK)
        return (
            pltpu.make_async_copy(real_hbm.at[at], both_ref.at[at, :, 0:order], in_sems.at[c, 0]),
            pltpu.make_async_copy(imag_hbm.at[at], both_ref.at[at, :, order : 2 * order], in_sems.at[c, 1]),
        )

    def leave(e):
        return pltpu.make_async_copy(small_ref.at[e], packed_hbm.at[e], out_sems.at[e])

    lists = (
        pltpu.make_async_copy(rows_hbm, rows_ref, list_sems.at[0]),
        pltpu.make_async_copy(slots_hbm, slots_ref, list_sems.at[1]),
    )
    for copy in lists:
        copy.start()
    first_far = near_count // CHUNK
    for c in [*range(first_far, chunks), *range(first_far)]:
        for copy in copies(c):
            copy.start()

    def clear(row, _):
        for slot in range(slots):
            table_ref[row * slots + slot] = -1
        return _

    lax.fori_loop(0, rb_dev, clear, 0)
    present_ref[...] = jnp.zeros_like(present_ref)
    for copy in lists:
        copy.wait()

    def link(c, entries):
        for t in [c * CHUNK + j for j in range(CHUNK)]:
            key = rows_ref[t] * slots + slots_ref[t]
            seen = table_ref[key]
            before = seen & 255
            length = seen >> 8
            joins = (seen >= 0) & (length < MERGE)
            back_ref[t] = jnp.where(joins, before, -1)
            done_ref[t] = 1
            done_ref[jnp.where(joins, before, tiles)] = 0
            table_ref[key] = t | (jnp.where(joins, length + 1, 1) << 8)
            entries = entries + jnp.where(joins, 0, 1)
        return entries

    entries = lax.fori_loop(first_far, chunks, link, 0)

    def fill(ref, e, t):
        for at in [slice(q, q + 128) for q in range(0, 2 * order, 128)]:
            ref[e, at] = jnp.zeros((128, order), F8) if t is None else both_ref[t, :, at].astype(F8).T

    def put(e, t):
        @pl.when(e < kept)
        def _():
            fill(kept_ref, e, t)

        @pl.when(e >= kept)
        def _():
            fill(small_ref, e - kept, t)
            leave(e - kept).start()

    def count(t):
        row = rows_ref[t]
        for at in [slice(q, q + order // 4) for q in range(0, order, order // 4)]:
            counted = both_ref[t, at, :order] + jnp.abs(both_ref[t, at, order:])
            present_ref[row, at] = present_ref[row, at] + counted

    def one(t, listed):
        count(t)
        closes = done_ref[t]

        @pl.when(closes == 1)
        def _():
            def add(prior):
                both_ref[t] = both_ref[t] + both_ref[prior]
                return back_ref[prior]

            lax.while_loop(lambda prior: prior >= 0, add, back_ref[t])
            put(listed, t)
            place = (slots_ref[t] - rb_dev) ^ central(slots - rb_dev)
            plan_ref[listed] = rows_ref[t] | (place << 8)

        return listed + closes

    def near_chunk(c, carry):
        for copy in copies(c):
            copy.wait()
        for j in range(CHUNK):
            count(c * CHUNK + j)
        return carry

    def far_chunk(c, listed):
        for copy in copies(c):
            copy.wait()
        for j in range(CHUNK):
            listed = one(c * CHUNK + j, listed)
        return listed

    short = (UNROLL - entries % UNROLL) % UNROLL
    for j in range(UNROLL - 1):

        @pl.when(j < short)
        def _():
            put(entries + j, None)
            plan_ref[entries + j] = (slots - rb_dev) << 8

    every = entries + short
    plan_ref[tiles] = every // UNROLL
    lax.fori_loop(first_far, chunks, far_chunk, 0)
    lax.fori_loop(0, first_far, near_chunk, 0)
    plan_copy = pltpu.make_async_copy(plan_ref, plan_hbm, list_sems.at[2])
    plan_copy.start()

    ones = jnp.ones((8, order), BF16)
    for r in range(rb_dev):
        degree = lax.dot_general(ones, present_ref[r], NT, preferred_element_type=F32)
        scale_ref[:, r * order : (r + 1) * order] = 1.0 / jnp.sqrt(jnp.maximum(degree, 1.0))

    def left(e, _):
        leave(e - kept).wait()
        return _

    lax.fori_loop(kept, every, left, 0)
    plan_copy.wait()


def in_hbm(x):
    return pltpu.with_memory_space_constraint(x, pltpu.HBM)


def tiles_call(rows, slots, real, imag, rb_dev, near_count):
    tiles, order, _ = real.shape
    nblk = lax.axis_size("blk")
    return pl.pallas_call(
        functools.partial(tiles_kernel, near_count),
        name="tiles",
        out_shape=(
            pltpu.HBM((tiles - near_count - KEPT, 2 * order, order), F8),
            pltpu.VMEM((KEPT, 2 * order, order), F8),
            sds((8, rb_dev * order), F32),
            pltpu.HBM((tiles + 32,), I32),
        ),
        in_specs=[ANY] * 4,
        out_specs=(ANY, VMEM, VMEM, ANY),
        scratch_shapes=[
            pltpu.SMEM((tiles,), I32),
            pltpu.SMEM((tiles,), I32),
            pltpu.SMEM((tiles + 32,), I32),
            pltpu.VMEM((tiles, order, 2 * order), BF16),
            pltpu.VMEM((tiles - near_count - KEPT, 2 * order, order), F8),
            pltpu.VMEM((rb_dev, order, order), BF16),
            pltpu.SMEM((rb_dev * (rb_dev + nblk),), I32),
            pltpu.SMEM((tiles,), I32),
            pltpu.SMEM((tiles + 1,), I32),
            pltpu.SemaphoreType.DMA((tiles // CHUNK, 2)),
            pltpu.SemaphoreType.DMA((tiles,)),
            pltpu.SemaphoreType.DMA((3,)),
        ],
        compiler_params=params(48),
        cost_estimate=pl.CostEstimate(flops=1 << 28, bytes_accessed=2 * real.size * 2, transcendentals=0),
    )(in_hbm(rows), in_hbm(slots), in_hbm(real), in_hbm(imag))


def rounded_block(field, scale_ref, r, order):
    at = slice(r * order, (r + 1) * order)
    return (field[:, at] * scale_ref[0:1, at]).astype(BF16)


def send_picked(wanted_ref, sent_ref, out_hbm, sems):
    me = lax.axis_index("blk")
    copies = [
        pltpu.make_async_copy(sent_ref.at[wanted_ref[i, 0, me]], out_hbm.at[i], sems.at[i])
        for i in range(out_hbm.shape[0])
    ]
    for copy in copies:
        copy.start()
    for copy in copies:
        copy.wait()


def first_kernel(y_ref, scale_ref, wanted_ref, out_hbm, sent_ref, out_sems):
    for r in range(sent_ref.shape[0]):
        sent_ref[r] = rounded_block(y_ref, scale_ref, r, sent_ref.shape[2])
    send_picked(wanted_ref, sent_ref, out_hbm, out_sems)


def load_groups(packed_hbm, tiles_ref, sems, count):
    def copy(g):
        at = pl.ds(g * UNROLL, UNROLL)
        return pltpu.make_async_copy(packed_hbm.at[at], tiles_ref.at[at], sems.at[g])

    def begin(g, _):
        copy(g).start()
        return _

    lax.fori_loop(0, count, begin, 0)
    return copy


def split_sources(count, source, x_ref):
    _, rows, width = x_ref.shape
    group, order = rows // 2, width // 2
    most = jnp.zeros((group, order), F32)
    for p in range(count):
        most = jnp.maximum(most, jnp.abs(source(p).astype(F32)))
    most = jnp.broadcast_to(jnp.max(most, axis=1, keepdims=True), (group, 128))
    most = jnp.maximum(jnp.maximum(most, jnp.abs(turn_rows(most))), TINY)
    power = jnp.floor(jnp.log2(most))
    size = jnp.exp2(power - TOP)
    inverse = jnp.exp2(TOP - power)[:, 0:1]
    for p in range(count):
        scaled = source(p).astype(F32) * inverse
        far = scaled * SPLIT
        high = far - (far - scaled)
        low = (scaled - high) * FINER
        for k, part in enumerate((high, low)):
            at = slice(k * group, (k + 1) * group)
            x_ref[p, at, :order] = part.astype(F8)
            x_ref[p, at, order:] = turn_rows(part).astype(F8)
    x_ref[count] = jnp.zeros_like(x_ref[count])
    return size[:, 0:1]


def multiply(plan_ref, lo, hi, tile, load, acc_ref):
    def group(g, _):
        done = []
        for j in range(UNROLL):
            code = plan_ref[g * UNROLL + j]
            product = jnp.dot(load(code >> 8), tile(g, j), preferred_element_type=F32)
            done.append((code & 255, product))
        for row, product in done:
            acc_ref[row] = acc_ref[row] + product
        return _

    lax.fori_loop(lo, hi, group, 0)


def collect(acc, size):
    group = size.shape[0]
    return (acc[:group] + acc[group:] * (1.0 / FINER)) * size


def near_kernel(
    step, rows_ref, slots_ref, real_hbm, imag_hbm, scale_ref, now_ref, before_ref, base_ref, tiles_ref, x_ref, acc_ref, sems
):
    rb_dev, _, order = x_ref.shape
    groups = sems.shape[0]

    def copies(g):
        at = pl.ds(g * NEAR_UNROLL, NEAR_UNROLL)
        return [
            pltpu.make_async_copy(hbm.at[at], tiles_ref.at[i, at], sems.at[g, i])
            for i, hbm in enumerate((real_hbm, imag_hbm))
        ]

    for g in range(groups):
        for copy in copies(g):
            copy.start()
    acc_ref[...] = jnp.zeros_like(acc_ref)
    for r in range(rb_dev):
        x_ref[r] = rounded_block(now_ref, scale_ref, r, order)

    def group(g, _):
        for copy in copies(g):
            copy.wait()
        done = []
        for t in [g * NEAR_UNROLL + j for j in range(NEAR_UNROLL)]:
            x = x_ref[slots_ref[t]]
            done.append([lax.dot_general(x, tiles_ref[i, t], NT, preferred_element_type=F32) for i in range(2)])
        for j, products in enumerate(done):
            row = rows_ref[g * NEAR_UNROLL + j]
            for i, product in enumerate(products):
                acc_ref[i, row] = acc_ref[i, row] + product
        return _

    lax.fori_loop(0, groups, group, 0)
    for r in range(rb_dev):
        at = slice(r * order, (r + 1) * order)
        applied = scale_ref[0:1, at] * (acc_ref[0, r] + turn_rows(acc_ref[1, r]))
        moved = ((1.0 - center) * now_ref[:, at] - applied) / half_width
        base_ref[:, at] = moved if step == 0 else 2.0 * moved - before_ref[:, at]


def step_kernel(step, plan_ref, wanted_ref, packed_hbm, kept_ref, scale_ref, base_ref, arrived_ref, *refs):
    last = step == STEPS - 1
    next_ref = refs[0]
    if not last:
        out_hbm, sent_ref, out_sems = refs[1:4]
    tiles_ref, x_ref, acc_ref, sems = refs[-4:]
    rb_dev, _, order = acc_ref.shape
    stay = KEPT // UNROLL
    groups = plan_ref[plan_ref.shape[0] - 32]
    copy = load_groups(packed_hbm, tiles_ref, sems, groups - stay)
    acc_ref[...] = jnp.zeros_like(acc_ref)
    size = split_sources(arrived_ref.shape[0], lambda p: arrived_ref[p], x_ref)
    size = size * ((1.0 if step == 0 else 2.0) / half_width)

    def loaded(g, j):
        if j == 0:
            copy(g - stay).wait()
        return tiles_ref[(g - stay) * UNROLL + j]

    def load(place):
        return x_ref[place]

    multiply(plan_ref, 0, jnp.minimum(stay, groups), lambda g, j: kept_ref[g * UNROLL + j], load, acc_ref)
    multiply(plan_ref, stay, groups, loaded, load, acc_ref)
    for r in range(rb_dev):
        at = slice(r * order, (r + 1) * order)
        scale = scale_ref[0:1, at]
        following = base_ref[:, at] - scale * collect(acc_ref[r], size)
        next_ref[:, at] = following
        if not last:
            sent_ref[r] = (following * scale).astype(BF16)
    if not last:
        send_picked(wanted_ref, sent_ref, out_hbm, out_sems)


def all_rows(own_ref, arrived, all_ref):
    c = lax.axis_index("col")
    all_ref[c] = own_ref[...].astype(BF16)
    for s, ref in enumerate(arrived, 1):
        all_ref[c ^ s] = ref[...]
    n, group, rows = all_ref.shape
    return all_ref[...].reshape(n * group, rows)


def gram_kernel(own_ref, *refs):
    arrived, (gram_ref, all_ref, full_ref) = refs[:-3], refs[-3:]
    rows = all_rows(own_ref, arrived, all_ref)
    full_ref[...] = lax.dot_general(rows, rows, NT, preferred_element_type=F32)
    half = gram_ref.shape[0]
    even = full_ref[pl.ds(0, half, stride=2), :]
    odd = full_ref[pl.ds(1, half, stride=2), :]
    gram_ref[...] = even + turn_lanes(odd)


PANEL = 64
PIECES = 4
SUB = 8


def eliminate(a, m, top):
    shape = a[0].shape
    here = lax.broadcasted_iota(I32, shape, 0)
    pivots = [None] * len(a)

    def column(rows, lane):
        return jnp.broadcast_to(rows[:, lane : lane + 1], shape)

    for step in range(0, len(a) * SUB, 4):
        own, k = divmod(step, SUB)
        head = [column(a[own], top + step + i) for i in range(4)]
        p, q = head[0][k : k + 1, :], head[2][k + 2 : k + 3, :]
        u, v = head[2][k : k + 1, :], head[3][k : k + 1, :]
        single = 1.0 / p
        det = p * q - (u * u + v * v)
        both = 1.0 / det
        pq, ub, vb, pb = q * both, u * both, v * both, p * both
        second = (here == k + 2) | (here == k + 3)
        last = det * single
        pivot = jnp.where(second, last, jnp.broadcast_to(p, shape))
        pivots[own] = pivot if k == 0 else jnp.where(here < k, pivots[own], pivot)
        rows = [[x[own][k + i : k + i + 1, :] for i in range(4)] for x in (a, m)]
        for g in range(own, len(a)):
            w = head if g == own else [column(a[g], top + step + i) for i in range(4)]
            c = [
                w[0] * pq - w[2] * ub - w[3] * vb,
                w[1] * pq + w[2] * vb - w[3] * ub,
                w[2] * pb - w[0] * ub + w[1] * vb,
                w[3] * pb - w[0] * vb - w[1] * ub,
            ]
            if g == own:
                below = here > k + 3
                c = [jnp.where(below, x, 0.0) for x in c]
                c[0] = jnp.where(second, w[0] * single, c[0])
                c[1] = jnp.where(second, w[1] * single, c[1])
            a[g], m[g] = (
                x[g] - (c[0] * r[0] + c[1] * r[1] + c[2] * r[2] + c[3] * r[3]) for x, r in zip((a, m), rows)
            )
    roots = [lax.rsqrt(x) for x in pivots]
    return [x * r for x, r in zip(a, roots)], [x * r for x, r in zip(m, roots)]


def factor_kernel(nodes, own_ref, all_ref, *refs):
    parts, (out_hbm, work_ref, inverse_ref, piece_ref, sems) = refs[:-5], refs[-5:]
    group = own_ref.shape[0]
    order = work_ref.shape[0]
    total = parts[0][...]
    for part in parts[1:]:
        total = total + part[...]
    half = total.shape[0]
    work_ref[pl.ds(0, half, stride=2), :] = total
    work_ref[pl.ds(1, half, stride=2), :] = -turn_lanes(total)
    row_at = lax.broadcasted_iota(I32, (order, order), 0)
    lane_at = lax.broadcasted_iota(I32, (order, order), 1)
    inverse_ref[...] = (row_at == lane_at).astype(F32)
    for top in range(0, order, PANEL):
        tops = range(top, top + PANEL, SUB)
        a, m = ([ref[r : r + SUB, :] for r in tops] for ref in (work_ref, inverse_ref))
        a, m = eliminate(a, m, top)
        a, m = jnp.concatenate(a, axis=0), jnp.concatenate(m, axis=0)
        inverse_ref[top : top + PANEL, :] = m
        rest = top + PANEL
        if rest < order:
            update = lax.dot_general(
                a, jnp.concatenate([a, m], axis=1), TN, precision=lax.Precision.HIGHEST, preferred_element_type=F32
            )
            work_ref[rest:, :] = work_ref[rest:, :] - update[rest:, :order]
            inverse_ref[rest:, :] = inverse_ref[rest:, :] - update[rest:, order:]
    c = lax.axis_index("col")
    mine = inverse_ref[pl.ds(pl.multiple_of(c * group, group), group), :]
    mine = mine * math.sqrt(nodes)
    high = mine.astype(BF16)
    low = (mine - high.astype(F32)).astype(BF16)
    own_lanes = (
        lax.broadcasted_iota(I32, (order, group), 0)
        == lax.broadcasted_iota(I32, (order, group), 1) + c * group
    ).astype(BF16)
    square = jnp.dot(high, own_lanes, preferred_element_type=F32).astype(BF16)
    left = jnp.concatenate([high, low], axis=0)
    width = own_ref.shape[1] // PIECES
    copies = []
    for i in range(PIECES):
        at = slice(i * width, (i + 1) * width)
        rows = all_ref[:, :, at].reshape(order, width)
        both = jnp.dot(left, rows, preferred_element_type=F32)
        own = own_ref[:, at]
        lost = (own - own.astype(BF16).astype(F32)).astype(BF16)
        piece_ref[i] = both[:group] + both[group:] + jnp.dot(square, lost, preferred_element_type=F32)
        copies.append(pltpu.make_async_copy(piece_ref.at[i], out_hbm.at[:, at], sems.at[i]))
        copies[-1].start()
    for copy in copies:
        copy.wait()


def central(nblk):
    return nblk // 2 + nblk // 8


def exchange(x):
    nblk = lax.axis_size("blk")
    group = [i ^ central(nblk) for i in range(nblk)]
    return lax.all_to_all(x, "blk", split_axis=0, concat_axis=0, tiled=True, axis_index_groups=[group])


def to_partner(x, axis, mask):
    n = lax.axis_size(axis)
    return lax.ppermute(x, axis, [(i, i ^ mask) for i in range(n)])


def sum_parts(part, nblk):
    wide = 1
    while 4 * wide < nblk:
        part = part + to_partner(part, "blk", wide)
        wide *= 2
    return [part] + [to_partner(part, "blk", s * wide) for s in range(1, nblk // wide)]


def per_device(y_start, tile_real, tile_imag, tile_rows, tile_slots, fetch_pick):
    group, rows = y_start.shape
    tiles, order, _ = tile_real.shape
    rb_dev = rows // order
    nblk = lax.axis_size("blk")
    ncol = lax.axis_size("col")
    near_count = LOC_RB * rb_dev
    wanted = exchange(jnp.broadcast_to(fetch_pick[None], (nblk, 1, nblk)))
    packed, kept, scale, plan = tiles_call(tile_rows, tile_slots, tile_real, tile_imag, rb_dev, near_count)

    out_blocks = pltpu.HBM((nblk, group, order), BF16)
    sent_scratch = [pltpu.VMEM((rb_dev, group, order), BF16), pltpu.SemaphoreType.DMA((nblk,))]
    blocks = pl.pallas_call(
        first_kernel,
        name="first",
        out_shape=out_blocks,
        in_specs=[VMEM, VMEM, SMEM],
        out_specs=ANY,
        scratch_shapes=sent_scratch,
        compiler_params=params(LIMIT),
    )(y_start, scale, wanted)

    vectors_here = sds((group, rows), F32)
    previous, current = y_start, y_start
    for step in range(STEPS):
        arrived = exchange(blocks)
        base = pl.pallas_call(
            functools.partial(near_kernel, step),
            name="near",
            out_shape=vectors_here,
            in_specs=[SMEM, SMEM, ANY, ANY] + [VMEM] * 3,
            out_specs=VMEM,
            scratch_shapes=[
                pltpu.VMEM((2, near_count, order, order), BF16),
                pltpu.VMEM((rb_dev, group, order), BF16),
                pltpu.VMEM((2, rb_dev, group, order), F32),
                pltpu.SemaphoreType.DMA((near_count // NEAR_UNROLL, 2)),
            ],
            compiler_params=params(LIMIT),
            cost_estimate=pl.CostEstimate(flops=1 << 28, bytes_accessed=1 << 21, transcendentals=0),
        )(in_hbm(tile_rows), in_hbm(tile_slots), in_hbm(tile_real), in_hbm(tile_imag), scale, current, previous)
        last = step == STEPS - 1
        out = pl.pallas_call(
            functools.partial(step_kernel, step),
            name="step",
            out_shape=[vectors_here] if last else [vectors_here, out_blocks],
            in_specs=[SMEM, SMEM, ANY] + [VMEM] * 4,
            out_specs=[VMEM] if last else [VMEM, ANY],
            scratch_shapes=([] if last else sent_scratch)
            + [
                pltpu.VMEM(packed.shape, F8),
                pltpu.VMEM((nblk + 1, 2 * group, 2 * order), F8),
                pltpu.VMEM((rb_dev, 2 * group, order), F32),
                pltpu.SemaphoreType.DMA((packed.shape[0] // UNROLL,)),
            ],
            compiler_params=params(LIMIT),
        )(in_hbm(plan), wanted, in_hbm(packed), pltpu.with_memory_space_constraint(kept, pltpu.VMEM), scale, base, arrived)
        previous, current = current, out[0]
        if not last:
            blocks = out[1]

    rounded = current.astype(BF16)
    if ncol == 4:
        beside, across = to_partner(rounded, "col", 1), to_partner(rounded, "col", 2)
        others = [beside, across, to_partner(across, "col", 1)]
    else:
        others = [to_partner(rounded, "col", s) for s in range(1, ncol)]
    vectors = group * ncol
    part, gathered = pl.pallas_call(
        gram_kernel,
        name="gram",
        out_shape=(sds((vectors // 2, vectors), F32), sds((ncol, group, rows), BF16)),
        in_specs=[VMEM] * (1 + len(others)),
        out_specs=(VMEM, VMEM),
        scratch_shapes=[pltpu.VMEM((vectors, vectors), F32)],
        compiler_params=params(LIMIT),
    )(current, *others)
    parts = sum_parts(part, nblk)
    return pl.pallas_call(
        functools.partial(factor_kernel, rows * nblk),
        name="factor",
        out_shape=pltpu.HBM((group, rows), F32),
        in_specs=[VMEM] * (2 + len(parts)),
        out_specs=ANY,
        scratch_shapes=[pltpu.VMEM((vectors, vectors), F32)] * 2
        + [pltpu.VMEM((PIECES, group, rows // PIECES), F32), pltpu.SemaphoreType.DMA((PIECES,))],
        compiler_params=params(LIMIT),
    )(current, gathered, *parts)


def solution(mesh):
    return jax.shard_map(
        per_device,
        mesh=mesh,
        in_specs=(
            P("col", "blk"),
            P("blk", None, None),
            P("blk", None, None),
            P("blk"),
            P("blk"),
            P("blk", None),
        ),
        out_specs=P("col", "blk"),
        check_vma=False,
    )
```

```python
import functools
import math

import jax
import jax.numpy as jnp
from jax import lax
from jax.experimental import pallas as pl
from jax.experimental.pallas import tpu as pltpu
from jax.sharding import PartitionSpec as P

LOC_RB = 2
STEPS = 4
UNROLL = 8
NEAR_UNROLL = 4
KEPT = 16
CHUNK = 8
MERGE = 16
TOP = 7.0
FINER = 16.0
SPLIT = float((1 << 20) + 1)
TINY = 1e-30
MIB = 1 << 20
LIMIT = 24

center = 1.25
half_width = 0.75

F32 = jnp.float32
BF16 = jnp.bfloat16
F8 = jnp.float8_e4m3fn
I32 = jnp.int32

VMEM = pl.BlockSpec(memory_space=pltpu.VMEM)
SMEM = pl.BlockSpec(memory_space=pltpu.SMEM)
ANY = pl.BlockSpec(memory_space=pl.ANY)

NT = (((1,), (1,)), ((), ()))
TN = (((0,), (0,)), ((), ()))


def sds(shape, dtype):
    return jax.ShapeDtypeStruct(shape, dtype)


def params(limit):
    return pltpu.CompilerParams(vmem_limit_bytes=limit * MIB)


def turn_rows(values):
    rows = values.shape[0]
    even = lax.broadcasted_iota(I32, values.shape, 0) % 2 == 0
    below = pltpu.roll(values, rows - 1, 0)
    above = pltpu.roll(values, 1, 0)
    return jnp.where(even, -below, above)


def turn_lanes(values):
    lanes = values.shape[1]
    even = lax.broadcasted_iota(I32, values.shape, 1) % 2 == 0
    after = pltpu.roll(values, lanes - 1, 1)
    before = pltpu.roll(values, 1, 1)
    return jnp.where(even, after, -before)


def tiles_kernel(
    near_count,
    rows_hbm,
    slots_hbm,
    real_hbm,
    imag_hbm,
    packed_hbm,
    kept_ref,
    scale_ref,
    plan_hbm,
    rows_ref,
    slots_ref,
    plan_ref,
    both_ref,
    small_ref,
    present_ref,
    table_ref,
    back_ref,
    done_ref,
    in_sems,
    out_sems,
    list_sems,
):
    kept = kept_ref.shape[0]
    tiles, order, _ = both_ref.shape
    rb_dev = present_ref.shape[0]
    slots = rb_dev + lax.axis_size("blk")
    chunks = tiles // CHUNK

    def copies(c):
        at = pl.ds(c * CHUNK, CHUNK)
        return (
            pltpu.make_async_copy(real_hbm.at[at], both_ref.at[at, :, 0:order], in_sems.at[c, 0]),
            pltpu.make_async_copy(imag_hbm.at[at], both_ref.at[at, :, order : 2 * order], in_sems.at[c, 1]),
        )

    def leave(e):
        return pltpu.make_async_copy(small_ref.at[e], packed_hbm.at[e], out_sems.at[e])

    lists = (
        pltpu.make_async_copy(rows_hbm, rows_ref, list_sems.at[0]),
        pltpu.make_async_copy(slots_hbm, slots_ref, list_sems.at[1]),
    )
    for copy in lists:
        copy.start()
    first_far = near_count // CHUNK
    for c in [*range(first_far, chunks), *range(first_far)]:
        for copy in copies(c):
            copy.start()

    def clear(row, _):
        for slot in range(slots):
            table_ref[row * slots + slot] = -1
        return _

    lax.fori_loop(0, rb_dev, clear, 0)
    present_ref[...] = jnp.zeros_like(present_ref)
    for copy in lists:
        copy.wait()

    def link(c, entries):
        for t in [c * CHUNK + j for j in range(CHUNK)]:
            key = rows_ref[t] * slots + slots_ref[t]
            seen = table_ref[key]
            before = seen & 255
            length = seen >> 8
            joins = (seen >= 0) & (length < MERGE)
            back_ref[t] = jnp.where(joins, before, -1)
            done_ref[t] = 1
            done_ref[jnp.where(joins, before, tiles)] = 0
            table_ref[key] = t | (jnp.where(joins, length + 1, 1) << 8)
            entries = entries + jnp.where(joins, 0, 1)
        return entries

    entries = lax.fori_loop(first_far, chunks, link, 0)

    def fill(ref, e, t):
        for at in [slice(q, q + 128) for q in range(0, 2 * order, 128)]:
            ref[e, at] = jnp.zeros((128, order), F8) if t is None else both_ref[t, :, at].astype(F8).T

    def put(e, t):
        @pl.when(e < kept)
        def _():
            fill(kept_ref, e, t)

        @pl.when(e >= kept)
        def _():
            fill(small_ref, e - kept, t)
            leave(e - kept).start()

    def count(t):
        row = rows_ref[t]
        for at in [slice(q, q + order // 4) for q in range(0, order, order // 4)]:
            counted = both_ref[t, at, :order] + jnp.abs(both_ref[t, at, order:])
            present_ref[row, at] = present_ref[row, at] + counted

    def one(t, listed):
        count(t)
        closes = done_ref[t]

        @pl.when(closes == 1)
        def _():
            def add(prior):
                both_ref[t] = both_ref[t] + both_ref[prior]
                return back_ref[prior]

            lax.while_loop(lambda prior: prior >= 0, add, back_ref[t])
            put(listed, t)
            place = (slots_ref[t] - rb_dev) ^ central(slots - rb_dev)
            plan_ref[listed] = rows_ref[t] | (place << 8)

        return listed + closes

    def near_chunk(c, carry):
        for copy in copies(c):
            copy.wait()
        for j in range(CHUNK):
            count(c * CHUNK + j)
        return carry

    def far_chunk(c, listed):
        for copy in copies(c):
            copy.wait()
        for j in range(CHUNK):
            listed = one(c * CHUNK + j, listed)
        return listed

    short = (UNROLL - entries % UNROLL) % UNROLL
    for j in range(UNROLL - 1):

        @pl.when(j < short)
        def _():
            put(entries + j, None)
            plan_ref[entries + j] = (slots - rb_dev) << 8

    every = entries + short
    plan_ref[tiles] = every // UNROLL
    lax.fori_loop(first_far, chunks, far_chunk, 0)
    lax.fori_loop(0, first_far, near_chunk, 0)
    plan_copy = pltpu.make_async_copy(plan_ref, plan_hbm, list_sems.at[2])
    plan_copy.start()

    ones = jnp.ones((8, order), BF16)
    for r in range(rb_dev):
        degree = lax.dot_general(ones, present_ref[r], NT, preferred_element_type=F32)
        scale_ref[:, r * order : (r + 1) * order] = 1.0 / jnp.sqrt(jnp.maximum(degree, 1.0))

    def left(e, _):
        leave(e - kept).wait()
        return _

    lax.fori_loop(kept, every, left, 0)
    plan_copy.wait()


def in_hbm(x):
    return pltpu.with_memory_space_constraint(x, pltpu.HBM)


def tiles_call(rows, slots, real, imag, rb_dev, near_count):
    tiles, order, _ = real.shape
    nblk = lax.axis_size("blk")
    return pl.pallas_call(
        functools.partial(tiles_kernel, near_count),
        name="tiles",
        out_shape=(
            pltpu.HBM((tiles - near_count - KEPT, 2 * order, order), F8),
            pltpu.VMEM((KEPT, 2 * order, order), F8),
            sds((8, rb_dev * order), F32),
            pltpu.HBM((tiles + 32,), I32),
        ),
        in_specs=[ANY] * 4,
        out_specs=(ANY, VMEM, VMEM, ANY),
        scratch_shapes=[
            pltpu.SMEM((tiles,), I32),
            pltpu.SMEM((tiles,), I32),
            pltpu.SMEM((tiles + 32,), I32),
            pltpu.VMEM((tiles, order, 2 * order), BF16),
            pltpu.VMEM((tiles - near_count - KEPT, 2 * order, order), F8),
            pltpu.VMEM((rb_dev, order, order), BF16),
            pltpu.SMEM((rb_dev * (rb_dev + nblk),), I32),
            pltpu.SMEM((tiles,), I32),
            pltpu.SMEM((tiles + 1,), I32),
            pltpu.SemaphoreType.DMA((tiles // CHUNK, 2)),
            pltpu.SemaphoreType.DMA((tiles,)),
            pltpu.SemaphoreType.DMA((3,)),
        ],
        compiler_params=params(48),
        cost_estimate=pl.CostEstimate(flops=1 << 28, bytes_accessed=2 * real.size * 2, transcendentals=0),
    )(in_hbm(rows), in_hbm(slots), in_hbm(real), in_hbm(imag))


def rounded_block(field, scale_ref, r, order):
    at = slice(r * order, (r + 1) * order)
    return (field[:, at] * scale_ref[0:1, at]).astype(BF16)


def send_picked(wanted_ref, sent_ref, out_hbm, sems):
    me = lax.axis_index("blk")
    copies = [
        pltpu.make_async_copy(sent_ref.at[wanted_ref[i, 0, me]], out_hbm.at[i], sems.at[i])
        for i in range(out_hbm.shape[0])
    ]
    for copy in copies:
        copy.start()
    for copy in copies:
        copy.wait()


def first_kernel(y_ref, scale_ref, wanted_ref, out_hbm, sent_ref, out_sems):
    for r in range(sent_ref.shape[0]):
        sent_ref[r] = rounded_block(y_ref, scale_ref, r, sent_ref.shape[2])
    send_picked(wanted_ref, sent_ref, out_hbm, out_sems)


def load_groups(packed_hbm, tiles_ref, sems, count):
    def copy(g):
        at = pl.ds(g * UNROLL, UNROLL)
        return pltpu.make_async_copy(packed_hbm.at[at], tiles_ref.at[at], sems.at[g])

    def begin(g, _):
        copy(g).start()
        return _

    lax.fori_loop(0, count, begin, 0)
    return copy


def split_sources(count, source, x_ref):
    _, rows, width = x_ref.shape
    group, order = rows // 2, width // 2
    most = jnp.zeros((group, order), F32)
    for p in range(count):
        most = jnp.maximum(most, jnp.abs(source(p).astype(F32)))
    most = jnp.broadcast_to(jnp.max(most, axis=1, keepdims=True), (group, 128))
    most = jnp.maximum(jnp.maximum(most, jnp.abs(turn_rows(most))), TINY)
    power = jnp.floor(jnp.log2(most))
    size = jnp.exp2(power - TOP)
    inverse = jnp.exp2(TOP - power)[:, 0:1]
    for p in range(count):
        scaled = source(p).astype(F32) * inverse
        far = scaled * SPLIT
        high = far - (far - scaled)
        low = (scaled - high) * FINER
        for k, part in enumerate((high, low)):
            at = slice(k * group, (k + 1) * group)
            x_ref[p, at, :order] = part.astype(F8)
            x_ref[p, at, order:] = turn_rows(part).astype(F8)
    x_ref[count] = jnp.zeros_like(x_ref[count])
    return size[:, 0:1]


def multiply(plan_ref, lo, hi, tile, load, acc_ref):
    def group(g, _):
        done = []
        for j in range(UNROLL):
            code = plan_ref[g * UNROLL + j]
            product = jnp.dot(load(code >> 8), tile(g, j), preferred_element_type=F32)
            done.append((code & 255, product))
        for row, product in done:
            acc_ref[row] = acc_ref[row] + product
        return _

    lax.fori_loop(lo, hi, group, 0)


def collect(acc, size):
    group = size.shape[0]
    return (acc[:group] + acc[group:] * (1.0 / FINER)) * size


def near_kernel(
    step, rows_ref, slots_ref, real_hbm, imag_hbm, scale_ref, now_ref, before_ref, base_ref, tiles_ref, x_ref, acc_ref, sems
):
    rb_dev, _, order = x_ref.shape
    groups = sems.shape[0]

    def copies(g):
        at = pl.ds(g * NEAR_UNROLL, NEAR_UNROLL)
        return [
            pltpu.make_async_copy(hbm.at[at], tiles_ref.at[i, at], sems.at[g, i])
            for i, hbm in enumerate((real_hbm, imag_hbm))
        ]

    for g in range(groups):
        for copy in copies(g):
            copy.start()
    acc_ref[...] = jnp.zeros_like(acc_ref)
    for r in range(rb_dev):
        x_ref[r] = rounded_block(now_ref, scale_ref, r, order)

    def group(g, _):
        for copy in copies(g):
            copy.wait()
        done = []
        for t in [g * NEAR_UNROLL + j for j in range(NEAR_UNROLL)]:
            x = x_ref[slots_ref[t]]
            done.append([lax.dot_general(x, tiles_ref[i, t], NT, preferred_element_type=F32) for i in range(2)])
        for j, products in enumerate(done):
            row = rows_ref[g * NEAR_UNROLL + j]
            for i, product in enumerate(products):
                acc_ref[i, row] = acc_ref[i, row] + product
        return _

    lax.fori_loop(0, groups, group, 0)
    for r in range(rb_dev):
        at = slice(r * order, (r + 1) * order)
        applied = scale_ref[0:1, at] * (acc_ref[0, r] + turn_rows(acc_ref[1, r]))
        moved = ((1.0 - center) * now_ref[:, at] - applied) / half_width
        base_ref[:, at] = moved if step == 0 else 2.0 * moved - before_ref[:, at]


def step_kernel(step, plan_ref, wanted_ref, packed_hbm, kept_ref, scale_ref, base_ref, arrived_ref, *refs):
    last = step == STEPS - 1
    next_ref = refs[0]
    if not last:
        out_hbm, sent_ref, out_sems = refs[1:4]
    tiles_ref, x_ref, acc_ref, sems = refs[-4:]
    rb_dev, _, order = acc_ref.shape
    stay = KEPT // UNROLL
    groups = plan_ref[plan_ref.shape[0] - 32]
    copy = load_groups(packed_hbm, tiles_ref, sems, groups - stay)
    acc_ref[...] = jnp.zeros_like(acc_ref)
    size = split_sources(arrived_ref.shape[0], lambda p: arrived_ref[p], x_ref)
    size = size * ((1.0 if step == 0 else 2.0) / half_width)

    def loaded(g, j):
        if j == 0:
            copy(g - stay).wait()
        return tiles_ref[(g - stay) * UNROLL + j]

    def load(place):
        return x_ref[place]

    multiply(plan_ref, 0, jnp.minimum(stay, groups), lambda g, j: kept_ref[g * UNROLL + j], load, acc_ref)
    multiply(plan_ref, stay, groups, loaded, load, acc_ref)
    for r in range(rb_dev):
        at = slice(r * order, (r + 1) * order)
        scale = scale_ref[0:1, at]
        following = base_ref[:, at] - scale * collect(acc_ref[r], size)
        next_ref[:, at] = following
        if not last:
            sent_ref[r] = (following * scale).astype(BF16)
    if not last:
        send_picked(wanted_ref, sent_ref, out_hbm, out_sems)


def all_rows(own_ref, arrived, all_ref):
    c = lax.axis_index("col")
    all_ref[c] = own_ref[...].astype(BF16)
    for s, ref in enumerate(arrived, 1):
        all_ref[c ^ s] = ref[...]
    n, group, rows = all_ref.shape
    return all_ref[...].reshape(n * group, rows)


def gram_kernel(own_ref, *refs):
    arrived, (gram_ref, all_ref, full_ref) = refs[:-3], refs[-3:]
    rows = all_rows(own_ref, arrived, all_ref)
    full_ref[...] = lax.dot_general(rows, rows, NT, preferred_element_type=F32)
    half = gram_ref.shape[0]
    even = full_ref[pl.ds(0, half, stride=2), :]
    odd = full_ref[pl.ds(1, half, stride=2), :]
    gram_ref[...] = even + turn_lanes(odd)


PANEL = 64
PIECES = 4
SUB = 8


def eliminate(a, m, top):
    shape = a[0].shape
    here = lax.broadcasted_iota(I32, shape, 0)
    pivots = [None] * len(a)

    def column(rows, lane):
        return jnp.broadcast_to(rows[:, lane : lane + 1], shape)

    for step in range(0, len(a) * SUB, 4):
        own, k = divmod(step, SUB)
        head = [column(a[own], top + step + i) for i in range(4)]
        p, q = head[0][k : k + 1, :], head[2][k + 2 : k + 3, :]
        u, v = head[2][k : k + 1, :], head[3][k : k + 1, :]
        single = 1.0 / p
        det = p * q - (u * u + v * v)
        both = 1.0 / det
        pq, ub, vb, pb = q * both, u * both, v * both, p * both
        second = (here == k + 2) | (here == k + 3)
        last = det * single
        pivot = jnp.where(second, last, jnp.broadcast_to(p, shape))
        pivots[own] = pivot if k == 0 else jnp.where(here < k, pivots[own], pivot)
        rows = [[x[own][k + i : k + i + 1, :] for i in range(4)] for x in (a, m)]
        for g in range(own, len(a)):
            w = head if g == own else [column(a[g], top + step + i) for i in range(4)]
            c = [
                w[0] * pq - w[2] * ub - w[3] * vb,
                w[1] * pq + w[2] * vb - w[3] * ub,
                w[2] * pb - w[0] * ub + w[1] * vb,
                w[3] * pb - w[0] * vb - w[1] * ub,
            ]
            if g == own:
                below = here > k + 3
                c = [jnp.where(below, x, 0.0) for x in c]
                c[0] = jnp.where(second, w[0] * single, c[0])
                c[1] = jnp.where(second, w[1] * single, c[1])
            a[g], m[g] = (
                x[g] - (c[0] * r[0] + c[1] * r[1] + c[2] * r[2] + c[3] * r[3]) for x, r in zip((a, m), rows)
            )
    roots = [lax.rsqrt(x) for x in pivots]
    return [x * r for x, r in zip(a, roots)], [x * r for x, r in zip(m, roots)]


def factor_kernel(nodes, own_ref, all_ref, *refs):
    parts, (out_hbm, work_ref, inverse_ref, piece_ref, sems) = refs[:-5], refs[-5:]
    group = own_ref.shape[0]
    order = work_ref.shape[0]
    total = parts[0][...]
    for part in parts[1:]:
        total = total + part[...]
    half = total.shape[0]
    work_ref[pl.ds(0, half, stride=2), :] = total
    work_ref[pl.ds(1, half, stride=2), :] = -turn_lanes(total)
    row_at = lax.broadcasted_iota(I32, (order, order), 0)
    lane_at = lax.broadcasted_iota(I32, (order, order), 1)
    inverse_ref[...] = (row_at == lane_at).astype(F32)
    for top in range(0, order, PANEL):
        tops = range(top, top + PANEL, SUB)
        a, m = ([ref[r : r + SUB, :] for r in tops] for ref in (work_ref, inverse_ref))
        a, m = eliminate(a, m, top)
        a, m = jnp.concatenate(a, axis=0), jnp.concatenate(m, axis=0)
        inverse_ref[top : top + PANEL, :] = m
        rest = top + PANEL
        if rest < order:
            update = lax.dot_general(
                a, jnp.concatenate([a, m], axis=1), TN, precision=lax.Precision.HIGHEST, preferred_element_type=F32
            )
            work_ref[rest:, :] = work_ref[rest:, :] - update[rest:, :order]
            inverse_ref[rest:, :] = inverse_ref[rest:, :] - update[rest:, order:]
    c = lax.axis_index("col")
    mine = inverse_ref[pl.ds(pl.multiple_of(c * group, group), group), :]
    mine = mine * math.sqrt(nodes)
    high = mine.astype(BF16)
    low = (mine - high.astype(F32)).astype(BF16)
    own_lanes = (
        lax.broadcasted_iota(I32, (order, group), 0)
        == lax.broadcasted_iota(I32, (order, group), 1) + c * group
    ).astype(BF16)
    square = jnp.dot(high, own_lanes, preferred_element_type=F32).astype(BF16)
    left = jnp.concatenate([high, low], axis=0)
    width = own_ref.shape[1] // PIECES
    copies = []
    for i in range(PIECES):
        at = slice(i * width, (i + 1) * width)
        rows = all_ref[:, :, at].reshape(order, width)
        both = jnp.dot(left, rows, preferred_element_type=F32)
        own = own_ref[:, at]
        lost = (own - own.astype(BF16).astype(F32)).astype(BF16)
        piece_ref[i] = both[:group] + both[group:] + jnp.dot(square, lost, preferred_element_type=F32)
        copies.append(pltpu.make_async_copy(piece_ref.at[i], out_hbm.at[:, at], sems.at[i]))
        copies[-1].start()
    for copy in copies:
        copy.wait()


def central(nblk):
    return nblk // 2 + nblk // 8


def exchange(x):
    nblk = lax.axis_size("blk")
    group = [i ^ central(nblk) for i in range(nblk)]
    return lax.all_to_all(x, "blk", split_axis=0, concat_axis=0, tiled=True, axis_index_groups=[group])


def to_partner(x, axis, mask):
    n = lax.axis_size(axis)
    return lax.ppermute(x, axis, [(i, i ^ mask) for i in range(n)])


def sum_parts(part, nblk):
    wide = 1
    while 4 * wide < nblk:
        part = part + to_partner(part, "blk", wide)
        wide *= 2
    return [part] + [to_partner(part, "blk", s * wide) for s in range(1, nblk // wide)]


def per_device(y_start, tile_real, tile_imag, tile_rows, tile_slots, fetch_pick):
    group, rows = y_start.shape
    tiles, order, _ = tile_real.shape
    rb_dev = rows // order
    nblk = lax.axis_size("blk")
    ncol = lax.axis_size("col")
    near_count = LOC_RB * rb_dev
    wanted = exchange(jnp.broadcast_to(fetch_pick[None], (nblk, 1, nblk)))
    packed, kept, scale, plan = tiles_call(tile_rows, tile_slots, tile_real, tile_imag, rb_dev, near_count)

    out_blocks = pltpu.HBM((nblk, group, order), BF16)
    sent_scratch = [pltpu.VMEM((rb_dev, group, order), BF16), pltpu.SemaphoreType.DMA((nblk,))]
    blocks = pl.pallas_call(
        first_kernel,
        name="first",
        out_shape=out_blocks,
        in_specs=[VMEM, VMEM, SMEM],
        out_specs=ANY,
        scratch_shapes=sent_scratch,
        compiler_params=params(LIMIT),
    )(y_start, scale, wanted)

    vectors_here = sds((group, rows), F32)
    previous, current = y_start, y_start
    for step in range(STEPS):
        arrived = exchange(blocks)
        base = pl.pallas_call(
            functools.partial(near_kernel, step),
            name="near",
            out_shape=vectors_here,
            in_specs=[SMEM, SMEM, ANY, ANY] + [VMEM] * 3,
            out_specs=VMEM,
            scratch_shapes=[
                pltpu.VMEM((2, near_count, order, order), BF16),
                pltpu.VMEM((rb_dev, group, order), BF16),
                pltpu.VMEM((2, rb_dev, group, order), F32),
                pltpu.SemaphoreType.DMA((near_count // NEAR_UNROLL, 2)),
            ],
            compiler_params=params(LIMIT),
            cost_estimate=pl.CostEstimate(flops=1 << 28, bytes_accessed=1 << 21, transcendentals=0),
        )(in_hbm(tile_rows), in_hbm(tile_slots), in_hbm(tile_real), in_hbm(tile_imag), scale, current, previous)
        last = step == STEPS - 1
        out = pl.pallas_call(
            functools.partial(step_kernel, step),
            name="step",
            out_shape=[vectors_here] if last else [vectors_here, out_blocks],
            in_specs=[SMEM, SMEM, ANY] + [VMEM] * 4,
            out_specs=[VMEM] if last else [VMEM, ANY],
            scratch_shapes=([] if last else sent_scratch)
            + [
                pltpu.VMEM(packed.shape, F8),
                pltpu.VMEM((nblk + 1, 2 * group, 2 * order), F8),
                pltpu.VMEM((rb_dev, 2 * group, order), F32),
                pltpu.SemaphoreType.DMA((packed.shape[0] // UNROLL,)),
            ],
            compiler_params=params(LIMIT),
        )(in_hbm(plan), wanted, in_hbm(packed), pltpu.with_memory_space_constraint(kept, pltpu.VMEM), scale, base, arrived)
        previous, current = current, out[0]
        if not last:
            blocks = out[1]

    rounded = current.astype(BF16)
    if ncol == 4:
        beside, across = to_partner(rounded, "col", 1), to_partner(rounded, "col", 2)
        others = [beside, across, to_partner(across, "col", 1)]
    else:
        others = [to_partner(rounded, "col", s) for s in range(1, ncol)]
    vectors = group * ncol
    part, gathered = pl.pallas_call(
        gram_kernel,
        name="gram",
        out_shape=(sds((vectors // 2, vectors), F32), sds((ncol, group, rows), BF16)),
        in_specs=[VMEM] * (1 + len(others)),
        out_specs=(VMEM, VMEM),
        scratch_shapes=[pltpu.VMEM((vectors, vectors), F32)],
        compiler_params=params(LIMIT),
    )(current, *others)
    parts = sum_parts(part, nblk)
    return pl.pallas_call(
        functools.partial(factor_kernel, rows * nblk),
        name="factor",
        out_shape=pltpu.HBM((group, rows), F32),
        in_specs=[VMEM] * (2 + len(parts)),
        out_specs=ANY,
        scratch_shapes=[pltpu.VMEM((vectors, vectors), F32)] * 2
        + [pltpu.VMEM((PIECES, group, rows // PIECES), F32), pltpu.SemaphoreType.DMA((PIECES,))],
        compiler_params=params(LIMIT),
    )(current, gathered, *parts)


def solution(mesh):
    return jax.shard_map(
        per_device,
        mesh=mesh,
        in_specs=(
            P("col", "blk"),
            P("blk", None, None),
            P("blk", None, None),
            P("blk"),
            P("blk"),
            P("blk", None),
        ),
        out_specs=P("col", "blk"),
        check_vma=False,
    )
```
